32 devices in a mesh: wide: 16 (over z, x, core), narrow: 2 (over y).
Axes of the slice: x: 2, y: 2, z: 4, core: 2. Of those that a mesh axis runs over, the one named last changes fastest.
Arguments:
- hidden_in: bfloat16 [1024, 6144], P('wide', 'narrow'), may hold values from -6 to 6
- w_query: bfloat16 [6144, 6144], P('narrow', 'wide'), may hold values from -1 to 1
- w_key: bfloat16 [6144, 6144], P('narrow', 'wide'), may hold values from -1 to 1
- w_value: bfloat16 [6144, 6144], P('narrow', 'wide'), may hold values from -0.078125 to 0.078125
- qkv_bias: float32 [3, 6144], P(None, 'wide'), may hold values from -3 to 3
- w_up: bfloat16 [6144, 24576], P('narrow', 'wide'), may hold values from -0.078125 to 0.078125
- up_bias: float32 [24576], P('wide'), may hold values from -3 to 3
- w_attn_out: bfloat16 [6144, 6144], P('wide', 'narrow'), may hold values from -0.078125 to 0.078125
- w_down: bfloat16 [24576, 6144], P('wide', 'narrow'), may hold values from -0.0390625 to 0.0390625
- out_bias: float32 [6144], P('narrow'), may hold values from -3 to 3
- norm_gain: float32 [2, 6144], P(None, 'narrow'), may hold values from 0.5 to 1.5
- norm_bias: float32 [2, 6144], P(None, 'narrow'), may hold values from -2 to 2
- seq_lens: int32 [8], replicated, may hold values from 1 to 512, 1024 in all
- sink_count: int32 [8], replicated, may hold values from 1 to 32, as said below
- page_table: int32 [64], replicated, may hold values from 0 to 63, each once
Outputs:
- hidden_out: bfloat16 [1024, 6144], P('wide', 'narrow')
- paged_cache: bfloat16 [2, 64, 16, 6144], P(None, 'narrow', None, 'wide')
The draws below stay inside these ranges and needn't reach their ends.
Inputs may be any that keep to these rules, and one draw needn't show every extreme that they name: `seq_lens`: the lengths are positive, add up to 1024, and the longest is exactly 512. `sink_count`: some sequence has exactly 32 sink tokens. `page_table`: every slot is named by exactly one page.
All inputs are finite; a program needn't handle non-finite values.
Results may differ from the reference program's by a relative error of at most 0.02.
Values may be sent and summed in bfloat16 or wider, within the bound.
No kernel may reach another device: no remote copies, remote signals or barrier semaphores. Data moves between devices by JAX's collectives and lax.ppermute only.
A program may use at most 128 MiB of HBM per device.

```python
import math
import jax
import jax.numpy as jnp
import numpy as np
from jax import lax

D = 6144
HEADS = 64
HEAD_DIM = 96
FF = 24576
ROTARY = 24
SEQS = 8
PAGE = 16
TOKENS = 1024
WINDOW = 64
NPAGES = 64
N_NARROW = 2


def sign_vector(key, count):
    return jnp.where(jax.random.normal(key, (count,), jnp.float32) > 0.0, 1.0, -1.0).astype(jnp.float32)


def align_direction(key):
    return sign_vector(jax.random.fold_in(key, 101), D)


def head_pattern(key):
    signs = sign_vector(jax.random.fold_in(key, 102), D)
    column = jnp.arange(D, dtype=jnp.int32)
    kept = (column % HEAD_DIM >= ROTARY).astype(jnp.float32)
    return signs * kept


def strength_factor():
    ratio = (HEAD_DIM - ROTARY) / HEAD_DIM ** 0.5
    return (7.348469 / ratio) ** 0.5


def projection_draw(key, dense, strength):
    direction = align_direction(key)
    pattern = head_pattern(key)
    extra = direction[:, None] * pattern[None, :] * (strength * strength_factor() / D)
    return (dense / D ** 0.5 + extra).astype(jnp.bfloat16)


def draw_w_query(key, part):
    base_key = jax.random.fold_in(key, 201)
    dense = jnp.clip(jax.random.normal(base_key, (D, D), jnp.float32), -6.0, 6.0)
    return projection_draw(key, dense, 12.0)


def draw_w_key(key, part):
    base_key = jax.random.fold_in(key, 202)
    dense = jnp.clip(jax.random.normal(base_key, (D, D), jnp.float32), -6.0, 6.0)
    return projection_draw(key, dense, 3.5)


def draw_hidden_in(key, part):
    picked = jax.random.bernoulli(jax.random.fold_in(key, 301), 1.0 / 16.0, (TOKENS, 1))
    base = jnp.clip(jax.random.normal(jax.random.fold_in(key, 302), (TOKENS, D), jnp.float32), -6.0, 6.0)
    strength = jax.random.uniform(jax.random.fold_in(key, 304), (TOKENS, 1), jnp.float32, 0.75, 0.98)
    direction = align_direction(key)
    aligned = jnp.sqrt(1.0 - strength * strength) * base + strength * direction[None, :]
    column = jnp.arange(D, dtype=jnp.float32) / D
    column_scale = 1.0 + 2.0 * column
    column_offset = column
    drawn = jnp.clip(base * column_scale[None, :] + column_offset[None, :], -6.0, 6.0)
    return jnp.where(picked, aligned, drawn).astype(jnp.bfloat16)


def draw_sink_count(key, part):
    most = WINDOW // 2
    counts = jax.random.randint(jax.random.fold_in(key, 401), (SEQS,), 1, most + 1, jnp.int32)
    chosen = jax.random.randint(jax.random.fold_in(key, 402), (), 0, SEQS, jnp.int32)
    return jnp.where(jnp.arange(SEQS, dtype=jnp.int32) == chosen, jnp.int32(most), counts).astype(jnp.int32)


def level_of(rng, extent, shards, smallest, high):
    factor_of = 1.0
    for dim, shards_of in shards:
        steps = jax.random.uniform(jax.random.fold_in(jax.random.fold_in(rng, 6), dim), (shards_of,), jnp.float32, smallest / len(shards), high / len(shards))
        factor_of = factor_of * jnp.repeat(jnp.exp(steps), extent[dim] // shards_of).reshape((-1,) + (1,) * (len(extent) - 1 - dim))
    return factor_of


def profile(amount, total, limit, lean):
    weights = [(1 << 20) // math.isqrt(standing ** lean) + 1 for standing in range(2, amount + 1)]
    rest, holding = total - limit - (amount - 1), [1] * (amount - 1)
    while rest > 0:
        candidates = [i for i in range(amount - 1) if holding[i] < limit]
        pool, remaining = sum([weights[i] for i in candidates]), rest
        for i in candidates:
            addition = min(limit - holding[i], max(1, remaining * weights[i] // pool), rest)
            holding[i] = holding[i] + addition
            rest = rest - addition
    return np.array([limit] + holding)


def uneven(key, amount, total, bound, slope):
    if amount == 2:
        one = jax.random.randint(key, (), max(1, total - bound), min(bound, total - 1) + 1)
        return jnp.stack([one, total - one])
    sizes = jnp.asarray(profile(amount, total, bound, slope), jnp.int32)
    pairs = (amount - 1) // 2
    giver, receiver = sizes[1:1 + 2 * pairs:2], sizes[2:2 + 2 * pairs:2]
    slack = jnp.minimum(giver - 1, bound - receiver)
    moved = jax.random.randint(jax.random.fold_in(key, 1), (pairs,), 0, 1 << 20) % (slack + 1)
    sizes = sizes.at[1:1 + 2 * pairs:2].set(giver - moved).at[2:2 + 2 * pairs:2].set(receiver + moved)
    return sizes[jax.random.permutation(jax.random.fold_in(key, 2), amount)]


def gaussian(key, shape, width, most, pieces=(), kind=jnp.bfloat16):
    drawn = width * jax.random.normal(key, shape, jnp.float32)
    if pieces:
        drawn = drawn * level_of(key, shape, pieces, -0.22, 0.18)
    return jnp.clip(drawn, -most, most).astype(kind)


def setup_inputs(seed: int = 0) -> dict:
    streams_of = jax.random.split(jax.random.key(seed), 16)
    return {
        "hidden_in": draw_hidden_in(jax.random.fold_in(streams_of[15], 71), 0),
        "w_query": draw_w_query(jax.random.fold_in(streams_of[15], 71), 0),
        "w_key": draw_w_key(jax.random.fold_in(streams_of[15], 71), 0),
        "w_value": gaussian(streams_of[3], (D, D), D ** -0.5, 0.078125, ((0, 2), (1, 16))),
        "qkv_bias": gaussian(streams_of[4], (3, D), 0.5, 3.0, ((1, 16),), jnp.float32),
        "w_up": gaussian(streams_of[5], (D, FF), D ** -0.5, 0.078125, ((0, 2), (1, 16))),
        "up_bias": gaussian(streams_of[6], (FF,), 0.5, 3.0, ((0, 16),), jnp.float32),
        "w_attn_out": gaussian(streams_of[7], (D, D), D ** -0.5, 0.078125, ((0, 16), (1, 2))),
        "w_down": gaussian(streams_of[8], (FF, D), FF ** -0.5, 0.0390625, ((0, 16), (1, 2))),
        "out_bias": gaussian(streams_of[9], (D,), 0.5, 3.0, ((0, 2),), jnp.float32),
        "norm_gain": jnp.clip(1.0 + 0.1 * jax.random.normal(streams_of[10], (2, D), jnp.float32), 0.5, 1.5),
        "norm_bias": gaussian(streams_of[11], (2, D), 0.3, 2.0, ((1, 2),), jnp.float32),
        "seq_lens": uneven(streams_of[12], SEQS, TOKENS, TOKENS // 2, 2).astype(jnp.int32),
        "sink_count": draw_sink_count(jax.random.fold_in(streams_of[15], 71), 0),
        "page_table": jax.random.permutation(streams_of[14], NPAGES).astype(jnp.int32),
    }


def segment_info(token_index, seq_lens, sink_count):
    seq_ends = jnp.cumsum(seq_lens).astype(jnp.int32)
    seq_starts = (seq_ends - seq_lens).astype(jnp.int32)
    inside = (token_index[:, None] >= seq_starts[None, :]) & (token_index[:, None] < seq_ends[None, :])
    member = inside.astype(jnp.int32)
    seq_number = jnp.arange(seq_lens.shape[0], dtype=jnp.int32)
    segment = lax.optimization_barrier(jnp.sum(member * seq_number[None, :], axis=1)).astype(jnp.int32)
    position = (token_index - lax.optimization_barrier(jnp.sum(member * seq_starts[None, :], axis=1))).astype(jnp.int32)
    sink_limit = lax.optimization_barrier(jnp.sum(member * sink_count[None, :], axis=1)).astype(jnp.int32)
    return (segment, position, sink_limit)

def rotate(values, position):
    half_rot = ROTARY // 2
    freq_index = jnp.arange(half_rot, dtype=jnp.float32)
    inverse = jnp.power(jnp.float32(10000.0), -2.0 * freq_index / ROTARY)
    angles = position.astype(jnp.float32)[:, None] * inverse[None, :]
    cosine = jnp.cos(angles)[:, None, :]
    sine_part = jnp.sin(angles)[:, None, :]
    first_half = values[..., :half_rot]
    second_half = values[..., half_rot:ROTARY]
    return jnp.concatenate([first_half * cosine - second_half * sine_part, second_half * cosine + first_half * sine_part, values[..., ROTARY:]], axis=-1)

def blocked(normed, weight):
    width_part = D // N_NARROW
    total = jnp.zeros((normed.shape[0], weight.shape[1]), jnp.float32)
    for block in range(N_NARROW):
        section = normed[:, block * width_part:(block + 1) * width_part].astype(jnp.float32)
        weight_rows = weight[block * width_part:(block + 1) * width_part].astype(jnp.float32)
        partial_term = jnp.dot(section, weight_rows, precision=lax.Precision.HIGHEST).astype(jnp.bfloat16)
        partial_term = lax.optimization_barrier(partial_term)
        total = total + partial_term.astype(jnp.float32)
    return total

def reference(hidden_in, w_query, w_key, w_value, qkv_bias, w_up, up_bias, w_attn_out, w_down, out_bias, norm_gain, norm_bias, seq_lens, sink_count, page_table):
    as_float = hidden_in.astype(jnp.float32)
    average = lax.optimization_barrier(jnp.sum(as_float, axis=1)) / D
    variance = lax.optimization_barrier(jnp.sum(as_float * as_float, axis=1)) / D - average * average
    scaled = (as_float - average[:, None]) * lax.rsqrt(variance + 1e-05)[:, None]
    attn_normed = (scaled * norm_gain[0] + norm_bias[0]).astype(jnp.bfloat16)
    mlp_normed = (scaled * norm_gain[1] + norm_bias[1]).astype(jnp.bfloat16)
    query_sum = blocked(attn_normed, w_query)
    key_sum = blocked(attn_normed, w_key)
    value_sum = blocked(attn_normed, w_value)
    unit_sum = blocked(mlp_normed, w_up)
    token_index = jnp.arange(TOKENS, dtype=jnp.int32)
    segment, position, sink_limit = segment_info(token_index, seq_lens, sink_count)
    queries = rotate((query_sum + qkv_bias[0]).reshape(TOKENS, HEADS, HEAD_DIM), position).astype(jnp.bfloat16)
    keys = rotate((key_sum + qkv_bias[1]).reshape(TOKENS, HEADS, HEAD_DIM), position).astype(jnp.bfloat16)
    values = (value_sum + qkv_bias[2]).astype(jnp.bfloat16).reshape(TOKENS, HEADS, HEAD_DIM)
    hidden_units = jax.nn.gelu(unit_sum + up_bias, approximate=False).astype(jnp.bfloat16)
    allowed = (segment[:, None] == segment[None, :]) & (position[None, :] <= position[:, None])
    allowed = allowed & ((position[:, None] - position[None, :] < WINDOW) | (position[None, :] < sink_limit[:, None]))
    scale = 1.0 / HEAD_DIM ** 0.5

    def one_head(operands):
        query_head, key_head, value_head = operands
        scores = jnp.dot(query_head.astype(jnp.float32), key_head.astype(jnp.float32).T, precision=lax.Precision.HIGHEST) * scale
        masked = jnp.where(allowed, scores, jnp.float32(-1e+30))
        top_score = lax.optimization_barrier(jnp.max(masked, axis=1, keepdims=True))
        weights = jnp.exp(masked - top_score)
        probs = (weights / lax.optimization_barrier(jnp.sum(weights, axis=1, keepdims=True))).astype(jnp.bfloat16)
        return jnp.dot(probs.astype(jnp.float32), value_head.astype(jnp.float32), precision=lax.Precision.HIGHEST).astype(jnp.bfloat16)
    per_head = lax.map(one_head, (jnp.transpose(queries, (1, 0, 2)), jnp.transpose(keys, (1, 0, 2)), jnp.transpose(values, (1, 0, 2))))
    attended = jnp.transpose(per_head, (1, 0, 2)).reshape(TOKENS, D)
    branch_total = jnp.dot(attended.astype(jnp.float32), w_attn_out.astype(jnp.float32), precision=lax.Precision.HIGHEST)
    branch_total = branch_total + jnp.dot(hidden_units.astype(jnp.float32), w_down.astype(jnp.float32), precision=lax.Precision.HIGHEST)
    hidden_out = (as_float + branch_total + out_bias).astype(jnp.bfloat16)
    stacked = jnp.stack([keys.reshape(NPAGES, PAGE, D), values.reshape(NPAGES, PAGE, D)])
    paged_cache = jnp.zeros_like(stacked).at[:, page_table].set(stacked)
    return (hidden_out, paged_cache)
```

```python
import jax
import jax.numpy as jnp
from jax import lax
from jax.sharding import PartitionSpec as P

D = 6144
HEAD_DIM = 96
ROTARY = 24
PAGE = 16


def segment_info(token_index, seq_lens, sink_count):
    seq_ends = jnp.cumsum(seq_lens)
    seq_starts = seq_ends - seq_lens
    inside = (token_index[:, None] >= seq_starts[None, :]) & (
        token_index[:, None] < seq_ends[None, :]
    )
    member = inside.astype(jnp.int32)
    seq_number = jnp.arange(seq_lens.shape[0], dtype=jnp.int32)
    segment = jnp.sum(member * seq_number[None, :], axis=1)
    position = token_index - jnp.sum(member * seq_starts[None, :], axis=1)
    sink_limit = jnp.sum(member * sink_count[None, :], axis=1)
    return (segment, position, sink_limit)


def rotate(values, position):
    half_rot = ROTARY // 2
    freq_index = jnp.arange(half_rot, dtype=jnp.float32)
    inverse = jnp.power(jnp.float32(10000.0), -2.0 * freq_index / ROTARY)
    angles = position.astype(jnp.float32)[:, None] * inverse[None, :]
    cosine = jnp.cos(angles)[:, None, :]
    sine_part = jnp.sin(angles)[:, None, :]
    first_half = values[..., :half_rot]
    second_half = values[..., half_rot:ROTARY]
    return jnp.concatenate(
        [
            first_half * cosine - second_half * sine_part,
            second_half * cosine + first_half * sine_part,
            values[..., ROTARY:],
        ],
        axis=-1,
    )


def local_generic(
    hidden_in,
    w_query,
    w_key,
    w_value,
    qkv_bias,
    w_up,
    up_bias,
    w_attn_out,
    w_down,
    out_bias,
    norm_gain,
    norm_bias,
    seq_lens,
    sink_count,
    page_table,
):
    wide_count = lax.axis_size("wide")
    narrow_count = lax.axis_size("narrow")
    narrow_index = lax.axis_index("narrow")
    tok_local, feat_local = hidden_in.shape
    sub_rows = tok_local // narrow_count
    total_tokens = tok_local * wide_count
    query_rows = wide_count * sub_rows
    head_cols = w_query.shape[1]
    heads_local = head_cols // HEAD_DIM
    as_float = hidden_in.astype(jnp.float32)
    partial_sum = jnp.sum(as_float, axis=1)
    partial_square = jnp.sum(as_float * as_float, axis=1)
    total_sum, total_square = lax.psum((partial_sum, partial_square), "narrow")
    average = total_sum / D
    variance = total_square / D - average * average
    scaled = (as_float - average[:, None]) * lax.rsqrt(variance + 1e-05)[:, None]
    attn_normed = (scaled * norm_gain[0] + norm_bias[0]).astype(jnp.bfloat16)
    mlp_normed = (scaled * norm_gain[1] + norm_bias[1]).astype(jnp.bfloat16)
    stacked = jnp.stack([attn_normed, mlp_normed]).reshape(2, narrow_count, sub_rows, feat_local)
    gathered = lax.all_gather(stacked, "wide", axis=2, tiled=True).reshape(
        2, total_tokens, feat_local
    )
    local_order = jnp.arange(query_rows, dtype=jnp.int32)
    local_tokens = (
        local_order // sub_rows * tok_local + narrow_index * sub_rows + local_order % sub_rows
    )
    local_seg, local_pos, local_sink = segment_info(local_tokens, seq_lens, sink_count)
    all_order = jnp.arange(total_tokens, dtype=jnp.int32)
    all_tokens = (
        all_order % query_rows // sub_rows * tok_local
        + all_order // query_rows * sub_rows
        + all_order % sub_rows
    )
    all_seg, all_pos, all_sink = segment_info(all_tokens, seq_lens, sink_count)
    qkv_weight = jnp.concatenate([w_query, w_key, w_value], axis=1)
    attn_part = gathered[0]
    mlp_part = gathered[1]
    summed = lax.psum_scatter(
        jnp.concatenate(
            [
                jnp.dot(attn_part, qkv_weight, preferred_element_type=jnp.float32),
                jnp.dot(mlp_part, w_up, preferred_element_type=jnp.float32),
            ],
            axis=1,
        ).astype(jnp.bfloat16),
        "narrow",
        scatter_dimension=0,
        tiled=True,
    ).astype(jnp.float32)
    query_sum = summed[:, :head_cols]
    key_sum = summed[:, head_cols : 2 * head_cols]
    value_sum = summed[:, 2 * head_cols : 3 * head_cols]
    unit_sum = summed[:, 3 * head_cols :]
    keys_local = (
        rotate((key_sum + qkv_bias[1]).reshape(query_rows, heads_local, HEAD_DIM), local_pos)
        .astype(jnp.bfloat16)
        .reshape(query_rows, head_cols)
    )
    values_local = (value_sum + qkv_bias[2]).astype(jnp.bfloat16)
    all_keys, all_values = (
        lax.all_gather(keys_local, "narrow", axis=0, tiled=True),
        lax.all_gather(values_local, "narrow", axis=0, tiled=True),
    )
    queries = rotate(
        (query_sum + qkv_bias[0]).reshape(query_rows, heads_local, HEAD_DIM), local_pos
    ).astype(jnp.bfloat16)
    hidden_units = jax.nn.gelu(unit_sum + up_bias, approximate=False).astype(jnp.bfloat16)
    window_span = total_tokens // 16
    allowed = (local_seg[:, None] == all_seg[None, :]) & (all_pos[None, :] <= local_pos[:, None])
    allowed = allowed & (
        (local_pos[:, None] - all_pos[None, :] < window_span)
        | (all_pos[None, :] < local_sink[:, None])
    )
    key_heads = all_keys.reshape(total_tokens, heads_local, HEAD_DIM)
    value_heads = all_values.reshape(total_tokens, heads_local, HEAD_DIM)
    scores = jnp.einsum("qhd,khd->hqk", queries, key_heads, preferred_element_type=jnp.float32) * (
        1.0 / HEAD_DIM**0.5
    )
    masked = jnp.where(allowed[None], scores, jnp.float32(-1e30))
    top_score = jnp.max(masked, axis=2, keepdims=True)
    weights = jnp.exp(masked - top_score)
    probs = (weights / jnp.sum(weights, axis=2, keepdims=True)).astype(jnp.bfloat16)
    attended = (
        jnp.einsum("hqk,khd->qhd", probs, value_heads, preferred_element_type=jnp.float32)
        .astype(jnp.bfloat16)
        .reshape(query_rows, head_cols)
    )
    full_out, full_down = (
        lax.all_gather(w_attn_out, "narrow", axis=1, tiled=True),
        lax.all_gather(w_down, "narrow", axis=1, tiled=True),
    )
    attn_part = attended
    own_rows = lax.psum_scatter(
        (
            jnp.dot(attn_part, full_out, preferred_element_type=jnp.float32)
            + jnp.dot(hidden_units, full_down, preferred_element_type=jnp.float32)
        ).astype(jnp.bfloat16),
        "wide",
        scatter_dimension=0,
        tiled=True,
    ).astype(jnp.float32)
    combined = lax.all_to_all(
        own_rows.astype(jnp.bfloat16), "narrow", split_axis=1, concat_axis=0, tiled=True
    ).astype(own_rows.dtype)
    hidden_out = (as_float + combined + out_bias).astype(jnp.bfloat16)
    pages_local = page_table.shape[0] // narrow_count
    slot_ids = narrow_index * pages_local + jnp.arange(pages_local, dtype=jnp.int32)
    matches = (page_table[None, :] == slot_ids[:, None]).astype(jnp.int32)
    source_page = jnp.sum(
        matches * jnp.arange(page_table.shape[0], dtype=jnp.int32)[None, :], axis=1
    )
    token_ids = (source_page[:, None] * PAGE + jnp.arange(PAGE, dtype=jnp.int32)[None, :]).reshape(
        -1
    )
    gather_rows = (
        token_ids % tok_local // sub_rows * query_rows
        + token_ids // tok_local * sub_rows
        + token_ids % sub_rows
    )
    cache_keys = jnp.take(all_keys, gather_rows, axis=0).reshape(pages_local, PAGE, head_cols)
    cache_values = jnp.take(all_values, gather_rows, axis=0).reshape(pages_local, PAGE, head_cols)
    paged_cache = jnp.stack([cache_keys, cache_values])
    return (hidden_out, paged_cache)


CHIP_RING = (0, 2, 4, 6, 7, 5, 3, 1)
CHIP_POS = (0, 7, 1, 6, 2, 5, 3, 4)


def local_ring(
    hidden_in,
    w_query,
    w_key,
    w_value,
    qkv_bias,
    w_up,
    up_bias,
    w_attn_out,
    w_down,
    out_bias,
    norm_gain,
    norm_bias,
    seq_lens,
    sink_count,
    page_table,
):
    wide_count = lax.axis_size("wide")
    wide_index = lax.axis_index("wide")
    n = lax.axis_index("narrow")
    chips = wide_count // 2
    rows, feat = hidden_in.shape
    total_tokens = rows * wide_count
    head_cols = w_query.shape[1]
    half = head_cols // 2
    heads_half = half // HEAD_DIM
    chip, core = wide_index // 2, wide_index % 2
    place = jnp.asarray(CHIP_POS, jnp.int32)[chip]
    ring = jnp.asarray(CHIP_RING, jnp.int32)
    step_sign = 2 * core - 1

    ring_pairs, swap_pairs = [], []
    for p in range(chips):
        here, after = CHIP_RING[p], CHIP_RING[(p + 1) % chips]
        ring_pairs.append((2 * here, 2 * after))
        ring_pairs.append((2 * after + 1, 2 * here + 1))
        swap_pairs.append((2 * here, 2 * here + 1))
        swap_pairs.append((2 * here + 1, 2 * here))
    along = lambda v: lax.ppermute(v, "wide", ring_pairs)
    swap = lambda v: lax.ppermute(v, "wide", swap_pairs)
    cross = lambda v: lax.ppermute(v, "narrow", [(0, 1), (1, 0)])

    owners = []
    for s in range(chips):
        owners.append(ring[(place + step_sign * s + chips) % chips] * 2 + core)
        owners.append(ring[(place - step_sign * s + chips) % chips] * 2 + 1 - core)
    owners = jnp.stack(owners)
    token_ids = (owners[:, None] * rows + jnp.arange(rows, dtype=jnp.int32)[None, :]).reshape(-1)

    as_float = hidden_in.astype(jnp.float32)
    stats = jnp.stack([jnp.sum(as_float, axis=1), jnp.sum(as_float * as_float, axis=1)])
    stats = stats + cross(stats)
    average = stats[0] / D
    variance = stats[1] / D - average * average
    stats = jnp.stack([average, lax.rsqrt(variance + 1e-05)])
    all_stats = lax.all_gather(stats, "wide", axis=0)

    blocks = [hidden_in]
    for s in range(1, chips):
        blocks.append(along(blocks[-1]))
    group = 2
    groups = chips // group
    row_group = 2 * group * rows

    def halves(weight):
        return (
            lax.dynamic_slice_in_dim(weight, (1 - n) * half, half, 1),
            lax.dynamic_slice_in_dim(weight, n * half, half, 1),
        )

    parts = [halves(w) for w in (w_query, w_key, w_value)]
    w_send = jnp.concatenate([p[0] for p in parts], axis=1)
    w_mine = jnp.concatenate([p[1] for p in parts], axis=1)
    w_send, w_mine = lax.optimization_barrier((w_send, w_mine))

    qkv_rows, up_rows = [], []
    for g in range(groups):
        mine = jnp.stack(blocks[g * group : (g + 1) * group])
        theirs = swap(mine)
        tokens_g = jnp.stack([mine, theirs], axis=1).reshape(row_group, feat).astype(jnp.float32)
        own = owners[2 * group * g : 2 * group * (g + 1)]
        stats_g = jnp.take(all_stats, own, axis=0)
        average_g = stats_g[:, 0].reshape(-1, 1)
        scale_g = stats_g[:, 1].reshape(-1, 1)
        scaled = (tokens_g - average_g) * scale_g
        attn_normed = (scaled * norm_gain[0] + norm_bias[0]).astype(jnp.bfloat16)
        mlp_normed = (scaled * norm_gain[1] + norm_bias[1]).astype(jnp.bfloat16)
        attn_normed, mlp_normed = lax.optimization_barrier((attn_normed, mlp_normed))
        qkv_send = jnp.dot(attn_normed, w_send, preferred_element_type=jnp.float32).astype(jnp.bfloat16)
        qkv_got = cross(qkv_send)
        qkv_mine = jnp.dot(attn_normed, w_mine, preferred_element_type=jnp.float32).astype(jnp.bfloat16)
        qkv_rows.append((qkv_mine, qkv_got))
        up_mine = jnp.dot(mlp_normed, w_up, preferred_element_type=jnp.float32).astype(jnp.bfloat16)
        up_rows.append((up_mine, cross(up_mine)))

    qkv = jnp.concatenate(
        [a.astype(jnp.float32) + b.astype(jnp.float32) for a, b in qkv_rows], axis=0
    )
    bias_half = lax.dynamic_slice_in_dim(qkv_bias, n * half, half, 1)
    seg, pos, sink = segment_info(token_ids, seq_lens, sink_count)
    heads = lambda v: v.reshape(total_tokens, heads_half, HEAD_DIM)
    queries = rotate(heads(qkv[:, :half] + bias_half[0]), pos).astype(jnp.bfloat16)
    keys = rotate(heads(qkv[:, half : 2 * half] + bias_half[1]), pos).astype(jnp.bfloat16)
    values = heads(qkv[:, 2 * half :] + bias_half[2]).astype(jnp.bfloat16)
    window_span = total_tokens // 16
    allowed = (seg[:, None] == seg[None, :]) & (pos[None, :] <= pos[:, None])
    allowed = allowed & (
        (pos[:, None] - pos[None, :] < window_span) | (pos[None, :] < sink[:, None])
    )
    scores = jnp.einsum("qhd,khd->hqk", queries, keys, preferred_element_type=jnp.float32) * (
        1.0 / HEAD_DIM**0.5
    )
    masked = jnp.where(allowed[None], scores, jnp.float32(-1e30))
    top_score = jnp.max(masked, axis=2, keepdims=True)
    weights = jnp.exp(masked - top_score)
    probs = (weights / jnp.sum(weights, axis=2, keepdims=True)).astype(jnp.bfloat16)
    att_mine = (
        jnp.einsum("hqk,khd->qhd", probs, values, preferred_element_type=jnp.float32)
        .astype(jnp.bfloat16)
        .reshape(total_tokens, half)
    )
    att_got = cross(att_mine)
    side = lambda a, b: jnp.concatenate(
        [jnp.where(n == 0, a, b), jnp.where(n == 0, b, a)], axis=-1
    )
    attended = side(att_mine, att_got)

    sums = []
    for g in range(groups):
        a, b = up_rows[g]
        units = a.astype(jnp.float32) + b.astype(jnp.float32) + up_bias
        units = (units * (1.0 + lax.erf(units * (0.5**0.5))) * 0.5).astype(jnp.bfloat16)
        units = lax.optimization_barrier(units)
        out = jnp.dot(units, w_down, preferred_element_type=jnp.float32) + jnp.dot(
            attended[g * row_group : (g + 1) * row_group],
            w_attn_out,
            preferred_element_type=jnp.float32,
        )
        out = out.astype(jnp.bfloat16).reshape(group, 2, rows, feat)
        got = swap(out[:, 1])
        for i in range(group):
            sums.append(out[i, 0].astype(jnp.float32) + got[i].astype(jnp.float32))
    running = sums[1].astype(jnp.bfloat16)
    for s in range(2, chips):
        running = (along(running).astype(jnp.float32) + sums[s]).astype(jnp.bfloat16)
    own_sum = along(running).astype(jnp.float32) + sums[0]
    hidden_out = (as_float + own_sum + out_bias).astype(jnp.bfloat16)

    pages = page_table.shape[0]
    per_device = pages // 2
    slots = (jnp.arange(pages, dtype=jnp.int32) + n * per_device) % pages
    page_of_slot = jnp.sum(
        (page_table[None, :] == slots[:, None]).astype(jnp.int32)
        * jnp.arange(pages, dtype=jnp.int32)[None, :],
        axis=1,
    )
    page_held = token_ids[::PAGE] // PAGE
    held_at = jnp.sum(
        (page_held[None, :] == page_of_slot[:, None]).astype(jnp.int32)
        * jnp.arange(pages, dtype=jnp.int32)[None, :],
        axis=1,
    )
    both = jnp.concatenate(
        [keys.reshape(pages, PAGE, half), values.reshape(pages, PAGE, half)], axis=2
    )
    paged = jnp.take(both, held_at, axis=0)
    cache_mine = paged[:per_device]
    cache_got = cross(paged[per_device:])
    paged_cache = jnp.stack(
        [
            side(cache_mine[..., :half], cache_got[..., :half]),
            side(cache_mine[..., half:], cache_got[..., half:]),
        ]
    )
    return (hidden_out, paged_cache)


def solution(mesh):
    in_specs = (
        P("wide", "narrow"),
        P("narrow", "wide"),
        P("narrow", "wide"),
        P("narrow", "wide"),
        P(None, "wide"),
        P("narrow", "wide"),
        P("wide"),
        P("wide", "narrow"),
        P("wide", "narrow"),
        P("narrow"),
        P(None, "narrow"),
        P(None, "narrow"),
        P(),
        P(),
        P(),
    )
    out_specs = (P("wide", "narrow"), P(None, "narrow", None, "wide"))
    ringed = mesh.shape["wide"] == 2 * len(CHIP_RING) and mesh.shape["narrow"] == 2
    local = local_ring if ringed else local_generic
    return jax.shard_map(local, mesh=mesh, in_specs=in_specs, out_specs=out_specs, check_vma=False)
```

```python
import functools

import jax
import jax.numpy as jnp
import numpy as np
from jax import lax
from jax.experimental import pallas as pl
from jax.experimental.pallas import tpu as pltpu
from jax.sharding import PartitionSpec as P

D = 6144
HEAD_DIM = 96
ROTARY = 24
PAGE = 16


def segment_info(token_index, seq_lens, sink_count):
    seq_ends = jnp.cumsum(seq_lens)
    seq_starts = seq_ends - seq_lens
    inside = (token_index[:, None] >= seq_starts[None, :]) & (
        token_index[:, None] < seq_ends[None, :]
    )
    member = inside.astype(jnp.int32)
    seq_number = jnp.arange(seq_lens.shape[0], dtype=jnp.int32)
    segment = jnp.sum(member * seq_number[None, :], axis=1)
    position = token_index - jnp.sum(member * seq_starts[None, :], axis=1)
    sink_limit = jnp.sum(member * sink_count[None, :], axis=1)
    return (segment, position, sink_limit)


def rotate(values, position):
    half_rot = ROTARY // 2
    freq_index = jnp.arange(half_rot, dtype=jnp.float32)
    inverse = jnp.power(jnp.float32(10000.0), -2.0 * freq_index / ROTARY)
    angles = position.astype(jnp.float32)[:, None] * inverse[None, :]
    cosine = jnp.cos(angles)[:, None, :]
    sine_part = jnp.sin(angles)[:, None, :]
    first_half = values[..., :half_rot]
    second_half = values[..., half_rot:ROTARY]
    return jnp.concatenate(
        [
            first_half * cosine - second_half * sine_part,
            second_half * cosine + first_half * sine_part,
            values[..., ROTARY:],
        ],
        axis=-1,
    )


def local_generic(
    hidden_in,
    w_query,
    w_key,
    w_value,
    qkv_bias,
    w_up,
    up_bias,
    w_attn_out,
    w_down,
    out_bias,
    norm_gain,
    norm_bias,
    seq_lens,
    sink_count,
    page_table,
):
    wide_count = lax.axis_size("wide")
    narrow_count = lax.axis_size("narrow")
    narrow_index = lax.axis_index("narrow")
    tok_local, feat_local = hidden_in.shape
    sub_rows = tok_local // narrow_count
    total_tokens = tok_local * wide_count
    query_rows = wide_count * sub_rows
    head_cols = w_query.shape[1]
    heads_local = head_cols // HEAD_DIM
    as_float = hidden_in.astype(jnp.float32)
    partial_sum = jnp.sum(as_float, axis=1)
    partial_square = jnp.sum(as_float * as_float, axis=1)
    total_sum, total_square = lax.psum((partial_sum, partial_square), "narrow")
    average = total_sum / D
    variance = total_square / D - average * average
    scaled = (as_float - average[:, None]) * lax.rsqrt(variance + 1e-05)[:, None]
    attn_normed = (scaled * norm_gain[0] + norm_bias[0]).astype(jnp.bfloat16)
    mlp_normed = (scaled * norm_gain[1] + norm_bias[1]).astype(jnp.bfloat16)
    stacked = jnp.stack([attn_normed, mlp_normed]).reshape(2, narrow_count, sub_rows, feat_local)
    gathered = lax.all_gather(stacked, "wide", axis=2, tiled=True).reshape(
        2, total_tokens, feat_local
    )
    local_order = jnp.arange(query_rows, dtype=jnp.int32)
    local_tokens = (
        local_order // sub_rows * tok_local + narrow_index * sub_rows + local_order % sub_rows
    )
    local_seg, local_pos, local_sink = segment_info(local_tokens, seq_lens, sink_count)
    all_order = jnp.arange(total_tokens, dtype=jnp.int32)
    all_tokens = (
        all_order % query_rows // sub_rows * tok_local
        + all_order // query_rows * sub_rows
        + all_order % sub_rows
    )
    all_seg, all_pos, all_sink = segment_info(all_tokens, seq_lens, sink_count)
    qkv_weight = jnp.concatenate([w_query, w_key, w_value], axis=1)
    attn_part = gathered[0]
    mlp_part = gathered[1]
    summed = lax.psum_scatter(
        jnp.concatenate(
            [
                jnp.dot(attn_part, qkv_weight, preferred_element_type=jnp.float32),
                jnp.dot(mlp_part, w_up, preferred_element_type=jnp.float32),
            ],
            axis=1,
        ).astype(jnp.bfloat16),
        "narrow",
        scatter_dimension=0,
        tiled=True,
    ).astype(jnp.float32)
    query_sum = summed[:, :head_cols]
    key_sum = summed[:, head_cols : 2 * head_cols]
    value_sum = summed[:, 2 * head_cols : 3 * head_cols]
    unit_sum = summed[:, 3 * head_cols :]
    keys_local = (
        rotate((key_sum + qkv_bias[1]).reshape(query_rows, heads_local, HEAD_DIM), local_pos)
        .astype(jnp.bfloat16)
        .reshape(query_rows, head_cols)
    )
    values_local = (value_sum + qkv_bias[2]).astype(jnp.bfloat16)
    all_keys, all_values = (
        lax.all_gather(keys_local, "narrow", axis=0, tiled=True),
        lax.all_gather(values_local, "narrow", axis=0, tiled=True),
    )
    queries = rotate(
        (query_sum + qkv_bias[0]).reshape(query_rows, heads_local, HEAD_DIM), local_pos
    ).astype(jnp.bfloat16)
    hidden_units = jax.nn.gelu(unit_sum + up_bias, approximate=False).astype(jnp.bfloat16)
    window_span = total_tokens // 16
    allowed = (local_seg[:, None] == all_seg[None, :]) & (all_pos[None, :] <= local_pos[:, None])
    allowed = allowed & (
        (local_pos[:, None] - all_pos[None, :] < window_span)
        | (all_pos[None, :] < local_sink[:, None])
    )
    key_heads = all_keys.reshape(total_tokens, heads_local, HEAD_DIM)
    value_heads = all_values.reshape(total_tokens, heads_local, HEAD_DIM)
    scores = jnp.einsum("qhd,khd->hqk", queries, key_heads, preferred_element_type=jnp.float32) * (
        1.0 / HEAD_DIM**0.5
    )
    masked = jnp.where(allowed[None], scores, jnp.float32(-1e30))
    top_score = jnp.max(masked, axis=2, keepdims=True)
    weights = jnp.exp(masked - top_score)
    probs = (weights / jnp.sum(weights, axis=2, keepdims=True)).astype(jnp.bfloat16)
    attended = (
        jnp.einsum("hqk,khd->qhd", probs, value_heads, preferred_element_type=jnp.float32)
        .astype(jnp.bfloat16)
        .reshape(query_rows, head_cols)
    )
    full_out, full_down = (
        lax.all_gather(w_attn_out, "narrow", axis=1, tiled=True),
        lax.all_gather(w_down, "narrow", axis=1, tiled=True),
    )
    attn_part = attended
    own_rows = lax.psum_scatter(
        (
            jnp.dot(attn_part, full_out, preferred_element_type=jnp.float32)
            + jnp.dot(hidden_units, full_down, preferred_element_type=jnp.float32)
        ).astype(jnp.bfloat16),
        "wide",
        scatter_dimension=0,
        tiled=True,
    ).astype(jnp.float32)
    combined = lax.all_to_all(
        own_rows.astype(jnp.bfloat16), "narrow", split_axis=1, concat_axis=0, tiled=True
    ).astype(own_rows.dtype)
    hidden_out = (as_float + combined + out_bias).astype(jnp.bfloat16)
    pages_local = page_table.shape[0] // narrow_count
    slot_ids = narrow_index * pages_local + jnp.arange(pages_local, dtype=jnp.int32)
    matches = (page_table[None, :] == slot_ids[:, None]).astype(jnp.int32)
    source_page = jnp.sum(
        matches * jnp.arange(page_table.shape[0], dtype=jnp.int32)[None, :], axis=1
    )
    token_ids = (source_page[:, None] * PAGE + jnp.arange(PAGE, dtype=jnp.int32)[None, :]).reshape(
        -1
    )
    gather_rows = (
        token_ids % tok_local // sub_rows * query_rows
        + token_ids // tok_local * sub_rows
        + token_ids % sub_rows
    )
    cache_keys = jnp.take(all_keys, gather_rows, axis=0).reshape(pages_local, PAGE, head_cols)
    cache_values = jnp.take(all_values, gather_rows, axis=0).reshape(pages_local, PAGE, head_cols)
    paged_cache = jnp.stack([cache_keys, cache_values])
    return (hidden_out, paged_cache)


CHIP_RING = (0, 2, 4, 6, 7, 5, 3, 1)
CHIPS = len(CHIP_RING)
GROUPS = ((0,), (1, 2), (3, 4), (5, 6), (7,))
STAT = 128
HEAD_PAD = 128
MIB = 1 << 20
VMEM = pl.BlockSpec(memory_space=pltpu.VMEM)
ANY = pl.BlockSpec(memory_space=pl.ANY)
SMEM = pl.BlockSpec(memory_space=pltpu.SMEM)


def owner_table():
    table = np.zeros((2 * CHIPS, 2 * CHIPS), np.int32)
    for place, chip in enumerate(CHIP_RING):
        for core in range(2):
            sign = 2 * core - 1
            order = []
            for group in GROUPS:
                order += [CHIP_RING[(place + sign * s) % CHIPS] * 2 + core for s in group]
                order += [CHIP_RING[(place - sign * s) % CHIPS] * 2 + 1 - core for s in group]
            table[2 * chip + core] = order
    return table


def sums_kernel(x_ref, out_ref):
    x = x_ref[...].astype(jnp.float32)
    first = jnp.sum(x, axis=1, keepdims=True)
    second = jnp.sum(x * x, axis=1, keepdims=True)
    lane = lax.broadcasted_iota(jnp.int32, out_ref.shape, 1)
    out_ref[...] = jnp.where(lane == 0, first, jnp.where(lane == 1, second, 0.0))


def block_kernel(x_ref, here_ref, there_ref, out_ref):
    feat = x_ref.shape[1]
    total = here_ref[...] + there_ref[...]
    average = total[:, 0:1] / D
    variance = total[:, 1:2] / D - average * average
    scale = lax.rsqrt(variance + 1e-05)
    lane = lax.broadcasted_iota(jnp.int32, (x_ref.shape[0], STAT), 1)
    tail = jnp.zeros((x_ref.shape[0], STAT), jnp.float32)
    for start, value in ((0, average), (3, scale)):
        for term in range(3):
            piece = value.astype(jnp.bfloat16).astype(jnp.float32)
            tail = jnp.where(lane == start + term, piece, tail)
            value = value - piece
    out_ref[:, :feat] = x_ref[...]
    out_ref[:, feat:] = tail.astype(jnp.bfloat16)


def project_kernel(count, n_ref, gain_ref, bias_ref, wq_ref, wk_ref, wv_ref, wu_ref, *refs):
    blocks = refs[:count]
    send_ref, mine_ref, up_ref, attn, mlp, wq, wk, wv, wu, sems = refs[count:]
    rows = blocks[0].shape[0]
    feat = wq.shape[0]
    cols = wq.shape[1]
    half = cols // 2
    tiles = wu.shape[0]
    copies = [
        pltpu.make_async_copy(src, dst, sems.at[i])
        for i, (src, dst) in enumerate(((wq_ref, wq), (wk_ref, wk), (wv_ref, wv)))
    ]
    copies += [
        pltpu.make_async_copy(wu_ref.at[:, t * cols : (t + 1) * cols], wu.at[t], sems.at[3 + t])
        for t in range(tiles)
    ]
    for copy in copies:
        copy.start()
    step = 512
    for b in range(count):
        tail = blocks[b][:, feat:].astype(jnp.float32)
        average = tail[:, 0:1] + tail[:, 1:2] + tail[:, 2:3]
        scale = tail[:, 3:4] + tail[:, 4:5] + tail[:, 5:6]
        for c in range(0, feat, step):
            at = slice(c, c + step)
            scaled = (blocks[b][:, at].astype(jnp.float32) - average) * scale
            here = slice(b * rows, (b + 1) * rows)
            attn[here, at] = (scaled * gain_ref[0:1, at] + bias_ref[0:1, at]).astype(jnp.bfloat16)
            mlp[here, at] = (scaled * gain_ref[1:2, at] + bias_ref[1:2, at]).astype(jnp.bfloat16)
    low, high = [], []
    for i, weight in enumerate((wq, wk, wv)):
        copies[i].wait()
        part = jnp.dot(attn[...], weight[...], preferred_element_type=jnp.float32)
        low.append(part[:, :half])
        high.append(part[:, half:])
    low = jnp.concatenate(low, axis=1).astype(jnp.bfloat16)
    high = jnp.concatenate(high, axis=1).astype(jnp.bfloat16)
    first = n_ref[0] == 0
    send_ref[...] = jnp.where(first, high, low)
    mine_ref[...] = jnp.where(first, low, high)
    for t in range(tiles):
        copies[3 + t].wait()
        part = jnp.dot(mlp[...], wu[t], preferred_element_type=jnp.float32)
        up_ref[:, t * cols : (t + 1) * cols] = part.astype(jnp.bfloat16)


def project(n, gain, bias, wq, wk, wv, wu, blocks):
    count = len(blocks)
    rows = blocks[0].shape[0] * count
    feat, cols = wq.shape
    hidden = wu.shape[1]
    tiles = hidden // cols
    return pl.pallas_call(
        functools.partial(project_kernel, count),
        out_shape=(
            jax.ShapeDtypeStruct((rows, 3 * cols // 2), jnp.bfloat16),
            jax.ShapeDtypeStruct((rows, 3 * cols // 2), jnp.bfloat16),
            jax.ShapeDtypeStruct((rows, hidden), jnp.bfloat16),
        ),
        in_specs=[SMEM, VMEM, VMEM, ANY, ANY, ANY, ANY] + [VMEM] * count,
        out_specs=(VMEM, VMEM, VMEM),
        scratch_shapes=[
            pltpu.VMEM((rows, feat), jnp.bfloat16),
            pltpu.VMEM((rows, feat), jnp.bfloat16),
            pltpu.VMEM((feat, cols), jnp.bfloat16),
            pltpu.VMEM((feat, cols), jnp.bfloat16),
            pltpu.VMEM((feat, cols), jnp.bfloat16),
            pltpu.VMEM((tiles, feat, cols), jnp.bfloat16),
            pltpu.SemaphoreType.DMA((3 + tiles,)),
        ],
        compiler_params=pltpu.CompilerParams(vmem_limit_bytes=36 * MIB),
        cost_estimate=pl.CostEstimate(
            flops=2 * rows * feat * (3 * cols + hidden),
            bytes_accessed=2 * feat * (3 * cols + hidden),
            transcendentals=0,
        ),
        name="project",
    )(n, gain, bias, wq, wk, wv, wu, *blocks)


def attend_kernel(count, span, bias_ref, cos_ref, sin_ref, query_ref, key_ref, *refs):
    mine, got = refs[:count], refs[count : 2 * count]
    att_ref, kv_ref, queries, keys, values = refs[2 * count :]
    heads = queries.shape[0]
    half = att_ref.shape[1]
    total = att_ref.shape[0]
    half_rot = ROTARY // 2
    offset = 0
    for g in range(count):
        rows = mine[g].shape[0]
        at = slice(offset, offset + rows)
        offset += rows
        summed = mine[g][...].astype(jnp.float32) + got[g][...].astype(jnp.float32) + bias_ref[...]
        cosine, sine = cos_ref[at, :], sin_ref[at, :]
        lane = lax.broadcasted_iota(jnp.int32, (rows, HEAD_PAD), 1)
        pad = jnp.zeros((rows, HEAD_PAD - HEAD_DIM), jnp.float32)
        for kind in range(3):
            kept = []
            for h in range(heads):
                begin = kind * half + h * HEAD_DIM
                u = jnp.concatenate([summed[:, begin : begin + HEAD_DIM], pad], axis=1)
                if kind < 2:
                    other = jnp.where(
                        lane < half_rot,
                        pltpu.roll(u, HEAD_PAD - half_rot, 1),
                        pltpu.roll(u, half_rot, 1),
                    )
                    u = u * cosine + other * sine
                (queries, keys, values)[kind][h, at, :] = u.astype(jnp.bfloat16)
                kept.append(u[:, :HEAD_DIM])
            if kind > 0:
                kv_ref[at, (kind - 1) * half : kind * half] = jnp.concatenate(kept, axis=1).astype(
                    jnp.bfloat16
                )
    tile = 256
    for start in range(0, total, tile):
        at = slice(start, start + tile)
        info = query_ref[at, :]
        token, begin, end = info[:, 0:1], info[:, 1:2], info[:, 2:3]
        key_token = key_ref[...]
        near = key_token > token - span
        allowed = (key_token >= begin) & (key_token <= token) & (near | (key_token < end))
        outs = []
        for h in range(heads):
            scores = lax.dot_general(
                queries[h, at, :],
                keys[h],
                (((1,), (1,)), ((), ())),
                preferred_element_type=jnp.float32,
            ) * (1.0 / HEAD_DIM**0.5)
            masked = jnp.where(allowed, scores, -1e30)
            weights = jnp.exp(masked - jnp.max(masked, axis=1, keepdims=True))
            probs = weights / jnp.sum(weights, axis=1, keepdims=True)
            out = jnp.dot(probs.astype(jnp.bfloat16), values[h], preferred_element_type=jnp.float32)
            outs.append(out[:, :HEAD_DIM])
        att_ref[at, :] = jnp.concatenate(outs, axis=1).astype(jnp.bfloat16)


def attend(span, bias, cosine, sine, query_info, key_token, mine, got):
    count = len(mine)
    total = cosine.shape[0]
    half = mine[0].shape[1] // 3
    heads = half // HEAD_DIM
    scratch = pltpu.VMEM((heads, total, HEAD_PAD), jnp.bfloat16)
    return pl.pallas_call(
        functools.partial(attend_kernel, count, span),
        out_shape=(
            jax.ShapeDtypeStruct((total, half), jnp.bfloat16),
            jax.ShapeDtypeStruct((total, 2 * half), jnp.bfloat16),
        ),
        in_specs=[VMEM] * (5 + 2 * count),
        out_specs=(VMEM, VMEM),
        scratch_shapes=[scratch, scratch, scratch],
        compiler_params=pltpu.CompilerParams(vmem_limit_bytes=36 * MIB),
        cost_estimate=pl.CostEstimate(
            flops=8 * heads * total * total * HEAD_PAD,
            bytes_accessed=16 * MIB,
            transcendentals=heads * total * total,
        ),
        name="attend",
    )(bias, cosine, sine, query_info, key_token, *mine, *got)


def output_kernel(
    offset, n_ref, bias_ref, mine_ref, got_ref, att_ref, other_ref, wo_ref, wd_ref, own_ref, sib_ref, *scratch
):
    units, wo, wd, sems = scratch
    rows = mine_ref.shape[0]
    half = att_ref.shape[1]
    tiles = wd.shape[0]
    width = wd.shape[2]
    own_rows = own_ref.shape[0]
    copies = []
    for t in range(tiles):
        at = slice(t * width, (t + 1) * width)
        copies.append(pltpu.make_async_copy(wd_ref.at[:, at], wd.at[t], sems.at[2 * t]))
        copies.append(pltpu.make_async_copy(wo_ref.at[:, at], wo.at[t], sems.at[2 * t + 1]))
    for copy in copies:
        copy.start()
    step = 384
    for c in range(0, mine_ref.shape[1], step):
        at = slice(c, c + step)
        u = mine_ref[:, at].astype(jnp.float32) + got_ref[:, at].astype(jnp.float32) + bias_ref[:, at]
        units[:, at] = (u * (1.0 + lax.erf(u * (0.5**0.5))) * 0.5).astype(jnp.bfloat16)
    n = n_ref[0]
    here = pl.ds(pl.multiple_of(n * half, 16), half)
    there = pl.ds(pl.multiple_of((1 - n) * half, 16), half)
    span = slice(offset, offset + rows)
    for t in range(tiles):
        copies[2 * t].wait()
        copies[2 * t + 1].wait()
        out = jnp.dot(units[...], wd[t], preferred_element_type=jnp.float32)
        out += jnp.dot(att_ref[span, :], wo[t, here, :], preferred_element_type=jnp.float32)
        out += jnp.dot(other_ref[span, :], wo[t, there, :], preferred_element_type=jnp.float32)
        out = out.astype(jnp.bfloat16)
        at = slice(t * width, (t + 1) * width)
        own_ref[:, at] = out[:own_rows]
        sib_ref[:, at] = out[own_rows:]


def output(n, offset, bias, mine, got, att, other, wo, wd):
    rows, hidden = mine.shape
    feat = wd.shape[1]
    width = 512
    tiles = feat // width
    shape = jax.ShapeDtypeStruct((rows // 2, feat), jnp.bfloat16)
    return pl.pallas_call(
        functools.partial(output_kernel, offset),
        out_shape=(shape, shape),
        in_specs=[SMEM] + [VMEM] * 5 + [ANY] * 2,
        out_specs=(VMEM, VMEM),
        scratch_shapes=[
            pltpu.VMEM((rows, hidden), jnp.bfloat16),
            pltpu.VMEM((tiles, wo.shape[0], width), jnp.bfloat16),
            pltpu.VMEM((tiles, hidden, width), jnp.bfloat16),
            pltpu.SemaphoreType.DMA((2 * tiles,)),
        ],
        compiler_params=pltpu.CompilerParams(vmem_limit_bytes=32 * MIB),
        cost_estimate=pl.CostEstimate(
            flops=2 * rows * feat * (hidden + wo.shape[0]),
            bytes_accessed=2 * feat * (hidden + wo.shape[0]),
            transcendentals=rows * hidden,
        ),
        name="output",
    )(n, bias, mine, got, att, other, wo, wd)


def local_ring(
    hidden_in,
    w_query,
    w_key,
    w_value,
    qkv_bias,
    w_up,
    up_bias,
    w_attn_out,
    w_down,
    out_bias,
    norm_gain,
    norm_bias,
    seq_lens,
    sink_count,
    page_table,
):
    wide_index = lax.axis_index("wide")
    n = lax.axis_index("narrow").astype(jnp.int32)
    n_arg = n.reshape(1)
    rows, feat = hidden_in.shape
    total_tokens = rows * 2 * CHIPS
    half = w_query.shape[1] // 2

    ring_pairs, swap_pairs = [], []
    for p in range(CHIPS):
        here, after = CHIP_RING[p], CHIP_RING[(p + 1) % CHIPS]
        ring_pairs += [(2 * here, 2 * after), (2 * after + 1, 2 * here + 1)]
        swap_pairs += [(2 * here, 2 * here + 1), (2 * here + 1, 2 * here)]
    along = lambda v: lax.ppermute(v, "wide", ring_pairs)
    swap = lambda v: lax.ppermute(v, "wide", swap_pairs)
    cross = lambda v: lax.ppermute(v, "narrow", [(0, 1), (1, 0)])

    sums = pl.pallas_call(
        sums_kernel,
        out_shape=jax.ShapeDtypeStruct((rows, STAT), jnp.float32),
        in_specs=[VMEM],
        out_specs=VMEM,
        name="row_sums",
    )(hidden_in)
    first_block = pl.pallas_call(
        block_kernel,
        out_shape=jax.ShapeDtypeStruct((rows, feat + STAT), jnp.bfloat16),
        in_specs=[VMEM] * 3,
        out_specs=VMEM,
        name="first_block",
    )(hidden_in, sums, cross(sums))

    owners = lax.dynamic_index_in_dim(jnp.asarray(owner_table()), wide_index, 0, keepdims=False)
    token_ids = (owners[:, None] * rows + jnp.arange(rows, dtype=jnp.int32)[None, :]).reshape(-1)
    _, pos, sink = segment_info(token_ids, seq_lens, sink_count)
    begin = token_ids - pos
    query_info = jnp.stack([token_ids, begin, begin + sink], axis=1)
    lane = jnp.arange(HEAD_PAD, dtype=jnp.int32)
    half_rot = ROTARY // 2
    freq_index = (lane % half_rot).astype(jnp.float32)
    inverse = jnp.power(jnp.float32(10000.0), -2.0 * freq_index / ROTARY)
    angles = pos.astype(jnp.float32)[:, None] * inverse[None, :]
    turned = (lane < ROTARY)[None, :]
    cosine = jnp.where(turned, jnp.cos(angles), 1.0)
    sine = jnp.where(turned, jnp.sin(angles), 0.0)
    sine = jnp.where((lane < half_rot)[None, :], -sine, sine)
    bias_half = lax.dynamic_slice_in_dim(qkv_bias, n * half, half, 1).reshape(1, 3 * half)

    blocks, others = [first_block], [swap(first_block)]
    for s in range(1, CHIPS):
        blocks.append(along(blocks[-1]))
        others.append(swap(blocks[-1]))
    mine, got, up_mine, up_got = [], [], [], []
    for group in GROUPS:
        send, kept, up = project(
            n_arg, norm_gain, norm_bias, w_query, w_key, w_value, w_up,
            [blocks[s] for s in group] + [others[s] for s in group],
        )
        got.append(cross(send))
        mine.append(kept)
        up_mine.append(up)
        up_got.append(cross(up))

    att_mine, kv = attend(
        total_tokens // 16, bias_half, cosine, sine, query_info, token_ids[None, :], mine, got
    )
    att_got = cross(att_mine)

    own, sib = [None] * CHIPS, [None] * CHIPS
    offset = 0
    for g, group in enumerate(GROUPS):
        a, b = output(
            n_arg, offset, up_bias[None, :], up_mine[g], up_got[g], att_mine, att_got, w_attn_out, w_down
        )
        offset += 2 * rows * len(group)
        b = swap(b)
        for i, s in enumerate(group):
            own[s] = a[i * rows : (i + 1) * rows]
            sib[s] = b[i * rows : (i + 1) * rows]
    running = (own[1].astype(jnp.float32) + sib[1].astype(jnp.float32)).astype(jnp.bfloat16)
    for s in range(2, CHIPS):
        running = (
            along(running).astype(jnp.float32)
            + own[s].astype(jnp.float32)
            + sib[s].astype(jnp.float32)
        ).astype(jnp.bfloat16)
    summed = (
        along(running).astype(jnp.float32) + own[0].astype(jnp.float32) + sib[0].astype(jnp.float32)
    )
    hidden_out = (hidden_in.astype(jnp.float32) + summed + out_bias).astype(jnp.bfloat16)

    pages = page_table.shape[0]
    per_device = pages // 2
    numbers = jnp.arange(pages, dtype=jnp.int32)
    slots = (numbers + n * per_device) % pages
    page_of_slot = jnp.sum(
        (page_table[None, :] == slots[:, None]).astype(jnp.int32) * numbers[None, :], axis=1
    )
    page_held = token_ids[::PAGE] // PAGE
    held_at = jnp.sum(
        (page_held[None, :] == page_of_slot[:, None]).astype(jnp.int32) * numbers[None, :], axis=1
    )
    paged = jnp.take(kv.reshape(pages, PAGE, 2 * half), held_at, axis=0)
    cache_mine = paged[:per_device]
    cache_got = cross(paged[per_device:])
    left = jnp.where(n == 0, cache_mine, cache_got)
    right = jnp.where(n == 0, cache_got, cache_mine)
    paged_cache = jnp.stack(
        [
            jnp.concatenate([left[..., :half], right[..., :half]], axis=-1),
            jnp.concatenate([left[..., half:], right[..., half:]], axis=-1),
        ]
    )
    return (hidden_out, paged_cache)


def solution(mesh):
    in_specs = (
        P("wide", "narrow"),
        P("narrow", "wide"),
        P("narrow", "wide"),
        P("narrow", "wide"),
        P(None, "wide"),
        P("narrow", "wide"),
        P("wide"),
        P("wide", "narrow"),
        P("wide", "narrow"),
        P("narrow"),
        P(None, "narrow"),
        P(None, "narrow"),
        P(),
        P(),
        P(),
    )
    out_specs = (P("wide", "narrow"), P(None, "narrow", None, "wide"))
    ringed = mesh.shape["wide"] == 2 * len(CHIP_RING) and mesh.shape["narrow"] == 2
    local = local_ring if ringed else local_generic
    return jax.shard_map(local, mesh=mesh, in_specs=in_specs, out_specs=out_specs, check_vma=False)
```

```python
import functools

import jax
import jax.numpy as jnp
import numpy as np
from jax import lax
from jax.experimental import pallas as pl
from jax.experimental.pallas import tpu as pltpu
from jax.sharding import PartitionSpec as P

D = 6144
HEAD_DIM = 96
ROTARY = 24
PAGE = 16


def segment_info(token_index, seq_lens, sink_count):
    seq_ends = jnp.cumsum(seq_lens)
    seq_starts = seq_ends - seq_lens
    inside = (token_index[:, None] >= seq_starts[None, :]) & (
        token_index[:, None] < seq_ends[None, :]
    )
    member = inside.astype(jnp.int32)
    seq_number = jnp.arange(seq_lens.shape[0], dtype=jnp.int32)
    segment = jnp.sum(member * seq_number[None, :], axis=1)
    position = token_index - jnp.sum(member * seq_starts[None, :], axis=1)
    sink_limit = jnp.sum(member * sink_count[None, :], axis=1)
    return (segment, position, sink_limit)


def rotate(values, position):
    half_rot = ROTARY // 2
    freq_index = jnp.arange(half_rot, dtype=jnp.float32)
    inverse = jnp.power(jnp.float32(10000.0), -2.0 * freq_index / ROTARY)
    angles = position.astype(jnp.float32)[:, None] * inverse[None, :]
    cosine = jnp.cos(angles)[:, None, :]
    sine_part = jnp.sin(angles)[:, None, :]
    first_half = values[..., :half_rot]
    second_half = values[..., half_rot:ROTARY]
    return jnp.concatenate(
        [
            first_half * cosine - second_half * sine_part,
            second_half * cosine + first_half * sine_part,
            values[..., ROTARY:],
        ],
        axis=-1,
    )


def local_generic(
    hidden_in,
    w_query,
    w_key,
    w_value,
    qkv_bias,
    w_up,
    up_bias,
    w_attn_out,
    w_down,
    out_bias,
    norm_gain,
    norm_bias,
    seq_lens,
    sink_count,
    page_table,
):
    wide_count = lax.axis_size("wide")
    narrow_count = lax.axis_size("narrow")
    narrow_index = lax.axis_index("narrow")
    tok_local, feat_local = hidden_in.shape
    sub_rows = tok_local // narrow_count
    total_tokens = tok_local * wide_count
    query_rows = wide_count * sub_rows
    head_cols = w_query.shape[1]
    heads_local = head_cols // HEAD_DIM
    as_float = hidden_in.astype(jnp.float32)
    partial_sum = jnp.sum(as_float, axis=1)
    partial_square = jnp.sum(as_float * as_float, axis=1)
    total_sum, total_square = lax.psum((partial_sum, partial_square), "narrow")
    average = total_sum / D
    variance = total_square / D - average * average
    scaled = (as_float - average[:, None]) * lax.rsqrt(variance + 1e-05)[:, None]
    attn_normed = (scaled * norm_gain[0] + norm_bias[0]).astype(jnp.bfloat16)
    mlp_normed = (scaled * norm_gain[1] + norm_bias[1]).astype(jnp.bfloat16)
    stacked = jnp.stack([attn_normed, mlp_normed]).reshape(2, narrow_count, sub_rows, feat_local)
    gathered = lax.all_gather(stacked, "wide", axis=2, tiled=True).reshape(
        2, total_tokens, feat_local
    )
    local_order = jnp.arange(query_rows, dtype=jnp.int32)
    local_tokens = (
        local_order // sub_rows * tok_local + narrow_index * sub_rows + local_order % sub_rows
    )
    local_seg, local_pos, local_sink = segment_info(local_tokens, seq_lens, sink_count)
    all_order = jnp.arange(total_tokens, dtype=jnp.int32)
    all_tokens = (
        all_order % query_rows // sub_rows * tok_local
        + all_order // query_rows * sub_rows
        + all_order % sub_rows
    )
    all_seg, all_pos, all_sink = segment_info(all_tokens, seq_lens, sink_count)
    qkv_weight = jnp.concatenate([w_query, w_key, w_value], axis=1)
    attn_part = gathered[0]
    mlp_part = gathered[1]
    summed = lax.psum_scatter(
        jnp.concatenate(
            [
                jnp.dot(attn_part, qkv_weight, preferred_element_type=jnp.float32),
                jnp.dot(mlp_part, w_up, preferred_element_type=jnp.float32),
            ],
            axis=1,
        ).astype(jnp.bfloat16),
        "narrow",
        scatter_dimension=0,
        tiled=True,
    ).astype(jnp.float32)
    query_sum = summed[:, :head_cols]
    key_sum = summed[:, head_cols : 2 * head_cols]
    value_sum = summed[:, 2 * head_cols : 3 * head_cols]
    unit_sum = summed[:, 3 * head_cols :]
    keys_local = (
        rotate((key_sum + qkv_bias[1]).reshape(query_rows, heads_local, HEAD_DIM), local_pos)
        .astype(jnp.bfloat16)
        .reshape(query_rows, head_cols)
    )
    values_local = (value_sum + qkv_bias[2]).astype(jnp.bfloat16)
    all_keys, all_values = (
        lax.all_gather(keys_local, "narrow", axis=0, tiled=True),
        lax.all_gather(values_local, "narrow", axis=0, tiled=True),
    )
    queries = rotate(
        (query_sum + qkv_bias[0]).reshape(query_rows, heads_local, HEAD_DIM), local_pos
    ).astype(jnp.bfloat16)
    hidden_units = jax.nn.gelu(unit_sum + up_bias, approximate=False).astype(jnp.bfloat16)
    window_span = total_tokens // 16
    allowed = (local_seg[:, None] == all_seg[None, :]) & (all_pos[None, :] <= local_pos[:, None])
    allowed = allowed & (
        (local_pos[:, None] - all_pos[None, :] < window_span)
        | (all_pos[None, :] < local_sink[:, None])
    )
    key_heads = all_keys.reshape(total_tokens, heads_local, HEAD_DIM)
    value_heads = all_values.reshape(total_tokens, heads_local, HEAD_DIM)
    scores = jnp.einsum("qhd,khd->hqk", queries, key_heads, preferred_element_type=jnp.float32) * (
        1.0 / HEAD_DIM**0.5
    )
    masked = jnp.where(allowed[None], scores, jnp.float32(-1e30))
    top_score = jnp.max(masked, axis=2, keepdims=True)
    weights = jnp.exp(masked - top_score)
    probs = (weights / jnp.sum(weights, axis=2, keepdims=True)).astype(jnp.bfloat16)
    attended = (
        jnp.einsum("hqk,khd->qhd", probs, value_heads, preferred_element_type=jnp.float32)
        .astype(jnp.bfloat16)
        .reshape(query_rows, head_cols)
    )
    full_out, full_down = (
        lax.all_gather(w_attn_out, "narrow", axis=1, tiled=True),
        lax.all_gather(w_down, "narrow", axis=1, tiled=True),
    )
    attn_part = attended
    own_rows = lax.psum_scatter(
        (
            jnp.dot(attn_part, full_out, preferred_element_type=jnp.float32)
            + jnp.dot(hidden_units, full_down, preferred_element_type=jnp.float32)
        ).astype(jnp.bfloat16),
        "wide",
        scatter_dimension=0,
        tiled=True,
    ).astype(jnp.float32)
    combined = lax.all_to_all(
        own_rows.astype(jnp.bfloat16), "narrow", split_axis=1, concat_axis=0, tiled=True
    ).astype(own_rows.dtype)
    hidden_out = (as_float + combined + out_bias).astype(jnp.bfloat16)
    pages_local = page_table.shape[0] // narrow_count
    slot_ids = narrow_index * pages_local + jnp.arange(pages_local, dtype=jnp.int32)
    matches = (page_table[None, :] == slot_ids[:, None]).astype(jnp.int32)
    source_page = jnp.sum(
        matches * jnp.arange(page_table.shape[0], dtype=jnp.int32)[None, :], axis=1
    )
    token_ids = (source_page[:, None] * PAGE + jnp.arange(PAGE, dtype=jnp.int32)[None, :]).reshape(
        -1
    )
    gather_rows = (
        token_ids % tok_local // sub_rows * query_rows
        + token_ids // tok_local * sub_rows
        + token_ids % sub_rows
    )
    cache_keys = jnp.take(all_keys, gather_rows, axis=0).reshape(pages_local, PAGE, head_cols)
    cache_values = jnp.take(all_values, gather_rows, axis=0).reshape(pages_local, PAGE, head_cols)
    paged_cache = jnp.stack([cache_keys, cache_values])
    return (hidden_out, paged_cache)


CHUNKS = 4
STAT = 128
HEAD_PAD = 128
MIB = 1 << 20
VMEM = pl.BlockSpec(memory_space=pltpu.VMEM)
ANY = pl.BlockSpec(memory_space=pl.ANY)
SMEM = pl.BlockSpec(memory_space=pltpu.SMEM)


def sums_kernel(x_ref, out_ref):
    x = x_ref[...].astype(jnp.float32)
    first = jnp.sum(x, axis=1, keepdims=True)
    second = jnp.sum(x * x, axis=1, keepdims=True)
    lane = lax.broadcasted_iota(jnp.int32, out_ref.shape, 1)
    out_ref[...] = jnp.where(lane == 0, first, jnp.where(lane == 1, second, 0.0))


def block_kernel(x_ref, here_ref, there_ref, out_ref):
    feat = x_ref.shape[1]
    total = here_ref[...] + there_ref[...]
    average = total[:, 0:1] / D
    variance = total[:, 1:2] / D - average * average
    scale = lax.rsqrt(variance + 1e-05)
    lane = lax.broadcasted_iota(jnp.int32, (x_ref.shape[0], STAT), 1)
    tail = jnp.zeros((x_ref.shape[0], STAT), jnp.float32)
    for start, value in ((0, average), (3, scale)):
        for term in range(3):
            piece = value.astype(jnp.bfloat16).astype(jnp.float32)
            tail = jnp.where(lane == start + term, piece, tail)
            value = value - piece
    out_ref[:, :feat] = x_ref[...]
    out_ref[:, feat:] = tail.astype(jnp.bfloat16)


def project_kernel(count, n_ref, gain_ref, bias_ref, wq_ref, wk_ref, wv_ref, wu_ref, *refs):
    blocks = refs[:count]
    send_ref, mine_ref, up_ref, attn, mlp, wq, wk, wv, wu, sems = refs[count:]
    rows = blocks[0].shape[0]
    feat = wq.shape[0]
    cols = wq.shape[1]
    half = cols // 2
    tiles = wu.shape[0]
    copies = [
        pltpu.make_async_copy(src, dst, sems.at[i])
        for i, (src, dst) in enumerate(((wq_ref, wq), (wk_ref, wk), (wv_ref, wv)))
    ]
    copies += [
        pltpu.make_async_copy(wu_ref.at[:, t * cols : (t + 1) * cols], wu.at[t], sems.at[3 + t])
        for t in range(tiles)
    ]
    for copy in copies:
        copy.start()
    step = 512
    for b in range(count):
        tail = blocks[b][:, feat:].astype(jnp.float32)
        average = tail[:, 0:1] + tail[:, 1:2] + tail[:, 2:3]
        scale = tail[:, 3:4] + tail[:, 4:5] + tail[:, 5:6]
        for c in range(0, feat, step):
            at = slice(c, c + step)
            scaled = (blocks[b][:, at].astype(jnp.float32) - average) * scale
            here = slice(b * rows, (b + 1) * rows)
            attn[here, at] = (scaled * gain_ref[0:1, at] + bias_ref[0:1, at]).astype(jnp.bfloat16)
            mlp[here, at] = (scaled * gain_ref[1:2, at] + bias_ref[1:2, at]).astype(jnp.bfloat16)
    low, high = [], []
    for i, weight in enumerate((wq, wk, wv)):
        copies[i].wait()
        part = jnp.dot(attn[...], weight[...], preferred_element_type=jnp.float32)
        low.append(part[:, :half])
        high.append(part[:, half:])
    low = jnp.concatenate(low, axis=1).astype(jnp.bfloat16)
    high = jnp.concatenate(high, axis=1).astype(jnp.bfloat16)
    first = n_ref[0] == 0
    send_ref[...] = jnp.where(first, high, low)
    mine_ref[...] = jnp.where(first, low, high)
    for t in range(tiles):
        copies[3 + t].wait()
        part = jnp.dot(mlp[...], wu[t], preferred_element_type=jnp.float32)
        up_ref[:, t * cols : (t + 1) * cols] = part.astype(jnp.bfloat16)


def project(n, gain, bias, wq, wk, wv, wu, blocks):
    count = len(blocks)
    rows = blocks[0].shape[0] * count
    feat, cols = wq.shape
    hidden = wu.shape[1]
    tiles = hidden // cols
    return pl.pallas_call(
        functools.partial(project_kernel, count),
        out_shape=(
            jax.ShapeDtypeStruct((rows, 3 * cols // 2), jnp.bfloat16),
            jax.ShapeDtypeStruct((rows, 3 * cols // 2), jnp.bfloat16),
            jax.ShapeDtypeStruct((rows, hidden), jnp.bfloat16),
        ),
        in_specs=[SMEM, VMEM, VMEM, ANY, ANY, ANY, ANY] + [VMEM] * count,
        out_specs=(VMEM, VMEM, VMEM),
        scratch_shapes=[
            pltpu.VMEM((rows, feat), jnp.bfloat16),
            pltpu.VMEM((rows, feat), jnp.bfloat16),
            pltpu.VMEM((feat, cols), jnp.bfloat16),
            pltpu.VMEM((feat, cols), jnp.bfloat16),
            pltpu.VMEM((feat, cols), jnp.bfloat16),
            pltpu.VMEM((tiles, feat, cols), jnp.bfloat16),
            pltpu.SemaphoreType.DMA((3 + tiles,)),
        ],
        compiler_params=pltpu.CompilerParams(vmem_limit_bytes=58 * MIB),
        cost_estimate=pl.CostEstimate(flops=1, bytes_accessed=1, transcendentals=0),
        name="project",
    )(n, gain, bias, wq, wk, wv, wu, *blocks)


def attend_kernel(count, span, bias_ref, cos_ref, sin_ref, query_ref, key_ref, *refs):
    mine, got = refs[:count], refs[count : 2 * count]
    att_ref, kv_ref, queries, keys, values = refs[2 * count :]
    heads = queries.shape[0]
    half = att_ref.shape[1]
    total = att_ref.shape[0]
    half_rot = ROTARY // 2
    offset = 0
    for g in range(count):
        rows = mine[g].shape[0]
        at = slice(offset, offset + rows)
        offset += rows
        summed = mine[g][...].astype(jnp.float32) + got[g][...].astype(jnp.float32) + bias_ref[...]
        cosine, sine = cos_ref[at, :], sin_ref[at, :]
        lane = lax.broadcasted_iota(jnp.int32, (rows, HEAD_PAD), 1)
        pad = jnp.zeros((rows, HEAD_PAD - HEAD_DIM), jnp.float32)
        for kind in range(3):
            kept = []
            for h in range(heads):
                begin = kind * half + h * HEAD_DIM
                u = jnp.concatenate([summed[:, begin : begin + HEAD_DIM], pad], axis=1)
                if kind < 2:
                    other = jnp.where(
                        lane < half_rot,
                        pltpu.roll(u, HEAD_PAD - half_rot, 1),
                        pltpu.roll(u, half_rot, 1),
                    )
                    u = u * cosine + other * sine
                (queries, keys, values)[kind][h, at, :] = u.astype(jnp.bfloat16)
                kept.append(u[:, :HEAD_DIM])
            if kind > 0:
                kv_ref[at, (kind - 1) * half : kind * half] = jnp.concatenate(kept, axis=1).astype(
                    jnp.bfloat16
                )
    tile = 256
    for start in range(0, total, tile):
        at = slice(start, start + tile)
        info = query_ref[at, :]
        token, begin, end = info[:, 0:1], info[:, 1:2], info[:, 2:3]
        key_token = key_ref[...]
        near = key_token > token - span
        allowed = (key_token >= begin) & (key_token <= token) & (near | (key_token < end))
        outs = []
        for h in range(heads):
            scores = lax.dot_general(
                queries[h, at, :],
                keys[h],
                (((1,), (1,)), ((), ())),
                preferred_element_type=jnp.float32,
            ) * (1.0 / HEAD_DIM**0.5)
            masked = jnp.where(allowed, scores, -1e30)
            weights = jnp.exp(masked - jnp.max(masked, axis=1, keepdims=True))
            probs = weights / jnp.sum(weights, axis=1, keepdims=True)
            out = jnp.dot(probs.astype(jnp.bfloat16), values[h], preferred_element_type=jnp.float32)
            outs.append(out[:, :HEAD_DIM])
        att_ref[at, :] = jnp.concatenate(outs, axis=1).astype(jnp.bfloat16)


def attend(span, bias, cosine, sine, query_info, key_token, mine, got):
    count = len(mine)
    total = cosine.shape[0]
    half = mine[0].shape[1] // 3
    heads = half // HEAD_DIM
    scratch = pltpu.VMEM((heads, total, HEAD_PAD), jnp.bfloat16)
    return pl.pallas_call(
        functools.partial(attend_kernel, count, span),
        out_shape=(
            jax.ShapeDtypeStruct((total, half), jnp.bfloat16),
            jax.ShapeDtypeStruct((total, 2 * half), jnp.bfloat16),
        ),
        in_specs=[VMEM] * (5 + 2 * count),
        out_specs=(VMEM, VMEM),
        scratch_shapes=[scratch, scratch, scratch],
        compiler_params=pltpu.CompilerParams(vmem_limit_bytes=58 * MIB),
        cost_estimate=pl.CostEstimate(flops=1, bytes_accessed=1, transcendentals=0),
        name="attend",
    )(bias, cosine, sine, query_info, key_token, *mine, *got)


def output_kernel(
    offset, n_ref, bias_ref, mine_ref, got_ref, att_ref, other_ref, wo_ref, wd_ref, own_ref, sib_ref, *scratch
):
    units, wo, wd, sems = scratch
    rows = mine_ref.shape[0]
    half = att_ref.shape[1]
    tiles = wd.shape[0]
    width = wd.shape[2]
    own_rows = own_ref.shape[0]
    copies = []
    for t in range(tiles):
        at = slice(t * width, (t + 1) * width)
        copies.append(pltpu.make_async_copy(wd_ref.at[:, at], wd.at[t], sems.at[2 * t]))
        copies.append(pltpu.make_async_copy(wo_ref.at[:, at], wo.at[t], sems.at[2 * t + 1]))
    for copy in copies:
        copy.start()
    step = 384
    for c in range(0, mine_ref.shape[1], step):
        at = slice(c, c + step)
        u = mine_ref[:, at].astype(jnp.float32) + got_ref[:, at].astype(jnp.float32) + bias_ref[:, at]
        units[:, at] = (u * (1.0 + lax.erf(u * (0.5**0.5))) * 0.5).astype(jnp.bfloat16)
    n = n_ref[0]
    here = pl.ds(pl.multiple_of(n * half, 16), half)
    there = pl.ds(pl.multiple_of((1 - n) * half, 16), half)
    span = slice(offset, offset + rows)
    for t in range(tiles):
        copies[2 * t].wait()
        copies[2 * t + 1].wait()
        out = jnp.dot(units[...], wd[t], preferred_element_type=jnp.float32)
        out += jnp.dot(att_ref[span, :], wo[t, here, :], preferred_element_type=jnp.float32)
        out += jnp.dot(other_ref[span, :], wo[t, there, :], preferred_element_type=jnp.float32)
        out = out.astype(jnp.bfloat16)
        at = slice(t * width, (t + 1) * width)
        own_ref[:, at] = out[:own_rows]
        sib_ref[:, at] = out[own_rows:]


def output(n, offset, bias, mine, got, att, other, wo, wd):
    rows, hidden = mine.shape
    feat = wd.shape[1]
    width = 512
    tiles = feat // width
    shape = jax.ShapeDtypeStruct((rows // 2, feat), jnp.bfloat16)
    return pl.pallas_call(
        functools.partial(output_kernel, offset),
        out_shape=(shape, shape),
        in_specs=[SMEM] + [VMEM] * 5 + [ANY] * 2,
        out_specs=(VMEM, VMEM),
        scratch_shapes=[
            pltpu.VMEM((rows, hidden), jnp.bfloat16),
            pltpu.VMEM((tiles, wo.shape[0], width), jnp.bfloat16),
            pltpu.VMEM((tiles, hidden, width), jnp.bfloat16),
            pltpu.SemaphoreType.DMA((2 * tiles,)),
        ],
        compiler_params=pltpu.CompilerParams(vmem_limit_bytes=58 * MIB),
        cost_estimate=pl.CostEstimate(flops=1, bytes_accessed=1, transcendentals=0),
        name="output",
    )(n, bias, mine, got, att, other, wo, wd)


def after(*values):
    return lax.optimization_barrier(values)


def local_pairs(
    hidden_in,
    w_query,
    w_key,
    w_value,
    qkv_bias,
    w_up,
    up_bias,
    w_attn_out,
    w_down,
    out_bias,
    norm_gain,
    norm_bias,
    seq_lens,
    sink_count,
    page_table,
):
    wide_index = lax.axis_index("wide")
    n = lax.axis_index("narrow").astype(jnp.int32)
    n_arg = n.reshape(1)
    rows, feat = hidden_in.shape
    total_tokens = rows * lax.axis_size("wide")
    half = w_query.shape[1] // 2

    chips = lax.axis_size("wide") // 2
    swap_pairs = [(w, w ^ 1) for w in range(2 * chips)]
    same_core = [list(range(core, 2 * chips, 2)) for core in range(2)]
    swap = lambda v: lax.ppermute(v, "wide", swap_pairs)
    cross = lambda v: lax.ppermute(v, "narrow", [(0, 1), (1, 0)])

    sums = pl.pallas_call(
        sums_kernel,
        out_shape=jax.ShapeDtypeStruct((rows, STAT), jnp.float32),
        in_specs=[VMEM],
        out_specs=VMEM,
        name="row_sums",
    )(hidden_in)
    first_block = pl.pallas_call(
        block_kernel,
        out_shape=jax.ShapeDtypeStruct((rows, feat + STAT), jnp.bfloat16),
        in_specs=[VMEM] * 3,
        out_specs=VMEM,
        name="first_block",
    )(hidden_in, sums, cross(sums))

    part = rows // CHUNKS
    core = wide_index % 2
    chip_order = 2 * jnp.arange(chips, dtype=jnp.int32)
    owners = jnp.concatenate([chip_order + core, chip_order + 1 - core])
    first_row = owners[None, :] * rows + part * jnp.arange(CHUNKS, dtype=jnp.int32)[:, None]
    token_ids = (
        first_row[:, :, None] + jnp.arange(part, dtype=jnp.int32)[None, None, :]
    ).reshape(-1)
    _, pos, sink = segment_info(token_ids, seq_lens, sink_count)
    begin = token_ids - pos
    query_info = jnp.stack([token_ids, begin, begin + sink], axis=1)
    lane = jnp.arange(HEAD_PAD, dtype=jnp.int32)
    half_rot = ROTARY // 2
    freq_index = (lane % half_rot).astype(jnp.float32)
    inverse = jnp.power(jnp.float32(10000.0), -2.0 * freq_index / ROTARY)
    angles = pos.astype(jnp.float32)[:, None] * inverse[None, :]
    turned = (lane < ROTARY)[None, :]
    cosine = jnp.where(turned, jnp.cos(angles), 1.0)
    sine = jnp.where(turned, jnp.sin(angles), 0.0)
    sine = jnp.where((lane < half_rot)[None, :], -sine, sine)
    bias_half = lax.dynamic_slice_in_dim(qkv_bias, n * half, half, 1).reshape(1, 3 * half)

    gathered = [
        lax.all_gather(
            first_block[c * part : (c + 1) * part],
            "wide",
            axis_index_groups=same_core,
            axis=0,
            tiled=True,
        )
        for c in range(CHUNKS)
    ]
    row_group = 2 * chips * part
    mine, got, up_mine, up_got = [], [], [], []
    for c in range(CHUNKS):
        block = gathered[c]
        if c > 0:
            block, mine[-1] = after(block, mine[-1])
        other = swap(block)
        if c == 2:
            block, got[0], up_got[0] = after(block, got[0], up_got[0])
        if c == 3:
            block, got[1] = after(block, got[1])
        send, kept, up = project(
            n_arg, norm_gain, norm_bias, w_query, w_key, w_value, w_up, [block, other]
        )
        mine.append(kept)
        got.append(cross(send))
        up_mine.append(up)
        up_got.append(cross(up) if c in (0, 1) else None)

    att_mine, kv = attend(
        total_tokens // 16, bias_half, cosine, sine, query_info, token_ids[None, :], mine, got
    )
    att_got = cross(att_mine)
    att_got, up_got[1] = after(att_got, up_got[1])
    up_got[2], up_got[3] = cross(up_mine[2]), cross(up_mine[3])

    results = []
    for c in range(CHUNKS):
        a, b = output(
            n_arg, c * row_group, up_bias[None, :], up_mine[c], up_got[c], att_mine, att_got,
            w_attn_out, w_down,
        )
        paired = (a.astype(jnp.float32) + swap(b).astype(jnp.float32)).astype(jnp.bfloat16)
        results.append(
            lax.psum_scatter(
                paired, "wide", scatter_dimension=0, axis_index_groups=same_core, tiled=True
            )
        )
    summed = jnp.concatenate(results, axis=0).astype(jnp.float32)
    hidden_out = (hidden_in.astype(jnp.float32) + summed + out_bias).astype(jnp.bfloat16)

    pages = page_table.shape[0]
    per_device = pages // 2
    numbers = jnp.arange(pages, dtype=jnp.int32)
    slots = (numbers + n * per_device) % pages
    page_of_slot = jnp.sum(
        (page_table[None, :] == slots[:, None]).astype(jnp.int32) * numbers[None, :], axis=1
    )
    page_held = token_ids[::PAGE] // PAGE
    held_at = jnp.sum(
        (page_held[None, :] == page_of_slot[:, None]).astype(jnp.int32) * numbers[None, :], axis=1
    )
    paged = jnp.take(kv.reshape(pages, PAGE, 2 * half), held_at, axis=0)
    cache_mine = paged[:per_device]
    cache_got = cross(paged[per_device:])
    left = jnp.where(n == 0, cache_mine, cache_got)
    right = jnp.where(n == 0, cache_got, cache_mine)
    paged_cache = jnp.stack(
        [
            jnp.concatenate([left[..., :half], right[..., :half]], axis=-1),
            jnp.concatenate([left[..., half:], right[..., half:]], axis=-1),
        ]
    )
    return (hidden_out, paged_cache)


def solution(mesh):
    in_specs = (
        P("wide", "narrow"),
        P("narrow", "wide"),
        P("narrow", "wide"),
        P("narrow", "wide"),
        P(None, "wide"),
        P("narrow", "wide"),
        P("wide"),
        P("wide", "narrow"),
        P("wide", "narrow"),
        P("narrow"),
        P(None, "narrow"),
        P(None, "narrow"),
        P(),
        P(),
        P(),
    )
    out_specs = (P("wide", "narrow"), P(None, "narrow", None, "wide"))
    paired = mesh.shape["narrow"] == 2 and mesh.shape["wide"] % 2 == 0
    local = local_pairs if paired else local_generic
    return jax.shard_map(local, mesh=mesh, in_specs=in_specs, out_specs=out_specs, check_vma=False)
```

```python
import functools

import jax
import jax.numpy as jnp
import numpy as np
from jax import lax
from jax.experimental import pallas as pl
from jax.experimental.pallas import tpu as pltpu
from jax.sharding import PartitionSpec as P

D = 6144
HEAD_DIM = 96
ROTARY = 24
PAGE = 16


def segment_info(token_index, seq_lens, sink_count):
    seq_ends = jnp.cumsum(seq_lens)
    seq_starts = seq_ends - seq_lens
    inside = (token_index[:, None] >= seq_starts[None, :]) & (
        token_index[:, None] < seq_ends[None, :]
    )
    member = inside.astype(jnp.int32)
    seq_number = jnp.arange(seq_lens.shape[0], dtype=jnp.int32)
    segment = jnp.sum(member * seq_number[None, :], axis=1)
    position = token_index - jnp.sum(member * seq_starts[None, :], axis=1)
    sink_limit = jnp.sum(member * sink_count[None, :], axis=1)
    return (segment, position, sink_limit)


def rotate(values, position):
    half_rot = ROTARY // 2
    freq_index = jnp.arange(half_rot, dtype=jnp.float32)
    inverse = jnp.power(jnp.float32(10000.0), -2.0 * freq_index / ROTARY)
    angles = position.astype(jnp.float32)[:, None] * inverse[None, :]
    cosine = jnp.cos(angles)[:, None, :]
    sine_part = jnp.sin(angles)[:, None, :]
    first_half = values[..., :half_rot]
    second_half = values[..., half_rot:ROTARY]
    return jnp.concatenate(
        [
            first_half * cosine - second_half * sine_part,
            second_half * cosine + first_half * sine_part,
            values[..., ROTARY:],
        ],
        axis=-1,
    )


def local_generic(
    hidden_in,
    w_query,
    w_key,
    w_value,
    qkv_bias,
    w_up,
    up_bias,
    w_attn_out,
    w_down,
    out_bias,
    norm_gain,
    norm_bias,
    seq_lens,
    sink_count,
    page_table,
):
    wide_count = lax.axis_size("wide")
    narrow_count = lax.axis_size("narrow")
    narrow_index = lax.axis_index("narrow")
    tok_local, feat_local = hidden_in.shape
    sub_rows = tok_local // narrow_count
    total_tokens = tok_local * wide_count
    query_rows = wide_count * sub_rows
    head_cols = w_query.shape[1]
    heads_local = head_cols // HEAD_DIM
    as_float = hidden_in.astype(jnp.float32)
    partial_sum = jnp.sum(as_float, axis=1)
    partial_square = jnp.sum(as_float * as_float, axis=1)
    total_sum, total_square = lax.psum((partial_sum, partial_square), "narrow")
    average = total_sum / D
    variance = total_square / D - average * average
    scaled = (as_float - average[:, None]) * lax.rsqrt(variance + 1e-05)[:, None]
    attn_normed = (scaled * norm_gain[0] + norm_bias[0]).astype(jnp.bfloat16)
    mlp_normed = (scaled * norm_gain[1] + norm_bias[1]).astype(jnp.bfloat16)
    stacked = jnp.stack([attn_normed, mlp_normed]).reshape(2, narrow_count, sub_rows, feat_local)
    gathered = lax.all_gather(stacked, "wide", axis=2, tiled=True).reshape(
        2, total_tokens, feat_local
    )
    local_order = jnp.arange(query_rows, dtype=jnp.int32)
    local_tokens = (
        local_order // sub_rows * tok_local + narrow_index * sub_rows + local_order % sub_rows
    )
    local_seg, local_pos, local_sink = segment_info(local_tokens, seq_lens, sink_count)
    all_order = jnp.arange(total_tokens, dtype=jnp.int32)
    all_tokens = (
        all_order % query_rows // sub_rows * tok_local
        + all_order // query_rows * sub_rows
        + all_order % sub_rows
    )
    all_seg, all_pos, all_sink = segment_info(all_tokens, seq_lens, sink_count)
    qkv_weight = jnp.concatenate([w_query, w_key, w_value], axis=1)
    attn_part = gathered[0]
    mlp_part = gathered[1]
    summed = lax.psum_scatter(
        jnp.concatenate(
            [
                jnp.dot(attn_part, qkv_weight, preferred_element_type=jnp.float32),
                jnp.dot(mlp_part, w_up, preferred_element_type=jnp.float32),
            ],
            axis=1,
        ).astype(jnp.bfloat16),
        "narrow",
        scatter_dimension=0,
        tiled=True,
    ).astype(jnp.float32)
    query_sum = summed[:, :head_cols]
    key_sum = summed[:, head_cols : 2 * head_cols]
    value_sum = summed[:, 2 * head_cols : 3 * head_cols]
    unit_sum = summed[:, 3 * head_cols :]
    keys_local = (
        rotate((key_sum + qkv_bias[1]).reshape(query_rows, heads_local, HEAD_DIM), local_pos)
        .astype(jnp.bfloat16)
        .reshape(query_rows, head_cols)
    )
    values_local = (value_sum + qkv_bias[2]).astype(jnp.bfloat16)
    all_keys, all_values = (
        lax.all_gather(keys_local, "narrow", axis=0, tiled=True),
        lax.all_gather(values_local, "narrow", axis=0, tiled=True),
    )
    queries = rotate(
        (query_sum + qkv_bias[0]).reshape(query_rows, heads_local, HEAD_DIM), local_pos
    ).astype(jnp.bfloat16)
    hidden_units = jax.nn.gelu(unit_sum + up_bias, approximate=False).astype(jnp.bfloat16)
    window_span = total_tokens // 16
    allowed = (local_seg[:, None] == all_seg[None, :]) & (all_pos[None, :] <= local_pos[:, None])
    allowed = allowed & (
        (local_pos[:, None] - all_pos[None, :] < window_span)
        | (all_pos[None, :] < local_sink[:, None])
    )
    key_heads = all_keys.reshape(total_tokens, heads_local, HEAD_DIM)
    value_heads = all_values.reshape(total_tokens, heads_local, HEAD_DIM)
    scores = jnp.einsum("qhd,khd->hqk", queries, key_heads, preferred_element_type=jnp.float32) * (
        1.0 / HEAD_DIM**0.5
    )
    masked = jnp.where(allowed[None], scores, jnp.float32(-1e30))
    top_score = jnp.max(masked, axis=2, keepdims=True)
    weights = jnp.exp(masked - top_score)
    probs = (weights / jnp.sum(weights, axis=2, keepdims=True)).astype(jnp.bfloat16)
    attended = (
        jnp.einsum("hqk,khd->qhd", probs, value_heads, preferred_element_type=jnp.float32)
        .astype(jnp.bfloat16)
        .reshape(query_rows, head_cols)
    )
    full_out, full_down = (
        lax.all_gather(w_attn_out, "narrow", axis=1, tiled=True),
        lax.all_gather(w_down, "narrow", axis=1, tiled=True),
    )
    attn_part = attended
    own_rows = lax.psum_scatter(
        (
            jnp.dot(attn_part, full_out, preferred_element_type=jnp.float32)
            + jnp.dot(hidden_units, full_down, preferred_element_type=jnp.float32)
        ).astype(jnp.bfloat16),
        "wide",
        scatter_dimension=0,
        tiled=True,
    ).astype(jnp.float32)
    combined = lax.all_to_all(
        own_rows.astype(jnp.bfloat16), "narrow", split_axis=1, concat_axis=0, tiled=True
    ).astype(own_rows.dtype)
    hidden_out = (as_float + combined + out_bias).astype(jnp.bfloat16)
    pages_local = page_table.shape[0] // narrow_count
    slot_ids = narrow_index * pages_local + jnp.arange(pages_local, dtype=jnp.int32)
    matches = (page_table[None, :] == slot_ids[:, None]).astype(jnp.int32)
    source_page = jnp.sum(
        matches * jnp.arange(page_table.shape[0], dtype=jnp.int32)[None, :], axis=1
    )
    token_ids = (source_page[:, None] * PAGE + jnp.arange(PAGE, dtype=jnp.int32)[None, :]).reshape(
        -1
    )
    gather_rows = (
        token_ids % tok_local // sub_rows * query_rows
        + token_ids // tok_local * sub_rows
        + token_ids % sub_rows
    )
    cache_keys = jnp.take(all_keys, gather_rows, axis=0).reshape(pages_local, PAGE, head_cols)
    cache_values = jnp.take(all_values, gather_rows, axis=0).reshape(pages_local, PAGE, head_cols)
    paged_cache = jnp.stack([cache_keys, cache_values])
    return (hidden_out, paged_cache)


CHIP_RING = (0, 2, 4, 6, 7, 5, 3, 1)
CHIPS = len(CHIP_RING)
PAIRS = ("o0", "f1", "b1", "f2", "b2", "f3", "b3", "f4")
STAT = 128
HEAD_PAD = 128
MIB = 1 << 20
VMEM = pl.BlockSpec(memory_space=pltpu.VMEM)
ANY = pl.BlockSpec(memory_space=pl.ANY)
SMEM = pl.BlockSpec(memory_space=pltpu.SMEM)


def owner_table():
    table = np.zeros((2 * CHIPS, 2 * CHIPS), np.int32)
    for place, chip in enumerate(CHIP_RING):
        for core in range(2):
            order = []
            for pair in PAIRS:
                shift = (-1 if pair[0] == "f" else 1) * int(pair[1]) * (1 - 2 * core)
                order.append(CHIP_RING[(place + shift) % CHIPS] * 2 + core)
                order.append(CHIP_RING[(place - shift) % CHIPS] * 2 + 1 - core)
            table[2 * chip + core] = order
    return table


def sums_kernel(x_ref, out_ref):
    x = x_ref[...].astype(jnp.float32)
    first = jnp.sum(x, axis=1, keepdims=True)
    second = jnp.sum(x * x, axis=1, keepdims=True)
    lane = lax.broadcasted_iota(jnp.int32, out_ref.shape, 1)
    out_ref[...] = jnp.where(lane == 0, first, jnp.where(lane == 1, second, 0.0))


def block_kernel(x_ref, here_ref, there_ref, out_ref):
    feat = x_ref.shape[1]
    total = here_ref[...] + there_ref[...]
    average = total[:, 0:1] / D
    variance = total[:, 1:2] / D - average * average
    scale = lax.rsqrt(variance + 1e-05)
    lane = lax.broadcasted_iota(jnp.int32, (x_ref.shape[0], STAT), 1)
    tail = jnp.zeros((x_ref.shape[0], STAT), jnp.float32)
    for start, value in ((0, average), (3, scale)):
        for term in range(3):
            piece = value.astype(jnp.bfloat16).astype(jnp.float32)
            tail = jnp.where(lane == start + term, piece, tail)
            value = value - piece
    out_ref[:, :feat] = x_ref[...]
    out_ref[:, feat:] = tail.astype(jnp.bfloat16)


def project_kernel(count, n_ref, gain_ref, bias_ref, wq_ref, wk_ref, wv_ref, wu_ref, *refs):
    blocks = refs[:count]
    ups = refs[count + 2 : count + 2 + count // 2]
    send_ref, mine_ref = refs[count : count + 2]
    attn, mlp, wqkv, wu, sems = refs[count + 2 + count // 2 :]
    rows = blocks[0].shape[0]
    feat = attn.shape[1]
    cols = wq_ref.shape[1]
    half = cols // 2
    tiles, _, width = wu.shape
    copies = [
        pltpu.make_async_copy(src, wqkv.at[:, i * cols : (i + 1) * cols], sems.at[i])
        for i, src in enumerate((wq_ref, wk_ref, wv_ref))
    ]
    copies += [
        pltpu.make_async_copy(wu_ref.at[:, t * width : (t + 1) * width], wu.at[t], sems.at[3 + t])
        for t in range(tiles)
    ]
    for copy in copies:
        copy.start()
    step = 512
    for b in range(count):
        tail = blocks[b][:, feat:].astype(jnp.float32)
        average = tail[:, 0:1] + tail[:, 1:2] + tail[:, 2:3]
        scale = tail[:, 3:4] + tail[:, 4:5] + tail[:, 5:6]
        for c in range(0, feat, step):
            at = slice(c, c + step)
            scaled = (blocks[b][:, at].astype(jnp.float32) - average) * scale
            here = slice(b * rows, (b + 1) * rows)
            attn[here, at] = (scaled * gain_ref[0:1, at] + bias_ref[0:1, at]).astype(jnp.bfloat16)
            mlp[here, at] = (scaled * gain_ref[1:2, at] + bias_ref[1:2, at]).astype(jnp.bfloat16)
    for i in range(3):
        copies[i].wait()
    part = jnp.dot(attn[...], wqkv[...], preferred_element_type=jnp.float32)
    low = [part[:, i * cols : i * cols + half] for i in range(3)]
    high = [part[:, i * cols + half : (i + 1) * cols] for i in range(3)]
    low = jnp.concatenate(low, axis=1).astype(jnp.bfloat16)
    high = jnp.concatenate(high, axis=1).astype(jnp.bfloat16)
    first = n_ref[0] == 0
    send_ref[...] = jnp.where(first, high, low)
    mine_ref[...] = jnp.where(first, low, high)
    for t in range(tiles):
        copies[3 + t].wait()
        part = jnp.dot(mlp[...], wu[t], preferred_element_type=jnp.float32).astype(jnp.bfloat16)
        for u, up in enumerate(ups):
            up[:, t * width : (t + 1) * width] = part[2 * u * rows : 2 * (u + 1) * rows]


def project(n, gain, bias, wq, wk, wv, wu, blocks):
    count = len(blocks)
    rows = blocks[0].shape[0] * count
    feat, cols = wq.shape
    hidden = wu.shape[1]
    width = 2 * cols
    up = jax.ShapeDtypeStruct((2 * blocks[0].shape[0], hidden), jnp.bfloat16)
    part = jax.ShapeDtypeStruct((rows, 3 * cols // 2), jnp.bfloat16)
    return pl.pallas_call(
        functools.partial(project_kernel, count),
        out_shape=(part, part) + (up,) * (count // 2),
        in_specs=[SMEM, VMEM, VMEM, ANY, ANY, ANY, ANY] + [VMEM] * count,
        out_specs=(VMEM,) * (2 + count // 2),
        scratch_shapes=[
            pltpu.VMEM((rows, feat), jnp.bfloat16),
            pltpu.VMEM((rows, feat), jnp.bfloat16),
            pltpu.VMEM((feat, 3 * cols), jnp.bfloat16),
            pltpu.VMEM((hidden // width, feat, width), jnp.bfloat16),
            pltpu.SemaphoreType.DMA((3 + hidden // width,)),
        ],
        compiler_params=pltpu.CompilerParams(vmem_limit_bytes=58 * MIB),
        name="project",
    )(n, gain, bias, wq, wk, wv, wu, *blocks)


def attend_kernel(count, span, bias_ref, cos_ref, sin_ref, query_ref, key_ref, *refs):
    mine, got = refs[:count], refs[count : 2 * count]
    att_ref, kv_ref, queries, keys, values = refs[2 * count :]
    heads = queries.shape[0]
    half = att_ref.shape[1]
    total = att_ref.shape[0]
    half_rot = ROTARY // 2
    offset = 0
    for g in range(count):
        rows = mine[g].shape[0]
        at = slice(offset, offset + rows)
        offset += rows
        summed = mine[g][...].astype(jnp.float32) + got[g][...].astype(jnp.float32) + bias_ref[...]
        cosine, sine = cos_ref[at, :], sin_ref[at, :]
        lane = lax.broadcasted_iota(jnp.int32, (rows, HEAD_PAD), 1)
        pad = jnp.zeros((rows, HEAD_PAD - HEAD_DIM), jnp.float32)
        for kind in range(3):
            kept = []
            for h in range(heads):
                begin = kind * half + h * HEAD_DIM
                u = jnp.concatenate([summed[:, begin : begin + HEAD_DIM], pad], axis=1)
                if kind < 2:
                    other = jnp.where(
                        lane < half_rot,
                        pltpu.roll(u, HEAD_PAD - half_rot, 1),
                        pltpu.roll(u, half_rot, 1),
                    )
                    u = u * cosine + other * sine
                (queries, keys, values)[kind][h, at, :] = u.astype(jnp.bfloat16)
                kept.append(u[:, :HEAD_DIM])
            if kind > 0:
                kv_ref[at, (kind - 1) * half : kind * half] = jnp.concatenate(kept, axis=1).astype(
                    jnp.bfloat16
                )
    tile = 256
    for start in range(0, total, tile):
        at = slice(start, start + tile)
        info = query_ref[at, :]
        token, begin, end = info[:, 0:1], info[:, 1:2], info[:, 2:3]
        key_token = key_ref[...]
        near = key_token > token - span
        allowed = (key_token >= begin) & (key_token <= token) & (near | (key_token < end))
        outs = []
        for h in range(heads):
            scores = lax.dot_general(
                queries[h, at, :],
                keys[h],
                (((1,), (1,)), ((), ())),
                preferred_element_type=jnp.float32,
            ) * (1.0 / HEAD_DIM**0.5)
            masked = jnp.where(allowed, scores, -1e30)
            weights = jnp.exp(masked - jnp.max(masked, axis=1, keepdims=True))
            probs = weights / jnp.sum(weights, axis=1, keepdims=True)
            out = jnp.dot(probs.astype(jnp.bfloat16), values[h], preferred_element_type=jnp.float32)
            outs.append(out[:, :HEAD_DIM])
        att_ref[at, :] = jnp.concatenate(outs, axis=1).astype(jnp.bfloat16)


def attend(span, bias, cosine, sine, query_info, key_token, mine, got):
    count = len(mine)
    total = cosine.shape[0]
    half = mine[0].shape[1] // 3
    heads = half // HEAD_DIM
    scratch = pltpu.VMEM((heads, total, HEAD_PAD), jnp.bfloat16)
    return pl.pallas_call(
        functools.partial(attend_kernel, count, span),
        out_shape=(
            jax.ShapeDtypeStruct((total, half), jnp.bfloat16),
            jax.ShapeDtypeStruct((total, 2 * half), jnp.bfloat16),
        ),
        in_specs=[VMEM] * (5 + 2 * count),
        out_specs=(VMEM, VMEM),
        scratch_shapes=[scratch, scratch, scratch],
        compiler_params=pltpu.CompilerParams(vmem_limit_bytes=58 * MIB),
        name="attend",
    )(bias, cosine, sine, query_info, key_token, *mine, *got)


def gelu(u):
    return u * (1.0 + lax.erf(u * (0.5**0.5))) * 0.5


def down_kernel(count, bias_ref, wd_ref, *refs):
    mine, got = refs[:count], refs[count : 2 * count]
    out_ref, units, wd, sems = refs[2 * count :]
    rows = mine[0].shape[0]
    tiles, _, width = wd.shape
    copies = [
        pltpu.make_async_copy(wd_ref.at[:, t * width : (t + 1) * width], wd.at[t], sems.at[t])
        for t in range(tiles)
    ]
    for copy in copies:
        copy.start()
    step = 384
    for i in range(count):
        for c in range(0, mine[i].shape[1], step):
            at = slice(c, c + step)
            u = mine[i][:, at].astype(jnp.float32) + got[i][:, at].astype(jnp.float32)
            u = gelu(u + bias_ref[:, at])
            units[i * rows : (i + 1) * rows, at] = u.astype(jnp.bfloat16)
    for t in range(tiles):
        copies[t].wait()
        out = jnp.dot(units[...], wd[t], preferred_element_type=jnp.float32)
        out_ref[:, t * width : (t + 1) * width] = out.astype(jnp.bfloat16)


def down(bias, mine, got, wd):
    count = len(mine)
    rows, hidden = mine[0].shape
    feat = wd.shape[1]
    width = 512
    return pl.pallas_call(
        functools.partial(down_kernel, count),
        out_shape=jax.ShapeDtypeStruct((count * rows, feat), jnp.bfloat16),
        in_specs=[VMEM, ANY] + [VMEM] * (2 * count),
        out_specs=VMEM,
        scratch_shapes=[
            pltpu.VMEM((count * rows, hidden), jnp.bfloat16),
            pltpu.VMEM((feat // width, hidden, width), jnp.bfloat16),
            pltpu.SemaphoreType.DMA((feat // width,)),
        ],
        compiler_params=pltpu.CompilerParams(vmem_limit_bytes=58 * MIB),
        name="down",
    )(bias, wd, *mine, *got)


def mix_kernel(offsets, n_ref, down_ref, att_ref, other_ref, wo_ref, own_ref, sib_ref):
    half = att_ref.shape[1]
    rows = own_ref.shape[0] // len(offsets)
    n = n_ref[0]
    here = pl.ds(pl.multiple_of(n * half, 16), half)
    there = pl.ds(pl.multiple_of((1 - n) * half, 16), half)
    mine = jnp.concatenate([att_ref[o : o + 2 * rows, :] for o in offsets], axis=0)
    other = jnp.concatenate([other_ref[o : o + 2 * rows, :] for o in offsets], axis=0)
    width = 512
    for c in range(0, own_ref.shape[1], width):
        at = slice(c, c + width)
        out = down_ref[:, at].astype(jnp.float32)
        out += jnp.dot(mine, wo_ref[here, at], preferred_element_type=jnp.float32)
        out += jnp.dot(other, wo_ref[there, at], preferred_element_type=jnp.float32)
        out = out.astype(jnp.bfloat16)
        for i in range(len(offsets)):
            own_ref[i * rows : (i + 1) * rows, at] = out[2 * i * rows : (2 * i + 1) * rows]
            sib_ref[i * rows : (i + 1) * rows, at] = out[(2 * i + 1) * rows : (2 * i + 2) * rows]


def mix(n, offsets, partial_down, att, other, wo):
    rows, feat = partial_down.shape
    shape = jax.ShapeDtypeStruct((rows // 2, feat), jnp.bfloat16)
    return pl.pallas_call(
        functools.partial(mix_kernel, offsets),
        out_shape=(shape, shape),
        in_specs=[SMEM] + [VMEM] * 4,
        out_specs=(VMEM, VMEM),
        compiler_params=pltpu.CompilerParams(vmem_limit_bytes=58 * MIB),
        name="mix",
    )(n, partial_down, att, other, wo)


def output_kernel(
    offset, n_ref, bias_ref, mine_ref, got_ref, att_ref, other_ref, wo_ref, wd_ref, own_ref, sib_ref, *scratch
):
    units, wo, wd, sems = scratch
    rows = mine_ref.shape[0]
    half = att_ref.shape[1]
    tiles, _, width = wd.shape
    own_rows = own_ref.shape[0]
    copies = []
    for t in range(tiles):
        at = slice(t * width, (t + 1) * width)
        copies.append(pltpu.make_async_copy(wd_ref.at[:, at], wd.at[t], sems.at[2 * t]))
        copies.append(pltpu.make_async_copy(wo_ref.at[:, at], wo.at[t], sems.at[2 * t + 1]))
    for copy in copies:
        copy.start()
    step = 384
    for c in range(0, mine_ref.shape[1], step):
        at = slice(c, c + step)
        u = mine_ref[:, at].astype(jnp.float32) + got_ref[:, at].astype(jnp.float32)
        units[:, at] = gelu(u + bias_ref[:, at]).astype(jnp.bfloat16)
    n = n_ref[0]
    here = pl.ds(pl.multiple_of(n * half, 16), half)
    there = pl.ds(pl.multiple_of((1 - n) * half, 16), half)
    span = slice(offset, offset + rows)
    for t in range(tiles):
        copies[2 * t].wait()
        copies[2 * t + 1].wait()
        out = jnp.dot(units[...], wd[t], preferred_element_type=jnp.float32)
        out += jnp.dot(att_ref[span, :], wo[t, here, :], preferred_element_type=jnp.float32)
        out += jnp.dot(other_ref[span, :], wo[t, there, :], preferred_element_type=jnp.float32)
        out = out.astype(jnp.bfloat16)
        at = slice(t * width, (t + 1) * width)
        own_ref[:, at] = out[:own_rows]
        sib_ref[:, at] = out[own_rows:]


def output(n, offset, bias, mine, got, att, other, wo, wd):
    rows, hidden = mine.shape
    feat = wd.shape[1]
    width = 512
    tiles = feat // width
    shape = jax.ShapeDtypeStruct((rows // 2, feat), jnp.bfloat16)
    return pl.pallas_call(
        functools.partial(output_kernel, offset),
        out_shape=(shape, shape),
        in_specs=[SMEM] + [VMEM] * 5 + [ANY] * 2,
        out_specs=(VMEM, VMEM),
        scratch_shapes=[
            pltpu.VMEM((rows, hidden), jnp.bfloat16),
            pltpu.VMEM((tiles, wo.shape[0], width), jnp.bfloat16),
            pltpu.VMEM((tiles, hidden, width), jnp.bfloat16),
            pltpu.SemaphoreType.DMA((2 * tiles,)),
        ],
        compiler_params=pltpu.CompilerParams(vmem_limit_bytes=58 * MIB),
        name="output",
    )(n, bias, mine, got, att, other, wo, wd)


def after(*values):
    return lax.optimization_barrier(values)


def local_ring(
    hidden_in,
    w_query,
    w_key,
    w_value,
    qkv_bias,
    w_up,
    up_bias,
    w_attn_out,
    w_down,
    out_bias,
    norm_gain,
    norm_bias,
    seq_lens,
    sink_count,
    page_table,
):
    wide_index = lax.axis_index("wide")
    n = lax.axis_index("narrow").astype(jnp.int32)
    n_arg = n.reshape(1)
    rows, feat = hidden_in.shape
    total_tokens = rows * lax.axis_size("wide")
    half = w_query.shape[1] // 2

    fwd_pairs, bwd_pairs, swap_pairs = [], [], []
    for p in range(CHIPS):
        here, next_chip = CHIP_RING[p], CHIP_RING[(p + 1) % CHIPS]
        fwd_pairs += [(2 * here, 2 * next_chip), (2 * next_chip + 1, 2 * here + 1)]
        bwd_pairs += [(2 * next_chip, 2 * here), (2 * here + 1, 2 * next_chip + 1)]
        swap_pairs += [(2 * here, 2 * here + 1), (2 * here + 1, 2 * here)]
    fwd = lambda v: lax.ppermute(v, "wide", fwd_pairs)
    bwd = lambda v: lax.ppermute(v, "wide", bwd_pairs)
    swap = lambda v: lax.ppermute(v, "wide", swap_pairs)
    cross = lambda v: lax.ppermute(v, "narrow", [(0, 1), (1, 0)])

    sums = pl.pallas_call(
        sums_kernel,
        out_shape=jax.ShapeDtypeStruct((rows, STAT), jnp.float32),
        in_specs=[VMEM],
        out_specs=VMEM,
        name="row_sums",
    )(hidden_in)
    first_block = pl.pallas_call(
        block_kernel,
        out_shape=jax.ShapeDtypeStruct((rows, feat + STAT), jnp.bfloat16),
        in_specs=[VMEM] * 3,
        out_specs=VMEM,
        name="first_block",
    )(hidden_in, sums, cross(sums))

    owners = lax.dynamic_index_in_dim(jnp.asarray(owner_table()), wide_index, 0, keepdims=False)
    token_ids = (owners[:, None] * rows + jnp.arange(rows, dtype=jnp.int32)[None, :]).reshape(-1)
    _, pos, sink = segment_info(token_ids, seq_lens, sink_count)
    begin = token_ids - pos
    query_info = jnp.stack([token_ids, begin, begin + sink], axis=1)
    lane = jnp.arange(HEAD_PAD, dtype=jnp.int32)
    half_rot = ROTARY // 2
    freq_index = (lane % half_rot).astype(jnp.float32)
    inverse = jnp.power(jnp.float32(10000.0), -2.0 * freq_index / ROTARY)
    angles = pos.astype(jnp.float32)[:, None] * inverse[None, :]
    turned = (lane < ROTARY)[None, :]
    cosine = jnp.where(turned, jnp.cos(angles), 1.0)
    sine = jnp.where(turned, jnp.sin(angles), 0.0)
    sine = jnp.where((lane < half_rot)[None, :], -sine, sine)
    bias_half = lax.dynamic_slice_in_dim(qkv_bias, n * half, half, 1).reshape(1, 3 * half)

    up_row = up_bias[None, :]

    def prepare(*blocks):
        return project(n_arg, norm_gain, norm_bias, w_query, w_key, w_value, w_up, list(blocks))

    def add(*terms):
        return sum(t.astype(jnp.float32) for t in terms).astype(jnp.bfloat16)

    def finish(name, u, v):
        return output(
            n_arg, PAIRS.index(name) * 2 * rows, up_row, u, v, att, other, w_attn_out, w_down
        )

    def pair(halves, *running):
        return add(halves[0], swap(halves[1]), *running)

    pages = page_table.shape[0]
    per_device = pages // 2
    numbers = jnp.arange(pages, dtype=jnp.int32)
    slots = (numbers + n * per_device) % pages
    page_of_slot = jnp.sum(
        (page_table[None, :] == slots[:, None]).astype(jnp.int32) * numbers[None, :], axis=1
    )
    page_held = token_ids[::PAGE] // PAGE
    held_at = jnp.sum(
        (page_held[None, :] == page_of_slot[:, None]).astype(jnp.int32) * numbers[None, :], axis=1
    )

    o0 = first_block
    f1, b1, s0 = fwd(o0), bwd(o0), swap(o0)
    send0, kept0, u_o0 = prepare(o0, s0)
    f1, b1, send0, kept0, u_o0 = after(f1, b1, send0, kept0, u_o0)
    got0, v_o0 = cross(send0), cross(u_o0)
    f2, b2 = fwd(f1), bwd(b1)
    send1, kept1, u_f1, u_b1 = prepare(f1, swap(f1), b1, swap(b1))
    f2, b2, got0, v_o0, send1, u_b1, u_f1 = after(f2, b2, got0, v_o0, send1, u_b1, u_f1)
    got1, v_b1 = cross(send1), cross(u_b1)
    f3, b3 = fwd(f2), bwd(b2)
    send2, kept2, u_f2, u_b2 = prepare(f2, swap(f2), b2, swap(b2))
    f3, b3, got1, v_b1, send2, u_f2, u_b2 = after(f3, b3, got1, v_b1, send2, u_f2, u_b2)
    got2, v_f2 = cross(send2), cross(u_f2)
    f4 = fwd(f3)
    send3, kept3, u_f3, u_b3 = prepare(f3, swap(f3), b3, swap(b3))
    f4, got2, v_f2, send3, u_f3, u_b3 = after(f4, got2, v_f2, send3, u_f3, u_b3)
    got3 = cross(send3)
    send4, kept4, u_f4 = prepare(f4, swap(f4))
    got3, send4, u_f4, u_f3, u_b3 = after(got3, send4, u_f4, u_f3, u_b3)
    got4 = cross(send4)
    got4, u_f4, cosine, sine, query_info, key_token, bias_half, held_at = after(
        got4, u_f4, cosine, sine, query_info, token_ids[None, :], bias_half, held_at
    )
    v_f4 = cross(u_f4)
    att, kv = attend(
        total_tokens // 16, bias_half, cosine, sine, query_info, key_token,
        [kept0, kept1, kept2, kept3, kept4], [got0, got1, got2, got3, got4],
    )
    v_f4, att, u_b3 = after(v_f4, att, u_b3)
    other = cross(att)
    early = down(up_row, [u_o0, u_b1, u_f2], [v_o0, v_b1, v_f2], w_down)
    other, early, u_b3, u_f3, u_b2, u_f1 = after(other, early, u_b3, u_f3, u_b2, u_f1)
    v_b3 = cross(u_b3)
    y_f4 = finish("f4", u_f4, v_f4)
    m_own, m_sib = mix(
        n_arg, tuple(PAIRS.index(p) * 2 * rows for p in ("o0", "b1", "f2")), early, att, other,
        w_attn_out,
    )
    v_b3, y_f4, m_own, m_sib, u_f3 = after(v_b3, y_f4, m_own, m_sib, u_f3)
    v_f3 = cross(u_f3)
    r_b = bwd(pair(y_f4))
    m_got = swap(m_sib)
    y_b3 = finish("b3", u_b3, v_b3)
    v_f3, r_b, m_got, y_b3, u_b2 = after(v_f3, r_b, m_got, y_b3, u_b2)
    v_b2 = cross(u_b2)
    r_f = fwd(pair(y_b3))
    y_f3 = finish("f3", u_f3, v_f3)
    v_b2, r_f, y_f3, r_b, u_f1 = after(v_b2, r_f, y_f3, r_b, u_f1)
    v_f1 = cross(u_f1)
    r_b = bwd(pair(y_f3, r_b))
    y_b2 = finish("b2", u_b2, v_b2)
    v_f1, r_b, y_b2, r_f, kv = after(v_f1, r_b, y_b2, r_f, kv)
    r_f = fwd(pair(y_b2, r_f))
    r_b = bwd(add(r_b, m_own[2 * rows :], m_got[2 * rows :]))
    y_f1 = finish("f1", u_f1, v_f1)
    r_f, r_b, y_f1, kv = after(r_f, r_b, y_f1, kv)
    r_f = fwd(add(r_f, m_own[rows : 2 * rows], m_got[rows : 2 * rows]))
    r_b = bwd(pair(y_f1, r_b))
    paged = jnp.take(kv.reshape(pages, PAGE, 2 * half), held_at, axis=0)
    cache_got = cross(paged[per_device:])
    summed = (
        r_b.astype(jnp.float32)
        + r_f.astype(jnp.float32)
        + m_own[:rows].astype(jnp.float32)
        + m_got[:rows].astype(jnp.float32)
    )
    hidden_out = (hidden_in.astype(jnp.float32) + summed + out_bias).astype(jnp.bfloat16)
    cache_mine = paged[:per_device]

    left = jnp.where(n == 0, cache_mine, cache_got)
    right = jnp.where(n == 0, cache_got, cache_mine)
    paged_cache = jnp.stack(
        [
            jnp.concatenate([left[..., :half], right[..., :half]], axis=-1),
            jnp.concatenate([left[..., half:], right[..., half:]], axis=-1),
        ]
    )
    return (hidden_out, paged_cache)


def solution(mesh):
    in_specs = (
        P("wide", "narrow"),
        P("narrow", "wide"),
        P("narrow", "wide"),
        P("narrow", "wide"),
        P(None, "wide"),
        P("narrow", "wide"),
        P("wide"),
        P("wide", "narrow"),
        P("wide", "narrow"),
        P("narrow"),
        P(None, "narrow"),
        P(None, "narrow"),
        P(),
        P(),
        P(),
    )
    out_specs = (P("wide", "narrow"), P(None, "narrow", None, "wide"))
    ringed = mesh.shape["wide"] == 2 * CHIPS and mesh.shape["narrow"] == 2
    local = local_ring if ringed else local_generic
    return jax.shard_map(local, mesh=mesh, in_specs=in_specs, out_specs=out_specs, check_vma=False)
```

```python
import functools

import jax
import jax.numpy as jnp
import numpy as np
from jax import lax
from jax.experimental import pallas as pl
from jax.experimental.pallas import tpu as pltpu
from jax.sharding import PartitionSpec as P

D = 6144
HEAD_DIM = 96
ROTARY = 24
PAGE = 16


def segment_info(token_index, seq_lens, sink_count):
    seq_ends = jnp.cumsum(seq_lens)
    seq_starts = seq_ends - seq_lens
    inside = (token_index[:, None] >= seq_starts[None, :]) & (
        token_index[:, None] < seq_ends[None, :]
    )
    member = inside.astype(jnp.int32)
    seq_number = jnp.arange(seq_lens.shape[0], dtype=jnp.int32)
    segment = jnp.sum(member * seq_number[None, :], axis=1)
    position = token_index - jnp.sum(member * seq_starts[None, :], axis=1)
    sink_limit = jnp.sum(member * sink_count[None, :], axis=1)
    return (segment, position, sink_limit)


def rotate(values, position):
    half_rot = ROTARY // 2
    freq_index = jnp.arange(half_rot, dtype=jnp.float32)
    inverse = jnp.power(jnp.float32(10000.0), -2.0 * freq_index / ROTARY)
    angles = position.astype(jnp.float32)[:, None] * inverse[None, :]
    cosine = jnp.cos(angles)[:, None, :]
    sine_part = jnp.sin(angles)[:, None, :]
    first_half = values[..., :half_rot]
    second_half = values[..., half_rot:ROTARY]
    return jnp.concatenate(
        [
            first_half * cosine - second_half * sine_part,
            second_half * cosine + first_half * sine_part,
            values[..., ROTARY:],
        ],
        axis=-1,
    )


def local_generic(
    hidden_in,
    w_query,
    w_key,
    w_value,
    qkv_bias,
    w_up,
    up_bias,
    w_attn_out,
    w_down,
    out_bias,
    norm_gain,
    norm_bias,
    seq_lens,
    sink_count,
    page_table,
):
    wide_count = lax.axis_size("wide")
    narrow_count = lax.axis_size("narrow")
    narrow_index = lax.axis_index("narrow")
    tok_local, feat_local = hidden_in.shape
    sub_rows = tok_local // narrow_count
    total_tokens = tok_local * wide_count
    query_rows = wide_count * sub_rows
    head_cols = w_query.shape[1]
    heads_local = head_cols // HEAD_DIM
    as_float = hidden_in.astype(jnp.float32)
    partial_sum = jnp.sum(as_float, axis=1)
    partial_square = jnp.sum(as_float * as_float, axis=1)
    total_sum, total_square = lax.psum((partial_sum, partial_square), "narrow")
    average = total_sum / D
    variance = total_square / D - average * average
    scaled = (as_float - average[:, None]) * lax.rsqrt(variance + 1e-05)[:, None]
    attn_normed = (scaled * norm_gain[0] + norm_bias[0]).astype(jnp.bfloat16)
    mlp_normed = (scaled * norm_gain[1] + norm_bias[1]).astype(jnp.bfloat16)
    stacked = jnp.stack([attn_normed, mlp_normed]).reshape(2, narrow_count, sub_rows, feat_local)
    gathered = lax.all_gather(stacked, "wide", axis=2, tiled=True).reshape(
        2, total_tokens, feat_local
    )
    local_order = jnp.arange(query_rows, dtype=jnp.int32)
    local_tokens = (
        local_order // sub_rows * tok_local + narrow_index * sub_rows + local_order % sub_rows
    )
    local_seg, local_pos, local_sink = segment_info(local_tokens, seq_lens, sink_count)
    all_order = jnp.arange(total_tokens, dtype=jnp.int32)
    all_tokens = (
        all_order % query_rows // sub_rows * tok_local
        + all_order // query_rows * sub_rows
        + all_order % sub_rows
    )
    all_seg, all_pos, all_sink = segment_info(all_tokens, seq_lens, sink_count)
    qkv_weight = jnp.concatenate([w_query, w_key, w_value], axis=1)
    attn_part = gathered[0]
    mlp_part = gathered[1]
    summed = lax.psum_scatter(
        jnp.concatenate(
            [
                jnp.dot(attn_part, qkv_weight, preferred_element_type=jnp.float32),
                jnp.dot(mlp_part, w_up, preferred_element_type=jnp.float32),
            ],
            axis=1,
        ).astype(jnp.bfloat16),
        "narrow",
        scatter_dimension=0,
        tiled=True,
    ).astype(jnp.float32)
    query_sum = summed[:, :head_cols]
    key_sum = summed[:, head_cols : 2 * head_cols]
    value_sum = summed[:, 2 * head_cols : 3 * head_cols]
    unit_sum = summed[:, 3 * head_cols :]
    keys_local = (
        rotate((key_sum + qkv_bias[1]).reshape(query_rows, heads_local, HEAD_DIM), local_pos)
        .astype(jnp.bfloat16)
        .reshape(query_rows, head_cols)
    )
    values_local = (value_sum + qkv_bias[2]).astype(jnp.bfloat16)
    all_keys, all_values = (
        lax.all_gather(keys_local, "narrow", axis=0, tiled=True),
        lax.all_gather(values_local, "narrow", axis=0, tiled=True),
    )
    queries = rotate(
        (query_sum + qkv_bias[0]).reshape(query_rows, heads_local, HEAD_DIM), local_pos
    ).astype(jnp.bfloat16)
    hidden_units = jax.nn.gelu(unit_sum + up_bias, approximate=False).astype(jnp.bfloat16)
    window_span = total_tokens // 16
    allowed = (local_seg[:, None] == all_seg[None, :]) & (all_pos[None, :] <= local_pos[:, None])
    allowed = allowed & (
        (local_pos[:, None] - all_pos[None, :] < window_span)
        | (all_pos[None, :] < local_sink[:, None])
    )
    key_heads = all_keys.reshape(total_tokens, heads_local, HEAD_DIM)
    value_heads = all_values.reshape(total_tokens, heads_local, HEAD_DIM)
    scores = jnp.einsum("qhd,khd->hqk", queries, key_heads, preferred_element_type=jnp.float32) * (
        1.0 / HEAD_DIM**0.5
    )
    masked = jnp.where(allowed[None], scores, jnp.float32(-1e30))
    top_score = jnp.max(masked, axis=2, keepdims=True)
    weights = jnp.exp(masked - top_score)
    probs = (weights / jnp.sum(weights, axis=2, keepdims=True)).astype(jnp.bfloat16)
    attended = (
        jnp.einsum("hqk,khd->qhd", probs, value_heads, preferred_element_type=jnp.float32)
        .astype(jnp.bfloat16)
        .reshape(query_rows, head_cols)
    )
    full_out, full_down = (
        lax.all_gather(w_attn_out, "narrow", axis=1, tiled=True),
        lax.all_gather(w_down, "narrow", axis=1, tiled=True),
    )
    attn_part = attended
    own_rows = lax.psum_scatter(
        (
            jnp.dot(attn_part, full_out, preferred_element_type=jnp.float32)
            + jnp.dot(hidden_units, full_down, preferred_element_type=jnp.float32)
        ).astype(jnp.bfloat16),
        "wide",
        scatter_dimension=0,
        tiled=True,
    ).astype(jnp.float32)
    combined = lax.all_to_all(
        own_rows.astype(jnp.bfloat16), "narrow", split_axis=1, concat_axis=0, tiled=True
    ).astype(own_rows.dtype)
    hidden_out = (as_float + combined + out_bias).astype(jnp.bfloat16)
    pages_local = page_table.shape[0] // narrow_count
    slot_ids = narrow_index * pages_local + jnp.arange(pages_local, dtype=jnp.int32)
    matches = (page_table[None, :] == slot_ids[:, None]).astype(jnp.int32)
    source_page = jnp.sum(
        matches * jnp.arange(page_table.shape[0], dtype=jnp.int32)[None, :], axis=1
    )
    token_ids = (source_page[:, None] * PAGE + jnp.arange(PAGE, dtype=jnp.int32)[None, :]).reshape(
        -1
    )
    gather_rows = (
        token_ids % tok_local // sub_rows * query_rows
        + token_ids // tok_local * sub_rows
        + token_ids % sub_rows
    )
    cache_keys = jnp.take(all_keys, gather_rows, axis=0).reshape(pages_local, PAGE, head_cols)
    cache_values = jnp.take(all_values, gather_rows, axis=0).reshape(pages_local, PAGE, head_cols)
    paged_cache = jnp.stack([cache_keys, cache_values])
    return (hidden_out, paged_cache)


CHIP_RING = (0, 2, 4, 6, 7, 5, 3, 1)
CHIPS = len(CHIP_RING)
PAIRS = ("o0", "f1", "b1", "f2", "b2", "f3", "b3", "f4")
STAT = 128
HEAD_PAD = 128
MIB = 1 << 20
VMEM = pl.BlockSpec(memory_space=pltpu.VMEM)
HBM = pl.BlockSpec(memory_space=pltpu.HBM)
SMEM = pl.BlockSpec(memory_space=pltpu.SMEM)


def owner_table():
    table = np.zeros((2 * CHIPS, 2 * CHIPS), np.int32)
    for place, chip in enumerate(CHIP_RING):
        for core in range(2):
            order = []
            for pair in PAIRS:
                shift = (-1 if pair[0] == "f" else 1) * int(pair[1]) * (1 - 2 * core)
                order.append(CHIP_RING[(place + shift) % CHIPS] * 2 + core)
                order.append(CHIP_RING[(place - shift) % CHIPS] * 2 + 1 - core)
            table[2 * chip + core] = order
    return table


def sums_kernel(x_ref, out_ref):
    x = x_ref[...].astype(jnp.float32)
    first = jnp.sum(x, axis=1, keepdims=True)
    second = jnp.sum(x * x, axis=1, keepdims=True)
    lane = lax.broadcasted_iota(jnp.int32, out_ref.shape, 1)
    out_ref[...] = jnp.where(lane == 0, first, jnp.where(lane == 1, second, 0.0))


def block_kernel(x_ref, here_ref, there_ref, out_ref):
    feat = x_ref.shape[1]
    total = here_ref[...] + there_ref[...]
    average = total[:, 0:1] / D
    variance = total[:, 1:2] / D - average * average
    scale = lax.rsqrt(variance + 1e-05)
    lane = lax.broadcasted_iota(jnp.int32, (x_ref.shape[0], STAT), 1)
    tail = jnp.zeros((x_ref.shape[0], STAT), jnp.float32)
    for start, value in ((0, average), (3, scale)):
        for term in range(3):
            piece = value.astype(jnp.bfloat16).astype(jnp.float32)
            tail = jnp.where(lane == start + term, piece, tail)
            value = value - piece
    out_ref[:, :feat] = x_ref[...]
    out_ref[:, feat:] = tail.astype(jnp.bfloat16)


def normalise(blocks, gain_ref, bias_ref, attn, mlp):
    rows = blocks[0].shape[0]
    feat = attn.shape[1]
    step = 512
    for b, block in enumerate(blocks):
        tail = block[:, feat:].astype(jnp.float32)
        average = tail[:, 0:1] + tail[:, 1:2] + tail[:, 2:3]
        scale = tail[:, 3:4] + tail[:, 4:5] + tail[:, 5:6]
        here = slice(b * rows, (b + 1) * rows)
        for c in range(0, feat, step):
            at = slice(c, c + step)
            scaled = (block[:, at].astype(jnp.float32) - average) * scale
            attn[here, at] = (scaled * gain_ref[0:1, at] + bias_ref[0:1, at]).astype(jnp.bfloat16)
            mlp[here, at] = (scaled * gain_ref[1:2, at] + bias_ref[1:2, at]).astype(jnp.bfloat16)


def project_kernel(count, first_call, n_ref, gain_ref, bias_ref, wq_ref, wk_ref, wv_ref, wu_ref, *refs):
    blocks, refs = refs[:count], refs[count:]
    send_ref, mine_ref, refs = refs[0], refs[1], refs[2:]
    ups, refs = refs[: count // 2], refs[count // 2 :]
    width = 384
    tiles = wu_ref.shape[1] // width
    copies = []
    if first_call:
        sources = (wq_ref, wk_ref, wv_ref)
        held, refs = refs[:4], refs[4:]
        attn, mlp, gain, bias, sems = refs
        affine = [
            pltpu.make_async_copy(gain_ref, gain, sems.at[3 + tiles]),
            pltpu.make_async_copy(bias_ref, bias, sems.at[4 + tiles]),
        ]
        for copy in affine:
            copy.start()
        gain_ref, bias_ref = gain, bias
        copies = [
            pltpu.make_async_copy(src, dst, sems.at[i])
            for i, (src, dst) in enumerate(zip(sources, held))
        ]
        for t in range(tiles):
            at = slice(t * width, (t + 1) * width)
            copies.append(pltpu.make_async_copy(wu_ref.at[:, at], held[3].at[:, at], sems.at[3 + t]))
        for copy in copies:
            copy.start()
        for copy in affine:
            copy.wait()
        wq_ref, wk_ref, wv_ref, wu_ref = held
    else:
        attn, mlp = refs
    rows = blocks[0].shape[0]
    half = wq_ref.shape[1] // 2
    normalise(blocks, gain_ref, bias_ref, attn, mlp)
    low, high = [], []
    for i, weight in enumerate((wq_ref, wk_ref, wv_ref)):
        if first_call:
            copies[i].wait()
        part = jnp.dot(attn[...], weight[...], preferred_element_type=jnp.float32)
        low.append(part[:, :half])
        high.append(part[:, half:])
    low = jnp.concatenate(low, axis=1).astype(jnp.bfloat16)
    high = jnp.concatenate(high, axis=1).astype(jnp.bfloat16)
    first = n_ref[0] == 0
    send_ref[...] = jnp.where(first, high, low)
    mine_ref[...] = jnp.where(first, low, high)
    for t in range(tiles):
        if first_call:
            copies[3 + t].wait()
        at = slice(t * width, (t + 1) * width)
        part = jnp.dot(mlp[...], wu_ref[:, at], preferred_element_type=jnp.float32)
        part = part.astype(jnp.bfloat16)
        for u, up in enumerate(ups):
            up[:, at] = part[2 * u * rows : 2 * (u + 1) * rows]


def project(n, gain, bias, weights, blocks, first_call=False):
    count = len(blocks)
    rows = blocks[0].shape[0] * count
    feat, cols = weights[0].shape
    hidden = weights[3].shape[1]
    up = jax.ShapeDtypeStruct((2 * blocks[0].shape[0], hidden), jnp.bfloat16)
    part = jax.ShapeDtypeStruct((rows, 3 * cols // 2), jnp.bfloat16)
    shapes = (part, part) + (up,) * (count // 2)
    scratch = [
        pltpu.VMEM((rows, feat), jnp.bfloat16),
        pltpu.VMEM((rows, feat), jnp.bfloat16),
    ]
    if first_call:
        shapes += tuple(jax.ShapeDtypeStruct(w.shape, w.dtype) for w in weights)
        scratch += [pltpu.VMEM(gain.shape, gain.dtype), pltpu.VMEM(bias.shape, bias.dtype)]
        scratch.append(pltpu.SemaphoreType.DMA((5 + hidden // 384,)))
    return pl.pallas_call(
        functools.partial(project_kernel, count, first_call),
        out_shape=shapes,
        in_specs=[SMEM] + [HBM if first_call else VMEM] * 6 + [VMEM] * count,
        out_specs=(VMEM,) * len(shapes),
        scratch_shapes=scratch,
        compiler_params=pltpu.CompilerParams(vmem_limit_bytes=(28 if first_call else 12) * MIB),
        name="project",
    )(n, gain, bias, *weights, *blocks)


def attend_kernel(count, span, bias_ref, cos_ref, sin_ref, query_ref, key_ref, *refs):
    mine, got = refs[:count], refs[count : 2 * count]
    att_ref, kv_ref, queries, keys, values = refs[2 * count :]
    heads = queries.shape[0]
    half = att_ref.shape[1]
    total = att_ref.shape[0]
    half_rot = ROTARY // 2
    offset = 0
    for g in range(count):
        rows = mine[g].shape[0]
        at = slice(offset, offset + rows)
        offset += rows
        summed = mine[g][...].astype(jnp.float32) + got[g][...].astype(jnp.float32) + bias_ref[...]
        cosine, sine = cos_ref[at, :], sin_ref[at, :]
        lane = lax.broadcasted_iota(jnp.int32, (rows, HEAD_PAD), 1)
        pad = jnp.zeros((rows, HEAD_PAD - HEAD_DIM), jnp.float32)
        for kind in range(3):
            kept = []
            for h in range(heads):
                begin = kind * half + h * HEAD_DIM
                u = jnp.concatenate([summed[:, begin : begin + HEAD_DIM], pad], axis=1)
                if kind < 2:
                    other = jnp.where(
                        lane < half_rot,
                        pltpu.roll(u, HEAD_PAD - half_rot, 1),
                        pltpu.roll(u, half_rot, 1),
                    )
                    u = u * cosine + other * sine
                (queries, keys, values)[kind][h, at, :] = u.astype(jnp.bfloat16)
                kept.append(u[:, :HEAD_DIM])
            if kind > 0:
                kv_ref[at, (kind - 1) * half : kind * half] = jnp.concatenate(kept, axis=1).astype(
                    jnp.bfloat16
                )
    tile = 256
    for start in range(0, total, tile):
        at = slice(start, start + tile)
        info = query_ref[at, :]
        token, begin, end = info[:, 0:1], info[:, 1:2], info[:, 2:3]
        key_token = key_ref[...]
        near = key_token > token - span
        allowed = (key_token >= begin) & (key_token <= token) & (near | (key_token < end))
        outs = []
        for h in range(heads):
            scores = lax.dot_general(
                queries[h, at, :],
                keys[h],
                (((1,), (1,)), ((), ())),
                preferred_element_type=jnp.float32,
            ) * (1.0 / HEAD_DIM**0.5)
            masked = jnp.where(allowed, scores, -1e30)
            weights = jnp.exp(masked - jnp.max(masked, axis=1, keepdims=True))
            probs = weights / jnp.sum(weights, axis=1, keepdims=True)
            out = jnp.dot(probs.astype(jnp.bfloat16), values[h], preferred_element_type=jnp.float32)
            outs.append(out[:, :HEAD_DIM])
        att_ref[at, :] = jnp.concatenate(outs, axis=1).astype(jnp.bfloat16)


def attend(span, bias, cosine, sine, query_info, key_token, mine, got):
    count = len(mine)
    total = cosine.shape[0]
    half = mine[0].shape[1] // 3
    heads = half // HEAD_DIM
    scratch = pltpu.VMEM((heads, total, HEAD_PAD), jnp.bfloat16)
    return pl.pallas_call(
        functools.partial(attend_kernel, count, span),
        out_shape=(
            jax.ShapeDtypeStruct((total, half), jnp.bfloat16),
            jax.ShapeDtypeStruct((total, 2 * half), jnp.bfloat16),
        ),
        in_specs=[VMEM] * (5 + 2 * count),
        out_specs=(VMEM, VMEM),
        scratch_shapes=[scratch, scratch, scratch],
        compiler_params=pltpu.CompilerParams(vmem_limit_bytes=16 * MIB),
        name="attend",
    )(bias, cosine, sine, query_info, key_token, *mine, *got)


def gelu(u):
    return u * (1.0 + lax.erf(u * (0.5**0.5))) * 0.5


def down_kernel(count, bias_ref, wd_ref, *refs):
    mine, got = refs[:count], refs[count : 2 * count]
    out_ref, units = refs[2 * count :]
    rows = mine[0].shape[0]
    step = 384
    for i in range(count):
        for c in range(0, mine[i].shape[1], step):
            at = slice(c, c + step)
            u = mine[i][:, at].astype(jnp.float32) + got[i][:, at].astype(jnp.float32)
            u = gelu(u + bias_ref[:, at])
            units[i * rows : (i + 1) * rows, at] = u.astype(jnp.bfloat16)
    width = 512
    for c in range(0, wd_ref.shape[1], width):
        at = slice(c, c + width)
        out = jnp.dot(units[...], wd_ref[:, at], preferred_element_type=jnp.float32)
        out_ref[:, at] = out.astype(jnp.bfloat16)


def down(bias, mine, got, wd):
    count = len(mine)
    rows, hidden = mine[0].shape
    return pl.pallas_call(
        functools.partial(down_kernel, count),
        out_shape=jax.ShapeDtypeStruct((count * rows, wd.shape[1]), jnp.bfloat16),
        in_specs=[VMEM] * (2 + 2 * count),
        out_specs=VMEM,
        scratch_shapes=[pltpu.VMEM((count * rows, hidden), jnp.bfloat16)],
        compiler_params=pltpu.CompilerParams(vmem_limit_bytes=12 * MIB),
        name="down",
    )(bias, wd, *mine, *got)


def mix_kernel(offsets, n_ref, down_ref, att_ref, other_ref, wo_ref, own_ref, sib_ref):
    half = att_ref.shape[1]
    rows = own_ref.shape[0] // len(offsets)
    n = n_ref[0]
    here = pl.ds(pl.multiple_of(n * half, 16), half)
    there = pl.ds(pl.multiple_of((1 - n) * half, 16), half)
    mine = jnp.concatenate([att_ref[o : o + 2 * rows, :] for o in offsets], axis=0)
    other = jnp.concatenate([other_ref[o : o + 2 * rows, :] for o in offsets], axis=0)
    width = 512
    for c in range(0, own_ref.shape[1], width):
        at = slice(c, c + width)
        out = down_ref[:, at].astype(jnp.float32)
        out += jnp.dot(mine, wo_ref[here, at], preferred_element_type=jnp.float32)
        out += jnp.dot(other, wo_ref[there, at], preferred_element_type=jnp.float32)
        out = out.astype(jnp.bfloat16)
        for i in range(len(offsets)):
            own_ref[i * rows : (i + 1) * rows, at] = out[2 * i * rows : (2 * i + 1) * rows]
            sib_ref[i * rows : (i + 1) * rows, at] = out[(2 * i + 1) * rows : (2 * i + 2) * rows]


def mix(n, offsets, partial_down, att, other, wo):
    rows, feat = partial_down.shape
    shape = jax.ShapeDtypeStruct((rows // 2, feat), jnp.bfloat16)
    return pl.pallas_call(
        functools.partial(mix_kernel, offsets),
        out_shape=(shape, shape),
        in_specs=[SMEM] + [VMEM] * 4,
        out_specs=(VMEM, VMEM),
        compiler_params=pltpu.CompilerParams(vmem_limit_bytes=8 * MIB),
        name="mix",
    )(n, partial_down, att, other, wo)


def output_kernel(
    offset, n_ref, bias_ref, mine_ref, got_ref, att_ref, other_ref, wo_ref, wd_ref, own_ref, sib_ref, units
):
    rows = mine_ref.shape[0]
    half = att_ref.shape[1]
    own_rows = own_ref.shape[0]
    step = 384
    for c in range(0, mine_ref.shape[1], step):
        at = slice(c, c + step)
        u = mine_ref[:, at].astype(jnp.float32) + got_ref[:, at].astype(jnp.float32)
        units[:, at] = gelu(u + bias_ref[:, at]).astype(jnp.bfloat16)
    n = n_ref[0]
    here = pl.ds(pl.multiple_of(n * half, 16), half)
    there = pl.ds(pl.multiple_of((1 - n) * half, 16), half)
    span = slice(offset, offset + rows)
    width = 512
    for c in range(0, wd_ref.shape[1], width):
        at = slice(c, c + width)
        out = jnp.dot(units[...], wd_ref[:, at], preferred_element_type=jnp.float32)
        out += jnp.dot(att_ref[span, :], wo_ref[here, at], preferred_element_type=jnp.float32)
        out += jnp.dot(other_ref[span, :], wo_ref[there, at], preferred_element_type=jnp.float32)
        out = out.astype(jnp.bfloat16)
        own_ref[:, at] = out[:own_rows]
        sib_ref[:, at] = out[own_rows:]


def output(n, offset, bias, mine, got, att, other, wo, wd):
    rows, hidden = mine.shape
    shape = jax.ShapeDtypeStruct((rows // 2, wd.shape[1]), jnp.bfloat16)
    return pl.pallas_call(
        functools.partial(output_kernel, offset),
        out_shape=(shape, shape),
        in_specs=[SMEM] + [VMEM] * 7,
        out_specs=(VMEM, VMEM),
        scratch_shapes=[pltpu.VMEM((rows, hidden), jnp.bfloat16)],
        compiler_params=pltpu.CompilerParams(vmem_limit_bytes=8 * MIB),
        name="output",
    )(n, bias, mine, got, att, other, wo, wd)


def after(*values):
    return lax.optimization_barrier(values)


def local_ring(
    hidden_in,
    w_query,
    w_key,
    w_value,
    qkv_bias,
    w_up,
    up_bias,
    w_attn_out,
    w_down,
    out_bias,
    norm_gain,
    norm_bias,
    seq_lens,
    sink_count,
    page_table,
):
    wide_index = lax.axis_index("wide")
    n = lax.axis_index("narrow").astype(jnp.int32)
    n_arg = n.reshape(1)
    rows, feat = hidden_in.shape
    total_tokens = rows * lax.axis_size("wide")
    half = w_query.shape[1] // 2

    fwd_pairs, bwd_pairs, swap_pairs = [], [], []
    for p in range(CHIPS):
        here, next_chip = CHIP_RING[p], CHIP_RING[(p + 1) % CHIPS]
        fwd_pairs += [(2 * here, 2 * next_chip), (2 * next_chip + 1, 2 * here + 1)]
        bwd_pairs += [(2 * next_chip, 2 * here), (2 * here + 1, 2 * next_chip + 1)]
        swap_pairs += [(2 * here, 2 * here + 1), (2 * here + 1, 2 * here)]
    fwd = lambda v: lax.ppermute(v, "wide", fwd_pairs)
    bwd = lambda v: lax.ppermute(v, "wide", bwd_pairs)
    swap = lambda v: lax.ppermute(v, "wide", swap_pairs)
    cross = lambda v: lax.ppermute(v, "narrow", [(0, 1), (1, 0)])

    sums = pl.pallas_call(
        sums_kernel,
        out_shape=jax.ShapeDtypeStruct((rows, STAT), jnp.float32),
        in_specs=[VMEM],
        out_specs=VMEM,
        name="row_sums",
    )(hidden_in)
    first_block = pl.pallas_call(
        block_kernel,
        out_shape=jax.ShapeDtypeStruct((rows, feat + STAT), jnp.bfloat16),
        in_specs=[VMEM] * 3,
        out_specs=VMEM,
        name="first_block",
    )(hidden_in, sums, cross(sums))

    owners = lax.dynamic_index_in_dim(jnp.asarray(owner_table()), wide_index, 0, keepdims=False)
    token_ids = (owners[:, None] * rows + jnp.arange(rows, dtype=jnp.int32)[None, :]).reshape(-1)
    _, pos, sink = segment_info(token_ids, seq_lens, sink_count)
    begin = token_ids - pos
    query_info = jnp.stack([token_ids, begin, begin + sink], axis=1)
    lane = jnp.arange(HEAD_PAD, dtype=jnp.int32)
    half_rot = ROTARY // 2
    freq_index = (lane % half_rot).astype(jnp.float32)
    inverse = jnp.power(jnp.float32(10000.0), -2.0 * freq_index / ROTARY)
    angles = pos.astype(jnp.float32)[:, None] * inverse[None, :]
    turned = (lane < ROTARY)[None, :]
    cosine = jnp.where(turned, jnp.cos(angles), 1.0)
    sine = jnp.where(turned, jnp.sin(angles), 0.0)
    sine = jnp.where((lane < half_rot)[None, :], -sine, sine)
    bias_half = lax.dynamic_slice_in_dim(qkv_bias, n * half, half, 1).reshape(1, 3 * half)

    up_row = up_bias[None, :]

    def prepare(*blocks):
        return project(n_arg, norm_gain, norm_bias, weights, list(blocks))

    def add(*terms):
        return sum(t.astype(jnp.float32) for t in terms).astype(jnp.bfloat16)

    def finish(name, u, v):
        return output(
            n_arg, PAIRS.index(name) * 2 * rows, up_row, u, v, att, other, w_attn_out, w_down
        )

    def pair(halves, *running):
        return add(halves[0], swap(halves[1]), *running)

    pages = page_table.shape[0]
    per_device = pages // 2
    numbers = jnp.arange(pages, dtype=jnp.int32)
    slots = (numbers + n * per_device) % pages
    page_of_slot = jnp.sum(
        (page_table[None, :] == slots[:, None]).astype(jnp.int32) * numbers[None, :], axis=1
    )
    page_held = token_ids[::PAGE] // PAGE
    held_at = jnp.sum(
        (page_held[None, :] == page_of_slot[:, None]).astype(jnp.int32) * numbers[None, :], axis=1
    )

    o0 = first_block
    f1, b1, s0 = fwd(o0), bwd(o0), swap(o0)
    send0, kept0, u_o0, *weights = project(
        n_arg, norm_gain, norm_bias, (w_query, w_key, w_value, w_up), [o0, s0], True
    )
    f1, b1, send0, kept0, u_o0 = after(f1, b1, send0, kept0, u_o0)
    got0, v_o0 = cross(send0), cross(u_o0)
    f2, b2 = fwd(f1), bwd(b1)
    send1, kept1, u_f1, u_b1 = prepare(f1, swap(f1), b1, swap(b1))
    f2, b2, got0, v_o0, send1, u_b1, u_f1 = after(f2, b2, got0, v_o0, send1, u_b1, u_f1)
    got1, v_b1 = cross(send1), cross(u_b1)
    f3, b3 = fwd(f2), bwd(b2)
    send2, kept2, u_f2, u_b2 = prepare(f2, swap(f2), b2, swap(b2))
    f3, b3, got1, v_b1, send2, u_f2, u_b2 = after(f3, b3, got1, v_b1, send2, u_f2, u_b2)
    got2, v_f2 = cross(send2), cross(u_f2)
    f4 = fwd(f3)
    send3, kept3, u_f3, u_b3 = prepare(f3, swap(f3), b3, swap(b3))
    f4, got2, v_f2, send3, u_f3, u_b3 = after(f4, got2, v_f2, send3, u_f3, u_b3)
    got3 = cross(send3)
    send4, kept4, u_f4 = prepare(f4, swap(f4))
    got3, send4, u_f4, u_f3, u_b3 = after(got3, send4, u_f4, u_f3, u_b3)
    got4 = cross(send4)
    got4, u_f4, cosine, sine, query_info, key_token, bias_half, held_at = after(
        got4, u_f4, cosine, sine, query_info, token_ids[None, :], bias_half, held_at
    )
    v_f4 = cross(u_f4)
    att, kv = attend(
        total_tokens // 16, bias_half, cosine, sine, query_info, key_token,
        [kept0, kept1, kept2, kept3, kept4], [got0, got1, got2, got3, got4],
    )
    v_f4, att, u_b3 = after(v_f4, att, u_b3)
    other = cross(att)
    early = down(up_row, [u_o0, u_b1, u_f2], [v_o0, v_b1, v_f2], w_down)
    other, early, u_b3, u_f3, u_b2, u_f1 = after(other, early, u_b3, u_f3, u_b2, u_f1)
    v_b3 = cross(u_b3)
    y_f4 = finish("f4", u_f4, v_f4)
    m_own, m_sib = mix(
        n_arg, tuple(PAIRS.index(p) * 2 * rows for p in ("o0", "b1", "f2")), early, att, other,
        w_attn_out,
    )
    v_b3, y_f4, m_own, m_sib, u_f3 = after(v_b3, y_f4, m_own, m_sib, u_f3)
    v_f3 = cross(u_f3)
    r_b = bwd(pair(y_f4))
    m_got = swap(m_sib)
    y_b3 = finish("b3", u_b3, v_b3)
    v_f3, r_b, m_got, y_b3, u_b2 = after(v_f3, r_b, m_got, y_b3, u_b2)
    v_b2 = cross(u_b2)
    r_f = fwd(pair(y_b3))
    y_f3 = finish("f3", u_f3, v_f3)
    v_b2, r_f, y_f3, r_b, u_f1 = after(v_b2, r_f, y_f3, r_b, u_f1)
    v_f1 = cross(u_f1)
    r_b = bwd(pair(y_f3, r_b))
    y_b2 = finish("b2", u_b2, v_b2)
    v_f1, r_b, y_b2, r_f, kv = after(v_f1, r_b, y_b2, r_f, kv)
    r_f = fwd(pair(y_b2, r_f))
    r_b = bwd(add(r_b, m_own[2 * rows :], m_got[2 * rows :]))
    y_f1 = finish("f1", u_f1, v_f1)
    r_f, r_b, y_f1, kv = after(r_f, r_b, y_f1, kv)
    r_f = fwd(add(r_f, m_own[rows : 2 * rows], m_got[rows : 2 * rows]))
    r_b = bwd(pair(y_f1, r_b))
    paged = jnp.take(kv.reshape(pages, PAGE, 2 * half), held_at, axis=0)
    cache_got = cross(paged[per_device:])
    summed = (
        r_b.astype(jnp.float32)
        + r_f.astype(jnp.float32)
        + m_own[:rows].astype(jnp.float32)
        + m_got[:rows].astype(jnp.float32)
    )
    hidden_out = (hidden_in.astype(jnp.float32) + summed + out_bias).astype(jnp.bfloat16)
    cache_mine = paged[:per_device]

    left = jnp.where(n == 0, cache_mine, cache_got)
    right = jnp.where(n == 0, cache_got, cache_mine)
    paged_cache = jnp.stack(
        [
            jnp.concatenate([left[..., :half], right[..., :half]], axis=-1),
            jnp.concatenate([left[..., half:], right[..., half:]], axis=-1),
        ]
    )
    return (hidden_out, paged_cache)


def solution(mesh):
    in_specs = (
        P("wide", "narrow"),
        P("narrow", "wide"),
        P("narrow", "wide"),
        P("narrow", "wide"),
        P(None, "wide"),
        P("narrow", "wide"),
        P("wide"),
        P("wide", "narrow"),
        P("wide", "narrow"),
        P("narrow"),
        P(None, "narrow"),
        P(None, "narrow"),
        P(),
        P(),
        P(),
    )
    out_specs = (P("wide", "narrow"), P(None, "narrow", None, "wide"))
    ringed = mesh.shape["wide"] == 2 * CHIPS and mesh.shape["narrow"] == 2
    local = local_ring if ringed else local_generic
    return jax.shard_map(local, mesh=mesh, in_specs=in_specs, out_specs=out_specs, check_vma=False)
```

```python
import functools

import jax
import jax.numpy as jnp
import numpy as np
from jax import lax
from jax.experimental import pallas as pl
from jax.experimental.pallas import tpu as pltpu
from jax.sharding import PartitionSpec as P

D = 6144
HEAD_DIM = 96
ROTARY = 24
PAGE = 16


def segment_info(token_index, seq_lens, sink_count):
    seq_ends = jnp.cumsum(seq_lens)
    seq_starts = seq_ends - seq_lens
    inside = (token_index[:, None] >= seq_starts[None, :]) & (
        token_index[:, None] < seq_ends[None, :]
    )
    member = inside.astype(jnp.int32)
    seq_number = jnp.arange(seq_lens.shape[0], dtype=jnp.int32)
    segment = jnp.sum(member * seq_number[None, :], axis=1)
    position = token_index - jnp.sum(member * seq_starts[None, :], axis=1)
    sink_limit = jnp.sum(member * sink_count[None, :], axis=1)
    return (segment, position, sink_limit)


def rotate(values, position):
    half_rot = ROTARY // 2
    freq_index = jnp.arange(half_rot, dtype=jnp.float32)
    inverse = jnp.power(jnp.float32(10000.0), -2.0 * freq_index / ROTARY)
    angles = position.astype(jnp.float32)[:, None] * inverse[None, :]
    cosine = jnp.cos(angles)[:, None, :]
    sine_part = jnp.sin(angles)[:, None, :]
    first_half = values[..., :half_rot]
    second_half = values[..., half_rot:ROTARY]
    return jnp.concatenate(
        [
            first_half * cosine - second_half * sine_part,
            second_half * cosine + first_half * sine_part,
            values[..., ROTARY:],
        ],
        axis=-1,
    )


def local_generic(
    hidden_in,
    w_query,
    w_key,
    w_value,
    qkv_bias,
    w_up,
    up_bias,
    w_attn_out,
    w_down,
    out_bias,
    norm_gain,
    norm_bias,
    seq_lens,
    sink_count,
    page_table,
):
    wide_count = lax.axis_size("wide")
    narrow_count = lax.axis_size("narrow")
    narrow_index = lax.axis_index("narrow")
    tok_local, feat_local = hidden_in.shape
    sub_rows = tok_local // narrow_count
    total_tokens = tok_local * wide_count
    query_rows = wide_count * sub_rows
    head_cols = w_query.shape[1]
    heads_local = head_cols // HEAD_DIM
    as_float = hidden_in.astype(jnp.float32)
    partial_sum = jnp.sum(as_float, axis=1)
    partial_square = jnp.sum(as_float * as_float, axis=1)
    total_sum, total_square = lax.psum((partial_sum, partial_square), "narrow")
    average = total_sum / D
    variance = total_square / D - average * average
    scaled = (as_float - average[:, None]) * lax.rsqrt(variance + 1e-05)[:, None]
    attn_normed = (scaled * norm_gain[0] + norm_bias[0]).astype(jnp.bfloat16)
    mlp_normed = (scaled * norm_gain[1] + norm_bias[1]).astype(jnp.bfloat16)
    stacked = jnp.stack([attn_normed, mlp_normed]).reshape(2, narrow_count, sub_rows, feat_local)
    gathered = lax.all_gather(stacked, "wide", axis=2, tiled=True).reshape(
        2, total_tokens, feat_local
    )
    local_order = jnp.arange(query_rows, dtype=jnp.int32)
    local_tokens = (
        local_order // sub_rows * tok_local + narrow_index * sub_rows + local_order % sub_rows
    )
    local_seg, local_pos, local_sink = segment_info(local_tokens, seq_lens, sink_count)
    all_order = jnp.arange(total_tokens, dtype=jnp.int32)
    all_tokens = (
        all_order % query_rows // sub_rows * tok_local
        + all_order // query_rows * sub_rows
        + all_order % sub_rows
    )
    all_seg, all_pos, all_sink = segment_info(all_tokens, seq_lens, sink_count)
    qkv_weight = jnp.concatenate([w_query, w_key, w_value], axis=1)
    attn_part = gathered[0]
    mlp_part = gathered[1]
    summed = lax.psum_scatter(
        jnp.concatenate(
            [
                jnp.dot(attn_part, qkv_weight, preferred_element_type=jnp.float32),
                jnp.dot(mlp_part, w_up, preferred_element_type=jnp.float32),
            ],
            axis=1,
        ).astype(jnp.bfloat16),
        "narrow",
        scatter_dimension=0,
        tiled=True,
    ).astype(jnp.float32)
    query_sum = summed[:, :head_cols]
    key_sum = summed[:, head_cols : 2 * head_cols]
    value_sum = summed[:, 2 * head_cols : 3 * head_cols]
    unit_sum = summed[:, 3 * head_cols :]
    keys_local = (
        rotate((key_sum + qkv_bias[1]).reshape(query_rows, heads_local, HEAD_DIM), local_pos)
        .astype(jnp.bfloat16)
        .reshape(query_rows, head_cols)
    )
    values_local = (value_sum + qkv_bias[2]).astype(jnp.bfloat16)
    all_keys, all_values = (
        lax.all_gather(keys_local, "narrow", axis=0, tiled=True),
        lax.all_gather(values_local, "narrow", axis=0, tiled=True),
    )
    queries = rotate(
        (query_sum + qkv_bias[0]).reshape(query_rows, heads_local, HEAD_DIM), local_pos
    ).astype(jnp.bfloat16)
    hidden_units = jax.nn.gelu(unit_sum + up_bias, approximate=False).astype(jnp.bfloat16)
    window_span = total_tokens // 16
    allowed = (local_seg[:, None] == all_seg[None, :]) & (all_pos[None, :] <= local_pos[:, None])
    allowed = allowed & (
        (local_pos[:, None] - all_pos[None, :] < window_span)
        | (all_pos[None, :] < local_sink[:, None])
    )
    key_heads = all_keys.reshape(total_tokens, heads_local, HEAD_DIM)
    value_heads = all_values.reshape(total_tokens, heads_local, HEAD_DIM)
    scores = jnp.einsum("qhd,khd->hqk", queries, key_heads, preferred_element_type=jnp.float32) * (
        1.0 / HEAD_DIM**0.5
    )
    masked = jnp.where(allowed[None], scores, jnp.float32(-1e30))
    top_score = jnp.max(masked, axis=2, keepdims=True)
    weights = jnp.exp(masked - top_score)
    probs = (weights / jnp.sum(weights, axis=2, keepdims=True)).astype(jnp.bfloat16)
    attended = (
        jnp.einsum("hqk,khd->qhd", probs, value_heads, preferred_element_type=jnp.float32)
        .astype(jnp.bfloat16)
        .reshape(query_rows, head_cols)
    )
    full_out, full_down = (
        lax.all_gather(w_attn_out, "narrow", axis=1, tiled=True),
        lax.all_gather(w_down, "narrow", axis=1, tiled=True),
    )
    attn_part = attended
    own_rows = lax.psum_scatter(
        (
            jnp.dot(attn_part, full_out, preferred_element_type=jnp.float32)
            + jnp.dot(hidden_units, full_down, preferred_element_type=jnp.float32)
        ).astype(jnp.bfloat16),
        "wide",
        scatter_dimension=0,
        tiled=True,
    ).astype(jnp.float32)
    combined = lax.all_to_all(
        own_rows.astype(jnp.bfloat16), "narrow", split_axis=1, concat_axis=0, tiled=True
    ).astype(own_rows.dtype)
    hidden_out = (as_float + combined + out_bias).astype(jnp.bfloat16)
    pages_local = page_table.shape[0] // narrow_count
    slot_ids = narrow_index * pages_local + jnp.arange(pages_local, dtype=jnp.int32)
    matches = (page_table[None, :] == slot_ids[:, None]).astype(jnp.int32)
    source_page = jnp.sum(
        matches * jnp.arange(page_table.shape[0], dtype=jnp.int32)[None, :], axis=1
    )
    token_ids = (source_page[:, None] * PAGE + jnp.arange(PAGE, dtype=jnp.int32)[None, :]).reshape(
        -1
    )
    gather_rows = (
        token_ids % tok_local // sub_rows * query_rows
        + token_ids // tok_local * sub_rows
        + token_ids % sub_rows
    )
    cache_keys = jnp.take(all_keys, gather_rows, axis=0).reshape(pages_local, PAGE, head_cols)
    cache_values = jnp.take(all_values, gather_rows, axis=0).reshape(pages_local, PAGE, head_cols)
    paged_cache = jnp.stack([cache_keys, cache_values])
    return (hidden_out, paged_cache)


CHIP_RING = (0, 2, 4, 6, 7, 5, 3, 1)
CHIPS = len(CHIP_RING)
PAIRS = ("o0", "f1", "b1", "f2", "b2", "f3", "b3", "f4")
STAT = 128
HEAD_PAD = 128
MIB = 1 << 20
VMEM = pl.BlockSpec(memory_space=pltpu.VMEM)
HBM = pl.BlockSpec(memory_space=pltpu.HBM)
SMEM = pl.BlockSpec(memory_space=pltpu.SMEM)


def owner_table():
    table = np.zeros((2 * CHIPS, 2 * CHIPS), np.int32)
    for place, chip in enumerate(CHIP_RING):
        for core in range(2):
            order = []
            for pair in PAIRS:
                shift = (-1 if pair[0] == "f" else 1) * int(pair[1]) * (1 - 2 * core)
                order.append(CHIP_RING[(place + shift) % CHIPS] * 2 + core)
                order.append(CHIP_RING[(place - shift) % CHIPS] * 2 + 1 - core)
            table[2 * chip + core] = order
    return table


def place_table():
    owners = owner_table()
    table = np.zeros_like(owners)
    for device in range(owners.shape[0]):
        table[device, owners[device]] = np.arange(owners.shape[1])
    return table


def sums_kernel(x_ref, gain_ref, bias_ref, out_ref, affine_ref):
    x = x_ref[...].astype(jnp.float32)
    first = jnp.sum(x, axis=1, keepdims=True)
    second = jnp.sum(x * x, axis=1, keepdims=True)
    lane = lax.broadcasted_iota(jnp.int32, out_ref.shape, 1)
    out_ref[...] = jnp.where(lane == 0, first, jnp.where(lane == 1, second, 0.0))
    affine_ref[0:2, :] = gain_ref[...]
    affine_ref[2:4, :] = bias_ref[...]


def block_kernel(x_ref, here_ref, there_ref, out_ref):
    feat = x_ref.shape[1]
    total = here_ref[...] + there_ref[...]
    average = total[:, 0:1] / D
    variance = total[:, 1:2] / D - average * average
    scale = lax.rsqrt(variance + 1e-05)
    lane = lax.broadcasted_iota(jnp.int32, (x_ref.shape[0], STAT), 1)
    tail = jnp.zeros((x_ref.shape[0], STAT), jnp.float32)
    for start, value in ((0, average), (3, scale)):
        for term in range(3):
            piece = value.astype(jnp.bfloat16).astype(jnp.float32)
            tail = jnp.where(lane == start + term, piece, tail)
            value = value - piece
    out_ref[:, :feat] = x_ref[...]
    out_ref[:, feat:] = tail.astype(jnp.bfloat16)


def tables_kernel(device_ref, owners_ref, lens_ref, sinks_ref, inverse_ref, info_ref, key_ref, cos_ref, sin_ref):
    device = device_ref[0]
    blocks = owners_ref.shape[1]
    rows = info_ref.shape[0] // blocks
    half_rot = ROTARY // 2
    lane = lax.broadcasted_iota(jnp.int32, (rows, HEAD_PAD), 1)
    sub = lax.broadcasted_iota(jnp.int32, (rows, HEAD_PAD), 0)
    key_lane = lax.broadcasted_iota(jnp.int32, key_ref.shape, 1)
    key = key_lane
    for j in range(blocks):
        first = owners_ref[device, j] * rows
        key = jnp.where(key_lane // rows == j, first + key_lane - j * rows, key)
        token = first + sub
        begin, end = jnp.zeros_like(token), jnp.zeros_like(token)
        start = jnp.int32(0)
        for s in range(lens_ref.shape[0]):
            inside = (token >= start) & (token < start + lens_ref[s])
            begin = jnp.where(inside, start, begin)
            end = jnp.where(inside, start + sinks_ref[s], end)
            start = start + lens_ref[s]
        at = slice(j * rows, (j + 1) * rows)
        info_ref[at, :] = jnp.where(lane == 0, token, jnp.where(lane == 1, begin, end))
        angles = (token - begin).astype(jnp.float32) * inverse_ref[...]
        turned = lane < ROTARY
        cos_ref[at, :] = jnp.where(turned, jnp.cos(angles), 1.0)
        sine = jnp.where(turned, jnp.sin(angles), 0.0)
        sin_ref[at, :] = jnp.where(lane < half_rot, -sine, sine)
    key_ref[...] = key


def tables(total, device, lens, sinks):
    freq_index = np.arange(HEAD_PAD) % (ROTARY // 2)
    inverse = (10000.0 ** (-2.0 * freq_index / ROTARY)).astype(np.float32)[None, :]
    wide = (total, HEAD_PAD)
    return pl.pallas_call(
        tables_kernel,
        out_shape=(
            jax.ShapeDtypeStruct(wide, jnp.int32),
            jax.ShapeDtypeStruct((1, total), jnp.int32),
            jax.ShapeDtypeStruct(wide, jnp.float32),
            jax.ShapeDtypeStruct(wide, jnp.float32),
        ),
        in_specs=[SMEM] * 4 + [VMEM],
        out_specs=(VMEM,) * 4,
        compiler_params=pltpu.CompilerParams(vmem_limit_bytes=8 * MIB),
        name="tables",
    )(device, jnp.asarray(owner_table()), lens, sinks, jnp.asarray(inverse))


def pages_kernel(device_ref, n_ref, places_ref, table_ref, kv_ref, out_ref):
    pages = table_ref.shape[0]
    per_owner = pages // places_ref.shape[1]
    device, shift = device_ref[0], n_ref[0] * (pages // 2)
    for p in range(pages):
        place = places_ref[device, p // per_owner] * per_owner + p % per_owner
        row = pl.multiple_of(place * PAGE, PAGE)
        out_ref[lax.rem(table_ref[p] + shift, pages)] = kv_ref[pl.ds(row, PAGE), :]


def ordered_pages(device, n, page_table, kv):
    return pl.pallas_call(
        pages_kernel,
        out_shape=jax.ShapeDtypeStruct((page_table.shape[0], PAGE, kv.shape[1]), kv.dtype),
        in_specs=[SMEM] * 4 + [VMEM],
        out_specs=VMEM,
        compiler_params=pltpu.CompilerParams(vmem_limit_bytes=8 * MIB),
        name="ordered_pages",
    )(device, n, jnp.asarray(place_table()), page_table, kv)


def normalise(blocks, affine_ref, attn, mlp):
    rows = blocks[0].shape[0]
    feat = attn.shape[1]
    step = 512
    for b, block in enumerate(blocks):
        tail = block[:, feat:].astype(jnp.float32)
        average = tail[:, 0:1] + tail[:, 1:2] + tail[:, 2:3]
        scale = tail[:, 3:4] + tail[:, 4:5] + tail[:, 5:6]
        here = slice(b * rows, (b + 1) * rows)
        for c in range(0, feat, step):
            at = slice(c, c + step)
            scaled = (block[:, at].astype(jnp.float32) - average) * scale
            attn[here, at] = (scaled * affine_ref[0:1, at] + affine_ref[2:3, at]).astype(jnp.bfloat16)
            mlp[here, at] = (scaled * affine_ref[1:2, at] + affine_ref[3:4, at]).astype(jnp.bfloat16)


def project_kernel(count, first_call, n_ref, affine_ref, wq_ref, wk_ref, wv_ref, wu_ref, *refs):
    blocks, refs = refs[:count], refs[count:]
    send_ref, mine_ref, refs = refs[0], refs[1], refs[2:]
    ups, refs = refs[: count // 2], refs[count // 2 :]
    width = 384
    tiles = wu_ref.shape[1] // width
    copies = []
    if first_call:
        sources = (wq_ref, wk_ref, wv_ref)
        held, refs = refs[:4], refs[4:]
        attn, mlp, sems = refs
        copies = [
            pltpu.make_async_copy(src, dst, sems.at[i])
            for i, (src, dst) in enumerate(zip(sources, held))
        ]
        for t in range(tiles):
            at = slice(t * width, (t + 1) * width)
            copies.append(pltpu.make_async_copy(wu_ref.at[:, at], held[3].at[:, at], sems.at[3 + t]))
        for copy in copies:
            copy.start()
        wq_ref, wk_ref, wv_ref, wu_ref = held
    else:
        attn, mlp = refs
    rows = blocks[0].shape[0]
    half = wq_ref.shape[1] // 2
    normalise(blocks, affine_ref, attn, mlp)
    low, high = [], []
    for i, weight in enumerate((wq_ref, wk_ref, wv_ref)):
        if first_call:
            copies[i].wait()
        part = jnp.dot(attn[...], weight[...], preferred_element_type=jnp.float32)
        low.append(part[:, :half])
        high.append(part[:, half:])
    low = jnp.concatenate(low, axis=1).astype(jnp.bfloat16)
    high = jnp.concatenate(high, axis=1).astype(jnp.bfloat16)
    first = n_ref[0] == 0
    send_ref[...] = jnp.where(first, high, low)
    mine_ref[...] = jnp.where(first, low, high)
    for t in range(tiles):
        if first_call:
            copies[3 + t].wait()
        at = slice(t * width, (t + 1) * width)
        part = jnp.dot(mlp[...], wu_ref[:, at], preferred_element_type=jnp.float32)
        part = part.astype(jnp.bfloat16)
        for u, up in enumerate(ups):
            up[:, at] = part[2 * u * rows : 2 * (u + 1) * rows]


def project(n, affine, weights, blocks, first_call=False):
    count = len(blocks)
    rows = blocks[0].shape[0] * count
    feat, cols = weights[0].shape
    hidden = weights[3].shape[1]
    up = jax.ShapeDtypeStruct((2 * blocks[0].shape[0], hidden), jnp.bfloat16)
    part = jax.ShapeDtypeStruct((rows, 3 * cols // 2), jnp.bfloat16)
    shapes = (part, part) + (up,) * (count // 2)
    scratch = [
        pltpu.VMEM((rows, feat), jnp.bfloat16),
        pltpu.VMEM((rows, feat), jnp.bfloat16),
    ]
    if first_call:
        shapes += tuple(jax.ShapeDtypeStruct(w.shape, w.dtype) for w in weights)
        scratch.append(pltpu.SemaphoreType.DMA((3 + hidden // 384,)))
    return pl.pallas_call(
        functools.partial(project_kernel, count, first_call),
        out_shape=shapes,
        in_specs=[SMEM, VMEM] + [HBM if first_call else VMEM] * 4 + [VMEM] * count,
        out_specs=(VMEM,) * len(shapes),
        scratch_shapes=scratch,
        compiler_params=pltpu.CompilerParams(vmem_limit_bytes=(44 if first_call else 7) * MIB),
        name="project",
    )(n, affine, *weights, *blocks)


def attend_kernel(count, span, n_ref, bias_ref, cos_ref, sin_ref, query_ref, key_ref, *refs):
    mine, got = refs[:count], refs[count : 2 * count]
    att_ref, kv_ref, queries, keys, values = refs[2 * count :]
    heads = queries.shape[0]
    half = att_ref.shape[1]
    total = att_ref.shape[0]
    half_rot = ROTARY // 2
    bias = jnp.where(n_ref[0] == 0, bias_ref[:, :half], bias_ref[:, half:])
    offset = 0
    for g in range(count):
        rows = mine[g].shape[0]
        at = slice(offset, offset + rows)
        offset += rows
        summed = mine[g][...].astype(jnp.float32) + got[g][...].astype(jnp.float32)
        cosine, sine = cos_ref[at, :], sin_ref[at, :]
        lane = lax.broadcasted_iota(jnp.int32, (rows, HEAD_PAD), 1)
        pad = jnp.zeros((rows, HEAD_PAD - HEAD_DIM), jnp.float32)
        for kind in range(3):
            kept = []
            for h in range(heads):
                begin = kind * half + h * HEAD_DIM
                u = summed[:, begin : begin + HEAD_DIM]
                u = u + bias[kind : kind + 1, h * HEAD_DIM : (h + 1) * HEAD_DIM]
                u = jnp.concatenate([u, pad], axis=1)
                if kind < 2:
                    other = jnp.where(
                        lane < half_rot,
                        pltpu.roll(u, HEAD_PAD - half_rot, 1),
                        pltpu.roll(u, half_rot, 1),
                    )
                    u = u * cosine + other * sine
                (queries, keys, values)[kind][h, at, :] = u.astype(jnp.bfloat16)
                kept.append(u[:, :HEAD_DIM])
            if kind > 0:
                kv_ref[at, (kind - 1) * half : kind * half] = jnp.concatenate(kept, axis=1).astype(
                    jnp.bfloat16
                )
    tile = 256
    for start in range(0, total, tile):
        at = slice(start, start + tile)
        info = query_ref[at, :]
        token, begin, end = info[:, 0:1], info[:, 1:2], info[:, 2:3]
        key_token = key_ref[...]
        near = key_token > token - span
        allowed = (key_token >= begin) & (key_token <= token) & (near | (key_token < end))
        outs = []
        for h in range(heads):
            scores = lax.dot_general(
                queries[h, at, :],
                keys[h],
                (((1,), (1,)), ((), ())),
                preferred_element_type=jnp.float32,
            ) * (1.0 / HEAD_DIM**0.5)
            masked = jnp.where(allowed, scores, -1e30)
            weights = jnp.exp(masked - jnp.max(masked, axis=1, keepdims=True))
            probs = weights / jnp.sum(weights, axis=1, keepdims=True)
            out = jnp.dot(probs.astype(jnp.bfloat16), values[h], preferred_element_type=jnp.float32)
            outs.append(out[:, :HEAD_DIM])
        att_ref[at, :] = jnp.concatenate(outs, axis=1).astype(jnp.bfloat16)


def attend(span, n, bias, cosine, sine, query_info, key_token, mine, got):
    count = len(mine)
    total = cosine.shape[0]
    half = mine[0].shape[1] // 3
    heads = half // HEAD_DIM
    scratch = pltpu.VMEM((heads, total, HEAD_PAD), jnp.bfloat16)
    return pl.pallas_call(
        functools.partial(attend_kernel, count, span),
        out_shape=(
            jax.ShapeDtypeStruct((total, half), jnp.bfloat16),
            jax.ShapeDtypeStruct((total, 2 * half), jnp.bfloat16),
        ),
        in_specs=[SMEM] + [VMEM] * (5 + 2 * count),
        out_specs=(VMEM, VMEM),
        scratch_shapes=[scratch, scratch, scratch],
        compiler_params=pltpu.CompilerParams(vmem_limit_bytes=10 * MIB),
        name="attend",
    )(n, bias, cosine, sine, query_info, key_token, *mine, *got)


def gelu(u):
    return u * (1.0 + lax.erf(u * (0.5**0.5))) * 0.5


def down_kernel(count, bias_ref, wd_ref, *refs):
    mine, got = refs[:count], refs[count : 2 * count]
    out_ref, units = refs[2 * count :]
    rows = mine[0].shape[0]
    step = 384
    for i in range(count):
        for c in range(0, mine[i].shape[1], step):
            at = slice(c, c + step)
            u = mine[i][:, at].astype(jnp.float32) + got[i][:, at].astype(jnp.float32)
            u = gelu(u + bias_ref[:, at])
            units[i * rows : (i + 1) * rows, at] = u.astype(jnp.bfloat16)
    width = 512
    for c in range(0, wd_ref.shape[1], width):
        at = slice(c, c + width)
        out = jnp.dot(units[...], wd_ref[:, at], preferred_element_type=jnp.float32)
        out_ref[:, at] = out.astype(jnp.bfloat16)


def down(bias, mine, got, wd):
    count = len(mine)
    rows, hidden = mine[0].shape
    return pl.pallas_call(
        functools.partial(down_kernel, count),
        out_shape=jax.ShapeDtypeStruct((count * rows, wd.shape[1]), jnp.bfloat16),
        in_specs=[VMEM] * (2 + 2 * count),
        out_specs=VMEM,
        scratch_shapes=[pltpu.VMEM((count * rows, hidden), jnp.bfloat16)],
        compiler_params=pltpu.CompilerParams(vmem_limit_bytes=6 * MIB),
        name="down",
    )(bias, wd, *mine, *got)


def mix_kernel(offsets, n_ref, down_ref, att_ref, other_ref, wo_ref, own_ref, sib_ref):
    half = att_ref.shape[1]
    rows = own_ref.shape[0] // len(offsets)
    n = n_ref[0]
    here = pl.ds(pl.multiple_of(n * half, 16), half)
    there = pl.ds(pl.multiple_of((1 - n) * half, 16), half)
    mine = jnp.concatenate([att_ref[o : o + 2 * rows, :] for o in offsets], axis=0)
    other = jnp.concatenate([other_ref[o : o + 2 * rows, :] for o in offsets], axis=0)
    width = 512
    for c in range(0, own_ref.shape[1], width):
        at = slice(c, c + width)
        out = down_ref[:, at].astype(jnp.float32)
        out += jnp.dot(mine, wo_ref[here, at], preferred_element_type=jnp.float32)
        out += jnp.dot(other, wo_ref[there, at], preferred_element_type=jnp.float32)
        out = out.astype(jnp.bfloat16)
        for i in range(len(offsets)):
            own_ref[i * rows : (i + 1) * rows, at] = out[2 * i * rows : (2 * i + 1) * rows]
            sib_ref[i * rows : (i + 1) * rows, at] = out[(2 * i + 1) * rows : (2 * i + 2) * rows]


def mix(n, offsets, partial_down, att, other, wo):
    rows, feat = partial_down.shape
    shape = jax.ShapeDtypeStruct((rows // 2, feat), jnp.bfloat16)
    return pl.pallas_call(
        functools.partial(mix_kernel, offsets),
        out_shape=(shape, shape),
        in_specs=[SMEM] + [VMEM] * 4,
        out_specs=(VMEM, VMEM),
        compiler_params=pltpu.CompilerParams(vmem_limit_bytes=5 * MIB),
        name="mix",
    )(n, partial_down, att, other, wo)


def output_kernel(
    offset, n_ref, bias_ref, mine_ref, got_ref, att_ref, other_ref, wo_ref, wd_ref, own_ref, sib_ref, units
):
    rows = mine_ref.shape[0]
    half = att_ref.shape[1]
    own_rows = own_ref.shape[0]
    step = 384
    for c in range(0, mine_ref.shape[1], step):
        at = slice(c, c + step)
        u = mine_ref[:, at].astype(jnp.float32) + got_ref[:, at].astype(jnp.float32)
        units[:, at] = gelu(u + bias_ref[:, at]).astype(jnp.bfloat16)
    n = n_ref[0]
    here = pl.ds(pl.multiple_of(n * half, 16), half)
    there = pl.ds(pl.multiple_of((1 - n) * half, 16), half)
    span = slice(offset, offset + rows)
    width = 512
    for c in range(0, wd_ref.shape[1], width):
        at = slice(c, c + width)
        out = jnp.dot(units[...], wd_ref[:, at], preferred_element_type=jnp.float32)
        out += jnp.dot(att_ref[span, :], wo_ref[here, at], preferred_element_type=jnp.float32)
        out += jnp.dot(other_ref[span, :], wo_ref[there, at], preferred_element_type=jnp.float32)
        out = out.astype(jnp.bfloat16)
        own_ref[:, at] = out[:own_rows]
        sib_ref[:, at] = out[own_rows:]


def output(n, offset, bias, mine, got, att, other, wo, wd):
    rows, hidden = mine.shape
    shape = jax.ShapeDtypeStruct((rows // 2, wd.shape[1]), jnp.bfloat16)
    return pl.pallas_call(
        functools.partial(output_kernel, offset),
        out_shape=(shape, shape),
        in_specs=[SMEM] + [VMEM] * 7,
        out_specs=(VMEM, VMEM),
        scratch_shapes=[pltpu.VMEM((rows, hidden), jnp.bfloat16)],
        compiler_params=pltpu.CompilerParams(vmem_limit_bytes=5 * MIB),
        name="output",
    )(n, bias, mine, got, att, other, wo, wd)


def after(*values):
    return lax.optimization_barrier(values)


def local_ring(
    hidden_in,
    w_query,
    w_key,
    w_value,
    qkv_bias,
    w_up,
    up_bias,
    w_attn_out,
    w_down,
    out_bias,
    norm_gain,
    norm_bias,
    seq_lens,
    sink_count,
    page_table,
):
    device = lax.axis_index("wide").astype(jnp.int32).reshape(1)
    n = lax.axis_index("narrow").astype(jnp.int32)
    n_arg = n.reshape(1)
    rows, feat = hidden_in.shape
    total_tokens = rows * lax.axis_size("wide")
    half = w_query.shape[1] // 2

    fwd_pairs, bwd_pairs, swap_pairs = [], [], []
    for p in range(CHIPS):
        here, next_chip = CHIP_RING[p], CHIP_RING[(p + 1) % CHIPS]
        fwd_pairs += [(2 * here, 2 * next_chip), (2 * next_chip + 1, 2 * here + 1)]
        bwd_pairs += [(2 * next_chip, 2 * here), (2 * here + 1, 2 * next_chip + 1)]
        swap_pairs += [(2 * here, 2 * here + 1), (2 * here + 1, 2 * here)]
    fwd = lambda v: lax.ppermute(v, "wide", fwd_pairs)
    bwd = lambda v: lax.ppermute(v, "wide", bwd_pairs)
    swap = lambda v: lax.ppermute(v, "wide", swap_pairs)
    cross = lambda v: lax.ppermute(v, "narrow", [(0, 1), (1, 0)])

    sums, affine = pl.pallas_call(
        sums_kernel,
        out_shape=(
            jax.ShapeDtypeStruct((rows, STAT), jnp.float32),
            jax.ShapeDtypeStruct((4, feat), jnp.float32),
        ),
        in_specs=[VMEM] * 3,
        out_specs=(VMEM, VMEM),
        compiler_params=pltpu.CompilerParams(vmem_limit_bytes=8 * MIB),
        name="row_sums",
    )(hidden_in, norm_gain, norm_bias)
    first_block = pl.pallas_call(
        block_kernel,
        out_shape=jax.ShapeDtypeStruct((rows, feat + STAT), jnp.bfloat16),
        in_specs=[VMEM] * 3,
        out_specs=VMEM,
        compiler_params=pltpu.CompilerParams(vmem_limit_bytes=8 * MIB),
        name="first_block",
    )(hidden_in, sums, cross(sums))

    up_row = up_bias[None, :]

    def prepare(*blocks):
        return project(n_arg, affine, weights, list(blocks))

    def add(*terms):
        return sum(t.astype(jnp.float32) for t in terms).astype(jnp.bfloat16)

    def finish(name, u, v):
        return output(
            n_arg, PAIRS.index(name) * 2 * rows, up_row, u, v, att, other, w_attn_out, w_down
        )

    def pair(halves, *running):
        return add(halves[0], swap(halves[1]), *running)

    per_device = page_table.shape[0] // 2
    o0 = first_block
    f1, b1, s0 = fwd(o0), bwd(o0), swap(o0)
    send0, kept0, u_o0, *weights = project(
        n_arg, affine, (w_query, w_key, w_value, w_up), [o0, s0], True
    )
    f1, b1, send0, kept0, u_o0 = after(f1, b1, send0, kept0, u_o0)
    got0, v_o0 = cross(send0), cross(u_o0)
    f2, b2 = fwd(f1), bwd(b1)
    send1, kept1, u_f1, u_b1 = prepare(f1, swap(f1), b1, swap(b1))
    f2, b2, got0, v_o0, send1, u_b1, u_f1 = after(f2, b2, got0, v_o0, send1, u_b1, u_f1)
    got1, v_b1 = cross(send1), cross(u_b1)
    f3, b3 = fwd(f2), bwd(b2)
    send2, kept2, u_f2, u_b2 = prepare(f2, swap(f2), b2, swap(b2))
    f3, b3, got1, v_b1, send2, u_f2, u_b2 = after(f3, b3, got1, v_b1, send2, u_f2, u_b2)
    got2, v_f2 = cross(send2), cross(u_f2)
    f4 = fwd(f3)
    send3, kept3, u_f3, u_b3 = prepare(f3, swap(f3), b3, swap(b3))
    f4, got2, v_f2, send3, u_f3, u_b3 = after(f4, got2, v_f2, send3, u_f3, u_b3)
    got3 = cross(send3)
    send4, kept4, u_f4 = project(n_arg, affine, [*weights[:3], w_up], [f4, swap(f4)])
    got3, send4, u_f4, u_f3, u_b3, late_device = after(got3, send4, u_f4, u_f3, u_b3, device)
    got4 = cross(send4)
    query_info, key_token, cosine, sine = tables(total_tokens, late_device, seq_lens, sink_count)
    got4, u_f4, cosine, sine, query_info, key_token = after(
        got4, u_f4, cosine, sine, query_info, key_token
    )
    v_f4 = cross(u_f4)
    att, kv = attend(
        total_tokens // 16, n_arg, qkv_bias, cosine, sine, query_info, key_token,
        [kept0, kept1, kept2, kept3, kept4], [got0, got1, got2, got3, got4],
    )
    v_f4, att, u_b3 = after(v_f4, att, u_b3)
    other = cross(att)
    early = down(up_row, [u_o0, u_b1, u_f2], [v_o0, v_b1, v_f2], w_down)
    other, early, u_b3, u_f3, u_b2, u_f1 = after(other, early, u_b3, u_f3, u_b2, u_f1)
    v_b3 = cross(u_b3)
    y_f4 = finish("f4", u_f4, v_f4)
    m_own, m_sib = mix(
        n_arg, tuple(PAIRS.index(p) * 2 * rows for p in ("o0", "b1", "f2")), early, att, other,
        w_attn_out,
    )
    v_b3, y_f4, m_own, m_sib, u_f3 = after(v_b3, y_f4, m_own, m_sib, u_f3)
    v_f3 = cross(u_f3)
    r_b = bwd(pair(y_f4))
    m_got = swap(m_sib)
    y_b3 = finish("b3", u_b3, v_b3)
    v_f3, r_b, m_got, y_b3, u_b2 = after(v_f3, r_b, m_got, y_b3, u_b2)
    v_b2 = cross(u_b2)
    r_f = fwd(pair(y_b3))
    y_f3 = finish("f3", u_f3, v_f3)
    v_b2, r_f, y_f3, r_b, u_f1 = after(v_b2, r_f, y_f3, r_b, u_f1)
    v_f1 = cross(u_f1)
    r_b = bwd(pair(y_f3, r_b))
    y_b2 = finish("b2", u_b2, v_b2)
    v_f1, r_b, y_b2, r_f, kv = after(v_f1, r_b, y_b2, r_f, kv)
    r_f = fwd(pair(y_b2, r_f))
    r_b = bwd(add(r_b, m_own[2 * rows :], m_got[2 * rows :]))
    y_f1 = finish("f1", u_f1, v_f1)
    r_f, r_b, y_f1, kv = after(r_f, r_b, y_f1, kv)
    r_f = fwd(add(r_f, m_own[rows : 2 * rows], m_got[rows : 2 * rows]))
    r_b = bwd(pair(y_f1, r_b))
    paged = ordered_pages(device, n_arg, page_table, kv)
    cache_got = cross(paged[per_device:])
    summed = (
        r_b.astype(jnp.float32)
        + r_f.astype(jnp.float32)
        + m_own[:rows].astype(jnp.float32)
        + m_got[:rows].astype(jnp.float32)
    )
    hidden_out = (hidden_in.astype(jnp.float32) + summed + out_bias).astype(jnp.bfloat16)
    cache_mine = paged[:per_device]

    left = jnp.where(n == 0, cache_mine, cache_got)
    right = jnp.where(n == 0, cache_got, cache_mine)
    paged_cache = jnp.stack(
        [
            jnp.concatenate([left[..., :half], right[..., :half]], axis=-1),
            jnp.concatenate([left[..., half:], right[..., half:]], axis=-1),
        ]
    )
    return (hidden_out, paged_cache)


def solution(mesh):
    in_specs = (
        P("wide", "narrow"),
        P("narrow", "wide"),
        P("narrow", "wide"),
        P("narrow", "wide"),
        P(None, "wide"),
        P("narrow", "wide"),
        P("wide"),
        P("wide", "narrow"),
        P("wide", "narrow"),
        P("narrow"),
        P(None, "narrow"),
        P(None, "narrow"),
        P(),
        P(),
        P(),
    )
    out_specs = (P("wide", "narrow"), P(None, "narrow", None, "wide"))
    ringed = mesh.shape["wide"] == 2 * CHIPS and mesh.shape["narrow"] == 2
    local = local_ring if ringed else local_generic
    return jax.shard_map(local, mesh=mesh, in_specs=in_specs, out_specs=out_specs, check_vma=False)
```

```python
import functools

import jax
import jax.numpy as jnp
import numpy as np
from jax import lax
from jax.experimental import pallas as pl
from jax.experimental.pallas import tpu as pltpu
from jax.sharding import PartitionSpec as P

D = 6144
HEAD_DIM = 96
ROTARY = 24
PAGE = 16


def segment_info(token_index, seq_lens, sink_count):
    seq_ends = jnp.cumsum(seq_lens)
    seq_starts = seq_ends - seq_lens
    inside = (token_index[:, None] >= seq_starts[None, :]) & (
        token_index[:, None] < seq_ends[None, :]
    )
    member = inside.astype(jnp.int32)
    seq_number = jnp.arange(seq_lens.shape[0], dtype=jnp.int32)
    segment = jnp.sum(member * seq_number[None, :], axis=1)
    position = token_index - jnp.sum(member * seq_starts[None, :], axis=1)
    sink_limit = jnp.sum(member * sink_count[None, :], axis=1)
    return (segment, position, sink_limit)


def rotate(values, position):
    half_rot = ROTARY // 2
    freq_index = jnp.arange(half_rot, dtype=jnp.float32)
    inverse = jnp.power(jnp.float32(10000.0), -2.0 * freq_index / ROTARY)
    angles = position.astype(jnp.float32)[:, None] * inverse[None, :]
    cosine = jnp.cos(angles)[:, None, :]
    sine_part = jnp.sin(angles)[:, None, :]
    first_half = values[..., :half_rot]
    second_half = values[..., half_rot:ROTARY]
    return jnp.concatenate(
        [
            first_half * cosine - second_half * sine_part,
            second_half * cosine + first_half * sine_part,
            values[..., ROTARY:],
        ],
        axis=-1,
    )


def local_generic(
    hidden_in,
    w_query,
    w_key,
    w_value,
    qkv_bias,
    w_up,
    up_bias,
    w_attn_out,
    w_down,
    out_bias,
    norm_gain,
    norm_bias,
    seq_lens,
    sink_count,
    page_table,
):
    wide_count = lax.axis_size("wide")
    narrow_count = lax.axis_size("narrow")
    narrow_index = lax.axis_index("narrow")
    tok_local, feat_local = hidden_in.shape
    sub_rows = tok_local // narrow_count
    total_tokens = tok_local * wide_count
    query_rows = wide_count * sub_rows
    head_cols = w_query.shape[1]
    heads_local = head_cols // HEAD_DIM
    as_float = hidden_in.astype(jnp.float32)
    partial_sum = jnp.sum(as_float, axis=1)
    partial_square = jnp.sum(as_float * as_float, axis=1)
    total_sum, total_square = lax.psum((partial_sum, partial_square), "narrow")
    average = total_sum / D
    variance = total_square / D - average * average
    scaled = (as_float - average[:, None]) * lax.rsqrt(variance + 1e-05)[:, None]
    attn_normed = (scaled * norm_gain[0] + norm_bias[0]).astype(jnp.bfloat16)
    mlp_normed = (scaled * norm_gain[1] + norm_bias[1]).astype(jnp.bfloat16)
    stacked = jnp.stack([attn_normed, mlp_normed]).reshape(2, narrow_count, sub_rows, feat_local)
    gathered = lax.all_gather(stacked, "wide", axis=2, tiled=True).reshape(
        2, total_tokens, feat_local
    )
    local_order = jnp.arange(query_rows, dtype=jnp.int32)
    local_tokens = (
        local_order // sub_rows * tok_local + narrow_index * sub_rows + local_order % sub_rows
    )
    local_seg, local_pos, local_sink = segment_info(local_tokens, seq_lens, sink_count)
    all_order = jnp.arange(total_tokens, dtype=jnp.int32)
    all_tokens = (
        all_order % query_rows // sub_rows * tok_local
        + all_order // query_rows * sub_rows
        + all_order % sub_rows
    )
    all_seg, all_pos, all_sink = segment_info(all_tokens, seq_lens, sink_count)
    qkv_weight = jnp.concatenate([w_query, w_key, w_value], axis=1)
    attn_part = gathered[0]
    mlp_part = gathered[1]
    summed = lax.psum_scatter(
        jnp.concatenate(
            [
                jnp.dot(attn_part, qkv_weight, preferred_element_type=jnp.float32),
                jnp.dot(mlp_part, w_up, preferred_element_type=jnp.float32),
            ],
            axis=1,
        ).astype(jnp.bfloat16),
        "narrow",
        scatter_dimension=0,
        tiled=True,
    ).astype(jnp.float32)
    query_sum = summed[:, :head_cols]
    key_sum = summed[:, head_cols : 2 * head_cols]
    value_sum = summed[:, 2 * head_cols : 3 * head_cols]
    unit_sum = summed[:, 3 * head_cols :]
    keys_local = (
        rotate((key_sum + qkv_bias[1]).reshape(query_rows, heads_local, HEAD_DIM), local_pos)
        .astype(jnp.bfloat16)
        .reshape(query_rows, head_cols)
    )
    values_local = (value_sum + qkv_bias[2]).astype(jnp.bfloat16)
    all_keys, all_values = (
        lax.all_gather(keys_local, "narrow", axis=0, tiled=True),
        lax.all_gather(values_local, "narrow", axis=0, tiled=True),
    )
    queries = rotate(
        (query_sum + qkv_bias[0]).reshape(query_rows, heads_local, HEAD_DIM), local_pos
    ).astype(jnp.bfloat16)
    hidden_units = jax.nn.gelu(unit_sum + up_bias, approximate=False).astype(jnp.bfloat16)
    window_span = total_tokens // 16
    allowed = (local_seg[:, None] == all_seg[None, :]) & (all_pos[None, :] <= local_pos[:, None])
    allowed = allowed & (
        (local_pos[:, None] - all_pos[None, :] < window_span)
        | (all_pos[None, :] < local_sink[:, None])
    )
    key_heads = all_keys.reshape(total_tokens, heads_local, HEAD_DIM)
    value_heads = all_values.reshape(total_tokens, heads_local, HEAD_DIM)
    scores = jnp.einsum("qhd,khd->hqk", queries, key_heads, preferred_element_type=jnp.float32) * (
        1.0 / HEAD_DIM**0.5
    )
    masked = jnp.where(allowed[None], scores, jnp.float32(-1e30))
    top_score = jnp.max(masked, axis=2, keepdims=True)
    weights = jnp.exp(masked - top_score)
    probs = (weights / jnp.sum(weights, axis=2, keepdims=True)).astype(jnp.bfloat16)
    attended = (
        jnp.einsum("hqk,khd->qhd", probs, value_heads, preferred_element_type=jnp.float32)
        .astype(jnp.bfloat16)
        .reshape(query_rows, head_cols)
    )
    full_out, full_down = (
        lax.all_gather(w_attn_out, "narrow", axis=1, tiled=True),
        lax.all_gather(w_down, "narrow", axis=1, tiled=True),
    )
    attn_part = attended
    own_rows = lax.psum_scatter(
        (
            jnp.dot(attn_part, full_out, preferred_element_type=jnp.float32)
            + jnp.dot(hidden_units, full_down, preferred_element_type=jnp.float32)
        ).astype(jnp.bfloat16),
        "wide",
        scatter_dimension=0,
        tiled=True,
    ).astype(jnp.float32)
    combined = lax.all_to_all(
        own_rows.astype(jnp.bfloat16), "narrow", split_axis=1, concat_axis=0, tiled=True
    ).astype(own_rows.dtype)
    hidden_out = (as_float + combined + out_bias).astype(jnp.bfloat16)
    pages_local = page_table.shape[0] // narrow_count
    slot_ids = narrow_index * pages_local + jnp.arange(pages_local, dtype=jnp.int32)
    matches = (page_table[None, :] == slot_ids[:, None]).astype(jnp.int32)
    source_page = jnp.sum(
        matches * jnp.arange(page_table.shape[0], dtype=jnp.int32)[None, :], axis=1
    )
    token_ids = (source_page[:, None] * PAGE + jnp.arange(PAGE, dtype=jnp.int32)[None, :]).reshape(
        -1
    )
    gather_rows = (
        token_ids % tok_local // sub_rows * query_rows
        + token_ids // tok_local * sub_rows
        + token_ids % sub_rows
    )
    cache_keys = jnp.take(all_keys, gather_rows, axis=0).reshape(pages_local, PAGE, head_cols)
    cache_values = jnp.take(all_values, gather_rows, axis=0).reshape(pages_local, PAGE, head_cols)
    paged_cache = jnp.stack([cache_keys, cache_values])
    return (hidden_out, paged_cache)


CHIP_RING = (0, 2, 4, 6, 7, 5, 3, 1)
CHIPS = len(CHIP_RING)
PAIRS = ("o0", "f1", "b1", "f2", "b2", "f3", "b3", "f4")
STAT = 128
HEAD_PAD = 128
LANE_GROUP = 32
MIB = 1 << 20
VMEM = pl.BlockSpec(memory_space=pltpu.VMEM)
HBM = pl.BlockSpec(memory_space=pltpu.HBM)
SMEM = pl.BlockSpec(memory_space=pltpu.SMEM)


def owner_table():
    table = np.zeros((2 * CHIPS, 2 * CHIPS), np.int32)
    for place, chip in enumerate(CHIP_RING):
        for core in range(2):
            order = []
            for pair in PAIRS:
                shift = (-1 if pair[0] == "f" else 1) * int(pair[1]) * (1 - 2 * core)
                order.append(CHIP_RING[(place + shift) % CHIPS] * 2 + core)
                order.append(CHIP_RING[(place - shift) % CHIPS] * 2 + 1 - core)
            table[2 * chip + core] = order
    return table


def place_table():
    owners = owner_table()
    table = np.zeros_like(owners)
    for device in range(owners.shape[0]):
        table[device, owners[device]] = np.arange(owners.shape[1])
    return table


def sums_kernel(x_ref, gain_ref, bias_ref, out_ref, affine_ref):
    x = x_ref[...].astype(jnp.float32)
    first = jnp.sum(x, axis=1, keepdims=True)
    second = jnp.sum(x * x, axis=1, keepdims=True)
    lane = lax.broadcasted_iota(jnp.int32, out_ref.shape, 1)
    out_ref[...] = jnp.where(lane == 0, first, jnp.where(lane == 1, second, 0.0))
    affine_ref[0:2, :] = gain_ref[...]
    affine_ref[2:4, :] = bias_ref[...]


def block_kernel(x_ref, here_ref, there_ref, out_ref):
    feat = x_ref.shape[1]
    total = here_ref[...] + there_ref[...]
    average = total[:, 0:1] / D
    variance = total[:, 1:2] / D - average * average
    scale = lax.rsqrt(variance + 1e-05)
    lane = lax.broadcasted_iota(jnp.int32, (x_ref.shape[0], STAT), 1)
    tail = jnp.zeros((x_ref.shape[0], STAT), jnp.float32)
    for start, value in ((0, average), (3, scale)):
        for term in range(3):
            piece = value.astype(jnp.bfloat16).astype(jnp.float32)
            tail = jnp.where(lane == start + term, piece, tail)
            value = value - piece
    out_ref[:, :feat] = x_ref[...]
    out_ref[:, feat:] = tail.astype(jnp.bfloat16)


def tables_kernel(device_ref, owners_ref, lens_ref, sinks_ref, inverse_ref, phase_ref, info_ref, key_ref, cos_ref, sin_ref):
    device = device_ref[0]
    blocks = owners_ref.shape[1]
    rows = info_ref.shape[0] // blocks
    half_rot = ROTARY // 2
    lane = lax.broadcasted_iota(jnp.int32, (rows, HEAD_PAD), 1)
    sub = lax.broadcasted_iota(jnp.int32, (rows, HEAD_PAD), 0)
    key_lane = lax.broadcasted_iota(jnp.int32, key_ref.shape, 1)
    key = key_lane
    shared = HEAD_PAD // LANE_GROUP
    for base in range(0, blocks, shared):
        position = jnp.zeros((rows, HEAD_PAD), jnp.int32)
        for g in range(shared):
            j = base + g
            first = owners_ref[device, j] * rows
            key = jnp.where(key_lane // rows == j, first + key_lane - j * rows, key)
            token = first + sub
            begin, end = jnp.zeros_like(token), jnp.zeros_like(token)
            start = jnp.int32(0)
            for s in range(lens_ref.shape[0]):
                inside = (token >= start) & (token < start + lens_ref[s])
                begin = jnp.where(inside, start, begin)
                end = jnp.where(inside, start + sinks_ref[s], end)
                start = start + lens_ref[s]
            info_ref[j * rows : (j + 1) * rows, :] = jnp.where(
                lane == 0, token, jnp.where(lane == 1, begin, end)
            )
            position = jnp.where(lane // LANE_GROUP == g, token - begin, position)
        waves = jnp.cos(position.astype(jnp.float32) * inverse_ref[...] - phase_ref[...])
        for g in range(shared):
            at = slice((base + g) * rows, (base + g + 1) * rows)
            here = pltpu.roll(waves, (HEAD_PAD - g * LANE_GROUP) % HEAD_PAD, 1)
            later = pltpu.roll(waves, (HEAD_PAD - g * LANE_GROUP + half_rot) % HEAD_PAD, 1)
            before = pltpu.roll(waves, (2 * HEAD_PAD - g * LANE_GROUP - half_rot) % HEAD_PAD, 1)
            cosine = jnp.where(lane < half_rot, here, later)
            cos_ref[at, :] = jnp.where(lane < ROTARY, cosine, 1.0)
            sine = jnp.where(lane < half_rot, -before, here)
            sin_ref[at, :] = jnp.where(lane < ROTARY, sine, 0.0)
    key_ref[...] = key


def tables(total, device, lens, sinks):
    half_rot = ROTARY // 2
    lane = np.arange(HEAD_PAD) % LANE_GROUP
    inverse = (10000.0 ** (-2.0 * (lane % half_rot) / ROTARY)).astype(np.float32)[None, :]
    phase = np.where(lane < half_rot, 0.0, np.pi / 2).astype(np.float32)[None, :]
    wide = (total, HEAD_PAD)
    return pl.pallas_call(
        tables_kernel,
        out_shape=(
            jax.ShapeDtypeStruct(wide, jnp.int32),
            jax.ShapeDtypeStruct((1, total), jnp.int32),
            jax.ShapeDtypeStruct(wide, jnp.float32),
            jax.ShapeDtypeStruct(wide, jnp.float32),
        ),
        in_specs=[SMEM] * 4 + [VMEM] * 2,
        out_specs=(VMEM,) * 4,
        compiler_params=pltpu.CompilerParams(vmem_limit_bytes=8 * MIB),
        name="tables",
    )(device, jnp.asarray(owner_table()), lens, sinks, jnp.asarray(inverse), jnp.asarray(phase))


def pages_kernel(device_ref, n_ref, places_ref, table_ref, kv_ref, out_ref):
    pages = table_ref.shape[0]
    per_owner = pages // places_ref.shape[1]
    device, shift = device_ref[0], n_ref[0] * (pages // 2)
    for p in range(pages):
        place = places_ref[device, p // per_owner] * per_owner + p % per_owner
        row = pl.multiple_of(place * PAGE, PAGE)
        out_ref[lax.rem(table_ref[p] + shift, pages)] = kv_ref[pl.ds(row, PAGE), :]


def ordered_pages(device, n, page_table, kv):
    return pl.pallas_call(
        pages_kernel,
        out_shape=jax.ShapeDtypeStruct((page_table.shape[0], PAGE, kv.shape[1]), kv.dtype),
        in_specs=[SMEM] * 4 + [VMEM],
        out_specs=VMEM,
        compiler_params=pltpu.CompilerParams(vmem_limit_bytes=8 * MIB),
        name="ordered_pages",
    )(device, n, jnp.asarray(place_table()), page_table, kv)


def normalise(blocks, affine_ref, attn, mlp):
    rows = blocks[0].shape[0]
    feat = attn.shape[1]
    step = 512
    for b, block in enumerate(blocks):
        tail = block[:, feat:].astype(jnp.float32)
        average = tail[:, 0:1] + tail[:, 1:2] + tail[:, 2:3]
        scale = tail[:, 3:4] + tail[:, 4:5] + tail[:, 5:6]
        here = slice(b * rows, (b + 1) * rows)
        for c in range(0, feat, step):
            at = slice(c, c + step)
            scaled = (block[:, at].astype(jnp.float32) - average) * scale
            attn[here, at] = (scaled * affine_ref[0:1, at] + affine_ref[2:3, at]).astype(jnp.bfloat16)
            mlp[here, at] = (scaled * affine_ref[1:2, at] + affine_ref[3:4, at]).astype(jnp.bfloat16)


def project_kernel(count, outs, first_call, n_ref, affine_ref, wq_ref, wk_ref, wv_ref, wu_ref, *refs):
    blocks, refs = refs[:count], refs[count:]
    mine_ref, refs = refs[0], refs[1:]
    sent_refs, refs = refs[: len(outs)], refs[len(outs) :]
    hidden = wu_ref.shape[1]
    width = 384
    tiles = hidden // width
    copies = []
    if first_call:
        held, (attn, mlp, sems) = refs[:4], refs[4:]
        copies = [
            pltpu.make_async_copy(src, dst, sems.at[i])
            for i, (src, dst) in enumerate(zip((wq_ref, wk_ref, wv_ref), held))
        ]
        for t in range(tiles):
            at = slice(t * width, (t + 1) * width)
            copies.append(pltpu.make_async_copy(wu_ref.at[:, at], held[3].at[:, at], sems.at[3 + t]))
        for copy in copies:
            copy.start()
        wq_ref, wk_ref, wv_ref, wu_ref = held
    else:
        attn, mlp = refs
    rows = 2 * blocks[0].shape[0]
    half = wq_ref.shape[1] // 2
    normalise(blocks, affine_ref, attn, mlp)
    low, high = [], []
    for i, weight in enumerate((wq_ref, wk_ref, wv_ref)):
        if first_call:
            copies[i].wait()
        part = jnp.dot(attn[...], weight[...], preferred_element_type=jnp.float32)
        low.append(part[:, :half])
        high.append(part[:, half:])
    low = jnp.concatenate(low, axis=1).astype(jnp.bfloat16)
    high = jnp.concatenate(high, axis=1).astype(jnp.bfloat16)
    first = n_ref[0] == 0
    mine_ref[...] = jnp.where(first, low, high)
    send = jnp.where(first, high, low)
    send = [send[p * rows : (p + 1) * rows] for p in range(count // 2)]
    gap = -(3 * half * len(send)) % 128
    if gap:
        send.append(jnp.zeros((rows, gap), jnp.bfloat16))
    send = jnp.concatenate(send, axis=1)
    for ref, items in zip(sent_refs, outs):
        if items[-1] == "q":
            ref[:, hidden * (len(items) - 1) :] = send
    for t in range(tiles):
        if first_call:
            copies[3 + t].wait()
        at = slice(t * width, (t + 1) * width)
        part = jnp.dot(mlp[...], wu_ref[:, at], preferred_element_type=jnp.float32)
        part = part.astype(jnp.bfloat16)
        for ref, items in zip(sent_refs, outs):
            for i, item in enumerate(items):
                if item != "q":
                    begin = i * hidden + t * width
                    ref[:, begin : begin + width] = part[item * rows : (item + 1) * rows]


def project(n, affine, weights, blocks, outs, first_call=False):
    count = len(blocks)
    rows = 2 * blocks[0].shape[0]
    feat, cols = weights[0].shape
    hidden = weights[3].shape[1]
    sent = 3 * cols // 2 * (count // 2)
    sent += -sent % 128
    shapes = [jax.ShapeDtypeStruct((rows * count // 2, 3 * cols // 2), jnp.bfloat16)]
    for items in outs:
        width = sum(sent if item == "q" else hidden for item in items)
        shapes.append(jax.ShapeDtypeStruct((rows, width), jnp.bfloat16))
    scratch = [pltpu.VMEM((rows * count // 2, feat), jnp.bfloat16)] * 2
    if first_call:
        shapes += [jax.ShapeDtypeStruct(w.shape, w.dtype) for w in weights]
        scratch.append(pltpu.SemaphoreType.DMA((3 + hidden // 384,)))
    return pl.pallas_call(
        functools.partial(project_kernel, count, outs, first_call),
        out_shape=tuple(shapes),
        in_specs=[SMEM, VMEM] + [HBM if first_call else VMEM] * 4 + [VMEM] * count,
        out_specs=(VMEM,) * len(shapes),
        scratch_shapes=scratch,
        compiler_params=pltpu.CompilerParams(vmem_limit_bytes=(46 if first_call else 9) * MIB),
        name="project",
    )(n, affine, *weights, *blocks)


def attend_kernel(count, span, offsets, n_ref, bias_ref, cos_ref, sin_ref, query_ref, key_ref, *refs):
    mine, got = refs[:count], refs[count : 2 * count]
    att_ref, kv_ref, queries, keys, values = refs[2 * count :]
    heads = queries.shape[0]
    half = kv_ref.shape[1] // 2
    total = kv_ref.shape[0]
    half_rot = ROTARY // 2
    bias = jnp.where(n_ref[0] == 0, bias_ref[:, :half], bias_ref[:, half:])
    offset = 0
    for g in range(count):
        rows = mine[g].shape[0]
        at = slice(offset, offset + rows)
        offset += rows
        pieces = []
        for p in range(rows // got[g].shape[0]):
            begin = offsets[g] + 3 * half * p
            pieces.append(got[g][:, begin : begin + 3 * half])
        sent = jnp.concatenate(pieces, axis=0)
        summed = mine[g][...].astype(jnp.float32) + sent.astype(jnp.float32)
        cosine, sine = cos_ref[at, :], sin_ref[at, :]
        lane = lax.broadcasted_iota(jnp.int32, (rows, HEAD_PAD), 1)
        pad = jnp.zeros((rows, HEAD_PAD - HEAD_DIM), jnp.float32)
        for kind in range(3):
            kept = []
            for h in range(heads):
                begin = kind * half + h * HEAD_DIM
                u = summed[:, begin : begin + HEAD_DIM]
                u = u + bias[kind : kind + 1, h * HEAD_DIM : (h + 1) * HEAD_DIM]
                u = jnp.concatenate([u, pad], axis=1)
                if kind < 2:
                    other = jnp.where(
                        lane < half_rot,
                        pltpu.roll(u, HEAD_PAD - half_rot, 1),
                        pltpu.roll(u, half_rot, 1),
                    )
                    u = u * cosine + other * sine
                (queries, keys, values)[kind][h, at, :] = u.astype(jnp.bfloat16)
                kept.append(u[:, :HEAD_DIM])
            if kind > 0:
                kv_ref[at, (kind - 1) * half : kind * half] = jnp.concatenate(kept, axis=1).astype(
                    jnp.bfloat16
                )
    tile = 256
    for start in range(0, total, tile):
        at = slice(start, start + tile)
        info = query_ref[at, :]
        token, begin, end = info[:, 0:1], info[:, 1:2], info[:, 2:3]
        key_token = key_ref[...]
        near = key_token > token - span
        allowed = (key_token >= begin) & (key_token <= token) & (near | (key_token < end))
        outs = []
        for h in range(heads):
            scores = lax.dot_general(
                queries[h, at, :],
                keys[h],
                (((1,), (1,)), ((), ())),
                preferred_element_type=jnp.float32,
            ) * (1.0 / HEAD_DIM**0.5)
            masked = jnp.where(allowed, scores, -1e30)
            weights = jnp.exp(masked - jnp.max(masked, axis=1, keepdims=True))
            probs = weights / jnp.sum(weights, axis=1, keepdims=True)
            out = jnp.dot(probs.astype(jnp.bfloat16), values[h], preferred_element_type=jnp.float32)
            outs.append(out[:, :HEAD_DIM])
        side = start // (total // 2)
        att_ref[start % (total // 2) : start % (total // 2) + tile, side * half : (side + 1) * half] = (
            jnp.concatenate(outs, axis=1).astype(jnp.bfloat16)
        )


def attend(span, offsets, n, bias, cosine, sine, query_info, key_token, mine, got):
    count = len(mine)
    total = cosine.shape[0]
    half = mine[0].shape[1] // 3
    heads = half // HEAD_DIM
    scratch = pltpu.VMEM((heads, total, HEAD_PAD), jnp.bfloat16)
    return pl.pallas_call(
        functools.partial(attend_kernel, count, span, offsets),
        out_shape=(
            jax.ShapeDtypeStruct((total // 2, 2 * half), jnp.bfloat16),
            jax.ShapeDtypeStruct((total, 2 * half), jnp.bfloat16),
        ),
        in_specs=[SMEM] + [VMEM] * (5 + 2 * count),
        out_specs=(VMEM, VMEM),
        scratch_shapes=[scratch, scratch, scratch],
        compiler_params=pltpu.CompilerParams(vmem_limit_bytes=10 * MIB),
        name="attend",
    )(n, bias, cosine, sine, query_info, key_token, *mine, *got)


def gelu(u):
    return u * (1.0 + lax.erf(u * (0.5**0.5))) * 0.5


def down_kernel(count, bias_ref, wd_ref, *refs):
    mine, got = refs[:count], refs[count : 2 * count]
    out_ref, units = refs[2 * count :]
    rows = mine[0].shape[0]
    step = 384
    for i in range(count):
        for c in range(0, units.shape[1], step):
            at = slice(c, c + step)
            u = mine[i][:, at].astype(jnp.float32) + got[i][:, at].astype(jnp.float32)
            u = gelu(u + bias_ref[:, at])
            units[i * rows : (i + 1) * rows, at] = u.astype(jnp.bfloat16)
    width = 512
    for c in range(0, wd_ref.shape[1], width):
        at = slice(c, c + width)
        out = jnp.dot(units[...], wd_ref[:, at], preferred_element_type=jnp.float32)
        out_ref[:, at] = out.astype(jnp.bfloat16)


def down(bias, mine, got, wd):
    count = len(mine)
    rows, hidden = mine[0].shape[0], wd.shape[0]
    return pl.pallas_call(
        functools.partial(down_kernel, count),
        out_shape=jax.ShapeDtypeStruct((count * rows, wd.shape[1]), jnp.bfloat16),
        in_specs=[VMEM] * (2 + 2 * count),
        out_specs=VMEM,
        scratch_shapes=[pltpu.VMEM((count * rows, hidden), jnp.bfloat16)],
        compiler_params=pltpu.CompilerParams(vmem_limit_bytes=6 * MIB),
        name="down",
    )(bias, wd, *mine, *got)


def attended_rows(ref, offset, rows):
    height, half = ref.shape[0], ref.shape[1] // 2
    side = offset // height
    return ref[offset % height : offset % height + rows, side * half : (side + 1) * half]


def mix_kernel(offsets, n_ref, down_ref, att_ref, other_ref, wo_ref, own_ref, sib_ref):
    half = att_ref.shape[1] // 2
    rows = own_ref.shape[0] // len(offsets)
    n = n_ref[0]
    here = pl.ds(pl.multiple_of(n * half, 16), half)
    there = pl.ds(pl.multiple_of((1 - n) * half, 16), half)
    mine = jnp.concatenate([attended_rows(att_ref, o, 2 * rows) for o in offsets], axis=0)
    other = jnp.concatenate([attended_rows(other_ref, o, 2 * rows) for o in offsets], axis=0)
    width = 512
    for c in range(0, own_ref.shape[1], width):
        at = slice(c, c + width)
        out = down_ref[:, at].astype(jnp.float32)
        out += jnp.dot(mine, wo_ref[here, at], preferred_element_type=jnp.float32)
        out += jnp.dot(other, wo_ref[there, at], preferred_element_type=jnp.float32)
        out = out.astype(jnp.bfloat16)
        for i in range(len(offsets)):
            own_ref[i * rows : (i + 1) * rows, at] = out[2 * i * rows : (2 * i + 1) * rows]
            sib_ref[i * rows : (i + 1) * rows, at] = out[(2 * i + 1) * rows : (2 * i + 2) * rows]


def mix(n, offsets, partial_down, att, other, wo):
    rows, feat = partial_down.shape
    shape = jax.ShapeDtypeStruct((rows // 2, feat), jnp.bfloat16)
    return pl.pallas_call(
        functools.partial(mix_kernel, offsets),
        out_shape=(shape, shape),
        in_specs=[SMEM] + [VMEM] * 4,
        out_specs=(VMEM, VMEM),
        compiler_params=pltpu.CompilerParams(vmem_limit_bytes=5 * MIB),
        name="mix",
    )(n, partial_down, att, other, wo)


def output_kernel(
    offset, column, n_ref, bias_ref, mine_ref, got_ref, att_ref, other_ref, wo_ref, wd_ref, own_ref, sib_ref, units
):
    rows = mine_ref.shape[0]
    half = att_ref.shape[1] // 2
    own_rows = own_ref.shape[0]
    step = 384
    for c in range(0, units.shape[1], step):
        at = slice(c, c + step)
        there = slice(column + c, column + c + step)
        u = mine_ref[:, there].astype(jnp.float32) + got_ref[:, there].astype(jnp.float32)
        units[:, at] = gelu(u + bias_ref[:, at]).astype(jnp.bfloat16)
    n = n_ref[0]
    here = pl.ds(pl.multiple_of(n * half, 16), half)
    there = pl.ds(pl.multiple_of((1 - n) * half, 16), half)
    mine = attended_rows(att_ref, offset, rows)
    other = attended_rows(other_ref, offset, rows)
    width = 512
    for c in range(0, wd_ref.shape[1], width):
        at = slice(c, c + width)
        out = jnp.dot(units[...], wd_ref[:, at], preferred_element_type=jnp.float32)
        out += jnp.dot(mine, wo_ref[here, at], preferred_element_type=jnp.float32)
        out += jnp.dot(other, wo_ref[there, at], preferred_element_type=jnp.float32)
        out = out.astype(jnp.bfloat16)
        own_ref[:, at] = out[:own_rows]
        sib_ref[:, at] = out[own_rows:]


def output(n, offset, column, bias, mine, got, att, other, wo, wd):
    rows, hidden = mine.shape[0], wd.shape[0]
    shape = jax.ShapeDtypeStruct((rows // 2, wd.shape[1]), jnp.bfloat16)
    return pl.pallas_call(
        functools.partial(output_kernel, offset, column),
        out_shape=(shape, shape),
        in_specs=[SMEM] + [VMEM] * 7,
        out_specs=(VMEM, VMEM),
        scratch_shapes=[pltpu.VMEM((rows, hidden), jnp.bfloat16)],
        compiler_params=pltpu.CompilerParams(vmem_limit_bytes=5 * MIB),
        name="output",
    )(n, bias, mine, got, att, other, wo, wd)


def after(*values):
    return lax.optimization_barrier(values)


def local_ring(
    hidden_in,
    w_query,
    w_key,
    w_value,
    qkv_bias,
    w_up,
    up_bias,
    w_attn_out,
    w_down,
    out_bias,
    norm_gain,
    norm_bias,
    seq_lens,
    sink_count,
    page_table,
):
    device = lax.axis_index("wide").astype(jnp.int32).reshape(1)
    n = lax.axis_index("narrow").astype(jnp.int32)
    n_arg = n.reshape(1)
    rows, feat = hidden_in.shape
    total_tokens = rows * lax.axis_size("wide")
    half = w_query.shape[1] // 2

    fwd_pairs, bwd_pairs, swap_pairs = [], [], []
    for p in range(CHIPS):
        here, next_chip = CHIP_RING[p], CHIP_RING[(p + 1) % CHIPS]
        fwd_pairs += [(2 * here, 2 * next_chip), (2 * next_chip + 1, 2 * here + 1)]
        bwd_pairs += [(2 * next_chip, 2 * here), (2 * here + 1, 2 * next_chip + 1)]
        swap_pairs += [(2 * here, 2 * here + 1), (2 * here + 1, 2 * here)]
    fwd = lambda v: lax.ppermute(v, "wide", fwd_pairs)
    bwd = lambda v: lax.ppermute(v, "wide", bwd_pairs)
    swap = lambda v: lax.ppermute(v, "wide", swap_pairs)
    cross = lambda v: lax.ppermute(v, "narrow", [(0, 1), (1, 0)])

    sums, affine = pl.pallas_call(
        sums_kernel,
        out_shape=(
            jax.ShapeDtypeStruct((rows, STAT), jnp.float32),
            jax.ShapeDtypeStruct((4, feat), jnp.float32),
        ),
        in_specs=[VMEM] * 3,
        out_specs=(VMEM, VMEM),
        compiler_params=pltpu.CompilerParams(vmem_limit_bytes=8 * MIB),
        name="row_sums",
    )(hidden_in, norm_gain, norm_bias)
    first_block = pl.pallas_call(
        block_kernel,
        out_shape=jax.ShapeDtypeStruct((rows, feat + STAT), jnp.bfloat16),
        in_specs=[VMEM] * 3,
        out_specs=VMEM,
        compiler_params=pltpu.CompilerParams(vmem_limit_bytes=8 * MIB),
        name="first_block",
    )(hidden_in, sums, cross(sums))

    up_row = up_bias[None, :]

    def add(*terms):
        return sum(t.astype(jnp.float32) for t in terms).astype(jnp.bfloat16)

    def finish(name, u, v, column=0):
        return output(
            n_arg, PAIRS.index(name) * 2 * rows, column, up_row, u, v, att, other, w_attn_out, w_down
        )

    def pair(halves, *running):
        return add(halves[0], swap(halves[1]), *running)

    per_device = page_table.shape[0] // 2
    hidden = w_up.shape[1]
    o0 = first_block
    f1, b1, s0 = fwd(o0), bwd(o0), swap(o0)
    kept0, send0, *weights = project(
        n_arg, affine, (w_query, w_key, w_value, w_up), [o0, s0], ((0, "q"),), True
    )
    f1, b1, send0, kept0 = after(f1, b1, send0, kept0)
    got0 = cross(send0)
    f2, b2 = fwd(f1), bwd(b1)
    kept1, send1, u_f1 = project(
        n_arg, affine, weights, [f1, swap(f1), b1, swap(b1)], ((1, "q"), (0,))
    )
    f2, b2, got0, send1, u_f1 = after(f2, b2, got0, send1, u_f1)
    got1 = cross(send1)
    f3, b3 = fwd(f2), bwd(b2)
    kept2, send2, u_b2 = project(
        n_arg, affine, weights, [f2, swap(f2), b2, swap(b2)], ((0, "q"), (1,))
    )
    f3, b3, got1, send2, u_b2, late_device = after(f3, b3, got1, send2, u_b2, device)
    got2 = cross(send2)
    f4, g3, h3 = fwd(f3), swap(f3), swap(b3)
    query_info, key_token, cosine, sine = tables(total_tokens, late_device, seq_lens, sink_count)
    f3, b3, f4, g3, h3, got2, u_b2, query_info, key_token, cosine, sine = after(
        f3, b3, f4, g3, h3, got2, u_b2, query_info, key_token, cosine, sine
    )
    v_b2 = cross(u_b2)
    kept3, send3, u_f3, u_far = project(
        n_arg, affine, weights, [f3, g3, b3, h3, f4, swap(f4)], (("q",), (0,), (2, 1))
    )
    v_b2, send3, u_f3, u_far = after(v_b2, send3, u_f3, u_far)
    got3 = cross(send3)
    early = down(up_row, [send0, send1, send2], [got0, got1, got2], w_down)
    got3, early, u_far = after(got3, early, u_far)
    v_far = cross(u_far)
    att, kv = attend(
        total_tokens // 16, (hidden, hidden, hidden, 0), n_arg, qkv_bias, cosine, sine,
        query_info, key_token, [kept0, kept1, kept2, kept3], [got0, got1, got2, got3],
    )
    v_far, att, u_f3 = after(v_far, att, u_f3)
    other = cross(att)
    other, u_f3, u_b2, u_f1 = after(other, u_f3, u_b2, u_f1)
    v_f3 = cross(u_f3)
    y_f4 = finish("f4", u_far, v_far)
    y_b3 = finish("b3", u_far, v_far, hidden)
    r_b, r_f = bwd(pair(y_f4)), fwd(pair(y_b3))
    y_b2 = finish("b2", u_b2, v_b2)
    m_own, m_sib = mix(
        n_arg, tuple(PAIRS.index(p) * 2 * rows for p in ("o0", "b1", "f2")), early, att, other,
        w_attn_out,
    )
    v_f3, r_b, r_f, y_b2, m_own, m_sib, u_f1 = after(v_f3, r_b, r_f, y_b2, m_own, m_sib, u_f1)
    v_f1 = cross(u_f1)
    m_got = swap(m_sib)
    y_f3 = finish("f3", u_f3, v_f3)
    r_f = fwd(pair(y_b2, r_f))
    r_b = bwd(pair(y_f3, r_b))
    v_f1, r_b, r_f, m_got, kv = after(v_f1, r_b, r_f, m_got, kv)
    r_f = fwd(add(r_f, m_own[rows : 2 * rows], m_got[rows : 2 * rows]))
    r_b = bwd(add(r_b, m_own[2 * rows :], m_got[2 * rows :]))
    y_f1 = finish("f1", u_f1, v_f1)
    paged = ordered_pages(device, n_arg, page_table, kv)
    r_f, r_b, y_f1, paged = after(r_f, r_b, y_f1, paged)
    r_b = bwd(pair(y_f1, r_b))
    cache_mine, cache_got = paged[:per_device], cross(paged[per_device:])
    summed = (
        r_b.astype(jnp.float32)
        + r_f.astype(jnp.float32)
        + m_own[:rows].astype(jnp.float32)
        + m_got[:rows].astype(jnp.float32)
    )
    hidden_out = (hidden_in.astype(jnp.float32) + summed + out_bias).astype(jnp.bfloat16)
    left = jnp.where(n == 0, cache_mine, cache_got)
    right = jnp.where(n == 0, cache_got, cache_mine)
    paged_cache = jnp.stack(
        [
            jnp.concatenate([left[..., :half], right[..., :half]], axis=-1),
            jnp.concatenate([left[..., half:], right[..., half:]], axis=-1),
        ]
    )
    return (hidden_out, paged_cache)


def solution(mesh):
    in_specs = (
        P("wide", "narrow"),
        P("narrow", "wide"),
        P("narrow", "wide"),
        P("narrow", "wide"),
        P(None, "wide"),
        P("narrow", "wide"),
        P("wide"),
        P("wide", "narrow"),
        P("wide", "narrow"),
        P("narrow"),
        P(None, "narrow"),
        P(None, "narrow"),
        P(),
        P(),
        P(),
    )
    out_specs = (P("wide", "narrow"), P(None, "narrow", None, "wide"))
    ringed = mesh.shape["wide"] == 2 * CHIPS and mesh.shape["narrow"] == 2
    local = local_ring if ringed else local_generic
    return jax.shard_map(local, mesh=mesh, in_specs=in_specs, out_specs=out_specs, check_vma=False)
```

```python
import functools

import jax
import jax.numpy as jnp
import numpy as np
from jax import lax
from jax.experimental import pallas as pl
from jax.experimental.pallas import tpu as pltpu
from jax.sharding import PartitionSpec as P

D = 6144
HEAD_DIM = 96
ROTARY = 24
PAGE = 16


def segment_info(token_index, seq_lens, sink_count):
    seq_ends = jnp.cumsum(seq_lens)
    seq_starts = seq_ends - seq_lens
    inside = (token_index[:, None] >= seq_starts[None, :]) & (
        token_index[:, None] < seq_ends[None, :]
    )
    member = inside.astype(jnp.int32)
    seq_number = jnp.arange(seq_lens.shape[0], dtype=jnp.int32)
    segment = jnp.sum(member * seq_number[None, :], axis=1)
    position = token_index - jnp.sum(member * seq_starts[None, :], axis=1)
    sink_limit = jnp.sum(member * sink_count[None, :], axis=1)
    return (segment, position, sink_limit)


def rotate(values, position):
    half_rot = ROTARY // 2
    freq_index = jnp.arange(half_rot, dtype=jnp.float32)
    inverse = jnp.power(jnp.float32(10000.0), -2.0 * freq_index / ROTARY)
    angles = position.astype(jnp.float32)[:, None] * inverse[None, :]
    cosine = jnp.cos(angles)[:, None, :]
    sine_part = jnp.sin(angles)[:, None, :]
    first_half = values[..., :half_rot]
    second_half = values[..., half_rot:ROTARY]
    return jnp.concatenate(
        [
            first_half * cosine - second_half * sine_part,
            second_half * cosine + first_half * sine_part,
            values[..., ROTARY:],
        ],
        axis=-1,
    )


def local_generic(
    hidden_in,
    w_query,
    w_key,
    w_value,
    qkv_bias,
    w_up,
    up_bias,
    w_attn_out,
    w_down,
    out_bias,
    norm_gain,
    norm_bias,
    seq_lens,
    sink_count,
    page_table,
):
    wide_count = lax.axis_size("wide")
    narrow_count = lax.axis_size("narrow")
    narrow_index = lax.axis_index("narrow")
    tok_local, feat_local = hidden_in.shape
    sub_rows = tok_local // narrow_count
    total_tokens = tok_local * wide_count
    query_rows = wide_count * sub_rows
    head_cols = w_query.shape[1]
    heads_local = head_cols // HEAD_DIM
    as_float = hidden_in.astype(jnp.float32)
    partial_sum = jnp.sum(as_float, axis=1)
    partial_square = jnp.sum(as_float * as_float, axis=1)
    total_sum, total_square = lax.psum((partial_sum, partial_square), "narrow")
    average = total_sum / D
    variance = total_square / D - average * average
    scaled = (as_float - average[:, None]) * lax.rsqrt(variance + 1e-05)[:, None]
    attn_normed = (scaled * norm_gain[0] + norm_bias[0]).astype(jnp.bfloat16)
    mlp_normed = (scaled * norm_gain[1] + norm_bias[1]).astype(jnp.bfloat16)
    stacked = jnp.stack([attn_normed, mlp_normed]).reshape(2, narrow_count, sub_rows, feat_local)
    gathered = lax.all_gather(stacked, "wide", axis=2, tiled=True).reshape(
        2, total_tokens, feat_local
    )
    local_order = jnp.arange(query_rows, dtype=jnp.int32)
    local_tokens = (
        local_order // sub_rows * tok_local + narrow_index * sub_rows + local_order % sub_rows
    )
    local_seg, local_pos, local_sink = segment_info(local_tokens, seq_lens, sink_count)
    all_order = jnp.arange(total_tokens, dtype=jnp.int32)
    all_tokens = (
        all_order % query_rows // sub_rows * tok_local
        + all_order // query_rows * sub_rows
        + all_order % sub_rows
    )
    all_seg, all_pos, all_sink = segment_info(all_tokens, seq_lens, sink_count)
    qkv_weight = jnp.concatenate([w_query, w_key, w_value], axis=1)
    attn_part = gathered[0]
    mlp_part = gathered[1]
    summed = lax.psum_scatter(
        jnp.concatenate(
            [
                jnp.dot(attn_part, qkv_weight, preferred_element_type=jnp.float32),
                jnp.dot(mlp_part, w_up, preferred_element_type=jnp.float32),
            ],
            axis=1,
        ).astype(jnp.bfloat16),
        "narrow",
        scatter_dimension=0,
        tiled=True,
    ).astype(jnp.float32)
    query_sum = summed[:, :head_cols]
    key_sum = summed[:, head_cols : 2 * head_cols]
    value_sum = summed[:, 2 * head_cols : 3 * head_cols]
    unit_sum = summed[:, 3 * head_cols :]
    keys_local = (
        rotate((key_sum + qkv_bias[1]).reshape(query_rows, heads_local, HEAD_DIM), local_pos)
        .astype(jnp.bfloat16)
        .reshape(query_rows, head_cols)
    )
    values_local = (value_sum + qkv_bias[2]).astype(jnp.bfloat16)
    all_keys, all_values = (
        lax.all_gather(keys_local, "narrow", axis=0, tiled=True),
        lax.all_gather(values_local, "narrow", axis=0, tiled=True),
    )
    queries = rotate(
        (query_sum + qkv_bias[0]).reshape(query_rows, heads_local, HEAD_DIM), local_pos
    ).astype(jnp.bfloat16)
    hidden_units = jax.nn.gelu(unit_sum + up_bias, approximate=False).astype(jnp.bfloat16)
    window_span = total_tokens // 16
    allowed = (local_seg[:, None] == all_seg[None, :]) & (all_pos[None, :] <= local_pos[:, None])
    allowed = allowed & (
        (local_pos[:, None] - all_pos[None, :] < window_span)
        | (all_pos[None, :] < local_sink[:, None])
    )
    key_heads = all_keys.reshape(total_tokens, heads_local, HEAD_DIM)
    value_heads = all_values.reshape(total_tokens, heads_local, HEAD_DIM)
    scores = jnp.einsum("qhd,khd->hqk", queries, key_heads, preferred_element_type=jnp.float32) * (
        1.0 / HEAD_DIM**0.5
    )
    masked = jnp.where(allowed[None], scores, jnp.float32(-1e30))
    top_score = jnp.max(masked, axis=2, keepdims=True)
    weights = jnp.exp(masked - top_score)
    probs = (weights / jnp.sum(weights, axis=2, keepdims=True)).astype(jnp.bfloat16)
    attended = (
        jnp.einsum("hqk,khd->qhd", probs, value_heads, preferred_element_type=jnp.float32)
        .astype(jnp.bfloat16)
        .reshape(query_rows, head_cols)
    )
    full_out, full_down = (
        lax.all_gather(w_attn_out, "narrow", axis=1, tiled=True),
        lax.all_gather(w_down, "narrow", axis=1, tiled=True),
    )
    attn_part = attended
    own_rows = lax.psum_scatter(
        (
            jnp.dot(attn_part, full_out, preferred_element_type=jnp.float32)
            + jnp.dot(hidden_units, full_down, preferred_element_type=jnp.float32)
        ).astype(jnp.bfloat16),
        "wide",
        scatter_dimension=0,
        tiled=True,
    ).astype(jnp.float32)
    combined = lax.all_to_all(
        own_rows.astype(jnp.bfloat16), "narrow", split_axis=1, concat_axis=0, tiled=True
    ).astype(own_rows.dtype)
    hidden_out = (as_float + combined + out_bias).astype(jnp.bfloat16)
    pages_local = page_table.shape[0] // narrow_count
    slot_ids = narrow_index * pages_local + jnp.arange(pages_local, dtype=jnp.int32)
    matches = (page_table[None, :] == slot_ids[:, None]).astype(jnp.int32)
    source_page = jnp.sum(
        matches * jnp.arange(page_table.shape[0], dtype=jnp.int32)[None, :], axis=1
    )
    token_ids = (source_page[:, None] * PAGE + jnp.arange(PAGE, dtype=jnp.int32)[None, :]).reshape(
        -1
    )
    gather_rows = (
        token_ids % tok_local // sub_rows * query_rows
        + token_ids // tok_local * sub_rows
        + token_ids % sub_rows
    )
    cache_keys = jnp.take(all_keys, gather_rows, axis=0).reshape(pages_local, PAGE, head_cols)
    cache_values = jnp.take(all_values, gather_rows, axis=0).reshape(pages_local, PAGE, head_cols)
    paged_cache = jnp.stack([cache_keys, cache_values])
    return (hidden_out, paged_cache)


CHIP_RING = (0, 2, 4, 6, 7, 5, 3, 1)
CHIPS = len(CHIP_RING)
PAIRS = ("o0", "f1", "b1", "f2", "b2", "f3", "b3", "f4")
STAT = 128
HEAD_PAD = 128
LANE_GROUP = 32
MIB = 1 << 20
VMEM = pl.BlockSpec(memory_space=pltpu.VMEM)
HBM = pl.BlockSpec(memory_space=pltpu.HBM)
SMEM = pl.BlockSpec(memory_space=pltpu.SMEM)


def owner_table():
    table = np.zeros((2 * CHIPS, 2 * CHIPS), np.int32)
    for place, chip in enumerate(CHIP_RING):
        for core in range(2):
            order = []
            for pair in PAIRS:
                shift = (-1 if pair[0] == "f" else 1) * int(pair[1]) * (1 - 2 * core)
                order.append(CHIP_RING[(place + shift) % CHIPS] * 2 + core)
                order.append(CHIP_RING[(place - shift) % CHIPS] * 2 + 1 - core)
            table[2 * chip + core] = order
    return table


def place_table():
    owners = owner_table()
    table = np.zeros_like(owners)
    for device in range(owners.shape[0]):
        table[device, owners[device]] = np.arange(owners.shape[1])
    return table


def sums_kernel(device_ref, n_ref, x_ref, out_ref, index_ref):
    x = x_ref[...].astype(jnp.float32)
    first = jnp.sum(x, axis=1, keepdims=True)
    second = jnp.sum(x * x, axis=1, keepdims=True)
    lane = lax.broadcasted_iota(jnp.int32, out_ref.shape, 1)
    out_ref[...] = jnp.where(lane == 0, first, jnp.where(lane == 1, second, 0.0))
    index_ref[0] = device_ref[0]
    index_ref[1] = n_ref[0]


def block_kernel(x_ref, gain_ref, bias_ref, here_ref, there_ref, out_ref, affine_ref):
    feat = x_ref.shape[1]
    total = here_ref[...] + there_ref[...]
    average = total[:, 0:1] / D
    variance = total[:, 1:2] / D - average * average
    scale = lax.rsqrt(variance + 1e-05)
    lane = lax.broadcasted_iota(jnp.int32, (x_ref.shape[0], STAT), 1)
    tail = jnp.zeros((x_ref.shape[0], STAT), jnp.float32)
    for start, value in ((0, average), (3, scale)):
        for term in range(3):
            piece = value.astype(jnp.bfloat16).astype(jnp.float32)
            tail = jnp.where(lane == start + term, piece, tail)
            value = value - piece
    out_ref[:, :feat] = x_ref[...]
    out_ref[:, feat:] = tail.astype(jnp.bfloat16)
    affine_ref[0:2, :] = gain_ref[...]
    affine_ref[2:4, :] = bias_ref[...]


def tables_kernel(index_ref, owners_ref, lens_ref, sinks_ref, inverse_ref, phase_ref, info_ref, key_ref, cos_ref, sin_ref):
    device = index_ref[0]
    blocks = owners_ref.shape[1]
    rows = info_ref.shape[0] // blocks
    half_rot = ROTARY // 2
    lane = lax.broadcasted_iota(jnp.int32, (rows, HEAD_PAD), 1)
    sub = lax.broadcasted_iota(jnp.int32, (rows, HEAD_PAD), 0)
    key_lane = lax.broadcasted_iota(jnp.int32, key_ref.shape, 1)
    key = key_lane
    shared = HEAD_PAD // LANE_GROUP
    for base in range(0, blocks, shared):
        position = jnp.zeros((rows, HEAD_PAD), jnp.int32)
        for g in range(shared):
            j = base + g
            first = owners_ref[device, j] * rows
            key = jnp.where(key_lane // rows == j, first + key_lane - j * rows, key)
            token = first + sub
            begin, end = jnp.zeros_like(token), jnp.zeros_like(token)
            start = jnp.int32(0)
            for s in range(lens_ref.shape[0]):
                inside = (token >= start) & (token < start + lens_ref[s])
                begin = jnp.where(inside, start, begin)
                end = jnp.where(inside, start + sinks_ref[s], end)
                start = start + lens_ref[s]
            info_ref[j * rows : (j + 1) * rows, :] = jnp.where(
                lane == 0, token, jnp.where(lane == 1, begin, end)
            )
            position = jnp.where(lane // LANE_GROUP == g, token - begin, position)
        waves = jnp.cos(position.astype(jnp.float32) * inverse_ref[...] - phase_ref[...])
        for g in range(shared):
            at = slice((base + g) * rows, (base + g + 1) * rows)
            here = pltpu.roll(waves, (HEAD_PAD - g * LANE_GROUP) % HEAD_PAD, 1)
            later = pltpu.roll(waves, (HEAD_PAD - g * LANE_GROUP + half_rot) % HEAD_PAD, 1)
            before = pltpu.roll(waves, (2 * HEAD_PAD - g * LANE_GROUP - half_rot) % HEAD_PAD, 1)
            cosine = jnp.where(lane < half_rot, here, later)
            cos_ref[at, :] = jnp.where(lane < ROTARY, cosine, 1.0)
            sine = jnp.where(lane < half_rot, -before, here)
            sin_ref[at, :] = jnp.where(lane < ROTARY, sine, 0.0)
    key_ref[...] = key


def tables(total, index, lens, sinks):
    half_rot = ROTARY // 2
    lane = np.arange(HEAD_PAD) % LANE_GROUP
    inverse = (10000.0 ** (-2.0 * (lane % half_rot) / ROTARY)).astype(np.float32)[None, :]
    phase = np.where(lane < half_rot, 0.0, np.pi / 2).astype(np.float32)[None, :]
    wide = (total, HEAD_PAD)
    return pl.pallas_call(
        tables_kernel,
        out_shape=(
            jax.ShapeDtypeStruct(wide, jnp.int32),
            jax.ShapeDtypeStruct((1, total), jnp.int32),
            jax.ShapeDtypeStruct(wide, jnp.float32),
            jax.ShapeDtypeStruct(wide, jnp.float32),
        ),
        in_specs=[SMEM] * 4 + [VMEM] * 2,
        out_specs=(VMEM,) * 4,
        compiler_params=pltpu.CompilerParams(vmem_limit_bytes=8 * MIB),
        name="tables",
    )(index, jnp.asarray(owner_table()), lens, sinks, jnp.asarray(inverse), jnp.asarray(phase))


def pages_kernel(index_ref, places_ref, table_ref, kv_ref, out_ref):
    pages = table_ref.shape[0]
    per_owner = pages // places_ref.shape[1]
    device, shift = index_ref[0], index_ref[1] * (pages // 2)
    for p in range(pages):
        place = places_ref[device, p // per_owner] * per_owner + p % per_owner
        row = pl.multiple_of(place * PAGE, PAGE)
        out_ref[lax.rem(table_ref[p] + shift, pages)] = kv_ref[pl.ds(row, PAGE), :]


def ordered_pages(index, page_table, kv):
    return pl.pallas_call(
        pages_kernel,
        out_shape=jax.ShapeDtypeStruct((page_table.shape[0], PAGE, kv.shape[1]), kv.dtype),
        in_specs=[SMEM] * 3 + [VMEM],
        out_specs=VMEM,
        compiler_params=pltpu.CompilerParams(vmem_limit_bytes=8 * MIB),
        name="ordered_pages",
    )(index, jnp.asarray(place_table()), page_table, kv)


def normalise(blocks, affine_ref, attn, mlp):
    rows = blocks[0].shape[0]
    feat = attn.shape[1]
    step = 512
    for b, block in enumerate(blocks):
        tail = block[:, feat:].astype(jnp.float32)
        average = tail[:, 0:1] + tail[:, 1:2] + tail[:, 2:3]
        scale = tail[:, 3:4] + tail[:, 4:5] + tail[:, 5:6]
        here = slice(b * rows, (b + 1) * rows)
        for c in range(0, feat, step):
            at = slice(c, c + step)
            scaled = (block[:, at].astype(jnp.float32) - average) * scale
            attn[here, at] = (scaled * affine_ref[0:1, at] + affine_ref[2:3, at]).astype(jnp.bfloat16)
            mlp[here, at] = (scaled * affine_ref[1:2, at] + affine_ref[3:4, at]).astype(jnp.bfloat16)


def project_kernel(count, outs, first_call, index_ref, affine_ref, wq_ref, wk_ref, wv_ref, wu_ref, *refs):
    blocks, refs = refs[:count], refs[count:]
    mine_ref, refs = refs[0], refs[1:]
    sent_refs, refs = refs[: len(outs)], refs[len(outs) :]
    hidden = wu_ref.shape[1]
    width = 384
    tiles = hidden // width
    copies = []
    if first_call:
        held, (attn, mlp, sems) = refs[:4], refs[4:]
        copies = [
            pltpu.make_async_copy(src, dst, sems.at[i])
            for i, (src, dst) in enumerate(zip((wq_ref, wk_ref, wv_ref), held))
        ]
        for t in range(tiles):
            at = slice(t * width, (t + 1) * width)
            copies.append(pltpu.make_async_copy(wu_ref.at[:, at], held[3].at[:, at], sems.at[3 + t]))
        for copy in copies:
            copy.start()
        wq_ref, wk_ref, wv_ref, wu_ref = held
    else:
        attn, mlp = refs
    rows = 2 * blocks[0].shape[0]
    half = wq_ref.shape[1] // 2
    normalise(blocks, affine_ref, attn, mlp)
    low, high = [], []
    for i, weight in enumerate((wq_ref, wk_ref, wv_ref)):
        if first_call:
            copies[i].wait()
        part = jnp.dot(attn[...], weight[...], preferred_element_type=jnp.float32)
        low.append(part[:, :half])
        high.append(part[:, half:])
    low = jnp.concatenate(low, axis=1).astype(jnp.bfloat16)
    high = jnp.concatenate(high, axis=1).astype(jnp.bfloat16)
    first = index_ref[1] == 0
    mine_ref[...] = jnp.where(first, low, high)
    send = jnp.where(first, high, low)
    send = [send[p * rows : (p + 1) * rows] for p in range(count // 2)]
    gap = -(3 * half * len(send)) % 128
    if gap:
        send.append(jnp.zeros((rows, gap), jnp.bfloat16))
    send = jnp.concatenate(send, axis=1)
    for ref, items in zip(sent_refs, outs):
        if items[-1] == "q":
            ref[:, hidden * (len(items) - 1) :] = send
    for t in range(tiles):
        if first_call:
            copies[3 + t].wait()
        at = slice(t * width, (t + 1) * width)
        part = jnp.dot(mlp[...], wu_ref[:, at], preferred_element_type=jnp.float32)
        part = part.astype(jnp.bfloat16)
        for ref, items in zip(sent_refs, outs):
            for i, item in enumerate(items):
                if item != "q":
                    begin = i * hidden + t * width
                    ref[:, begin : begin + width] = part[item * rows : (item + 1) * rows]


def project(n, affine, weights, blocks, outs, first_call=False):
    count = len(blocks)
    rows = 2 * blocks[0].shape[0]
    feat, cols = weights[0].shape
    hidden = weights[3].shape[1]
    sent = 3 * cols // 2 * (count // 2)
    sent += -sent % 128
    shapes = [jax.ShapeDtypeStruct((rows * count // 2, 3 * cols // 2), jnp.bfloat16)]
    for items in outs:
        width = sum(sent if item == "q" else hidden for item in items)
        shapes.append(jax.ShapeDtypeStruct((rows, width), jnp.bfloat16))
    scratch = [pltpu.VMEM((rows * count // 2, feat), jnp.bfloat16)] * 2
    if first_call:
        shapes += [jax.ShapeDtypeStruct(w.shape, w.dtype) for w in weights]
        scratch.append(pltpu.SemaphoreType.DMA((3 + hidden // 384,)))
    return pl.pallas_call(
        functools.partial(project_kernel, count, outs, first_call),
        out_shape=tuple(shapes),
        in_specs=[SMEM, VMEM] + [HBM if first_call else VMEM] * 4 + [VMEM] * count,
        out_specs=(VMEM,) * len(shapes),
        scratch_shapes=scratch,
        compiler_params=pltpu.CompilerParams(vmem_limit_bytes=(46 if first_call else 9) * MIB),
        name="project",
    )(n, affine, *weights, *blocks)


def attend_kernel(count, span, offsets, index_ref, bias_ref, cos_ref, sin_ref, query_ref, key_ref, *refs):
    mine, got = refs[:count], refs[count : 2 * count]
    att_ref, kv_ref, queries, keys, values = refs[2 * count :]
    heads = queries.shape[0]
    half = kv_ref.shape[1] // 2
    total = kv_ref.shape[0]
    half_rot = ROTARY // 2
    bias = jnp.where(index_ref[1] == 0, bias_ref[:, :half], bias_ref[:, half:])
    offset = 0
    for g in range(count):
        rows = mine[g].shape[0]
        at = slice(offset, offset + rows)
        offset += rows
        pieces = []
        for p in range(rows // got[g].shape[0]):
            begin = offsets[g] + 3 * half * p
            pieces.append(got[g][:, begin : begin + 3 * half])
        sent = jnp.concatenate(pieces, axis=0)
        summed = mine[g][...].astype(jnp.float32) + sent.astype(jnp.float32)
        cosine, sine = cos_ref[at, :], sin_ref[at, :]
        lane = lax.broadcasted_iota(jnp.int32, (rows, HEAD_PAD), 1)
        pad = jnp.zeros((rows, HEAD_PAD - HEAD_DIM), jnp.float32)
        for kind in range(3):
            kept = []
            for h in range(heads):
                begin = kind * half + h * HEAD_DIM
                u = summed[:, begin : begin + HEAD_DIM]
                u = u + bias[kind : kind + 1, h * HEAD_DIM : (h + 1) * HEAD_DIM]
                u = jnp.concatenate([u, pad], axis=1)
                if kind < 2:
                    other = jnp.where(
                        lane < half_rot,
                        pltpu.roll(u, HEAD_PAD - half_rot, 1),
                        pltpu.roll(u, half_rot, 1),
                    )
                    u = u * cosine + other * sine
                (queries, keys, values)[kind][h, at, :] = u.astype(jnp.bfloat16)
                kept.append(u[:, :HEAD_DIM])
            if kind > 0:
                kv_ref[at, (kind - 1) * half : kind * half] = jnp.concatenate(kept, axis=1).astype(
                    jnp.bfloat16
                )
    tile = 256
    for start in range(0, total, tile):
        at = slice(start, start + tile)
        info = query_ref[at, :]
        token, begin, end = info[:, 0:1], info[:, 1:2], info[:, 2:3]
        key_token = key_ref[...]
        near = key_token > token - span
        allowed = (key_token >= begin) & (key_token <= token) & (near | (key_token < end))
        outs = []
        for h in range(heads):
            scores = lax.dot_general(
                queries[h, at, :],
                keys[h],
                (((1,), (1,)), ((), ())),
                preferred_element_type=jnp.float32,
            ) * (1.0 / HEAD_DIM**0.5)
            masked = jnp.where(allowed, scores, -1e30)
            weights = jnp.exp(masked - jnp.max(masked, axis=1, keepdims=True))
            probs = weights / jnp.sum(weights, axis=1, keepdims=True)
            out = jnp.dot(probs.astype(jnp.bfloat16), values[h], preferred_element_type=jnp.float32)
            outs.append(out[:, :HEAD_DIM])
        side = start // (total // 2)
        att_ref[start % (total // 2) : start % (total // 2) + tile, side * half : (side + 1) * half] = (
            jnp.concatenate(outs, axis=1).astype(jnp.bfloat16)
        )


def attend(span, offsets, n, bias, cosine, sine, query_info, key_token, mine, got):
    count = len(mine)
    total = cosine.shape[0]
    half = mine[0].shape[1] // 3
    heads = half // HEAD_DIM
    scratch = pltpu.VMEM((heads, total, HEAD_PAD), jnp.bfloat16)
    return pl.pallas_call(
        functools.partial(attend_kernel, count, span, offsets),
        out_shape=(
            jax.ShapeDtypeStruct((total // 2, 2 * half), jnp.bfloat16),
            jax.ShapeDtypeStruct((total, 2 * half), jnp.bfloat16),
        ),
        in_specs=[SMEM] + [VMEM] * (5 + 2 * count),
        out_specs=(VMEM, VMEM),
        scratch_shapes=[scratch, scratch, scratch],
        compiler_params=pltpu.CompilerParams(vmem_limit_bytes=10 * MIB),
        name="attend",
    )(n, bias, cosine, sine, query_info, key_token, *mine, *got)


def gelu(u):
    return u * (1.0 + lax.erf(u * (0.5**0.5))) * 0.5


def down_kernel(count, bias_ref, wd_ref, *refs):
    mine, got = refs[:count], refs[count : 2 * count]
    out_ref, units = refs[2 * count :]
    rows = mine[0].shape[0]
    step = 384
    for i in range(count):
        for c in range(0, units.shape[1], step):
            at = slice(c, c + step)
            u = mine[i][:, at].astype(jnp.float32) + got[i][:, at].astype(jnp.float32)
            u = gelu(u + bias_ref[:, at])
            units[i * rows : (i + 1) * rows, at] = u.astype(jnp.bfloat16)
    width = 512
    for c in range(0, wd_ref.shape[1], width):
        at = slice(c, c + width)
        out = jnp.dot(units[...], wd_ref[:, at], preferred_element_type=jnp.float32)
        out_ref[:, at] = out.astype(jnp.bfloat16)


def down(bias, mine, got, wd):
    count = len(mine)
    rows, hidden = mine[0].shape[0], wd.shape[0]
    return pl.pallas_call(
        functools.partial(down_kernel, count),
        out_shape=jax.ShapeDtypeStruct((count * rows, wd.shape[1]), jnp.bfloat16),
        in_specs=[VMEM] * (2 + 2 * count),
        out_specs=VMEM,
        scratch_shapes=[pltpu.VMEM((count * rows, hidden), jnp.bfloat16)],
        compiler_params=pltpu.CompilerParams(vmem_limit_bytes=6 * MIB),
        name="down",
    )(bias, wd, *mine, *got)


def attended_rows(ref, offset, rows):
    height, half = ref.shape[0], ref.shape[1] // 2
    side = offset // height
    return ref[offset % height : offset % height + rows, side * half : (side + 1) * half]


def mix_kernel(offsets, index_ref, down_ref, att_ref, other_ref, wo_ref, own_ref, sib_ref):
    half = att_ref.shape[1] // 2
    rows = own_ref.shape[0] // len(offsets)
    n = index_ref[1]
    here = pl.ds(pl.multiple_of(n * half, 16), half)
    there = pl.ds(pl.multiple_of((1 - n) * half, 16), half)
    mine = jnp.concatenate([attended_rows(att_ref, o, 2 * rows) for o in offsets], axis=0)
    other = jnp.concatenate([attended_rows(other_ref, o, 2 * rows) for o in offsets], axis=0)
    width = 512
    for c in range(0, own_ref.shape[1], width):
        at = slice(c, c + width)
        out = down_ref[:, at].astype(jnp.float32)
        out += jnp.dot(mine, wo_ref[here, at], preferred_element_type=jnp.float32)
        out += jnp.dot(other, wo_ref[there, at], preferred_element_type=jnp.float32)
        out = out.astype(jnp.bfloat16)
        for i in range(len(offsets)):
            own_ref[i * rows : (i + 1) * rows, at] = out[2 * i * rows : (2 * i + 1) * rows]
            sib_ref[i * rows : (i + 1) * rows, at] = out[(2 * i + 1) * rows : (2 * i + 2) * rows]


def mix(n, offsets, partial_down, att, other, wo):
    rows, feat = partial_down.shape
    shape = jax.ShapeDtypeStruct((rows // 2, feat), jnp.bfloat16)
    return pl.pallas_call(
        functools.partial(mix_kernel, offsets),
        out_shape=(shape, shape),
        in_specs=[SMEM] + [VMEM] * 4,
        out_specs=(VMEM, VMEM),
        compiler_params=pltpu.CompilerParams(vmem_limit_bytes=5 * MIB),
        name="mix",
    )(n, partial_down, att, other, wo)


def output_kernel(
    offset, column, index_ref, bias_ref, mine_ref, got_ref, att_ref, other_ref, wo_ref, wd_ref, own_ref, sib_ref, units
):
    rows = mine_ref.shape[0]
    half = att_ref.shape[1] // 2
    own_rows = own_ref.shape[0]
    step = 384
    for c in range(0, units.shape[1], step):
        at = slice(c, c + step)
        there = slice(column + c, column + c + step)
        u = mine_ref[:, there].astype(jnp.float32) + got_ref[:, there].astype(jnp.float32)
        units[:, at] = gelu(u + bias_ref[:, at]).astype(jnp.bfloat16)
    n = index_ref[1]
    here = pl.ds(pl.multiple_of(n * half, 16), half)
    there = pl.ds(pl.multiple_of((1 - n) * half, 16), half)
    mine = attended_rows(att_ref, offset, rows)
    other = attended_rows(other_ref, offset, rows)
    width = 512
    for c in range(0, wd_ref.shape[1], width):
        at = slice(c, c + width)
        out = jnp.dot(units[...], wd_ref[:, at], preferred_element_type=jnp.float32)
        out += jnp.dot(mine, wo_ref[here, at], preferred_element_type=jnp.float32)
        out += jnp.dot(other, wo_ref[there, at], preferred_element_type=jnp.float32)
        out = out.astype(jnp.bfloat16)
        own_ref[:, at] = out[:own_rows]
        sib_ref[:, at] = out[own_rows:]


def output(n, offset, column, bias, mine, got, att, other, wo, wd):
    rows, hidden = mine.shape[0], wd.shape[0]
    shape = jax.ShapeDtypeStruct((rows // 2, wd.shape[1]), jnp.bfloat16)
    return pl.pallas_call(
        functools.partial(output_kernel, offset, column),
        out_shape=(shape, shape),
        in_specs=[SMEM] + [VMEM] * 7,
        out_specs=(VMEM, VMEM),
        scratch_shapes=[pltpu.VMEM((rows, hidden), jnp.bfloat16)],
        compiler_params=pltpu.CompilerParams(vmem_limit_bytes=5 * MIB),
        name="output",
    )(n, bias, mine, got, att, other, wo, wd)


def after(*values):
    return lax.optimization_barrier(values)


def local_ring(
    hidden_in,
    w_query,
    w_key,
    w_value,
    qkv_bias,
    w_up,
    up_bias,
    w_attn_out,
    w_down,
    out_bias,
    norm_gain,
    norm_bias,
    seq_lens,
    sink_count,
    page_table,
):
    device = lax.axis_index("wide").astype(jnp.int32).reshape(1)
    n = lax.axis_index("narrow").astype(jnp.int32)
    n_arg = n.reshape(1)
    rows, feat = hidden_in.shape
    total_tokens = rows * lax.axis_size("wide")
    half = w_query.shape[1] // 2

    fwd_pairs, bwd_pairs, swap_pairs = [], [], []
    for p in range(CHIPS):
        here, next_chip = CHIP_RING[p], CHIP_RING[(p + 1) % CHIPS]
        fwd_pairs += [(2 * here, 2 * next_chip), (2 * next_chip + 1, 2 * here + 1)]
        bwd_pairs += [(2 * next_chip, 2 * here), (2 * here + 1, 2 * next_chip + 1)]
        swap_pairs += [(2 * here, 2 * here + 1), (2 * here + 1, 2 * here)]
    fwd = lambda v: lax.ppermute(v, "wide", fwd_pairs)
    bwd = lambda v: lax.ppermute(v, "wide", bwd_pairs)
    swap = lambda v: lax.ppermute(v, "wide", swap_pairs)
    cross = lambda v: lax.ppermute(v, "narrow", [(0, 1), (1, 0)])

    first_side, n_arg = after(n == 0, n_arg)
    sums, index = pl.pallas_call(
        sums_kernel,
        out_shape=(
            jax.ShapeDtypeStruct((rows, STAT), jnp.float32),
            jax.ShapeDtypeStruct((2,), jnp.int32),
        ),
        in_specs=[SMEM, SMEM, VMEM],
        out_specs=(VMEM, SMEM),
        compiler_params=pltpu.CompilerParams(vmem_limit_bytes=8 * MIB),
        name="row_sums",
    )(device, n_arg, hidden_in)
    first_block, affine = pl.pallas_call(
        block_kernel,
        out_shape=(
            jax.ShapeDtypeStruct((rows, feat + STAT), jnp.bfloat16),
            jax.ShapeDtypeStruct((4, feat), jnp.float32),
        ),
        in_specs=[VMEM] * 5,
        out_specs=(VMEM, VMEM),
        compiler_params=pltpu.CompilerParams(vmem_limit_bytes=8 * MIB),
        name="first_block",
    )(hidden_in, norm_gain, norm_bias, sums, cross(sums))

    up_row = up_bias[None, :]

    def add(*terms):
        return sum(t.astype(jnp.float32) for t in terms).astype(jnp.bfloat16)

    def finish(name, u, v, column=0):
        return output(
            index, PAIRS.index(name) * 2 * rows, column, up_row, u, v, att, other, w_attn_out, w_down
        )

    def pair(halves, *running):
        return add(halves[0], swap(halves[1]), *running)

    per_device = page_table.shape[0] // 2
    hidden = w_up.shape[1]
    o0 = first_block
    f1, b1, s0 = fwd(o0), bwd(o0), swap(o0)
    kept0, send0, *weights = project(
        index, affine, (w_query, w_key, w_value, w_up), [o0, s0], ((0, "q"),), True
    )
    f1, b1, send0, kept0 = after(f1, b1, send0, kept0)
    got0 = cross(send0)
    f2, b2 = fwd(f1), bwd(b1)
    kept1, send1, u_f1 = project(
        index, affine, weights, [f1, swap(f1), b1, swap(b1)], ((1, "q"), (0,))
    )
    f2, b2, got0, send1, u_f1 = after(f2, b2, got0, send1, u_f1)
    got1 = cross(send1)
    f3, b3 = fwd(f2), bwd(b2)
    kept2, send2, u_b2 = project(
        index, affine, weights, [f2, swap(f2), b2, swap(b2)], ((0, "q"), (1,))
    )
    f3, b3, got1, send2, u_b2, late_index = after(f3, b3, got1, send2, u_b2, index)
    got2 = cross(send2)
    f4, g3, h3 = fwd(f3), swap(f3), swap(b3)
    query_info, key_token, cosine, sine = tables(total_tokens, late_index, seq_lens, sink_count)
    f3, b3, f4, g3, h3, got2, u_b2, query_info, key_token, cosine, sine = after(
        f3, b3, f4, g3, h3, got2, u_b2, query_info, key_token, cosine, sine
    )
    v_b2 = cross(u_b2)
    kept3, send3, u_f4, u_mid = project(
        index, affine, weights, [f3, g3, b3, h3, f4, swap(f4)], (("q",), (2,), (0, 1))
    )
    v_b2, send3, u_f4, u_mid = after(v_b2, send3, u_f4, u_mid)
    got3 = cross(send3)
    early = down(up_row, [send0, send1, send2], [got0, got1, got2], w_down)
    got3, early, u_f4 = after(got3, early, u_f4)
    v_f4 = cross(u_f4)
    att, kv = attend(
        total_tokens // 16, (hidden, hidden, hidden, 0), index, qkv_bias, cosine, sine,
        query_info, key_token, [kept0, kept1, kept2, kept3], [got0, got1, got2, got3],
    )
    v_f4, att, u_mid = after(v_f4, att, u_mid)
    other = cross(att)
    other, u_mid, u_b2, u_f1 = after(other, u_mid, u_b2, u_f1)
    v_mid = cross(u_mid)
    y_f4 = finish("f4", u_f4, v_f4)
    r_b = bwd(pair(y_f4))
    y_b2 = finish("b2", u_b2, v_b2)
    m_own, m_sib = mix(
        index, tuple(PAIRS.index(p) * 2 * rows for p in ("o0", "b1", "f2")), early, att, other,
        w_attn_out,
    )
    v_mid, r_b, y_b2, m_own, m_sib, u_f1, kv = after(v_mid, r_b, y_b2, m_own, m_sib, u_f1, kv)
    v_f1 = cross(u_f1)
    y_f3 = finish("f3", u_mid, v_mid)
    r_b = bwd(pair(y_f3, r_b))
    y_b3 = finish("b3", u_mid, v_mid, hidden)
    r_f = fwd(pair(y_b3))
    m_got, p_b2 = swap(m_sib), pair(y_b2)
    paged = ordered_pages(index, page_table, kv)
    v_f1, r_b, r_f, m_got, p_b2, paged = after(v_f1, r_b, r_f, m_got, p_b2, paged)
    cache_mine, cache_got = paged[:per_device], cross(paged[per_device:])
    r_b = bwd(add(r_b, m_own[2 * rows :], m_got[2 * rows :]))
    r_f = fwd(add(r_f, p_b2))
    y_f1 = finish("f1", u_f1, v_f1)
    r_f, r_b, y_f1, cache_mine, cache_got = after(r_f, r_b, y_f1, cache_mine, cache_got)
    r_b = bwd(pair(y_f1, r_b))
    r_f = fwd(add(r_f, m_own[rows : 2 * rows], m_got[rows : 2 * rows]))
    summed = (
        r_b.astype(jnp.float32)
        + r_f.astype(jnp.float32)
        + m_own[:rows].astype(jnp.float32)
        + m_got[:rows].astype(jnp.float32)
    )
    hidden_out = (hidden_in.astype(jnp.float32) + summed + out_bias).astype(jnp.bfloat16)
    left = jnp.where(first_side, cache_mine, cache_got)
    right = jnp.where(first_side, cache_got, cache_mine)
    paged_cache = jnp.stack(
        [
            jnp.concatenate([left[..., :half], right[..., :half]], axis=-1),
            jnp.concatenate([left[..., half:], right[..., half:]], axis=-1),
        ]
    )
    return (hidden_out, paged_cache)


def solution(mesh):
    in_specs = (
        P("wide", "narrow"),
        P("narrow", "wide"),
        P("narrow", "wide"),
        P("narrow", "wide"),
        P(None, "wide"),
        P("narrow", "wide"),
        P("wide"),
        P("wide", "narrow"),
        P("wide", "narrow"),
        P("narrow"),
        P(None, "narrow"),
        P(None, "narrow"),
        P(),
        P(),
        P(),
    )
    out_specs = (P("wide", "narrow"), P(None, "narrow", None, "wide"))
    ringed = mesh.shape["wide"] == 2 * CHIPS and mesh.shape["narrow"] == 2
    local = local_ring if ringed else local_generic
    return jax.shard_map(local, mesh=mesh, in_specs=in_specs, out_specs=out_specs, check_vma=False)
```

```python
import functools

import jax
import jax.numpy as jnp
import numpy as np
from jax import lax
from jax.experimental import pallas as pl
from jax.experimental.pallas import tpu as pltpu
from jax.sharding import PartitionSpec as P

D = 6144
HEAD_DIM = 96
ROTARY = 24
PAGE = 16


def segment_info(token_index, seq_lens, sink_count):
    seq_ends = jnp.cumsum(seq_lens)
    seq_starts = seq_ends - seq_lens
    inside = (token_index[:, None] >= seq_starts[None, :]) & (
        token_index[:, None] < seq_ends[None, :]
    )
    member = inside.astype(jnp.int32)
    seq_number = jnp.arange(seq_lens.shape[0], dtype=jnp.int32)
    segment = jnp.sum(member * seq_number[None, :], axis=1)
    position = token_index - jnp.sum(member * seq_starts[None, :], axis=1)
    sink_limit = jnp.sum(member * sink_count[None, :], axis=1)
    return (segment, position, sink_limit)


def rotate(values, position):
    half_rot = ROTARY // 2
    freq_index = jnp.arange(half_rot, dtype=jnp.float32)
    inverse = jnp.power(jnp.float32(10000.0), -2.0 * freq_index / ROTARY)
    angles = position.astype(jnp.float32)[:, None] * inverse[None, :]
    cosine = jnp.cos(angles)[:, None, :]
    sine_part = jnp.sin(angles)[:, None, :]
    first_half = values[..., :half_rot]
    second_half = values[..., half_rot:ROTARY]
    return jnp.concatenate(
        [
            first_half * cosine - second_half * sine_part,
            second_half * cosine + first_half * sine_part,
            values[..., ROTARY:],
        ],
        axis=-1,
    )


def local_generic(
    hidden_in,
    w_query,
    w_key,
    w_value,
    qkv_bias,
    w_up,
    up_bias,
    w_attn_out,
    w_down,
    out_bias,
    norm_gain,
    norm_bias,
    seq_lens,
    sink_count,
    page_table,
):
    wide_count = lax.axis_size("wide")
    narrow_count = lax.axis_size("narrow")
    narrow_index = lax.axis_index("narrow")
    tok_local, feat_local = hidden_in.shape
    sub_rows = tok_local // narrow_count
    total_tokens = tok_local * wide_count
    query_rows = wide_count * sub_rows
    head_cols = w_query.shape[1]
    heads_local = head_cols // HEAD_DIM
    as_float = hidden_in.astype(jnp.float32)
    partial_sum = jnp.sum(as_float, axis=1)
    partial_square = jnp.sum(as_float * as_float, axis=1)
    total_sum, total_square = lax.psum((partial_sum, partial_square), "narrow")
    average = total_sum / D
    variance = total_square / D - average * average
    scaled = (as_float - average[:, None]) * lax.rsqrt(variance + 1e-05)[:, None]
    attn_normed = (scaled * norm_gain[0] + norm_bias[0]).astype(jnp.bfloat16)
    mlp_normed = (scaled * norm_gain[1] + norm_bias[1]).astype(jnp.bfloat16)
    stacked = jnp.stack([attn_normed, mlp_normed]).reshape(2, narrow_count, sub_rows, feat_local)
    gathered = lax.all_gather(stacked, "wide", axis=2, tiled=True).reshape(
        2, total_tokens, feat_local
    )
    local_order = jnp.arange(query_rows, dtype=jnp.int32)
    local_tokens = (
        local_order // sub_rows * tok_local + narrow_index * sub_rows + local_order % sub_rows
    )
    local_seg, local_pos, local_sink = segment_info(local_tokens, seq_lens, sink_count)
    all_order = jnp.arange(total_tokens, dtype=jnp.int32)
    all_tokens = (
        all_order % query_rows // sub_rows * tok_local
        + all_order // query_rows * sub_rows
        + all_order % sub_rows
    )
    all_seg, all_pos, all_sink = segment_info(all_tokens, seq_lens, sink_count)
    qkv_weight = jnp.concatenate([w_query, w_key, w_value], axis=1)
    attn_part = gathered[0]
    mlp_part = gathered[1]
    summed = lax.psum_scatter(
        jnp.concatenate(
            [
                jnp.dot(attn_part, qkv_weight, preferred_element_type=jnp.float32),
                jnp.dot(mlp_part, w_up, preferred_element_type=jnp.float32),
            ],
            axis=1,
        ).astype(jnp.bfloat16),
        "narrow",
        scatter_dimension=0,
        tiled=True,
    ).astype(jnp.float32)
    query_sum = summed[:, :head_cols]
    key_sum = summed[:, head_cols : 2 * head_cols]
    value_sum = summed[:, 2 * head_cols : 3 * head_cols]
    unit_sum = summed[:, 3 * head_cols :]
    keys_local = (
        rotate((key_sum + qkv_bias[1]).reshape(query_rows, heads_local, HEAD_DIM), local_pos)
        .astype(jnp.bfloat16)
        .reshape(query_rows, head_cols)
    )
    values_local = (value_sum + qkv_bias[2]).astype(jnp.bfloat16)
    all_keys, all_values = (
        lax.all_gather(keys_local, "narrow", axis=0, tiled=True),
        lax.all_gather(values_local, "narrow", axis=0, tiled=True),
    )
    queries = rotate(
        (query_sum + qkv_bias[0]).reshape(query_rows, heads_local, HEAD_DIM), local_pos
    ).astype(jnp.bfloat16)
    hidden_units = jax.nn.gelu(unit_sum + up_bias, approximate=False).astype(jnp.bfloat16)
    window_span = total_tokens // 16
    allowed = (local_seg[:, None] == all_seg[None, :]) & (all_pos[None, :] <= local_pos[:, None])
    allowed = allowed & (
        (local_pos[:, None] - all_pos[None, :] < window_span)
        | (all_pos[None, :] < local_sink[:, None])
    )
    key_heads = all_keys.reshape(total_tokens, heads_local, HEAD_DIM)
    value_heads = all_values.reshape(total_tokens, heads_local, HEAD_DIM)
    scores = jnp.einsum("qhd,khd->hqk", queries, key_heads, preferred_element_type=jnp.float32) * (
        1.0 / HEAD_DIM**0.5
    )
    masked = jnp.where(allowed[None], scores, jnp.float32(-1e30))
    top_score = jnp.max(masked, axis=2, keepdims=True)
    weights = jnp.exp(masked - top_score)
    probs = (weights / jnp.sum(weights, axis=2, keepdims=True)).astype(jnp.bfloat16)
    attended = (
        jnp.einsum("hqk,khd->qhd", probs, value_heads, preferred_element_type=jnp.float32)
        .astype(jnp.bfloat16)
        .reshape(query_rows, head_cols)
    )
    full_out, full_down = (
        lax.all_gather(w_attn_out, "narrow", axis=1, tiled=True),
        lax.all_gather(w_down, "narrow", axis=1, tiled=True),
    )
    attn_part = attended
    own_rows = lax.psum_scatter(
        (
            jnp.dot(attn_part, full_out, preferred_element_type=jnp.float32)
            + jnp.dot(hidden_units, full_down, preferred_element_type=jnp.float32)
        ).astype(jnp.bfloat16),
        "wide",
        scatter_dimension=0,
        tiled=True,
    ).astype(jnp.float32)
    combined = lax.all_to_all(
        own_rows.astype(jnp.bfloat16), "narrow", split_axis=1, concat_axis=0, tiled=True
    ).astype(own_rows.dtype)
    hidden_out = (as_float + combined + out_bias).astype(jnp.bfloat16)
    pages_local = page_table.shape[0] // narrow_count
    slot_ids = narrow_index * pages_local + jnp.arange(pages_local, dtype=jnp.int32)
    matches = (page_table[None, :] == slot_ids[:, None]).astype(jnp.int32)
    source_page = jnp.sum(
        matches * jnp.arange(page_table.shape[0], dtype=jnp.int32)[None, :], axis=1
    )
    token_ids = (source_page[:, None] * PAGE + jnp.arange(PAGE, dtype=jnp.int32)[None, :]).reshape(
        -1
    )
    gather_rows = (
        token_ids % tok_local // sub_rows * query_rows
        + token_ids // tok_local * sub_rows
        + token_ids % sub_rows
    )
    cache_keys = jnp.take(all_keys, gather_rows, axis=0).reshape(pages_local, PAGE, head_cols)
    cache_values = jnp.take(all_values, gather_rows, axis=0).reshape(pages_local, PAGE, head_cols)
    paged_cache = jnp.stack([cache_keys, cache_values])
    return (hidden_out, paged_cache)


CHIP_RING = (0, 2, 4, 6, 7, 5, 3, 1)
CHIPS = len(CHIP_RING)
PAIRS = ("o0", "f1", "b1", "f2", "b2", "f3", "b3", "f4")
STAT = 128
HEAD_PAD = 128
LANE_GROUP = 32
MIB = 1 << 20
VMEM = pl.BlockSpec(memory_space=pltpu.VMEM)
HBM = pl.BlockSpec(memory_space=pltpu.HBM)
SMEM = pl.BlockSpec(memory_space=pltpu.SMEM)


def owner_table():
    table = np.zeros((2 * CHIPS, 2 * CHIPS), np.int32)
    for place, chip in enumerate(CHIP_RING):
        for core in range(2):
            order = []
            for pair in PAIRS:
                shift = (-1 if pair[0] == "f" else 1) * int(pair[1]) * (1 - 2 * core)
                order.append(CHIP_RING[(place + shift) % CHIPS] * 2 + core)
                order.append(CHIP_RING[(place - shift) % CHIPS] * 2 + 1 - core)
            table[2 * chip + core] = order
    return table


def place_table():
    owners = owner_table()
    table = np.zeros_like(owners)
    for device in range(owners.shape[0]):
        table[device, owners[device]] = np.arange(owners.shape[1])
    return table


def sums_kernel(device_ref, n_ref, x_ref, out_ref, index_ref):
    x = x_ref[...].astype(jnp.float32)
    first = jnp.sum(x, axis=1, keepdims=True)
    second = jnp.sum(x * x, axis=1, keepdims=True)
    lane = lax.broadcasted_iota(jnp.int32, out_ref.shape, 1)
    out_ref[...] = jnp.where(lane == 0, first, jnp.where(lane == 1, second, 0.0))
    index_ref[0] = device_ref[0]
    index_ref[1] = n_ref[0]


def block_kernel(x_ref, gain_ref, bias_ref, here_ref, there_ref, out_ref, affine_ref):
    feat = x_ref.shape[1]
    total = here_ref[...] + there_ref[...]
    average = total[:, 0:1] / D
    variance = total[:, 1:2] / D - average * average
    scale = lax.rsqrt(variance + 1e-05)
    lane = lax.broadcasted_iota(jnp.int32, (x_ref.shape[0], STAT), 1)
    tail = jnp.zeros((x_ref.shape[0], STAT), jnp.float32)
    for start, value in ((0, average), (3, scale)):
        for term in range(3):
            piece = value.astype(jnp.bfloat16).astype(jnp.float32)
            tail = jnp.where(lane == start + term, piece, tail)
            value = value - piece
    out_ref[:, :feat] = x_ref[...]
    out_ref[:, feat:] = tail.astype(jnp.bfloat16)
    affine_ref[0:2, :] = gain_ref[...]
    affine_ref[2:4, :] = bias_ref[...]


def tables_kernel(index_ref, owners_ref, lens_ref, sinks_ref, inverse_ref, phase_ref, info_ref, key_ref, cos_ref, sin_ref):
    device = index_ref[0]
    blocks = owners_ref.shape[1]
    rows = info_ref.shape[0] // blocks
    half_rot = ROTARY // 2
    lane = lax.broadcasted_iota(jnp.int32, (rows, HEAD_PAD), 1)
    sub = lax.broadcasted_iota(jnp.int32, (rows, HEAD_PAD), 0)
    key_lane = lax.broadcasted_iota(jnp.int32, key_ref.shape, 1)
    key = key_lane
    shared = HEAD_PAD // LANE_GROUP
    for base in range(0, blocks, shared):
        position = jnp.zeros((rows, HEAD_PAD), jnp.int32)
        for g in range(shared):
            j = base + g
            first = owners_ref[device, j] * rows
            key = jnp.where(key_lane // rows == j, first + key_lane - j * rows, key)
            token = first + sub
            begin, end = jnp.zeros_like(token), jnp.zeros_like(token)
            start = jnp.int32(0)
            for s in range(lens_ref.shape[0]):
                inside = (token >= start) & (token < start + lens_ref[s])
                begin = jnp.where(inside, start, begin)
                end = jnp.where(inside, start + sinks_ref[s], end)
                start = start + lens_ref[s]
            info_ref[j * rows : (j + 1) * rows, :] = jnp.where(
                lane == 0, token, jnp.where(lane == 1, begin, end)
            )
            position = jnp.where(lane // LANE_GROUP == g, token - begin, position)
        waves = jnp.cos(position.astype(jnp.float32) * inverse_ref[...] - phase_ref[...])
        for g in range(shared):
            at = slice((base + g) * rows, (base + g + 1) * rows)
            here = pltpu.roll(waves, (HEAD_PAD - g * LANE_GROUP) % HEAD_PAD, 1)
            later = pltpu.roll(waves, (HEAD_PAD - g * LANE_GROUP + half_rot) % HEAD_PAD, 1)
            before = pltpu.roll(waves, (2 * HEAD_PAD - g * LANE_GROUP - half_rot) % HEAD_PAD, 1)
            cosine = jnp.where(lane < half_rot, here, later)
            cos_ref[at, :] = jnp.where(lane < ROTARY, cosine, 1.0)
            sine = jnp.where(lane < half_rot, -before, here)
            sin_ref[at, :] = jnp.where(lane < ROTARY, sine, 0.0)
    key_ref[...] = key


def tables(total, index, lens, sinks):
    half_rot = ROTARY // 2
    lane = np.arange(HEAD_PAD) % LANE_GROUP
    inverse = (10000.0 ** (-2.0 * (lane % half_rot) / ROTARY)).astype(np.float32)[None, :]
    phase = np.where(lane < half_rot, 0.0, np.pi / 2).astype(np.float32)[None, :]
    wide = (total, HEAD_PAD)
    return pl.pallas_call(
        tables_kernel,
        out_shape=(
            jax.ShapeDtypeStruct(wide, jnp.int32),
            jax.ShapeDtypeStruct((1, total), jnp.int32),
            jax.ShapeDtypeStruct(wide, jnp.float32),
            jax.ShapeDtypeStruct(wide, jnp.float32),
        ),
        in_specs=[SMEM] * 4 + [VMEM] * 2,
        out_specs=(VMEM,) * 4,
        compiler_params=pltpu.CompilerParams(vmem_limit_bytes=8 * MIB),
        name="tables",
    )(index, jnp.asarray(owner_table()), lens, sinks, jnp.asarray(inverse), jnp.asarray(phase))


def pages_kernel(index_ref, places_ref, table_ref, kv_ref, out_ref):
    pages = table_ref.shape[0]
    per_owner = pages // places_ref.shape[1]
    device, shift = index_ref[0], index_ref[1] * (pages // 2)
    for p in range(pages):
        place = places_ref[device, p // per_owner] * per_owner + p % per_owner
        row = pl.multiple_of(place * PAGE, PAGE)
        out_ref[lax.rem(table_ref[p] + shift, pages)] = kv_ref[pl.ds(row, PAGE), :]


def ordered_pages(index, page_table, kv):
    return pl.pallas_call(
        pages_kernel,
        out_shape=jax.ShapeDtypeStruct((page_table.shape[0], PAGE, kv.shape[1]), kv.dtype),
        in_specs=[SMEM] * 3 + [VMEM],
        out_specs=VMEM,
        compiler_params=pltpu.CompilerParams(vmem_limit_bytes=8 * MIB),
        name="ordered_pages",
    )(index, jnp.asarray(place_table()), page_table, kv)


def normalise(blocks, affine_ref, attn, mlp):
    rows = blocks[0].shape[0]
    feat = attn.shape[1]
    step = 512
    for b, block in enumerate(blocks):
        tail = block[:, feat:].astype(jnp.float32)
        average = tail[:, 0:1] + tail[:, 1:2] + tail[:, 2:3]
        scale = tail[:, 3:4] + tail[:, 4:5] + tail[:, 5:6]
        here = slice(b * rows, (b + 1) * rows)
        for c in range(0, feat, step):
            at = slice(c, c + step)
            scaled = (block[:, at].astype(jnp.float32) - average) * scale
            attn[here, at] = (scaled * affine_ref[0:1, at] + affine_ref[2:3, at]).astype(jnp.bfloat16)
            mlp[here, at] = (scaled * affine_ref[1:2, at] + affine_ref[3:4, at]).astype(jnp.bfloat16)


def project_kernel(count, outs, first_call, index_ref, affine_ref, wq_ref, wk_ref, wv_ref, wu_ref, *refs):
    blocks, refs = refs[:count], refs[count:]
    mine_ref, refs = refs[0], refs[1:]
    sent_refs, refs = refs[: len(outs)], refs[len(outs) :]
    hidden = wu_ref.shape[1]
    width = 384
    tiles = hidden // width
    copies = []
    if first_call:
        held, (attn, mlp, sems) = refs[:4], refs[4:]
        copies = [
            pltpu.make_async_copy(src, dst, sems.at[i])
            for i, (src, dst) in enumerate(zip((wq_ref, wk_ref, wv_ref), held))
        ]
        for t in range(tiles):
            at = slice(t * width, (t + 1) * width)
            copies.append(pltpu.make_async_copy(wu_ref.at[:, at], held[3].at[:, at], sems.at[3 + t]))
        for copy in copies:
            copy.start()
        wq_ref, wk_ref, wv_ref, wu_ref = held
    else:
        attn, mlp = refs
    rows = 2 * blocks[0].shape[0]
    half = wq_ref.shape[1] // 2
    normalise(blocks, affine_ref, attn, mlp)
    low, high = [], []
    for i, weight in enumerate((wq_ref, wk_ref, wv_ref)):
        if first_call:
            copies[i].wait()
        part = jnp.dot(attn[...], weight[...], preferred_element_type=jnp.float32)
        low.append(part[:, :half])
        high.append(part[:, half:])
    low = jnp.concatenate(low, axis=1).astype(jnp.bfloat16)
    high = jnp.concatenate(high, axis=1).astype(jnp.bfloat16)
    first = index_ref[1] == 0
    mine_ref[...] = jnp.where(first, low, high)
    send = jnp.where(first, high, low)
    send = [send[p * rows : (p + 1) * rows] for p in range(count // 2)]
    gap = -(3 * half * len(send)) % 128
    if gap:
        send.append(jnp.zeros((rows, gap), jnp.bfloat16))
    send = jnp.concatenate(send, axis=1)
    for ref, items in zip(sent_refs, outs):
        if items[-1] == "q":
            ref[:, hidden * (len(items) - 1) :] = send
    for t in range(tiles):
        if first_call:
            copies[3 + t].wait()
        at = slice(t * width, (t + 1) * width)
        part = jnp.dot(mlp[...], wu_ref[:, at], preferred_element_type=jnp.float32)
        part = part.astype(jnp.bfloat16)
        for ref, items in zip(sent_refs, outs):
            for i, item in enumerate(items):
                if item != "q":
                    begin = i * hidden + t * width
                    ref[:, begin : begin + width] = part[item * rows : (item + 1) * rows]


def project(n, affine, weights, blocks, outs, first_call=False):
    count = len(blocks)
    rows = 2 * blocks[0].shape[0]
    feat, cols = weights[0].shape
    hidden = weights[3].shape[1]
    sent = 3 * cols // 2 * (count // 2)
    sent += -sent % 128
    shapes = [jax.ShapeDtypeStruct((rows * count // 2, 3 * cols // 2), jnp.bfloat16)]
    for items in outs:
        width = sum(sent if item == "q" else hidden for item in items)
        shapes.append(jax.ShapeDtypeStruct((rows, width), jnp.bfloat16))
    scratch = [pltpu.VMEM((rows * count // 2, feat), jnp.bfloat16)] * 2
    if first_call:
        shapes += [jax.ShapeDtypeStruct(w.shape, w.dtype) for w in weights]
        scratch.append(pltpu.SemaphoreType.DMA((3 + hidden // 384,)))
    return pl.pallas_call(
        functools.partial(project_kernel, count, outs, first_call),
        out_shape=tuple(shapes),
        in_specs=[SMEM, VMEM] + [HBM if first_call else VMEM] * 4 + [VMEM] * count,
        out_specs=(VMEM,) * len(shapes),
        scratch_shapes=scratch,
        compiler_params=pltpu.CompilerParams(vmem_limit_bytes=(46 if first_call else 9) * MIB),
        name="project",
    )(n, affine, *weights, *blocks)


def attend_kernel(count, span, offsets, index_ref, bias_ref, cos_ref, sin_ref, query_ref, key_ref, *refs):
    mine, got = refs[:count], refs[count : 2 * count]
    att_ref, kv_ref, queries, keys, values = refs[2 * count :]
    heads = queries.shape[0]
    half = kv_ref.shape[1] // 2
    total = kv_ref.shape[0]
    half_rot = ROTARY // 2
    bias = jnp.where(index_ref[1] == 0, bias_ref[:, :half], bias_ref[:, half:])
    offset = 0
    for g in range(count):
        rows = mine[g].shape[0]
        at = slice(offset, offset + rows)
        offset += rows
        pieces = []
        for p in range(rows // got[g].shape[0]):
            begin = offsets[g] + 3 * half * p
            pieces.append(got[g][:, begin : begin + 3 * half])
        sent = jnp.concatenate(pieces, axis=0)
        summed = mine[g][...].astype(jnp.float32) + sent.astype(jnp.float32)
        cosine, sine = cos_ref[at, :], sin_ref[at, :]
        lane = lax.broadcasted_iota(jnp.int32, (rows, HEAD_PAD), 1)
        pad = jnp.zeros((rows, HEAD_PAD - HEAD_DIM), jnp.float32)
        for kind in range(3):
            kept = []
            for h in range(heads):
                begin = kind * half + h * HEAD_DIM
                u = summed[:, begin : begin + HEAD_DIM]
                u = u + bias[kind : kind + 1, h * HEAD_DIM : (h + 1) * HEAD_DIM]
                u = jnp.concatenate([u, pad], axis=1)
                if kind < 2:
                    other = jnp.where(
                        lane < half_rot,
                        pltpu.roll(u, HEAD_PAD - half_rot, 1),
                        pltpu.roll(u, half_rot, 1),
                    )
                    u = u * cosine + other * sine
                (queries, keys, values)[kind][h, at, :] = u.astype(jnp.bfloat16)
                kept.append(u[:, :HEAD_DIM])
            if kind > 0:
                kv_ref[at, (kind - 1) * half : kind * half] = jnp.concatenate(kept, axis=1).astype(
                    jnp.bfloat16
                )
    tile = 256
    for start in range(0, total, tile):
        at = slice(start, start + tile)
        info = query_ref[at, :]
        token, begin, end = info[:, 0:1], info[:, 1:2], info[:, 2:3]
        key_token = key_ref[...]
        near = key_token > token - span
        allowed = (key_token >= begin) & (key_token <= token) & (near | (key_token < end))
        outs = []
        for h in range(heads):
            scores = lax.dot_general(
                queries[h, at, :],
                keys[h],
                (((1,), (1,)), ((), ())),
                preferred_element_type=jnp.float32,
            ) * (1.0 / HEAD_DIM**0.5)
            masked = jnp.where(allowed, scores, -1e30)
            weights = jnp.exp(masked - jnp.max(masked, axis=1, keepdims=True))
            probs = weights / jnp.sum(weights, axis=1, keepdims=True)
            out = jnp.dot(probs.astype(jnp.bfloat16), values[h], preferred_element_type=jnp.float32)
            outs.append(out[:, :HEAD_DIM])
        side = start // (total // 2)
        att_ref[start % (total // 2) : start % (total // 2) + tile, side * half : (side + 1) * half] = (
            jnp.concatenate(outs, axis=1).astype(jnp.bfloat16)
        )


def attend(span, offsets, n, bias, cosine, sine, query_info, key_token, mine, got):
    count = len(mine)
    total = cosine.shape[0]
    half = mine[0].shape[1] // 3
    heads = half // HEAD_DIM
    scratch = pltpu.VMEM((heads, total, HEAD_PAD), jnp.bfloat16)
    return pl.pallas_call(
        functools.partial(attend_kernel, count, span, offsets),
        out_shape=(
            jax.ShapeDtypeStruct((total // 2, 2 * half), jnp.bfloat16),
            jax.ShapeDtypeStruct((total, 2 * half), jnp.bfloat16),
        ),
        in_specs=[SMEM] + [VMEM] * (5 + 2 * count),
        out_specs=(VMEM, VMEM),
        scratch_shapes=[scratch, scratch, scratch],
        compiler_params=pltpu.CompilerParams(vmem_limit_bytes=10 * MIB),
        name="attend",
    )(n, bias, cosine, sine, query_info, key_token, *mine, *got)


def gelu(u):
    return u * (1.0 + lax.erf(u * (0.5**0.5))) * 0.5


def down_kernel(count, bias_ref, wd_ref, *refs):
    mine, got = refs[:count], refs[count : 2 * count]
    out_ref, units = refs[2 * count :]
    rows = mine[0].shape[0]
    step = 384
    for i in range(count):
        for c in range(0, units.shape[1], step):
            at = slice(c, c + step)
            u = mine[i][:, at].astype(jnp.float32) + got[i][:, at].astype(jnp.float32)
            u = gelu(u + bias_ref[:, at])
            units[i * rows : (i + 1) * rows, at] = u.astype(jnp.bfloat16)
    width = 512
    for c in range(0, wd_ref.shape[1], width):
        at = slice(c, c + width)
        out = jnp.dot(units[...], wd_ref[:, at], preferred_element_type=jnp.float32)
        out_ref[:, at] = out.astype(jnp.bfloat16)


def down(bias, mine, got, wd):
    count = len(mine)
    rows, hidden = mine[0].shape[0], wd.shape[0]
    return pl.pallas_call(
        functools.partial(down_kernel, count),
        out_shape=jax.ShapeDtypeStruct((count * rows, wd.shape[1]), jnp.bfloat16),
        in_specs=[VMEM] * (2 + 2 * count),
        out_specs=VMEM,
        scratch_shapes=[pltpu.VMEM((count * rows, hidden), jnp.bfloat16)],
        compiler_params=pltpu.CompilerParams(vmem_limit_bytes=6 * MIB),
        name="down",
    )(bias, wd, *mine, *got)


def attended_rows(ref, offset, rows):
    height, half = ref.shape[0], ref.shape[1] // 2
    side = offset // height
    return ref[offset % height : offset % height + rows, side * half : (side + 1) * half]


def mix_kernel(offsets, index_ref, down_ref, att_ref, other_ref, wo_ref, own_ref, sib_ref):
    half = att_ref.shape[1] // 2
    rows = own_ref.shape[0] // len(offsets)
    n = index_ref[1]
    here = pl.ds(pl.multiple_of(n * half, 16), half)
    there = pl.ds(pl.multiple_of((1 - n) * half, 16), half)
    mine = jnp.concatenate([attended_rows(att_ref, o, 2 * rows) for o in offsets], axis=0)
    other = jnp.concatenate([attended_rows(other_ref, o, 2 * rows) for o in offsets], axis=0)
    width = 512
    for c in range(0, own_ref.shape[1], width):
        at = slice(c, c + width)
        out = down_ref[:, at].astype(jnp.float32)
        out += jnp.dot(mine, wo_ref[here, at], preferred_element_type=jnp.float32)
        out += jnp.dot(other, wo_ref[there, at], preferred_element_type=jnp.float32)
        out = out.astype(jnp.bfloat16)
        for i in range(len(offsets)):
            own_ref[i * rows : (i + 1) * rows, at] = out[2 * i * rows : (2 * i + 1) * rows]
            sib_ref[i * rows : (i + 1) * rows, at] = out[(2 * i + 1) * rows : (2 * i + 2) * rows]


def mix(n, offsets, partial_down, att, other, wo):
    rows, feat = partial_down.shape
    shape = jax.ShapeDtypeStruct((rows // 2, feat), jnp.bfloat16)
    return pl.pallas_call(
        functools.partial(mix_kernel, offsets),
        out_shape=(shape, shape),
        in_specs=[SMEM] + [VMEM] * 4,
        out_specs=(VMEM, VMEM),
        compiler_params=pltpu.CompilerParams(vmem_limit_bytes=5 * MIB),
        name="mix",
    )(n, partial_down, att, other, wo)


def output_kernel(
    offset, column, index_ref, bias_ref, mine_ref, got_ref, att_ref, other_ref, wo_ref, wd_ref, own_ref, sib_ref, units
):
    rows = mine_ref.shape[0]
    half = att_ref.shape[1] // 2
    own_rows = own_ref.shape[0]
    step = 384
    for c in range(0, units.shape[1], step):
        at = slice(c, c + step)
        there = slice(column + c, column + c + step)
        u = mine_ref[:, there].astype(jnp.float32) + got_ref[:, there].astype(jnp.float32)
        units[:, at] = gelu(u + bias_ref[:, at]).astype(jnp.bfloat16)
    n = index_ref[1]
    here = pl.ds(pl.multiple_of(n * half, 16), half)
    there = pl.ds(pl.multiple_of((1 - n) * half, 16), half)
    mine = attended_rows(att_ref, offset, rows)
    other = attended_rows(other_ref, offset, rows)
    width = 512
    for c in range(0, wd_ref.shape[1], width):
        at = slice(c, c + width)
        out = jnp.dot(units[...], wd_ref[:, at], preferred_element_type=jnp.float32)
        out += jnp.dot(mine, wo_ref[here, at], preferred_element_type=jnp.float32)
        out += jnp.dot(other, wo_ref[there, at], preferred_element_type=jnp.float32)
        out = out.astype(jnp.bfloat16)
        own_ref[:, at] = out[:own_rows]
        sib_ref[:, at] = out[own_rows:]


def output(n, offset, column, bias, mine, got, att, other, wo, wd):
    rows, hidden = mine.shape[0], wd.shape[0]
    shape = jax.ShapeDtypeStruct((rows // 2, wd.shape[1]), jnp.bfloat16)
    return pl.pallas_call(
        functools.partial(output_kernel, offset, column),
        out_shape=(shape, shape),
        in_specs=[SMEM] + [VMEM] * 7,
        out_specs=(VMEM, VMEM),
        scratch_shapes=[pltpu.VMEM((rows, hidden), jnp.bfloat16)],
        compiler_params=pltpu.CompilerParams(vmem_limit_bytes=5 * MIB),
        name="output",
    )(n, bias, mine, got, att, other, wo, wd)


def after(*values):
    return lax.optimization_barrier(values)


def local_ring(
    hidden_in,
    w_query,
    w_key,
    w_value,
    qkv_bias,
    w_up,
    up_bias,
    w_attn_out,
    w_down,
    out_bias,
    norm_gain,
    norm_bias,
    seq_lens,
    sink_count,
    page_table,
):
    device = lax.axis_index("wide").astype(jnp.int32).reshape(1)
    n = lax.axis_index("narrow").astype(jnp.int32)
    n_arg = n.reshape(1)
    rows, feat = hidden_in.shape
    total_tokens = rows * lax.axis_size("wide")
    half = w_query.shape[1] // 2

    fwd_pairs, bwd_pairs, swap_pairs = [], [], []
    for p in range(CHIPS):
        here, next_chip = CHIP_RING[p], CHIP_RING[(p + 1) % CHIPS]
        fwd_pairs += [(2 * here, 2 * next_chip), (2 * next_chip + 1, 2 * here + 1)]
        bwd_pairs += [(2 * next_chip, 2 * here), (2 * here + 1, 2 * next_chip + 1)]
        swap_pairs += [(2 * here, 2 * here + 1), (2 * here + 1, 2 * here)]
    fwd = lambda v: lax.ppermute(v, "wide", fwd_pairs)
    bwd = lambda v: lax.ppermute(v, "wide", bwd_pairs)
    swap = lambda v: lax.ppermute(v, "wide", swap_pairs)
    cross = lambda v: lax.ppermute(v, "narrow", [(0, 1), (1, 0)])

    first_side, n_arg = after(n == 0, n_arg)
    sums, index = pl.pallas_call(
        sums_kernel,
        out_shape=(
            jax.ShapeDtypeStruct((rows, STAT), jnp.float32),
            jax.ShapeDtypeStruct((2,), jnp.int32),
        ),
        in_specs=[SMEM, SMEM, VMEM],
        out_specs=(VMEM, SMEM),
        compiler_params=pltpu.CompilerParams(vmem_limit_bytes=8 * MIB),
        name="row_sums",
    )(device, n_arg, hidden_in)
    first_block, affine = pl.pallas_call(
        block_kernel,
        out_shape=(
            jax.ShapeDtypeStruct((rows, feat + STAT), jnp.bfloat16),
            jax.ShapeDtypeStruct((4, feat), jnp.float32),
        ),
        in_specs=[VMEM] * 5,
        out_specs=(VMEM, VMEM),
        compiler_params=pltpu.CompilerParams(vmem_limit_bytes=8 * MIB),
        name="first_block",
    )(hidden_in, norm_gain, norm_bias, sums, cross(sums))

    up_row = up_bias[None, :]

    def add(*terms):
        return sum(t.astype(jnp.float32) for t in terms).astype(jnp.bfloat16)

    def finish(name, u, v, column=0):
        return output(
            index, PAIRS.index(name) * 2 * rows, column, up_row, u, v, att, other, w_attn_out, w_down
        )

    def pair(halves, *running):
        return add(halves[0], swap(halves[1]), *running)

    per_device = page_table.shape[0] // 2
    hidden = w_up.shape[1]
    o0 = first_block
    f1, b1, s0 = fwd(o0), bwd(o0), swap(o0)
    kept0, send0, *weights = project(
        index, affine, (w_query, w_key, w_value, w_up), [o0, s0], ((0, "q"),), True
    )
    f1, b1, send0, kept0 = after(f1, b1, send0, kept0)
    got0 = cross(send0)
    f2, b2 = fwd(f1), bwd(b1)
    kept1, send1, u_f1 = project(
        index, affine, weights, [f1, swap(f1), b1, swap(b1)], ((1, "q"), (0,))
    )
    f2, b2, got0, send1, u_f1 = after(f2, b2, got0, send1, u_f1)
    got1 = cross(send1)
    f3 = fwd(f2)
    kept2, send2, u_b2 = project(
        index, affine, weights, [f2, swap(f2), b2, swap(b2)], ((0, "q"), (1,))
    )
    f3, b2, got1, send2, u_b2, late_index = after(f3, b2, got1, send2, u_b2, index)
    got2 = cross(send2)
    f4, b3 = fwd(f3), bwd(b2)
    kept3, send3 = project(index, affine, weights, [f3, swap(f3)], ((0, "q"),))
    query_info, key_token, cosine, sine = tables(total_tokens, late_index, seq_lens, sink_count)
    b3, f4, got2, send3, query_info, key_token, cosine, sine = after(
        b3, f4, got2, send3, query_info, key_token, cosine, sine
    )
    got3 = cross(send3)
    kept4, send4, u_f4, u_b3 = project(
        index, affine, weights, [b3, swap(b3), f4, swap(f4)], (("q",), (1,), (0,))
    )
    got3, send4, u_f4, u_b3 = after(got3, send4, u_f4, u_b3)
    got4 = cross(send4)
    early_pairs = ("o0", "b1", "f2", "f3")
    early = down(up_row, [send0, send1, send2, send3], [got0, got1, got2, got3], w_down)
    got4, early, u_f4 = after(got4, early, u_f4)
    v_f4 = cross(u_f4)
    att, kv = attend(
        total_tokens // 16, (hidden, hidden, hidden, hidden, 0), index, qkv_bias, cosine, sine,
        query_info, key_token, [kept0, kept1, kept2, kept3, kept4], [got0, got1, got2, got3, got4],
    )
    v_f4, att, u_b3 = after(v_f4, att, u_b3)
    other = cross(att)
    other, u_b3, u_b2, u_f1 = after(other, u_b3, u_b2, u_f1)
    v_b3 = cross(u_b3)
    r_b = bwd(pair(finish("f4", u_f4, v_f4)))
    m_own, m_sib = mix(
        index, tuple(PAIRS.index(p) * 2 * rows for p in early_pairs), early, att, other, w_attn_out
    )
    v_b3, r_b, m_own, m_sib, u_b2 = after(v_b3, r_b, m_own, m_sib, u_b2)
    m_got = swap(m_sib)

    def mixed(name):
        at = slice(early_pairs.index(name) * rows, (early_pairs.index(name) + 1) * rows)
        return m_own[at], m_got[at]

    v_b2 = cross(u_b2)
    r_f = fwd(pair(finish("b3", u_b3, v_b3)))
    r_b = bwd(add(r_b, *mixed("f3")))
    v_b2, r_b, r_f, m_own, m_got, u_f1, kv = after(v_b2, r_b, r_f, m_own, m_got, u_f1, kv)
    v_f1 = cross(u_f1)
    r_f = fwd(pair(finish("b2", u_b2, v_b2), r_f))
    r_b = bwd(add(r_b, *mixed("f2")))
    paged = ordered_pages(index, page_table, kv)
    r_f, r_b, v_f1, paged = after(r_f, r_b, v_f1, paged)
    cache_mine, cache_got = paged[:per_device], cross(paged[per_device:])
    r_b = bwd(pair(finish("f1", u_f1, v_f1), r_b))
    r_f = fwd(add(r_f, *mixed("b1")))
    summed = sum(t.astype(jnp.float32) for t in (r_b, r_f, *mixed("o0")))
    hidden_out = (hidden_in.astype(jnp.float32) + summed + out_bias).astype(jnp.bfloat16)
    left = jnp.where(first_side, cache_mine, cache_got)
    right = jnp.where(first_side, cache_got, cache_mine)
    paged_cache = jnp.stack(
        [
            jnp.concatenate([left[..., :half], right[..., :half]], axis=-1),
            jnp.concatenate([left[..., half:], right[..., half:]], axis=-1),
        ]
    )
    return (hidden_out, paged_cache)


def solution(mesh):
    in_specs = (
        P("wide", "narrow"),
        P("narrow", "wide"),
        P("narrow", "wide"),
        P("narrow", "wide"),
        P(None, "wide"),
        P("narrow", "wide"),
        P("wide"),
        P("wide", "narrow"),
        P("wide", "narrow"),
        P("narrow"),
        P(None, "narrow"),
        P(None, "narrow"),
        P(),
        P(),
        P(),
    )
    out_specs = (P("wide", "narrow"), P(None, "narrow", None, "wide"))
    ringed = mesh.shape["wide"] == 2 * CHIPS and mesh.shape["narrow"] == 2
    local = local_ring if ringed else local_generic
    return jax.shard_map(local, mesh=mesh, in_specs=in_specs, out_specs=out_specs, check_vma=False)
```

```python
import functools

import jax
import jax.numpy as jnp
import numpy as np
from jax import lax
from jax.experimental import pallas as pl
from jax.experimental.pallas import tpu as pltpu
from jax.sharding import PartitionSpec as P

D = 6144
HEAD_DIM = 96
ROTARY = 24
PAGE = 16


def segment_info(token_index, seq_lens, sink_count):
    seq_ends = jnp.cumsum(seq_lens)
    seq_starts = seq_ends - seq_lens
    inside = (token_index[:, None] >= seq_starts[None, :]) & (
        token_index[:, None] < seq_ends[None, :]
    )
    member = inside.astype(jnp.int32)
    seq_number = jnp.arange(seq_lens.shape[0], dtype=jnp.int32)
    segment = jnp.sum(member * seq_number[None, :], axis=1)
    position = token_index - jnp.sum(member * seq_starts[None, :], axis=1)
    sink_limit = jnp.sum(member * sink_count[None, :], axis=1)
    return (segment, position, sink_limit)


def rotate(values, position):
    half_rot = ROTARY // 2
    freq_index = jnp.arange(half_rot, dtype=jnp.float32)
    inverse = jnp.power(jnp.float32(10000.0), -2.0 * freq_index / ROTARY)
    angles = position.astype(jnp.float32)[:, None] * inverse[None, :]
    cosine = jnp.cos(angles)[:, None, :]
    sine_part = jnp.sin(angles)[:, None, :]
    first_half = values[..., :half_rot]
    second_half = values[..., half_rot:ROTARY]
    return jnp.concatenate(
        [
            first_half * cosine - second_half * sine_part,
            second_half * cosine + first_half * sine_part,
            values[..., ROTARY:],
        ],
        axis=-1,
    )


def local_generic(
    hidden_in,
    w_query,
    w_key,
    w_value,
    qkv_bias,
    w_up,
    up_bias,
    w_attn_out,
    w_down,
    out_bias,
    norm_gain,
    norm_bias,
    seq_lens,
    sink_count,
    page_table,
):
    wide_count = lax.axis_size("wide")
    narrow_count = lax.axis_size("narrow")
    narrow_index = lax.axis_index("narrow")
    tok_local, feat_local = hidden_in.shape
    sub_rows = tok_local // narrow_count
    total_tokens = tok_local * wide_count
    query_rows = wide_count * sub_rows
    head_cols = w_query.shape[1]
    heads_local = head_cols // HEAD_DIM
    as_float = hidden_in.astype(jnp.float32)
    partial_sum = jnp.sum(as_float, axis=1)
    partial_square = jnp.sum(as_float * as_float, axis=1)
    total_sum, total_square = lax.psum((partial_sum, partial_square), "narrow")
    average = total_sum / D
    variance = total_square / D - average * average
    scaled = (as_float - average[:, None]) * lax.rsqrt(variance + 1e-05)[:, None]
    attn_normed = (scaled * norm_gain[0] + norm_bias[0]).astype(jnp.bfloat16)
    mlp_normed = (scaled * norm_gain[1] + norm_bias[1]).astype(jnp.bfloat16)
    stacked = jnp.stack([attn_normed, mlp_normed]).reshape(2, narrow_count, sub_rows, feat_local)
    gathered = lax.all_gather(stacked, "wide", axis=2, tiled=True).reshape(
        2, total_tokens, feat_local
    )
    local_order = jnp.arange(query_rows, dtype=jnp.int32)
    local_tokens = (
        local_order // sub_rows * tok_local + narrow_index * sub_rows + local_order % sub_rows
    )
    local_seg, local_pos, local_sink = segment_info(local_tokens, seq_lens, sink_count)
    all_order = jnp.arange(total_tokens, dtype=jnp.int32)
    all_tokens = (
        all_order % query_rows // sub_rows * tok_local
        + all_order // query_rows * sub_rows
        + all_order % sub_rows
    )
    all_seg, all_pos, all_sink = segment_info(all_tokens, seq_lens, sink_count)
    qkv_weight = jnp.concatenate([w_query, w_key, w_value], axis=1)
    attn_part = gathered[0]
    mlp_part = gathered[1]
    summed = lax.psum_scatter(
        jnp.concatenate(
            [
                jnp.dot(attn_part, qkv_weight, preferred_element_type=jnp.float32),
                jnp.dot(mlp_part, w_up, preferred_element_type=jnp.float32),
            ],
            axis=1,
        ).astype(jnp.bfloat16),
        "narrow",
        scatter_dimension=0,
        tiled=True,
    ).astype(jnp.float32)
    query_sum = summed[:, :head_cols]
    key_sum = summed[:, head_cols : 2 * head_cols]
    value_sum = summed[:, 2 * head_cols : 3 * head_cols]
    unit_sum = summed[:, 3 * head_cols :]
    keys_local = (
        rotate((key_sum + qkv_bias[1]).reshape(query_rows, heads_local, HEAD_DIM), local_pos)
        .astype(jnp.bfloat16)
        .reshape(query_rows, head_cols)
    )
    values_local = (value_sum + qkv_bias[2]).astype(jnp.bfloat16)
    all_keys, all_values = (
        lax.all_gather(keys_local, "narrow", axis=0, tiled=True),
        lax.all_gather(values_local, "narrow", axis=0, tiled=True),
    )
    queries = rotate(
        (query_sum + qkv_bias[0]).reshape(query_rows, heads_local, HEAD_DIM), local_pos
    ).astype(jnp.bfloat16)
    hidden_units = jax.nn.gelu(unit_sum + up_bias, approximate=False).astype(jnp.bfloat16)
    window_span = total_tokens // 16
    allowed = (local_seg[:, None] == all_seg[None, :]) & (all_pos[None, :] <= local_pos[:, None])
    allowed = allowed & (
        (local_pos[:, None] - all_pos[None, :] < window_span)
        | (all_pos[None, :] < local_sink[:, None])
    )
    key_heads = all_keys.reshape(total_tokens, heads_local, HEAD_DIM)
    value_heads = all_values.reshape(total_tokens, heads_local, HEAD_DIM)
    scores = jnp.einsum("qhd,khd->hqk", queries, key_heads, preferred_element_type=jnp.float32) * (
        1.0 / HEAD_DIM**0.5
    )
    masked = jnp.where(allowed[None], scores, jnp.float32(-1e30))
    top_score = jnp.max(masked, axis=2, keepdims=True)
    weights = jnp.exp(masked - top_score)
    probs = (weights / jnp.sum(weights, axis=2, keepdims=True)).astype(jnp.bfloat16)
    attended = (
        jnp.einsum("hqk,khd->qhd", probs, value_heads, preferred_element_type=jnp.float32)
        .astype(jnp.bfloat16)
        .reshape(query_rows, head_cols)
    )
    full_out, full_down = (
        lax.all_gather(w_attn_out, "narrow", axis=1, tiled=True),
        lax.all_gather(w_down, "narrow", axis=1, tiled=True),
    )
    attn_part = attended
    own_rows = lax.psum_scatter(
        (
            jnp.dot(attn_part, full_out, preferred_element_type=jnp.float32)
            + jnp.dot(hidden_units, full_down, preferred_element_type=jnp.float32)
        ).astype(jnp.bfloat16),
        "wide",
        scatter_dimension=0,
        tiled=True,
    ).astype(jnp.float32)
    combined = lax.all_to_all(
        own_rows.astype(jnp.bfloat16), "narrow", split_axis=1, concat_axis=0, tiled=True
    ).astype(own_rows.dtype)
    hidden_out = (as_float + combined + out_bias).astype(jnp.bfloat16)
    pages_local = page_table.shape[0] // narrow_count
    slot_ids = narrow_index * pages_local + jnp.arange(pages_local, dtype=jnp.int32)
    matches = (page_table[None, :] == slot_ids[:, None]).astype(jnp.int32)
    source_page = jnp.sum(
        matches * jnp.arange(page_table.shape[0], dtype=jnp.int32)[None, :], axis=1
    )
    token_ids = (source_page[:, None] * PAGE + jnp.arange(PAGE, dtype=jnp.int32)[None, :]).reshape(
        -1
    )
    gather_rows = (
        token_ids % tok_local // sub_rows * query_rows
        + token_ids // tok_local * sub_rows
        + token_ids % sub_rows
    )
    cache_keys = jnp.take(all_keys, gather_rows, axis=0).reshape(pages_local, PAGE, head_cols)
    cache_values = jnp.take(all_values, gather_rows, axis=0).reshape(pages_local, PAGE, head_cols)
    paged_cache = jnp.stack([cache_keys, cache_values])
    return (hidden_out, paged_cache)


CHIP_RING = (0, 2, 4, 6, 7, 5, 3, 1)
CHIPS = len(CHIP_RING)
PAIRS = ("o0", "f1", "b1", "f2", "b2", "f3", "b3", "f4")
STAT = 128
HEAD_PAD = 128
LANE_GROUP = 32
MIB = 1 << 20
VMEM = pl.BlockSpec(memory_space=pltpu.VMEM)
HBM = pl.BlockSpec(memory_space=pltpu.HBM)
SMEM = pl.BlockSpec(memory_space=pltpu.SMEM)


def owner_table():
    table = np.zeros((2 * CHIPS, 2 * CHIPS), np.int32)
    for place, chip in enumerate(CHIP_RING):
        for core in range(2):
            order = []
            for pair in PAIRS:
                shift = (-1 if pair[0] == "f" else 1) * int(pair[1]) * (1 - 2 * core)
                order.append(CHIP_RING[(place + shift) % CHIPS] * 2 + core)
                order.append(CHIP_RING[(place - shift) % CHIPS] * 2 + 1 - core)
            table[2 * chip + core] = order
    return table


def place_table():
    owners = owner_table()
    table = np.zeros_like(owners)
    for device in range(owners.shape[0]):
        table[device, owners[device]] = np.arange(owners.shape[1])
    return table


def sums_kernel(device_ref, n_ref, x_ref, out_ref, index_ref):
    x = x_ref[...].astype(jnp.float32)
    first = jnp.sum(x, axis=1, keepdims=True)
    second = jnp.sum(x * x, axis=1, keepdims=True)
    lane = lax.broadcasted_iota(jnp.int32, out_ref.shape, 1)
    out_ref[...] = jnp.where(lane == 0, first, jnp.where(lane == 1, second, 0.0))
    index_ref[0] = device_ref[0]
    index_ref[1] = n_ref[0]


def block_kernel(x_ref, gain_ref, bias_ref, here_ref, there_ref, out_ref, affine_ref):
    feat = x_ref.shape[1]
    total = here_ref[...] + there_ref[...]
    average = total[:, 0:1] / D
    variance = total[:, 1:2] / D - average * average
    scale = lax.rsqrt(variance + 1e-05)
    lane = lax.broadcasted_iota(jnp.int32, (x_ref.shape[0], STAT), 1)
    tail = jnp.zeros((x_ref.shape[0], STAT), jnp.float32)
    for start, value in ((0, average), (3, scale)):
        for term in range(3):
            piece = value.astype(jnp.bfloat16).astype(jnp.float32)
            tail = jnp.where(lane == start + term, piece, tail)
            value = value - piece
    out_ref[:, :feat] = x_ref[...]
    out_ref[:, feat:] = tail.astype(jnp.bfloat16)
    affine_ref[0:2, :] = gain_ref[...]
    affine_ref[2:4, :] = bias_ref[...]


def tables_kernel(index_ref, owners_ref, lens_ref, sinks_ref, inverse_ref, phase_ref, info_ref, key_ref, cos_ref, sin_ref):
    device = index_ref[0]
    blocks = owners_ref.shape[1]
    rows = info_ref.shape[0] // blocks
    half_rot = ROTARY // 2
    lane = lax.broadcasted_iota(jnp.int32, (rows, HEAD_PAD), 1)
    sub = lax.broadcasted_iota(jnp.int32, (rows, HEAD_PAD), 0)
    key_lane = lax.broadcasted_iota(jnp.int32, key_ref.shape, 1)
    key = key_lane
    shared = HEAD_PAD // LANE_GROUP
    for base in range(0, blocks, shared):
        position = jnp.zeros((rows, HEAD_PAD), jnp.int32)
        for g in range(shared):
            j = base + g
            first = owners_ref[device, j] * rows
            key = jnp.where(key_lane // rows == j, first + key_lane - j * rows, key)
            token = first + sub
            begin, end = jnp.zeros_like(token), jnp.zeros_like(token)
            start = jnp.int32(0)
            for s in range(lens_ref.shape[0]):
                inside = (token >= start) & (token < start + lens_ref[s])
                begin = jnp.where(inside, start, begin)
                end = jnp.where(inside, start + sinks_ref[s], end)
                start = start + lens_ref[s]
            info_ref[j * rows : (j + 1) * rows, :] = jnp.where(
                lane == 0, token, jnp.where(lane == 1, begin, end)
            )
            position = jnp.where(lane // LANE_GROUP == g, token - begin, position)
        waves = jnp.cos(position.astype(jnp.float32) * inverse_ref[...] - phase_ref[...])
        for g in range(shared):
            at = slice((base + g) * rows, (base + g + 1) * rows)
            here = pltpu.roll(waves, (HEAD_PAD - g * LANE_GROUP) % HEAD_PAD, 1)
            later = pltpu.roll(waves, (HEAD_PAD - g * LANE_GROUP + half_rot) % HEAD_PAD, 1)
            before = pltpu.roll(waves, (2 * HEAD_PAD - g * LANE_GROUP - half_rot) % HEAD_PAD, 1)
            cosine = jnp.where(lane < half_rot, here, later)
            cos_ref[at, :] = jnp.where(lane < ROTARY, cosine, 1.0)
            sine = jnp.where(lane < half_rot, -before, here)
            sin_ref[at, :] = jnp.where(lane < ROTARY, sine, 0.0)
    key_ref[...] = key


def tables(total, index, lens, sinks):
    half_rot = ROTARY // 2
    lane = np.arange(HEAD_PAD) % LANE_GROUP
    inverse = (10000.0 ** (-2.0 * (lane % half_rot) / ROTARY)).astype(np.float32)[None, :]
    phase = np.where(lane < half_rot, 0.0, np.pi / 2).astype(np.float32)[None, :]
    wide = (total, HEAD_PAD)
    return pl.pallas_call(
        tables_kernel,
        out_shape=(
            jax.ShapeDtypeStruct(wide, jnp.int32),
            jax.ShapeDtypeStruct((1, total), jnp.int32),
            jax.ShapeDtypeStruct(wide, jnp.float32),
            jax.ShapeDtypeStruct(wide, jnp.float32),
        ),
        in_specs=[SMEM] * 4 + [VMEM] * 2,
        out_specs=(VMEM,) * 4,
        compiler_params=pltpu.CompilerParams(vmem_limit_bytes=8 * MIB),
        name="tables",
    )(index, jnp.asarray(owner_table()), lens, sinks, jnp.asarray(inverse), jnp.asarray(phase))


def pages_kernel(index_ref, places_ref, table_ref, kv_ref, out_ref):
    pages = table_ref.shape[0]
    per_owner = pages // places_ref.shape[1]
    device, shift = index_ref[0], index_ref[1] * (pages // 2)
    for p in range(pages):
        place = places_ref[device, p // per_owner] * per_owner + p % per_owner
        row = pl.multiple_of(place * PAGE, PAGE)
        out_ref[lax.rem(table_ref[p] + shift, pages)] = kv_ref[pl.ds(row, PAGE), :]


def ordered_pages(index, page_table, kv):
    return pl.pallas_call(
        pages_kernel,
        out_shape=jax.ShapeDtypeStruct((page_table.shape[0], PAGE, kv.shape[1]), kv.dtype),
        in_specs=[SMEM] * 3 + [VMEM],
        out_specs=VMEM,
        compiler_params=pltpu.CompilerParams(vmem_limit_bytes=8 * MIB),
        name="ordered_pages",
    )(index, jnp.asarray(place_table()), page_table, kv)


def normalise(blocks, affine_ref, attn, mlp):
    rows = blocks[0].shape[0]
    feat = attn.shape[1]
    step = 512
    for b, block in enumerate(blocks):
        tail = block[:, feat:].astype(jnp.float32)
        average = tail[:, 0:1] + tail[:, 1:2] + tail[:, 2:3]
        scale = tail[:, 3:4] + tail[:, 4:5] + tail[:, 5:6]
        here = slice(b * rows, (b + 1) * rows)
        for c in range(0, feat, step):
            at = slice(c, c + step)
            scaled = (block[:, at].astype(jnp.float32) - average) * scale
            attn[here, at] = (scaled * affine_ref[0:1, at] + affine_ref[2:3, at]).astype(jnp.bfloat16)
            mlp[here, at] = (scaled * affine_ref[1:2, at] + affine_ref[3:4, at]).astype(jnp.bfloat16)


def project_kernel(count, outs, first_call, index_ref, affine_ref, wq_ref, wk_ref, wv_ref, wu_ref, *refs):
    blocks, refs = refs[:count], refs[count:]
    mine_ref, refs = refs[0], refs[1:]
    sent_refs, refs = refs[: len(outs)], refs[len(outs) :]
    hidden = wu_ref.shape[1]
    width = 384
    tiles = hidden // width
    copies = []
    if first_call:
        held, (attn, mlp, sems) = refs[:4], refs[4:]
        copies = [
            pltpu.make_async_copy(src, dst, sems.at[i])
            for i, (src, dst) in enumerate(zip((wq_ref, wk_ref, wv_ref), held))
        ]
        for t in range(tiles):
            at = slice(t * width, (t + 1) * width)
            copies.append(pltpu.make_async_copy(wu_ref.at[:, at], held[3].at[:, at], sems.at[3 + t]))
        for copy in copies:
            copy.start()
        wq_ref, wk_ref, wv_ref, wu_ref = held
    else:
        attn, mlp = refs
    rows = 2 * blocks[0].shape[0]
    half = wq_ref.shape[1] // 2
    normalise(blocks, affine_ref, attn, mlp)
    low, high = [], []
    for i, weight in enumerate((wq_ref, wk_ref, wv_ref)):
        if first_call:
            copies[i].wait()
        part = jnp.dot(attn[...], weight[...], preferred_element_type=jnp.float32)
        low.append(part[:, :half])
        high.append(part[:, half:])
    low = jnp.concatenate(low, axis=1).astype(jnp.bfloat16)
    high = jnp.concatenate(high, axis=1).astype(jnp.bfloat16)
    first = index_ref[1] == 0
    mine_ref[...] = jnp.where(first, low, high)
    send = jnp.where(first, high, low)
    send = [send[p * rows : (p + 1) * rows] for p in range(count // 2)]
    gap = -(3 * half * len(send)) % 128
    if gap:
        send.append(jnp.zeros((rows, gap), jnp.bfloat16))
    send = jnp.concatenate(send, axis=1)
    for ref, items in zip(sent_refs, outs):
        if items[-1] == "q":
            ref[:, hidden * (len(items) - 1) :] = send
    for t in range(tiles):
        if first_call:
            copies[3 + t].wait()
        at = slice(t * width, (t + 1) * width)
        part = jnp.dot(mlp[...], wu_ref[:, at], preferred_element_type=jnp.float32)
        part = part.astype(jnp.bfloat16)
        for ref, items in zip(sent_refs, outs):
            for i, item in enumerate(items):
                if item != "q":
                    begin = i * hidden + t * width
                    ref[:, begin : begin + width] = part[item * rows : (item + 1) * rows]


def project(n, affine, weights, blocks, outs, first_call=False):
    count = len(blocks)
    rows = 2 * blocks[0].shape[0]
    feat, cols = weights[0].shape
    hidden = weights[3].shape[1]
    sent = 3 * cols // 2 * (count // 2)
    sent += -sent % 128
    shapes = [jax.ShapeDtypeStruct((rows * count // 2, 3 * cols // 2), jnp.bfloat16)]
    for items in outs:
        width = sum(sent if item == "q" else hidden for item in items)
        shapes.append(jax.ShapeDtypeStruct((rows, width), jnp.bfloat16))
    scratch = [pltpu.VMEM((rows * count // 2, feat), jnp.bfloat16)] * 2
    if first_call:
        shapes += [jax.ShapeDtypeStruct(w.shape, w.dtype) for w in weights]
        scratch.append(pltpu.SemaphoreType.DMA((3 + hidden // 384,)))
    return pl.pallas_call(
        functools.partial(project_kernel, count, outs, first_call),
        out_shape=tuple(shapes),
        in_specs=[SMEM, VMEM] + [HBM if first_call else VMEM] * 4 + [VMEM] * count,
        out_specs=(VMEM,) * len(shapes),
        scratch_shapes=scratch,
        compiler_params=pltpu.CompilerParams(vmem_limit_bytes=(46 if first_call else 9) * MIB),
        name="project",
    )(n, affine, *weights, *blocks)


def attend_kernel(count, span, offsets, index_ref, bias_ref, cos_ref, sin_ref, query_ref, key_ref, *refs):
    mine, got = refs[:count], refs[count : 2 * count]
    att_ref, kv_ref, queries, keys, values = refs[2 * count :]
    heads = queries.shape[0]
    half = kv_ref.shape[1] // 2
    total = kv_ref.shape[0]
    half_rot = ROTARY // 2
    bias = jnp.where(index_ref[1] == 0, bias_ref[:, :half], bias_ref[:, half:])
    offset = 0
    for g in range(count):
        rows = mine[g].shape[0]
        at = slice(offset, offset + rows)
        offset += rows
        pieces = []
        for p in range(rows // got[g].shape[0]):
            begin = offsets[g] + 3 * half * p
            pieces.append(got[g][:, begin : begin + 3 * half])
        sent = jnp.concatenate(pieces, axis=0)
        summed = mine[g][...].astype(jnp.float32) + sent.astype(jnp.float32)
        cosine, sine = cos_ref[at, :], sin_ref[at, :]
        lane = lax.broadcasted_iota(jnp.int32, (rows, HEAD_PAD), 1)
        pad = jnp.zeros((rows, HEAD_PAD - HEAD_DIM), jnp.float32)
        for kind in range(3):
            kept = []
            for h in range(heads):
                begin = kind * half + h * HEAD_DIM
                u = summed[:, begin : begin + HEAD_DIM]
                u = u + bias[kind : kind + 1, h * HEAD_DIM : (h + 1) * HEAD_DIM]
                u = jnp.concatenate([u, pad], axis=1)
                if kind < 2:
                    other = jnp.where(
                        lane < half_rot,
                        pltpu.roll(u, HEAD_PAD - half_rot, 1),
                        pltpu.roll(u, half_rot, 1),
                    )
                    u = u * cosine + other * sine
                (queries, keys, values)[kind][h, at, :] = u.astype(jnp.bfloat16)
                kept.append(u[:, :HEAD_DIM])
            if kind > 0:
                kv_ref[at, (kind - 1) * half : kind * half] = jnp.concatenate(kept, axis=1).astype(
                    jnp.bfloat16
                )
    tile = 256
    for start in range(0, total, tile):
        at = slice(start, start + tile)
        info = query_ref[at, :]
        token, begin, end = info[:, 0:1], info[:, 1:2], info[:, 2:3]
        key_token = key_ref[...]
        near = key_token > token - span
        allowed = (key_token >= begin) & (key_token <= token) & (near | (key_token < end))
        outs = []
        for h in range(heads):
            scores = lax.dot_general(
                queries[h, at, :],
                keys[h],
                (((1,), (1,)), ((), ())),
                preferred_element_type=jnp.float32,
            ) * (1.0 / HEAD_DIM**0.5)
            masked = jnp.where(allowed, scores, -1e30)
            weights = jnp.exp(masked - jnp.max(masked, axis=1, keepdims=True))
            probs = weights / jnp.sum(weights, axis=1, keepdims=True)
            out = jnp.dot(probs.astype(jnp.bfloat16), values[h], preferred_element_type=jnp.float32)
            outs.append(out[:, :HEAD_DIM])
        side = start // (total // 2)
        att_ref[start % (total // 2) : start % (total // 2) + tile, side * half : (side + 1) * half] = (
            jnp.concatenate(outs, axis=1).astype(jnp.bfloat16)
        )


def attend(span, offsets, n, bias, cosine, sine, query_info, key_token, mine, got):
    count = len(mine)
    total = cosine.shape[0]
    half = mine[0].shape[1] // 3
    heads = half // HEAD_DIM
    scratch = pltpu.VMEM((heads, total, HEAD_PAD), jnp.bfloat16)
    return pl.pallas_call(
        functools.partial(attend_kernel, count, span, offsets),
        out_shape=(
            jax.ShapeDtypeStruct((total // 2, 2 * half), jnp.bfloat16),
            jax.ShapeDtypeStruct((total, 2 * half), jnp.bfloat16),
        ),
        in_specs=[SMEM] + [VMEM] * (5 + 2 * count),
        out_specs=(VMEM, VMEM),
        scratch_shapes=[scratch, scratch, scratch],
        compiler_params=pltpu.CompilerParams(vmem_limit_bytes=10 * MIB),
        name="attend",
    )(n, bias, cosine, sine, query_info, key_token, *mine, *got)


def gelu(u):
    return u * (1.0 + lax.erf(u * (0.5**0.5))) * 0.5


def down_kernel(count, bias_ref, wd_ref, *refs):
    mine, got = refs[:count], refs[count : 2 * count]
    out_ref, units = refs[2 * count :]
    rows = mine[0].shape[0]
    step = 384
    for i in range(count):
        for c in range(0, units.shape[1], step):
            at = slice(c, c + step)
            u = mine[i][:, at].astype(jnp.float32) + got[i][:, at].astype(jnp.float32)
            u = gelu(u + bias_ref[:, at])
            units[i * rows : (i + 1) * rows, at] = u.astype(jnp.bfloat16)
    width, tall = 512, 2 * rows
    for c in range(0, wd_ref.shape[1], width):
        at = slice(c, c + width)
        for r in range(0, units.shape[0], tall):
            here = slice(r, r + tall)
            out = jnp.dot(units[here, :], wd_ref[:, at], preferred_element_type=jnp.float32)
            out_ref[here, at] = out.astype(jnp.bfloat16)


def down(bias, mine, got, wd):
    count = len(mine)
    rows, hidden = mine[0].shape[0], wd.shape[0]
    return pl.pallas_call(
        functools.partial(down_kernel, count),
        out_shape=jax.ShapeDtypeStruct((count * rows, wd.shape[1]), jnp.bfloat16),
        in_specs=[VMEM] * (2 + 2 * count),
        out_specs=VMEM,
        scratch_shapes=[pltpu.VMEM((count * rows, hidden), jnp.bfloat16)],
        compiler_params=pltpu.CompilerParams(vmem_limit_bytes=6 * MIB),
        name="down",
    )(bias, wd, *mine, *got)


def attended_rows(ref, offset, rows):
    height, half = ref.shape[0], ref.shape[1] // 2
    side = offset // height
    return ref[offset % height : offset % height + rows, side * half : (side + 1) * half]


def mix_kernel(offsets, index_ref, down_ref, att_ref, other_ref, wo_ref, own_ref, sib_ref):
    half = att_ref.shape[1] // 2
    rows = own_ref.shape[0] // len(offsets)
    n = index_ref[1]
    here = pl.ds(pl.multiple_of(n * half, 16), half)
    there = pl.ds(pl.multiple_of((1 - n) * half, 16), half)
    mine = jnp.concatenate([attended_rows(att_ref, o, 2 * rows) for o in offsets], axis=0)
    other = jnp.concatenate([attended_rows(other_ref, o, 2 * rows) for o in offsets], axis=0)
    width = 512
    for c in range(0, own_ref.shape[1], width):
        at = slice(c, c + width)
        out = down_ref[:, at].astype(jnp.float32)
        out += jnp.dot(mine, wo_ref[here, at], preferred_element_type=jnp.float32)
        out += jnp.dot(other, wo_ref[there, at], preferred_element_type=jnp.float32)
        out = out.astype(jnp.bfloat16)
        for i in range(len(offsets)):
            own_ref[i * rows : (i + 1) * rows, at] = out[2 * i * rows : (2 * i + 1) * rows]
            sib_ref[i * rows : (i + 1) * rows, at] = out[(2 * i + 1) * rows : (2 * i + 2) * rows]


def mix(n, offsets, partial_down, att, other, wo):
    rows, feat = partial_down.shape
    shape = jax.ShapeDtypeStruct((rows // 2, feat), jnp.bfloat16)
    return pl.pallas_call(
        functools.partial(mix_kernel, offsets),
        out_shape=(shape, shape),
        in_specs=[SMEM] + [VMEM] * 4,
        out_specs=(VMEM, VMEM),
        compiler_params=pltpu.CompilerParams(vmem_limit_bytes=5 * MIB),
        name="mix",
    )(n, partial_down, att, other, wo)


def output_kernel(
    offset, column, index_ref, bias_ref, mine_ref, got_ref, att_ref, other_ref, wo_ref, wd_ref, own_ref, sib_ref, units
):
    rows = mine_ref.shape[0]
    half = att_ref.shape[1] // 2
    own_rows = own_ref.shape[0]
    step = 384
    for c in range(0, units.shape[1], step):
        at = slice(c, c + step)
        there = slice(column + c, column + c + step)
        u = mine_ref[:, there].astype(jnp.float32) + got_ref[:, there].astype(jnp.float32)
        units[:, at] = gelu(u + bias_ref[:, at]).astype(jnp.bfloat16)
    n = index_ref[1]
    here = pl.ds(pl.multiple_of(n * half, 16), half)
    there = pl.ds(pl.multiple_of((1 - n) * half, 16), half)
    mine = attended_rows(att_ref, offset, rows)
    other = attended_rows(other_ref, offset, rows)
    width = 512
    for c in range(0, wd_ref.shape[1], width):
        at = slice(c, c + width)
        out = jnp.dot(units[...], wd_ref[:, at], preferred_element_type=jnp.float32)
        out += jnp.dot(mine, wo_ref[here, at], preferred_element_type=jnp.float32)
        out += jnp.dot(other, wo_ref[there, at], preferred_element_type=jnp.float32)
        out = out.astype(jnp.bfloat16)
        own_ref[:, at] = out[:own_rows]
        sib_ref[:, at] = out[own_rows:]


def output(n, offset, column, bias, mine, got, att, other, wo, wd):
    rows, hidden = mine.shape[0], wd.shape[0]
    shape = jax.ShapeDtypeStruct((rows // 2, wd.shape[1]), jnp.bfloat16)
    return pl.pallas_call(
        functools.partial(output_kernel, offset, column),
        out_shape=(shape, shape),
        in_specs=[SMEM] + [VMEM] * 7,
        out_specs=(VMEM, VMEM),
        scratch_shapes=[pltpu.VMEM((rows, hidden), jnp.bfloat16)],
        compiler_params=pltpu.CompilerParams(vmem_limit_bytes=5 * MIB),
        name="output",
    )(n, bias, mine, got, att, other, wo, wd)


def after(*values):
    return lax.optimization_barrier(values)


def local_ring(
    hidden_in,
    w_query,
    w_key,
    w_value,
    qkv_bias,
    w_up,
    up_bias,
    w_attn_out,
    w_down,
    out_bias,
    norm_gain,
    norm_bias,
    seq_lens,
    sink_count,
    page_table,
):
    device = lax.axis_index("wide").astype(jnp.int32).reshape(1)
    n = lax.axis_index("narrow").astype(jnp.int32)
    n_arg = n.reshape(1)
    rows, feat = hidden_in.shape
    total_tokens = rows * lax.axis_size("wide")
    half = w_query.shape[1] // 2

    fwd_pairs, bwd_pairs, swap_pairs = [], [], []
    for p in range(CHIPS):
        here, next_chip = CHIP_RING[p], CHIP_RING[(p + 1) % CHIPS]
        fwd_pairs += [(2 * here, 2 * next_chip), (2 * next_chip + 1, 2 * here + 1)]
        bwd_pairs += [(2 * next_chip, 2 * here), (2 * here + 1, 2 * next_chip + 1)]
        swap_pairs += [(2 * here, 2 * here + 1), (2 * here + 1, 2 * here)]
    fwd = lambda v: lax.ppermute(v, "wide", fwd_pairs)
    bwd = lambda v: lax.ppermute(v, "wide", bwd_pairs)
    swap = lambda v: lax.ppermute(v, "wide", swap_pairs)
    cross = lambda v: lax.ppermute(v, "narrow", [(0, 1), (1, 0)])

    first_side, n_arg = after(n == 0, n_arg)
    sums, index = pl.pallas_call(
        sums_kernel,
        out_shape=(
            jax.ShapeDtypeStruct((rows, STAT), jnp.float32),
            jax.ShapeDtypeStruct((2,), jnp.int32),
        ),
        in_specs=[SMEM, SMEM, VMEM],
        out_specs=(VMEM, SMEM),
        compiler_params=pltpu.CompilerParams(vmem_limit_bytes=8 * MIB),
        name="row_sums",
    )(device, n_arg, hidden_in)
    first_block, affine = pl.pallas_call(
        block_kernel,
        out_shape=(
            jax.ShapeDtypeStruct((rows, feat + STAT), jnp.bfloat16),
            jax.ShapeDtypeStruct((4, feat), jnp.float32),
        ),
        in_specs=[VMEM] * 5,
        out_specs=(VMEM, VMEM),
        compiler_params=pltpu.CompilerParams(vmem_limit_bytes=8 * MIB),
        name="first_block",
    )(hidden_in, norm_gain, norm_bias, sums, cross(sums))

    up_row = up_bias[None, :]

    def add(*terms):
        return sum(t.astype(jnp.float32) for t in terms).astype(jnp.bfloat16)

    def finish(name, u, v, column=0):
        return output(
            index, PAIRS.index(name) * 2 * rows, column, up_row, u, v, att, other, w_attn_out, w_down
        )

    def pair(halves, *running):
        return add(halves[0], swap(halves[1]), *running)

    per_device = page_table.shape[0] // 2
    hidden = w_up.shape[1]
    o0 = first_block
    f1, b1, s0 = fwd(o0), bwd(o0), swap(o0)
    kept0, send0, *weights = project(
        index, affine, (w_query, w_key, w_value, w_up), [o0, s0], ((0, "q"),), True
    )
    f1, b1, send0, kept0 = after(f1, b1, send0, kept0)
    got0 = cross(send0)
    f2, b2 = fwd(f1), bwd(b1)
    kept1, send1, u_f1 = project(
        index, affine, weights, [f1, swap(f1), b1, swap(b1)], ((1, "q"), (0,))
    )
    f2, b2, got0, send1, u_f1 = after(f2, b2, got0, send1, u_f1)
    got1 = cross(send1)
    f3 = fwd(f2)
    kept2, send2, u_b2 = project(
        index, affine, weights, [f2, swap(f2), b2, swap(b2)], ((0, "q"), (1,))
    )
    f3, b2, got1, send2, u_b2, late_index = after(f3, b2, got1, send2, u_b2, index)
    got2 = cross(send2)
    f4, b3 = fwd(f3), bwd(b2)
    kept3, send3 = project(index, affine, weights, [f3, swap(f3)], ((0, "q"),))
    query_info, key_token, cosine, sine = tables(total_tokens, late_index, seq_lens, sink_count)
    b3, f4, got2, send3, query_info, key_token, cosine, sine = after(
        b3, f4, got2, send3, query_info, key_token, cosine, sine
    )
    got3 = cross(send3)
    kept4, send4, u_far = project(
        index, affine, weights, [b3, swap(b3), f4, swap(f4)], (("q",), (1, 0))
    )
    got3, send4, u_far = after(got3, send4, u_far)
    got4 = cross(send4)
    early_pairs = ("o0", "b1", "f2", "f3")
    early = down(up_row, [send0, send1, send2, send3], [got0, got1, got2, got3], w_down)
    got4, early, u_far = after(got4, early, u_far)
    v_far = cross(u_far)
    att, kv = attend(
        total_tokens // 16, (hidden, hidden, hidden, hidden, 0), index, qkv_bias, cosine, sine,
        query_info, key_token, [kept0, kept1, kept2, kept3, kept4], [got0, got1, got2, got3, got4],
    )
    v_far, att = after(v_far, att)
    other = cross(att)
    other, u_b2, u_f1, kv = after(other, u_b2, u_f1, kv)
    v_b2 = cross(u_b2)
    r_b = bwd(pair(finish("f4", u_far, v_far)))
    y_b3 = finish("b3", u_far, v_far, hidden)
    m_own, m_sib = mix(
        index, tuple(PAIRS.index(p) * 2 * rows for p in early_pairs), early, att, other, w_attn_out
    )
    m_got = swap(m_sib)
    v_b2, r_b, y_b3, m_own, m_got, u_f1, kv = after(v_b2, r_b, y_b3, m_own, m_got, u_f1, kv)

    def mixed(name):
        at = slice(early_pairs.index(name) * rows, (early_pairs.index(name) + 1) * rows)
        return m_own[at], m_got[at]

    v_f1 = cross(u_f1)
    r_b, r_f = bwd(add(r_b, *mixed("f3"))), fwd(pair(y_b3))
    y_b2 = finish("b2", u_b2, v_b2)
    paged = ordered_pages(index, page_table, kv)
    v_f1, r_b, r_f, y_b2, m_own, m_got, paged = after(v_f1, r_b, r_f, y_b2, m_own, m_got, paged)
    cache_mine, cache_got = paged[:per_device], cross(paged[per_device:])
    r_b, r_f = bwd(add(r_b, *mixed("f2"))), fwd(pair(y_b2, r_f))
    y_f1 = finish("f1", u_f1, v_f1)
    r_b, r_f, y_f1, cache_mine, cache_got = after(r_b, r_f, y_f1, cache_mine, cache_got)
    r_f, r_b = fwd(add(r_f, *mixed("b1"))), bwd(pair(y_f1, r_b))
    summed = sum(t.astype(jnp.float32) for t in (r_b, r_f, *mixed("o0")))
    hidden_out = (hidden_in.astype(jnp.float32) + summed + out_bias).astype(jnp.bfloat16)
    left = jnp.where(first_side, cache_mine, cache_got)
    right = jnp.where(first_side, cache_got, cache_mine)
    paged_cache = jnp.stack(
        [
            jnp.concatenate([left[..., :half], right[..., :half]], axis=-1),
            jnp.concatenate([left[..., half:], right[..., half:]], axis=-1),
        ]
    )
    return (hidden_out, paged_cache)


def solution(mesh):
    in_specs = (
        P("wide", "narrow"),
        P("narrow", "wide"),
        P("narrow", "wide"),
        P("narrow", "wide"),
        P(None, "wide"),
        P("narrow", "wide"),
        P("wide"),
        P("wide", "narrow"),
        P("wide", "narrow"),
        P("narrow"),
        P(None, "narrow"),
        P(None, "narrow"),
        P(),
        P(),
        P(),
    )
    out_specs = (P("wide", "narrow"), P(None, "narrow", None, "wide"))
    ringed = mesh.shape["wide"] == 2 * CHIPS and mesh.shape["narrow"] == 2
    local = local_ring if ringed else local_generic
    return jax.shard_map(local, mesh=mesh, in_specs=in_specs, out_specs=out_specs, check_vma=False)
```

```python
import functools

import jax
import jax.numpy as jnp
import numpy as np
from jax import lax
from jax.experimental import pallas as pl
from jax.experimental.pallas import tpu as pltpu
from jax.sharding import PartitionSpec as P

D = 6144
HEAD_DIM = 96
ROTARY = 24
PAGE = 16


def segment_info(token_index, seq_lens, sink_count):
    seq_ends = jnp.cumsum(seq_lens)
    seq_starts = seq_ends - seq_lens
    inside = (token_index[:, None] >= seq_starts[None, :]) & (
        token_index[:, None] < seq_ends[None, :]
    )
    member = inside.astype(jnp.int32)
    seq_number = jnp.arange(seq_lens.shape[0], dtype=jnp.int32)
    segment = jnp.sum(member * seq_number[None, :], axis=1)
    position = token_index - jnp.sum(member * seq_starts[None, :], axis=1)
    sink_limit = jnp.sum(member * sink_count[None, :], axis=1)
    return (segment, position, sink_limit)


def rotate(values, position):
    half_rot = ROTARY // 2
    freq_index = jnp.arange(half_rot, dtype=jnp.float32)
    inverse = jnp.power(jnp.float32(10000.0), -2.0 * freq_index / ROTARY)
    angles = position.astype(jnp.float32)[:, None] * inverse[None, :]
    cosine = jnp.cos(angles)[:, None, :]
    sine_part = jnp.sin(angles)[:, None, :]
    first_half = values[..., :half_rot]
    second_half = values[..., half_rot:ROTARY]
    return jnp.concatenate(
        [
            first_half * cosine - second_half * sine_part,
            second_half * cosine + first_half * sine_part,
            values[..., ROTARY:],
        ],
        axis=-1,
    )


def local_generic(
    hidden_in,
    w_query,
    w_key,
    w_value,
    qkv_bias,
    w_up,
    up_bias,
    w_attn_out,
    w_down,
    out_bias,
    norm_gain,
    norm_bias,
    seq_lens,
    sink_count,
    page_table,
):
    wide_count = lax.axis_size("wide")
    narrow_count = lax.axis_size("narrow")
    narrow_index = lax.axis_index("narrow")
    tok_local, feat_local = hidden_in.shape
    sub_rows = tok_local // narrow_count
    total_tokens = tok_local * wide_count
    query_rows = wide_count * sub_rows
    head_cols = w_query.shape[1]
    heads_local = head_cols // HEAD_DIM
    as_float = hidden_in.astype(jnp.float32)
    partial_sum = jnp.sum(as_float, axis=1)
    partial_square = jnp.sum(as_float * as_float, axis=1)
    total_sum, total_square = lax.psum((partial_sum, partial_square), "narrow")
    average = total_sum / D
    variance = total_square / D - average * average
    scaled = (as_float - average[:, None]) * lax.rsqrt(variance + 1e-05)[:, None]
    attn_normed = (scaled * norm_gain[0] + norm_bias[0]).astype(jnp.bfloat16)
    mlp_normed = (scaled * norm_gain[1] + norm_bias[1]).astype(jnp.bfloat16)
    stacked = jnp.stack([attn_normed, mlp_normed]).reshape(2, narrow_count, sub_rows, feat_local)
    gathered = lax.all_gather(stacked, "wide", axis=2, tiled=True).reshape(
        2, total_tokens, feat_local
    )
    local_order = jnp.arange(query_rows, dtype=jnp.int32)
    local_tokens = (
        local_order // sub_rows * tok_local + narrow_index * sub_rows + local_order % sub_rows
    )
    local_seg, local_pos, local_sink = segment_info(local_tokens, seq_lens, sink_count)
    all_order = jnp.arange(total_tokens, dtype=jnp.int32)
    all_tokens = (
        all_order % query_rows // sub_rows * tok_local
        + all_order // query_rows * sub_rows
        + all_order % sub_rows
    )
    all_seg, all_pos, all_sink = segment_info(all_tokens, seq_lens, sink_count)
    qkv_weight = jnp.concatenate([w_query, w_key, w_value], axis=1)
    attn_part = gathered[0]
    mlp_part = gathered[1]
    summed = lax.psum_scatter(
        jnp.concatenate(
            [
                jnp.dot(attn_part, qkv_weight, preferred_element_type=jnp.float32),
                jnp.dot(mlp_part, w_up, preferred_element_type=jnp.float32),
            ],
            axis=1,
        ).astype(jnp.bfloat16),
        "narrow",
        scatter_dimension=0,
        tiled=True,
    ).astype(jnp.float32)
    query_sum = summed[:, :head_cols]
    key_sum = summed[:, head_cols : 2 * head_cols]
    value_sum = summed[:, 2 * head_cols : 3 * head_cols]
    unit_sum = summed[:, 3 * head_cols :]
    keys_local = (
        rotate((key_sum + qkv_bias[1]).reshape(query_rows, heads_local, HEAD_DIM), local_pos)
        .astype(jnp.bfloat16)
        .reshape(query_rows, head_cols)
    )
    values_local = (value_sum + qkv_bias[2]).astype(jnp.bfloat16)
    all_keys, all_values = (
        lax.all_gather(keys_local, "narrow", axis=0, tiled=True),
        lax.all_gather(values_local, "narrow", axis=0, tiled=True),
    )
    queries = rotate(
        (query_sum + qkv_bias[0]).reshape(query_rows, heads_local, HEAD_DIM), local_pos
    ).astype(jnp.bfloat16)
    hidden_units = jax.nn.gelu(unit_sum + up_bias, approximate=False).astype(jnp.bfloat16)
    window_span = total_tokens // 16
    allowed = (local_seg[:, None] == all_seg[None, :]) & (all_pos[None, :] <= local_pos[:, None])
    allowed = allowed & (
        (local_pos[:, None] - all_pos[None, :] < window_span)
        | (all_pos[None, :] < local_sink[:, None])
    )
    key_heads = all_keys.reshape(total_tokens, heads_local, HEAD_DIM)
    value_heads = all_values.reshape(total_tokens, heads_local, HEAD_DIM)
    scores = jnp.einsum("qhd,khd->hqk", queries, key_heads, preferred_element_type=jnp.float32) * (
        1.0 / HEAD_DIM**0.5
    )
    masked = jnp.where(allowed[None], scores, jnp.float32(-1e30))
    top_score = jnp.max(masked, axis=2, keepdims=True)
    weights = jnp.exp(masked - top_score)
    probs = (weights / jnp.sum(weights, axis=2, keepdims=True)).astype(jnp.bfloat16)
    attended = (
        jnp.einsum("hqk,khd->qhd", probs, value_heads, preferred_element_type=jnp.float32)
        .astype(jnp.bfloat16)
        .reshape(query_rows, head_cols)
    )
    full_out, full_down = (
        lax.all_gather(w_attn_out, "narrow", axis=1, tiled=True),
        lax.all_gather(w_down, "narrow", axis=1, tiled=True),
    )
    attn_part = attended
    own_rows = lax.psum_scatter(
        (
            jnp.dot(attn_part, full_out, preferred_element_type=jnp.float32)
            + jnp.dot(hidden_units, full_down, preferred_element_type=jnp.float32)
        ).astype(jnp.bfloat16),
        "wide",
        scatter_dimension=0,
        tiled=True,
    ).astype(jnp.float32)
    combined = lax.all_to_all(
        own_rows.astype(jnp.bfloat16), "narrow", split_axis=1, concat_axis=0, tiled=True
    ).astype(own_rows.dtype)
    hidden_out = (as_float + combined + out_bias).astype(jnp.bfloat16)
    pages_local = page_table.shape[0] // narrow_count
    slot_ids = narrow_index * pages_local + jnp.arange(pages_local, dtype=jnp.int32)
    matches = (page_table[None, :] == slot_ids[:, None]).astype(jnp.int32)
    source_page = jnp.sum(
        matches * jnp.arange(page_table.shape[0], dtype=jnp.int32)[None, :], axis=1
    )
    token_ids = (source_page[:, None] * PAGE + jnp.arange(PAGE, dtype=jnp.int32)[None, :]).reshape(
        -1
    )
    gather_rows = (
        token_ids % tok_local // sub_rows * query_rows
        + token_ids // tok_local * sub_rows
        + token_ids % sub_rows
    )
    cache_keys = jnp.take(all_keys, gather_rows, axis=0).reshape(pages_local, PAGE, head_cols)
    cache_values = jnp.take(all_values, gather_rows, axis=0).reshape(pages_local, PAGE, head_cols)
    paged_cache = jnp.stack([cache_keys, cache_values])
    return (hidden_out, paged_cache)


CHIP_RING = (0, 2, 4, 6, 7, 5, 3, 1)
CHIPS = len(CHIP_RING)
PAIRS = ("o0", "f1", "b1", "f2", "b2", "f3", "b3", "f4")
STAT = 128
HEAD_PAD = 128
LANE_GROUP = 32
MIB = 1 << 20
VMEM = pl.BlockSpec(memory_space=pltpu.VMEM)
HBM = pl.BlockSpec(memory_space=pltpu.HBM)
SMEM = pl.BlockSpec(memory_space=pltpu.SMEM)


def owner_table():
    table = np.zeros((2 * CHIPS, 2 * CHIPS), np.int32)
    for place, chip in enumerate(CHIP_RING):
        for core in range(2):
            order = []
            for pair in PAIRS:
                shift = (-1 if pair[0] == "f" else 1) * int(pair[1]) * (1 - 2 * core)
                order.append(CHIP_RING[(place + shift) % CHIPS] * 2 + core)
                order.append(CHIP_RING[(place - shift) % CHIPS] * 2 + 1 - core)
            table[2 * chip + core] = order
    return table


def place_table():
    owners = owner_table()
    table = np.zeros_like(owners)
    for device in range(owners.shape[0]):
        table[device, owners[device]] = np.arange(owners.shape[1])
    return table


def sums_kernel(device_ref, n_ref, x_ref, out_ref, index_ref):
    x = x_ref[...].astype(jnp.float32)
    first = jnp.sum(x, axis=1, keepdims=True)
    second = jnp.sum(x * x, axis=1, keepdims=True)
    lane = lax.broadcasted_iota(jnp.int32, out_ref.shape, 1)
    out_ref[...] = jnp.where(lane == 0, first, jnp.where(lane == 1, second, 0.0))
    index_ref[0] = device_ref[0]
    index_ref[1] = n_ref[0]


def block_kernel(x_ref, gain_ref, bias_ref, here_ref, there_ref, out_ref, affine_ref):
    feat = x_ref.shape[1]
    total = here_ref[...] + there_ref[...]
    average = total[:, 0:1] / D
    variance = total[:, 1:2] / D - average * average
    scale = lax.rsqrt(variance + 1e-05)
    lane = lax.broadcasted_iota(jnp.int32, (x_ref.shape[0], STAT), 1)
    tail = jnp.zeros((x_ref.shape[0], STAT), jnp.float32)
    for start, value in ((0, average), (3, scale)):
        for term in range(3):
            piece = value.astype(jnp.bfloat16).astype(jnp.float32)
            tail = jnp.where(lane == start + term, piece, tail)
            value = value - piece
    out_ref[:, :feat] = x_ref[...]
    out_ref[:, feat:] = tail.astype(jnp.bfloat16)
    affine_ref[0:2, :] = gain_ref[...]
    affine_ref[2:4, :] = bias_ref[...]


def tables_kernel(index_ref, owners_ref, lens_ref, sinks_ref, inverse_ref, phase_ref, info_ref, key_ref, cos_ref, sin_ref):
    device = index_ref[0]
    blocks = owners_ref.shape[1]
    rows = info_ref.shape[0] // blocks
    half_rot = ROTARY // 2
    lane = lax.broadcasted_iota(jnp.int32, (rows, HEAD_PAD), 1)
    sub = lax.broadcasted_iota(jnp.int32, (rows, HEAD_PAD), 0)
    key_lane = lax.broadcasted_iota(jnp.int32, key_ref.shape, 1)
    key = key_lane
    shared = HEAD_PAD // LANE_GROUP
    for base in range(0, blocks, shared):
        position = jnp.zeros((rows, HEAD_PAD), jnp.int32)
        for g in range(shared):
            j = base + g
            first = owners_ref[device, j] * rows
            key = jnp.where(key_lane // rows == j, first + key_lane - j * rows, key)
            token = first + sub
            begin, end = jnp.zeros_like(token), jnp.zeros_like(token)
            start = jnp.int32(0)
            for s in range(lens_ref.shape[0]):
                inside = (token >= start) & (token < start + lens_ref[s])
                begin = jnp.where(inside, start, begin)
                end = jnp.where(inside, start + sinks_ref[s], end)
                start = start + lens_ref[s]
            info_ref[j * rows : (j + 1) * rows, :] = jnp.where(
                lane == 0, token, jnp.where(lane == 1, begin, end)
            )
            position = jnp.where(lane // LANE_GROUP == g, token - begin, position)
        waves = jnp.cos(position.astype(jnp.float32) * inverse_ref[...] - phase_ref[...])
        for g in range(shared):
            at = slice((base + g) * rows, (base + g + 1) * rows)
            here = pltpu.roll(waves, (HEAD_PAD - g * LANE_GROUP) % HEAD_PAD, 1)
            later = pltpu.roll(waves, (HEAD_PAD - g * LANE_GROUP + half_rot) % HEAD_PAD, 1)
            before = pltpu.roll(waves, (2 * HEAD_PAD - g * LANE_GROUP - half_rot) % HEAD_PAD, 1)
            cosine = jnp.where(lane < half_rot, here, later)
            cos_ref[at, :] = jnp.where(lane < ROTARY, cosine, 1.0)
            sine = jnp.where(lane < half_rot, -before, here)
            sin_ref[at, :] = jnp.where(lane < ROTARY, sine, 0.0)
    key_ref[...] = key


def tables(total, index, lens, sinks):
    half_rot = ROTARY // 2
    lane = np.arange(HEAD_PAD) % LANE_GROUP
    inverse = (10000.0 ** (-2.0 * (lane % half_rot) / ROTARY)).astype(np.float32)[None, :]
    phase = np.where(lane < half_rot, 0.0, np.pi / 2).astype(np.float32)[None, :]
    wide = (total, HEAD_PAD)
    return pl.pallas_call(
        tables_kernel,
        out_shape=(
            jax.ShapeDtypeStruct(wide, jnp.int32),
            jax.ShapeDtypeStruct((1, total), jnp.int32),
            jax.ShapeDtypeStruct(wide, jnp.float32),
            jax.ShapeDtypeStruct(wide, jnp.float32),
        ),
        in_specs=[SMEM] * 4 + [VMEM] * 2,
        out_specs=(VMEM,) * 4,
        compiler_params=pltpu.CompilerParams(vmem_limit_bytes=8 * MIB),
        name="tables",
    )(index, jnp.asarray(owner_table()), lens, sinks, jnp.asarray(inverse), jnp.asarray(phase))


def pages_kernel(index_ref, places_ref, table_ref, kv_ref, out_ref):
    pages = table_ref.shape[0]
    per_owner = pages // places_ref.shape[1]
    device, shift = index_ref[0], index_ref[1] * (pages // 2)
    for p in range(pages):
        place = places_ref[device, p // per_owner] * per_owner + p % per_owner
        row = pl.multiple_of(place * PAGE, PAGE)
        out_ref[lax.rem(table_ref[p] + shift, pages)] = kv_ref[pl.ds(row, PAGE), :]


def ordered_pages(index, page_table, kv):
    return pl.pallas_call(
        pages_kernel,
        out_shape=jax.ShapeDtypeStruct((page_table.shape[0], PAGE, kv.shape[1]), kv.dtype),
        in_specs=[SMEM] * 3 + [VMEM],
        out_specs=VMEM,
        compiler_params=pltpu.CompilerParams(vmem_limit_bytes=8 * MIB),
        name="ordered_pages",
    )(index, jnp.asarray(place_table()), page_table, kv)


def tile_at(t, width, base=0):
    return pl.ds(pl.multiple_of(base + t * width, 128), width)


def normalise(blocks, affine_ref, attn, mlp):
    rows = blocks[0].shape[0]
    feat = attn.shape[1]
    step = 512
    for b, block in enumerate(blocks):
        tail = block[:, feat:].astype(jnp.float32)
        average = tail[:, 0:1] + tail[:, 1:2] + tail[:, 2:3]
        scale = tail[:, 3:4] + tail[:, 4:5] + tail[:, 5:6]
        here = slice(b * rows, (b + 1) * rows)

        @pl.loop(0, feat // step)
        def _(t):
            at = tile_at(t, step)
            scaled = (block[:, at].astype(jnp.float32) - average) * scale
            attn[here, at] = (scaled * affine_ref[0:1, at] + affine_ref[2:3, at]).astype(jnp.bfloat16)
            mlp[here, at] = (scaled * affine_ref[1:2, at] + affine_ref[3:4, at]).astype(jnp.bfloat16)


def project_kernel(count, outs, first_call, index_ref, affine_ref, wq_ref, wk_ref, wv_ref, wu_ref, *refs):
    blocks, refs = refs[:count], refs[count:]
    mine_ref, refs = refs[0], refs[1:]
    sent_refs, refs = refs[: len(outs)], refs[len(outs) :]
    hidden = wu_ref.shape[1]
    width = 384
    tiles = hidden // width
    copies = []
    if first_call:
        held, (attn, mlp, sems) = refs[:4], refs[4:]
        copies = [
            pltpu.make_async_copy(src, dst, sems.at[i])
            for i, (src, dst) in enumerate(zip((wq_ref, wk_ref, wv_ref), held))
        ]
        for t in range(tiles):
            at = slice(t * width, (t + 1) * width)
            copies.append(pltpu.make_async_copy(wu_ref.at[:, at], held[3].at[:, at], sems.at[3 + t]))
        for copy in copies:
            copy.start()
        source = wu_ref
        wq_ref, wk_ref, wv_ref, wu_ref = held
    else:
        attn, mlp = refs
    rows = 2 * blocks[0].shape[0]
    half = wq_ref.shape[1] // 2
    normalise(blocks, affine_ref, attn, mlp)
    low, high = [], []
    for i, weight in enumerate((wq_ref, wk_ref, wv_ref)):
        if first_call:
            copies[i].wait()
        part = jnp.dot(attn[...], weight[...], preferred_element_type=jnp.float32)
        low.append(part[:, :half])
        high.append(part[:, half:])
    low = jnp.concatenate(low, axis=1).astype(jnp.bfloat16)
    high = jnp.concatenate(high, axis=1).astype(jnp.bfloat16)
    first = index_ref[1] == 0
    mine_ref[...] = jnp.where(first, low, high)
    send = jnp.where(first, high, low)
    send = [send[p * rows : (p + 1) * rows] for p in range(count // 2)]
    gap = -(3 * half * len(send)) % 128
    if gap:
        send.append(jnp.zeros((rows, gap), jnp.bfloat16))
    send = jnp.concatenate(send, axis=1)
    for ref, items in zip(sent_refs, outs):
        if items[-1] == "q":
            ref[:, hidden * (len(items) - 1) :] = send

    @pl.loop(0, tiles)
    def _(t):
        at = tile_at(t, width)
        if first_call:
            pltpu.make_async_copy(source.at[:, at], wu_ref.at[:, at], sems.at[3 + t]).wait()
        part = jnp.dot(mlp[...], wu_ref[:, at], preferred_element_type=jnp.float32)
        part = part.astype(jnp.bfloat16)
        for ref, items in zip(sent_refs, outs):
            for i, item in enumerate(items):
                if item != "q":
                    ref[:, tile_at(t, width, i * hidden)] = part[item * rows : (item + 1) * rows]


def project(n, affine, weights, blocks, outs, first_call=False):
    count = len(blocks)
    rows = 2 * blocks[0].shape[0]
    feat, cols = weights[0].shape
    hidden = weights[3].shape[1]
    sent = 3 * cols // 2 * (count // 2)
    sent += -sent % 128
    shapes = [jax.ShapeDtypeStruct((rows * count // 2, 3 * cols // 2), jnp.bfloat16)]
    for items in outs:
        width = sum(sent if item == "q" else hidden for item in items)
        shapes.append(jax.ShapeDtypeStruct((rows, width), jnp.bfloat16))
    scratch = [pltpu.VMEM((rows * count // 2, feat), jnp.bfloat16)] * 2
    if first_call:
        shapes += [jax.ShapeDtypeStruct(w.shape, w.dtype) for w in weights]
        scratch.append(pltpu.SemaphoreType.DMA((3 + hidden // 384,)))
    return pl.pallas_call(
        functools.partial(project_kernel, count, outs, first_call),
        out_shape=tuple(shapes),
        in_specs=[SMEM, VMEM] + [HBM if first_call else VMEM] * 4 + [VMEM] * count,
        out_specs=(VMEM,) * len(shapes),
        scratch_shapes=scratch,
        compiler_params=pltpu.CompilerParams(vmem_limit_bytes=(46 if first_call else 9) * MIB),
        name="project",
    )(n, affine, *weights, *blocks)


def attend_kernel(count, span, offsets, index_ref, bias_ref, cos_ref, sin_ref, query_ref, key_ref, *refs):
    mine, got = refs[:count], refs[count : 2 * count]
    att_ref, kv_ref, queries, keys, values = refs[2 * count :]
    heads = queries.shape[0]
    half = kv_ref.shape[1] // 2
    total = kv_ref.shape[0]
    half_rot = ROTARY // 2
    bias = jnp.where(index_ref[1] == 0, bias_ref[:, :half], bias_ref[:, half:])
    offset = 0
    for g in range(count):
        rows = mine[g].shape[0]
        at = slice(offset, offset + rows)
        offset += rows
        pieces = []
        for p in range(rows // got[g].shape[0]):
            begin = offsets[g] + 3 * half * p
            pieces.append(got[g][:, begin : begin + 3 * half])
        sent = jnp.concatenate(pieces, axis=0)
        summed = mine[g][...].astype(jnp.float32) + sent.astype(jnp.float32)
        cosine, sine = cos_ref[at, :], sin_ref[at, :]
        lane = lax.broadcasted_iota(jnp.int32, (rows, HEAD_PAD), 1)
        pad = jnp.zeros((rows, HEAD_PAD - HEAD_DIM), jnp.float32)
        for kind in range(3):
            kept = []
            for h in range(heads):
                begin = kind * half + h * HEAD_DIM
                u = summed[:, begin : begin + HEAD_DIM]
                u = u + bias[kind : kind + 1, h * HEAD_DIM : (h + 1) * HEAD_DIM]
                u = jnp.concatenate([u, pad], axis=1)
                if kind < 2:
                    other = jnp.where(
                        lane < half_rot,
                        pltpu.roll(u, HEAD_PAD - half_rot, 1),
                        pltpu.roll(u, half_rot, 1),
                    )
                    u = u * cosine + other * sine
                (queries, keys, values)[kind][h, at, :] = u.astype(jnp.bfloat16)
                kept.append(u[:, :HEAD_DIM])
            if kind > 0:
                kv_ref[at, (kind - 1) * half : kind * half] = jnp.concatenate(kept, axis=1).astype(
                    jnp.bfloat16
                )
    tile = 256
    for start in range(0, total, tile):
        at = slice(start, start + tile)
        info = query_ref[at, :]
        token, begin, end = info[:, 0:1], info[:, 1:2], info[:, 2:3]
        key_token = key_ref[...]
        near = key_token > token - span
        allowed = (key_token >= begin) & (key_token <= token) & (near | (key_token < end))
        outs = []
        for h in range(heads):
            scores = lax.dot_general(
                queries[h, at, :],
                keys[h],
                (((1,), (1,)), ((), ())),
                preferred_element_type=jnp.float32,
            ) * (1.0 / HEAD_DIM**0.5)
            masked = jnp.where(allowed, scores, -1e30)
            weights = jnp.exp(masked - jnp.max(masked, axis=1, keepdims=True))
            probs = weights / jnp.sum(weights, axis=1, keepdims=True)
            out = jnp.dot(probs.astype(jnp.bfloat16), values[h], preferred_element_type=jnp.float32)
            outs.append(out[:, :HEAD_DIM])
        side = start // (total // 2)
        att_ref[start % (total // 2) : start % (total // 2) + tile, side * half : (side + 1) * half] = (
            jnp.concatenate(outs, axis=1).astype(jnp.bfloat16)
        )


def attend(span, offsets, n, bias, cosine, sine, query_info, key_token, mine, got):
    count = len(mine)
    total = cosine.shape[0]
    half = mine[0].shape[1] // 3
    heads = half // HEAD_DIM
    scratch = pltpu.VMEM((heads, total, HEAD_PAD), jnp.bfloat16)
    return pl.pallas_call(
        functools.partial(attend_kernel, count, span, offsets),
        out_shape=(
            jax.ShapeDtypeStruct((total // 2, 2 * half), jnp.bfloat16),
            jax.ShapeDtypeStruct((total, 2 * half), jnp.bfloat16),
        ),
        in_specs=[SMEM] + [VMEM] * (5 + 2 * count),
        out_specs=(VMEM, VMEM),
        scratch_shapes=[scratch, scratch, scratch],
        compiler_params=pltpu.CompilerParams(vmem_limit_bytes=10 * MIB),
        name="attend",
    )(n, bias, cosine, sine, query_info, key_token, *mine, *got)


def gelu(u):
    return u * (1.0 + lax.erf(u * (0.5**0.5))) * 0.5


def down_kernel(count, bias_ref, wd_ref, *refs):
    mine, got = refs[:count], refs[count : 2 * count]
    out_ref, units = refs[2 * count :]
    rows = mine[0].shape[0]
    step = 384
    for i in range(count):

        @pl.loop(0, units.shape[1] // step)
        def _(t):
            at = tile_at(t, step)
            u = mine[i][:, at].astype(jnp.float32) + got[i][:, at].astype(jnp.float32)
            u = gelu(u + bias_ref[:, at])
            units[i * rows : (i + 1) * rows, at] = u.astype(jnp.bfloat16)

    width, tall = 512, 2 * rows
    for r in range(0, units.shape[0], tall):

        @pl.loop(0, wd_ref.shape[1] // width)
        def _(t):
            at = tile_at(t, width)
            here = slice(r, r + tall)
            out = jnp.dot(units[here, :], wd_ref[:, at], preferred_element_type=jnp.float32)
            out_ref[here, at] = out.astype(jnp.bfloat16)


def down(bias, mine, got, wd):
    count = len(mine)
    rows, hidden = mine[0].shape[0], wd.shape[0]
    return pl.pallas_call(
        functools.partial(down_kernel, count),
        out_shape=jax.ShapeDtypeStruct((count * rows, wd.shape[1]), jnp.bfloat16),
        in_specs=[VMEM] * (2 + 2 * count),
        out_specs=VMEM,
        scratch_shapes=[pltpu.VMEM((count * rows, hidden), jnp.bfloat16)],
        compiler_params=pltpu.CompilerParams(vmem_limit_bytes=6 * MIB),
        name="down",
    )(bias, wd, *mine, *got)


def attended_rows(ref, offset, rows):
    height, half = ref.shape[0], ref.shape[1] // 2
    side = offset // height
    return ref[offset % height : offset % height + rows, side * half : (side + 1) * half]


def mix_kernel(offsets, index_ref, down_ref, att_ref, other_ref, wo_ref, own_ref, sib_ref):
    half = att_ref.shape[1] // 2
    rows = own_ref.shape[0] // len(offsets)
    n = index_ref[1]
    here = pl.ds(pl.multiple_of(n * half, 16), half)
    there = pl.ds(pl.multiple_of((1 - n) * half, 16), half)
    mine = jnp.concatenate([attended_rows(att_ref, o, 2 * rows) for o in offsets], axis=0)
    other = jnp.concatenate([attended_rows(other_ref, o, 2 * rows) for o in offsets], axis=0)
    width = 512
    for c in range(0, own_ref.shape[1], width):
        at = slice(c, c + width)
        out = down_ref[:, at].astype(jnp.float32)
        out += jnp.dot(mine, wo_ref[here, at], preferred_element_type=jnp.float32)
        out += jnp.dot(other, wo_ref[there, at], preferred_element_type=jnp.float32)
        out = out.astype(jnp.bfloat16)
        for i in range(len(offsets)):
            own_ref[i * rows : (i + 1) * rows, at] = out[2 * i * rows : (2 * i + 1) * rows]
            sib_ref[i * rows : (i + 1) * rows, at] = out[(2 * i + 1) * rows : (2 * i + 2) * rows]


def mix(n, offsets, partial_down, att, other, wo):
    rows, feat = partial_down.shape
    shape = jax.ShapeDtypeStruct((rows // 2, feat), jnp.bfloat16)
    return pl.pallas_call(
        functools.partial(mix_kernel, offsets),
        out_shape=(shape, shape),
        in_specs=[SMEM] + [VMEM] * 4,
        out_specs=(VMEM, VMEM),
        compiler_params=pltpu.CompilerParams(vmem_limit_bytes=5 * MIB),
        name="mix",
    )(n, partial_down, att, other, wo)


def output_kernel(
    offset, column, index_ref, bias_ref, mine_ref, got_ref, att_ref, other_ref, wo_ref, wd_ref, own_ref, sib_ref, units
):
    rows = mine_ref.shape[0]
    half = att_ref.shape[1] // 2
    own_rows = own_ref.shape[0]
    step = 384

    @pl.loop(0, units.shape[1] // step)
    def _(t):
        at, there = tile_at(t, step), tile_at(t, step, column)
        u = mine_ref[:, there].astype(jnp.float32) + got_ref[:, there].astype(jnp.float32)
        units[:, at] = gelu(u + bias_ref[:, at]).astype(jnp.bfloat16)

    n = index_ref[1]
    here = pl.ds(pl.multiple_of(n * half, 16), half)
    there = pl.ds(pl.multiple_of((1 - n) * half, 16), half)
    mine = attended_rows(att_ref, offset, rows)
    other = attended_rows(other_ref, offset, rows)
    width = 512

    @pl.loop(0, wd_ref.shape[1] // width)
    def _(t):
        at = tile_at(t, width)
        out = jnp.dot(units[...], wd_ref[:, at], preferred_element_type=jnp.float32)
        out += jnp.dot(mine, wo_ref[here, at], preferred_element_type=jnp.float32)
        out += jnp.dot(other, wo_ref[there, at], preferred_element_type=jnp.float32)
        out = out.astype(jnp.bfloat16)
        own_ref[:, at] = out[:own_rows]
        sib_ref[:, at] = out[own_rows:]


def output(n, offset, column, bias, mine, got, att, other, wo, wd):
    rows, hidden = mine.shape[0], wd.shape[0]
    shape = jax.ShapeDtypeStruct((rows // 2, wd.shape[1]), jnp.bfloat16)
    return pl.pallas_call(
        functools.partial(output_kernel, offset, column),
        out_shape=(shape, shape),
        in_specs=[SMEM] + [VMEM] * 7,
        out_specs=(VMEM, VMEM),
        scratch_shapes=[pltpu.VMEM((rows, hidden), jnp.bfloat16)],
        compiler_params=pltpu.CompilerParams(vmem_limit_bytes=5 * MIB),
        name="output",
    )(n, bias, mine, got, att, other, wo, wd)


def after(*values):
    return lax.optimization_barrier(values)


def local_ring(
    hidden_in,
    w_query,
    w_key,
    w_value,
    qkv_bias,
    w_up,
    up_bias,
    w_attn_out,
    w_down,
    out_bias,
    norm_gain,
    norm_bias,
    seq_lens,
    sink_count,
    page_table,
):
    device = lax.axis_index("wide").astype(jnp.int32).reshape(1)
    n = lax.axis_index("narrow").astype(jnp.int32)
    n_arg = n.reshape(1)
    rows, feat = hidden_in.shape
    total_tokens = rows * lax.axis_size("wide")
    half = w_query.shape[1] // 2

    fwd_pairs, bwd_pairs, swap_pairs = [], [], []
    for p in range(CHIPS):
        here, next_chip = CHIP_RING[p], CHIP_RING[(p + 1) % CHIPS]
        fwd_pairs += [(2 * here, 2 * next_chip), (2 * next_chip + 1, 2 * here + 1)]
        bwd_pairs += [(2 * next_chip, 2 * here), (2 * here + 1, 2 * next_chip + 1)]
        swap_pairs += [(2 * here, 2 * here + 1), (2 * here + 1, 2 * here)]
    fwd = lambda v: lax.ppermute(v, "wide", fwd_pairs)
    bwd = lambda v: lax.ppermute(v, "wide", bwd_pairs)
    swap = lambda v: lax.ppermute(v, "wide", swap_pairs)
    cross = lambda v: lax.ppermute(v, "narrow", [(0, 1), (1, 0)])

    first_side, n_arg = after(n == 0, n_arg)
    sums, index = pl.pallas_call(
        sums_kernel,
        out_shape=(
            jax.ShapeDtypeStruct((rows, STAT), jnp.float32),
            jax.ShapeDtypeStruct((2,), jnp.int32),
        ),
        in_specs=[SMEM, SMEM, VMEM],
        out_specs=(VMEM, SMEM),
        compiler_params=pltpu.CompilerParams(vmem_limit_bytes=8 * MIB),
        name="row_sums",
    )(device, n_arg, hidden_in)
    first_block, affine = pl.pallas_call(
        block_kernel,
        out_shape=(
            jax.ShapeDtypeStruct((rows, feat + STAT), jnp.bfloat16),
            jax.ShapeDtypeStruct((4, feat), jnp.float32),
        ),
        in_specs=[VMEM] * 5,
        out_specs=(VMEM, VMEM),
        compiler_params=pltpu.CompilerParams(vmem_limit_bytes=8 * MIB),
        name="first_block",
    )(hidden_in, norm_gain, norm_bias, sums, cross(sums))

    up_row = up_bias[None, :]

    def add(*terms):
        return sum(t.astype(jnp.float32) for t in terms).astype(jnp.bfloat16)

    def finish(name, u, v, column=0):
        return output(
            index, PAIRS.index(name) * 2 * rows, column, up_row, u, v, att, other, w_attn_out, w_down
        )

    def pair(halves, *running):
        return add(halves[0], swap(halves[1]), *running)

    per_device = page_table.shape[0] // 2
    hidden = w_up.shape[1]
    o0 = first_block
    f1, b1, s0 = fwd(o0), bwd(o0), swap(o0)
    kept0, send0, *weights = project(
        index, affine, (w_query, w_key, w_value, w_up), [o0, s0], ((0, "q"),), True
    )
    f1, b1, send0, kept0 = after(f1, b1, send0, kept0)
    got0 = cross(send0)
    f2, b2 = fwd(f1), bwd(b1)
    kept1, send1, u_f1 = project(
        index, affine, weights, [f1, swap(f1), b1, swap(b1)], ((1, "q"), (0,))
    )
    f2, b2, got0, send1, u_f1 = after(f2, b2, got0, send1, u_f1)
    got1 = cross(send1)
    f3 = fwd(f2)
    kept2, send2, u_b2 = project(
        index, affine, weights, [f2, swap(f2), b2, swap(b2)], ((0, "q"), (1,))
    )
    f3, b2, got1, send2, u_b2, late_index = after(f3, b2, got1, send2, u_b2, index)
    got2 = cross(send2)
    f4, b3 = fwd(f3), bwd(b2)
    kept3, send3 = project(index, affine, weights, [f3, swap(f3)], ((0, "q"),))
    query_info, key_token, cosine, sine = tables(total_tokens, late_index, seq_lens, sink_count)
    b3, f4, got2, send3, query_info, key_token, cosine, sine = after(
        b3, f4, got2, send3, query_info, key_token, cosine, sine
    )
    got3 = cross(send3)
    kept4, send4, u_far = project(
        index, affine, weights, [b3, swap(b3), f4, swap(f4)], (("q",), (1, 0))
    )
    got3, send4, u_far = after(got3, send4, u_far)
    got4 = cross(send4)
    early_pairs = ("o0", "b1", "f2", "f3")
    early = down(up_row, [send0, send1, send2, send3], [got0, got1, got2, got3], w_down)
    got4, early, u_far = after(got4, early, u_far)
    v_far = cross(u_far)
    att, kv = attend(
        total_tokens // 16, (hidden, hidden, hidden, hidden, 0), index, qkv_bias, cosine, sine,
        query_info, key_token, [kept0, kept1, kept2, kept3, kept4], [got0, got1, got2, got3, got4],
    )
    v_far, att = after(v_far, att)
    other = cross(att)
    other, u_b2, u_f1, kv = after(other, u_b2, u_f1, kv)
    v_b2 = cross(u_b2)
    y_f4 = finish("f4", u_far, v_far)
    s_f4, early = after(pair(y_f4), early)
    r_b = bwd(s_f4)
    y_b3 = finish("b3", u_far, v_far, hidden)
    m_own, m_sib = mix(
        index, tuple(PAIRS.index(p) * 2 * rows for p in early_pairs), early, att, other, w_attn_out
    )
    m_got = swap(m_sib)
    r_b, y_b3, m_own, m_got, u_f1, kv = after(r_b, y_b3, m_own, m_got, u_f1, kv)

    def mixed(name):
        at = slice(early_pairs.index(name) * rows, (early_pairs.index(name) + 1) * rows)
        return m_own[at], m_got[at]

    v_f1 = cross(u_f1)
    r_b, r_f = bwd(add(r_b, *mixed("f3"))), fwd(pair(y_b3))
    y_b2 = finish("b2", u_b2, v_b2)
    paged = ordered_pages(index, page_table, kv)
    r_b, r_f, y_b2, m_own, m_got, paged = after(r_b, r_f, y_b2, m_own, m_got, paged)
    cache_mine, cache_got = paged[:per_device], cross(paged[per_device:])
    r_b, r_f = bwd(add(r_b, *mixed("f2"))), fwd(pair(y_b2, r_f))
    y_f1 = finish("f1", u_f1, v_f1)
    r_b, r_f, y_f1, cache_mine, cache_got = after(r_b, r_f, y_f1, cache_mine, cache_got)
    r_f, r_b = fwd(add(r_f, *mixed("b1"))), bwd(pair(y_f1, r_b))
    summed = sum(t.astype(jnp.float32) for t in (r_b, r_f, *mixed("o0")))
    hidden_out = (hidden_in.astype(jnp.float32) + summed + out_bias).astype(jnp.bfloat16)
    left = jnp.where(first_side, cache_mine, cache_got)
    right = jnp.where(first_side, cache_got, cache_mine)
    paged_cache = jnp.stack(
        [
            jnp.concatenate([left[..., :half], right[..., :half]], axis=-1),
            jnp.concatenate([left[..., half:], right[..., half:]], axis=-1),
        ]
    )
    return (hidden_out, paged_cache)


def solution(mesh):
    in_specs = (
        P("wide", "narrow"),
        P("narrow", "wide"),
        P("narrow", "wide"),
        P("narrow", "wide"),
        P(None, "wide"),
        P("narrow", "wide"),
        P("wide"),
        P("wide", "narrow"),
        P("wide", "narrow"),
        P("narrow"),
        P(None, "narrow"),
        P(None, "narrow"),
        P(),
        P(),
        P(),
    )
    out_specs = (P("wide", "narrow"), P(None, "narrow", None, "wide"))
    ringed = mesh.shape["wide"] == 2 * CHIPS and mesh.shape["narrow"] == 2
    local = local_ring if ringed else local_generic
    return jax.shard_map(local, mesh=mesh, in_specs=in_specs, out_specs=out_specs, check_vma=False)
```

```python
import functools

import jax
import jax.numpy as jnp
import numpy as np
from jax import lax
from jax.experimental import pallas as pl
from jax.experimental.pallas import tpu as pltpu
from jax.sharding import PartitionSpec as P

D = 6144
HEAD_DIM = 96
ROTARY = 24
PAGE = 16


def segment_info(token_index, seq_lens, sink_count):
    seq_ends = jnp.cumsum(seq_lens)
    seq_starts = seq_ends - seq_lens
    inside = (token_index[:, None] >= seq_starts[None, :]) & (
        token_index[:, None] < seq_ends[None, :]
    )
    member = inside.astype(jnp.int32)
    seq_number = jnp.arange(seq_lens.shape[0], dtype=jnp.int32)
    segment = jnp.sum(member * seq_number[None, :], axis=1)
    position = token_index - jnp.sum(member * seq_starts[None, :], axis=1)
    sink_limit = jnp.sum(member * sink_count[None, :], axis=1)
    return (segment, position, sink_limit)


def rotate(values, position):
    half_rot = ROTARY // 2
    freq_index = jnp.arange(half_rot, dtype=jnp.float32)
    inverse = jnp.power(jnp.float32(10000.0), -2.0 * freq_index / ROTARY)
    angles = position.astype(jnp.float32)[:, None] * inverse[None, :]
    cosine = jnp.cos(angles)[:, None, :]
    sine_part = jnp.sin(angles)[:, None, :]
    first_half = values[..., :half_rot]
    second_half = values[..., half_rot:ROTARY]
    return jnp.concatenate(
        [
            first_half * cosine - second_half * sine_part,
            second_half * cosine + first_half * sine_part,
            values[..., ROTARY:],
        ],
        axis=-1,
    )


def local_generic(
    hidden_in,
    w_query,
    w_key,
    w_value,
    qkv_bias,
    w_up,
    up_bias,
    w_attn_out,
    w_down,
    out_bias,
    norm_gain,
    norm_bias,
    seq_lens,
    sink_count,
    page_table,
):
    wide_count = lax.axis_size("wide")
    narrow_count = lax.axis_size("narrow")
    narrow_index = lax.axis_index("narrow")
    tok_local, feat_local = hidden_in.shape
    sub_rows = tok_local // narrow_count
    total_tokens = tok_local * wide_count
    query_rows = wide_count * sub_rows
    head_cols = w_query.shape[1]
    heads_local = head_cols // HEAD_DIM
    as_float = hidden_in.astype(jnp.float32)
    partial_sum = jnp.sum(as_float, axis=1)
    partial_square = jnp.sum(as_float * as_float, axis=1)
    total_sum, total_square = lax.psum((partial_sum, partial_square), "narrow")
    average = total_sum / D
    variance = total_square / D - average * average
    scaled = (as_float - average[:, None]) * lax.rsqrt(variance + 1e-05)[:, None]
    attn_normed = (scaled * norm_gain[0] + norm_bias[0]).astype(jnp.bfloat16)
    mlp_normed = (scaled * norm_gain[1] + norm_bias[1]).astype(jnp.bfloat16)
    stacked = jnp.stack([attn_normed, mlp_normed]).reshape(2, narrow_count, sub_rows, feat_local)
    gathered = lax.all_gather(stacked, "wide", axis=2, tiled=True).reshape(
        2, total_tokens, feat_local
    )
    local_order = jnp.arange(query_rows, dtype=jnp.int32)
    local_tokens = (
        local_order // sub_rows * tok_local + narrow_index * sub_rows + local_order % sub_rows
    )
    local_seg, local_pos, local_sink = segment_info(local_tokens, seq_lens, sink_count)
    all_order = jnp.arange(total_tokens, dtype=jnp.int32)
    all_tokens = (
        all_order % query_rows // sub_rows * tok_local
        + all_order // query_rows * sub_rows
        + all_order % sub_rows
    )
    all_seg, all_pos, all_sink = segment_info(all_tokens, seq_lens, sink_count)
    qkv_weight = jnp.concatenate([w_query, w_key, w_value], axis=1)
    attn_part = gathered[0]
    mlp_part = gathered[1]
    summed = lax.psum_scatter(
        jnp.concatenate(
            [
                jnp.dot(attn_part, qkv_weight, preferred_element_type=jnp.float32),
                jnp.dot(mlp_part, w_up, preferred_element_type=jnp.float32),
            ],
            axis=1,
        ).astype(jnp.bfloat16),
        "narrow",
        scatter_dimension=0,
        tiled=True,
    ).astype(jnp.float32)
    query_sum = summed[:, :head_cols]
    key_sum = summed[:, head_cols : 2 * head_cols]
    value_sum = summed[:, 2 * head_cols : 3 * head_cols]
    unit_sum = summed[:, 3 * head_cols :]
    keys_local = (
        rotate((key_sum + qkv_bias[1]).reshape(query_rows, heads_local, HEAD_DIM), local_pos)
        .astype(jnp.bfloat16)
        .reshape(query_rows, head_cols)
    )
    values_local = (value_sum + qkv_bias[2]).astype(jnp.bfloat16)
    all_keys, all_values = (
        lax.all_gather(keys_local, "narrow", axis=0, tiled=True),
        lax.all_gather(values_local, "narrow", axis=0, tiled=True),
    )
    queries = rotate(
        (query_sum + qkv_bias[0]).reshape(query_rows, heads_local, HEAD_DIM), local_pos
    ).astype(jnp.bfloat16)
    hidden_units = jax.nn.gelu(unit_sum + up_bias, approximate=False).astype(jnp.bfloat16)
    window_span = total_tokens // 16
    allowed = (local_seg[:, None] == all_seg[None, :]) & (all_pos[None, :] <= local_pos[:, None])
    allowed = allowed & (
        (local_pos[:, None] - all_pos[None, :] < window_span)
        | (all_pos[None, :] < local_sink[:, None])
    )
    key_heads = all_keys.reshape(total_tokens, heads_local, HEAD_DIM)
    value_heads = all_values.reshape(total_tokens, heads_local, HEAD_DIM)
    scores = jnp.einsum("qhd,khd->hqk", queries, key_heads, preferred_element_type=jnp.float32) * (
        1.0 / HEAD_DIM**0.5
    )
    masked = jnp.where(allowed[None], scores, jnp.float32(-1e30))
    top_score = jnp.max(masked, axis=2, keepdims=True)
    weights = jnp.exp(masked - top_score)
    probs = (weights / jnp.sum(weights, axis=2, keepdims=True)).astype(jnp.bfloat16)
    attended = (
        jnp.einsum("hqk,khd->qhd", probs, value_heads, preferred_element_type=jnp.float32)
        .astype(jnp.bfloat16)
        .reshape(query_rows, head_cols)
    )
    full_out, full_down = (
        lax.all_gather(w_attn_out, "narrow", axis=1, tiled=True),
        lax.all_gather(w_down, "narrow", axis=1, tiled=True),
    )
    attn_part = attended
    own_rows = lax.psum_scatter(
        (
            jnp.dot(attn_part, full_out, preferred_element_type=jnp.float32)
            + jnp.dot(hidden_units, full_down, preferred_element_type=jnp.float32)
        ).astype(jnp.bfloat16),
        "wide",
        scatter_dimension=0,
        tiled=True,
    ).astype(jnp.float32)
    combined = lax.all_to_all(
        own_rows.astype(jnp.bfloat16), "narrow", split_axis=1, concat_axis=0, tiled=True
    ).astype(own_rows.dtype)
    hidden_out = (as_float + combined + out_bias).astype(jnp.bfloat16)
    pages_local = page_table.shape[0] // narrow_count
    slot_ids = narrow_index * pages_local + jnp.arange(pages_local, dtype=jnp.int32)
    matches = (page_table[None, :] == slot_ids[:, None]).astype(jnp.int32)
    source_page = jnp.sum(
        matches * jnp.arange(page_table.shape[0], dtype=jnp.int32)[None, :], axis=1
    )
    token_ids = (source_page[:, None] * PAGE + jnp.arange(PAGE, dtype=jnp.int32)[None, :]).reshape(
        -1
    )
    gather_rows = (
        token_ids % tok_local // sub_rows * query_rows
        + token_ids // tok_local * sub_rows
        + token_ids % sub_rows
    )
    cache_keys = jnp.take(all_keys, gather_rows, axis=0).reshape(pages_local, PAGE, head_cols)
    cache_values = jnp.take(all_values, gather_rows, axis=0).reshape(pages_local, PAGE, head_cols)
    paged_cache = jnp.stack([cache_keys, cache_values])
    return (hidden_out, paged_cache)


CHIP_RING = (0, 2, 4, 6, 7, 5, 3, 1)
CHIPS = len(CHIP_RING)
PAIRS = ("o0", "f1", "b1", "f2", "b2", "f3", "b3", "f4")
STAT = 128
HEAD_PAD = 128
LANE_GROUP = 32
MIB = 1 << 20
VMEM = pl.BlockSpec(memory_space=pltpu.VMEM)
HBM = pl.BlockSpec(memory_space=pltpu.HBM)
SMEM = pl.BlockSpec(memory_space=pltpu.SMEM)


def owner_table():
    table = np.zeros((2 * CHIPS, 2 * CHIPS), np.int32)
    for place, chip in enumerate(CHIP_RING):
        for core in range(2):
            order = []
            for pair in PAIRS:
                shift = (-1 if pair[0] == "f" else 1) * int(pair[1]) * (1 - 2 * core)
                order.append(CHIP_RING[(place + shift) % CHIPS] * 2 + core)
                order.append(CHIP_RING[(place - shift) % CHIPS] * 2 + 1 - core)
            table[2 * chip + core] = order
    return table


def place_table():
    owners = owner_table()
    table = np.zeros_like(owners)
    for device in range(owners.shape[0]):
        table[device, owners[device]] = np.arange(owners.shape[1])
    return table


def sums_kernel(device_ref, n_ref, x_ref, out_ref, index_ref):
    x = x_ref[...].astype(jnp.float32)
    first = jnp.sum(x, axis=1, keepdims=True)
    second = jnp.sum(x * x, axis=1, keepdims=True)
    lane = lax.broadcasted_iota(jnp.int32, out_ref.shape, 1)
    out_ref[...] = jnp.where(lane == 0, first, jnp.where(lane == 1, second, 0.0))
    index_ref[0] = device_ref[0]
    index_ref[1] = n_ref[0]


def block_kernel(x_ref, gain_ref, bias_ref, here_ref, there_ref, out_ref, affine_ref):
    feat = x_ref.shape[1]
    total = here_ref[...] + there_ref[...]
    average = total[:, 0:1] / D
    variance = total[:, 1:2] / D - average * average
    scale = lax.rsqrt(variance + 1e-05)
    lane = lax.broadcasted_iota(jnp.int32, (x_ref.shape[0], STAT), 1)
    tail = jnp.zeros((x_ref.shape[0], STAT), jnp.float32)
    for start, value in ((0, average), (3, scale)):
        for term in range(3):
            piece = value.astype(jnp.bfloat16).astype(jnp.float32)
            tail = jnp.where(lane == start + term, piece, tail)
            value = value - piece
    out_ref[:, :feat] = x_ref[...]
    out_ref[:, feat:] = tail.astype(jnp.bfloat16)
    affine_ref[0:2, :] = gain_ref[...]
    affine_ref[2:4, :] = bias_ref[...]


def tables_kernel(index_ref, owners_ref, lens_ref, sinks_ref, inverse_ref, phase_ref, info_ref, key_ref, cos_ref, sin_ref):
    device = index_ref[0]
    blocks = owners_ref.shape[1]
    rows = info_ref.shape[0] // blocks
    half_rot = ROTARY // 2
    lane = lax.broadcasted_iota(jnp.int32, (rows, HEAD_PAD), 1)
    sub = lax.broadcasted_iota(jnp.int32, (rows, HEAD_PAD), 0)
    key_lane = lax.broadcasted_iota(jnp.int32, key_ref.shape, 1)
    key = key_lane
    shared = HEAD_PAD // LANE_GROUP
    for base in range(0, blocks, shared):
        position = jnp.zeros((rows, HEAD_PAD), jnp.int32)
        for g in range(shared):
            j = base + g
            first = owners_ref[device, j] * rows
            key = jnp.where(key_lane // rows == j, first + key_lane - j * rows, key)
            token = first + sub
            begin, end = jnp.zeros_like(token), jnp.zeros_like(token)
            start = jnp.int32(0)
            for s in range(lens_ref.shape[0]):
                inside = (token >= start) & (token < start + lens_ref[s])
                begin = jnp.where(inside, start, begin)
                end = jnp.where(inside, start + sinks_ref[s], end)
                start = start + lens_ref[s]
            info_ref[j * rows : (j + 1) * rows, :] = jnp.where(
                lane == 0, token, jnp.where(lane == 1, begin, end)
            )
            position = jnp.where(lane // LANE_GROUP == g, token - begin, position)
        waves = jnp.cos(position.astype(jnp.float32) * inverse_ref[...] - phase_ref[...])
        for g in range(shared):
            at = slice((base + g) * rows, (base + g + 1) * rows)
            here = pltpu.roll(waves, (HEAD_PAD - g * LANE_GROUP) % HEAD_PAD, 1)
            later = pltpu.roll(waves, (HEAD_PAD - g * LANE_GROUP + half_rot) % HEAD_PAD, 1)
            before = pltpu.roll(waves, (2 * HEAD_PAD - g * LANE_GROUP - half_rot) % HEAD_PAD, 1)
            cosine = jnp.where(lane < half_rot, here, later)
            cos_ref[at, :] = jnp.where(lane < ROTARY, cosine, 1.0)
            sine = jnp.where(lane < half_rot, -before, here)
            sin_ref[at, :] = jnp.where(lane < ROTARY, sine, 0.0)
    key_ref[...] = key


def tables(total, index, lens, sinks):
    half_rot = ROTARY // 2
    lane = np.arange(HEAD_PAD) % LANE_GROUP
    inverse = (10000.0 ** (-2.0 * (lane % half_rot) / ROTARY)).astype(np.float32)[None, :]
    phase = np.where(lane < half_rot, 0.0, np.pi / 2).astype(np.float32)[None, :]
    wide = (total, HEAD_PAD)
    return pl.pallas_call(
        tables_kernel,
        out_shape=(
            jax.ShapeDtypeStruct(wide, jnp.int32),
            jax.ShapeDtypeStruct((1, total), jnp.int32),
            jax.ShapeDtypeStruct(wide, jnp.float32),
            jax.ShapeDtypeStruct(wide, jnp.float32),
        ),
        in_specs=[SMEM] * 4 + [VMEM] * 2,
        out_specs=(VMEM,) * 4,
        compiler_params=pltpu.CompilerParams(vmem_limit_bytes=8 * MIB),
        name="tables",
    )(index, jnp.asarray(owner_table()), lens, sinks, jnp.asarray(inverse), jnp.asarray(phase))


def pages_kernel(index_ref, places_ref, table_ref, kv_ref, out_ref):
    pages = table_ref.shape[0]
    per_owner = pages // places_ref.shape[1]
    device, shift = index_ref[0], index_ref[1] * (pages // 2)
    for p in range(pages):
        place = places_ref[device, p // per_owner] * per_owner + p % per_owner
        row = pl.multiple_of(place * PAGE, PAGE)
        out_ref[lax.rem(table_ref[p] + shift, pages)] = kv_ref[pl.ds(row, PAGE), :]


def ordered_pages(index, page_table, kv):
    return pl.pallas_call(
        pages_kernel,
        out_shape=jax.ShapeDtypeStruct((page_table.shape[0], PAGE, kv.shape[1]), kv.dtype),
        in_specs=[SMEM] * 3 + [VMEM],
        out_specs=VMEM,
        compiler_params=pltpu.CompilerParams(vmem_limit_bytes=8 * MIB),
        name="ordered_pages",
    )(index, jnp.asarray(place_table()), page_table, kv)


def normalise(blocks, affine_ref, attn, mlp):
    rows = blocks[0].shape[0]
    feat = attn.shape[1]
    step = 512
    for b, block in enumerate(blocks):
        tail = block[:, feat:].astype(jnp.float32)
        average = tail[:, 0:1] + tail[:, 1:2] + tail[:, 2:3]
        scale = tail[:, 3:4] + tail[:, 4:5] + tail[:, 5:6]
        here = slice(b * rows, (b + 1) * rows)
        for c in range(0, feat, step):
            at = slice(c, c + step)
            scaled = (block[:, at].astype(jnp.float32) - average) * scale
            attn[here, at] = (scaled * affine_ref[0:1, at] + affine_ref[2:3, at]).astype(jnp.bfloat16)
            mlp[here, at] = (scaled * affine_ref[1:2, at] + affine_ref[3:4, at]).astype(jnp.bfloat16)


def project_kernel(count, outs, first_call, index_ref, affine_ref, wq_ref, wk_ref, wv_ref, wu_ref, *refs):
    blocks, refs = refs[:count], refs[count:]
    mine_ref, refs = refs[0], refs[1:]
    sent_refs, refs = refs[: len(outs)], refs[len(outs) :]
    hidden = wu_ref.shape[1]
    width = 384
    tiles = hidden // width
    copies = []
    if first_call:
        held, (attn, mlp, sems) = refs[:4], refs[4:]
        copies = [
            pltpu.make_async_copy(src, dst, sems.at[i])
            for i, (src, dst) in enumerate(zip((wq_ref, wk_ref, wv_ref), held))
        ]
        for t in range(tiles):
            at = slice(t * width, (t + 1) * width)
            copies.append(pltpu.make_async_copy(wu_ref.at[:, at], held[3].at[:, at], sems.at[3 + t]))
        for copy in copies:
            copy.start()
        wq_ref, wk_ref, wv_ref, wu_ref = held
    else:
        attn, mlp = refs
    rows = 2 * blocks[0].shape[0]
    half = wq_ref.shape[1] // 2
    normalise(blocks, affine_ref, attn, mlp)
    low, high = [], []
    for i, weight in enumerate((wq_ref, wk_ref, wv_ref)):
        if first_call:
            copies[i].wait()
        part = jnp.dot(attn[...], weight[...], preferred_element_type=jnp.float32)
        low.append(part[:, :half])
        high.append(part[:, half:])
    low = jnp.concatenate(low, axis=1).astype(jnp.bfloat16)
    high = jnp.concatenate(high, axis=1).astype(jnp.bfloat16)
    first = index_ref[1] == 0
    mine_ref[...] = jnp.where(first, low, high)
    send = jnp.where(first, high, low)
    send = [send[p * rows : (p + 1) * rows] for p in range(count // 2)]
    gap = -(3 * half * len(send)) % 128
    if gap:
        send.append(jnp.zeros((rows, gap), jnp.bfloat16))
    send = jnp.concatenate(send, axis=1)
    for ref, items in zip(sent_refs, outs):
        if items[-1] == "q":
            ref[:, hidden * (len(items) - 1) :] = send
    for t in range(tiles):
        if first_call:
            copies[3 + t].wait()
        at = slice(t * width, (t + 1) * width)
        part = jnp.dot(mlp[...], wu_ref[:, at], preferred_element_type=jnp.float32)
        part = part.astype(jnp.bfloat16)
        for ref, items in zip(sent_refs, outs):
            for i, item in enumerate(items):
                if item != "q":
                    begin = i * hidden + t * width
                    ref[:, begin : begin + width] = part[item * rows : (item + 1) * rows]


def project(n, affine, weights, blocks, outs, first_call=False):
    count = len(blocks)
    rows = 2 * blocks[0].shape[0]
    feat, cols = weights[0].shape
    hidden = weights[3].shape[1]
    sent = 3 * cols // 2 * (count // 2)
    sent += -sent % 128
    shapes = [jax.ShapeDtypeStruct((rows * count // 2, 3 * cols // 2), jnp.bfloat16)]
    for items in outs:
        width = sum(sent if item == "q" else hidden for item in items)
        shapes.append(jax.ShapeDtypeStruct((rows, width), jnp.bfloat16))
    scratch = [pltpu.VMEM((rows * count // 2, feat), jnp.bfloat16)] * 2
    if first_call:
        shapes += [jax.ShapeDtypeStruct(w.shape, w.dtype) for w in weights]
        scratch.append(pltpu.SemaphoreType.DMA((3 + hidden // 384,)))
    return pl.pallas_call(
        functools.partial(project_kernel, count, outs, first_call),
        out_shape=tuple(shapes),
        in_specs=[SMEM, VMEM] + [HBM if first_call else VMEM] * 4 + [VMEM] * count,
        out_specs=(VMEM,) * len(shapes),
        scratch_shapes=scratch,
        compiler_params=pltpu.CompilerParams(vmem_limit_bytes=(46 if first_call else 9) * MIB),
        name="project",
    )(n, affine, *weights, *blocks)


def attend_kernel(count, span, offsets, index_ref, bias_ref, cos_ref, sin_ref, query_ref, key_ref, *refs):
    mine, got = refs[:count], refs[count : 2 * count]
    att_ref, kv_ref, queries, keys, values = refs[2 * count :]
    heads = queries.shape[0]
    half = kv_ref.shape[1] // 2
    total = kv_ref.shape[0]
    half_rot = ROTARY // 2
    bias = jnp.where(index_ref[1] == 0, bias_ref[:, :half], bias_ref[:, half:])
    offset = 0
    for g in range(count):
        rows = mine[g].shape[0]
        at = slice(offset, offset + rows)
        offset += rows
        pieces = []
        for p in range(rows // got[g].shape[0]):
            begin = offsets[g] + 3 * half * p
            pieces.append(got[g][:, begin : begin + 3 * half])
        sent = jnp.concatenate(pieces, axis=0)
        summed = mine[g][...].astype(jnp.float32) + sent.astype(jnp.float32)
        cosine, sine = cos_ref[at, :], sin_ref[at, :]
        lane = lax.broadcasted_iota(jnp.int32, (rows, HEAD_PAD), 1)
        pad = jnp.zeros((rows, HEAD_PAD - HEAD_DIM), jnp.float32)
        for kind in range(3):
            kept = []
            for h in range(heads):
                begin = kind * half + h * HEAD_DIM
                u = summed[:, begin : begin + HEAD_DIM]
                u = u + bias[kind : kind + 1, h * HEAD_DIM : (h + 1) * HEAD_DIM]
                u = jnp.concatenate([u, pad], axis=1)
                if kind < 2:
                    other = jnp.where(
                        lane < half_rot,
                        pltpu.roll(u, HEAD_PAD - half_rot, 1),
                        pltpu.roll(u, half_rot, 1),
                    )
                    u = u * cosine + other * sine
                (queries, keys, values)[kind][h, at, :] = u.astype(jnp.bfloat16)
                kept.append(u[:, :HEAD_DIM])
            if kind > 0:
                kv_ref[at, (kind - 1) * half : kind * half] = jnp.concatenate(kept, axis=1).astype(
                    jnp.bfloat16
                )
    tile = 256
    for start in range(0, total, tile):
        at = slice(start, start + tile)
        info = query_ref[at, :]
        token, begin, end = info[:, 0:1], info[:, 1:2], info[:, 2:3]
        key_token = key_ref[...]
        near = key_token > token - span
        allowed = (key_token >= begin) & (key_token <= token) & (near | (key_token < end))
        outs = []
        for h in range(heads):
            scores = lax.dot_general(
                queries[h, at, :],
                keys[h],
                (((1,), (1,)), ((), ())),
                preferred_element_type=jnp.float32,
            ) * (1.0 / HEAD_DIM**0.5)
            masked = jnp.where(allowed, scores, -1e30)
            weights = jnp.exp(masked - jnp.max(masked, axis=1, keepdims=True))
            probs = weights / jnp.sum(weights, axis=1, keepdims=True)
            out = jnp.dot(probs.astype(jnp.bfloat16), values[h], preferred_element_type=jnp.float32)
            outs.append(out[:, :HEAD_DIM])
        side = start // (total // 2)
        att_ref[start % (total // 2) : start % (total // 2) + tile, side * half : (side + 1) * half] = (
            jnp.concatenate(outs, axis=1).astype(jnp.bfloat16)
        )


def attend(span, offsets, n, bias, cosine, sine, query_info, key_token, mine, got):
    count = len(mine)
    total = cosine.shape[0]
    half = mine[0].shape[1] // 3
    heads = half // HEAD_DIM
    scratch = pltpu.VMEM((heads, total, HEAD_PAD), jnp.bfloat16)
    return pl.pallas_call(
        functools.partial(attend_kernel, count, span, offsets),
        out_shape=(
            jax.ShapeDtypeStruct((total // 2, 2 * half), jnp.bfloat16),
            jax.ShapeDtypeStruct((total, 2 * half), jnp.bfloat16),
        ),
        in_specs=[SMEM] + [VMEM] * (5 + 2 * count),
        out_specs=(VMEM, VMEM),
        scratch_shapes=[scratch, scratch, scratch],
        compiler_params=pltpu.CompilerParams(vmem_limit_bytes=10 * MIB),
        name="attend",
    )(n, bias, cosine, sine, query_info, key_token, *mine, *got)


def gelu(u):
    return u * (1.0 + lax.erf(u * (0.5**0.5))) * 0.5


def down_kernel(count, bias_ref, wd_ref, *refs):
    mine, got = refs[:count], refs[count : 2 * count]
    out_ref, units = refs[2 * count :]
    rows = mine[0].shape[0]
    step = 384
    for i in range(count):
        for c in range(0, units.shape[1], step):
            at = slice(c, c + step)
            u = mine[i][:, at].astype(jnp.float32) + got[i][:, at].astype(jnp.float32)
            u = gelu(u + bias_ref[:, at])
            units[i * rows : (i + 1) * rows, at] = u.astype(jnp.bfloat16)
    width = 512
    for c in range(0, wd_ref.shape[1], width):
        at = slice(c, c + width)
        out = jnp.dot(units[...], wd_ref[:, at], preferred_element_type=jnp.float32)
        out_ref[:, at] = out.astype(jnp.bfloat16)


def down(bias, mine, got, wd):
    count = len(mine)
    rows, hidden = mine[0].shape[0], wd.shape[0]
    return pl.pallas_call(
        functools.partial(down_kernel, count),
        out_shape=jax.ShapeDtypeStruct((count * rows, wd.shape[1]), jnp.bfloat16),
        in_specs=[VMEM] * (2 + 2 * count),
        out_specs=VMEM,
        scratch_shapes=[pltpu.VMEM((count * rows, hidden), jnp.bfloat16)],
        compiler_params=pltpu.CompilerParams(vmem_limit_bytes=6 * MIB),
        name="down",
    )(bias, wd, *mine, *got)


def attended_rows(ref, offset, rows):
    height, half = ref.shape[0], ref.shape[1] // 2
    side = offset // height
    return ref[offset % height : offset % height + rows, side * half : (side + 1) * half]


def mix_kernel(offsets, index_ref, down_ref, att_ref, other_ref, wo_ref, own_ref, sib_ref):
    half = att_ref.shape[1] // 2
    rows = own_ref.shape[0] // len(offsets)
    n = index_ref[1]
    here = pl.ds(pl.multiple_of(n * half, 16), half)
    there = pl.ds(pl.multiple_of((1 - n) * half, 16), half)
    mine = jnp.concatenate([attended_rows(att_ref, o, 2 * rows) for o in offsets], axis=0)
    other = jnp.concatenate([attended_rows(other_ref, o, 2 * rows) for o in offsets], axis=0)
    width = 512
    for c in range(0, own_ref.shape[1], width):
        at = slice(c, c + width)
        out = down_ref[:, at].astype(jnp.float32)
        out += jnp.dot(mine, wo_ref[here, at], preferred_element_type=jnp.float32)
        out += jnp.dot(other, wo_ref[there, at], preferred_element_type=jnp.float32)
        out = out.astype(jnp.bfloat16)
        for i in range(len(offsets)):
            own_ref[i * rows : (i + 1) * rows, at] = out[2 * i * rows : (2 * i + 1) * rows]
            sib_ref[i * rows : (i + 1) * rows, at] = out[(2 * i + 1) * rows : (2 * i + 2) * rows]


def mix(n, offsets, partial_down, att, other, wo):
    rows, feat = partial_down.shape
    shape = jax.ShapeDtypeStruct((rows // 2, feat), jnp.bfloat16)
    return pl.pallas_call(
        functools.partial(mix_kernel, offsets),
        out_shape=(shape, shape),
        in_specs=[SMEM] + [VMEM] * 4,
        out_specs=(VMEM, VMEM),
        compiler_params=pltpu.CompilerParams(vmem_limit_bytes=5 * MIB),
        name="mix",
    )(n, partial_down, att, other, wo)


def output_kernel(
    offset, column, index_ref, bias_ref, mine_ref, got_ref, att_ref, other_ref, wo_ref, wd_ref, own_ref, sib_ref, units
):
    rows = mine_ref.shape[0]
    half = att_ref.shape[1] // 2
    own_rows = own_ref.shape[0]
    step = 384
    for c in range(0, units.shape[1], step):
        at = slice(c, c + step)
        there = slice(column + c, column + c + step)
        u = mine_ref[:, there].astype(jnp.float32) + got_ref[:, there].astype(jnp.float32)
        units[:, at] = gelu(u + bias_ref[:, at]).astype(jnp.bfloat16)
    n = index_ref[1]
    here = pl.ds(pl.multiple_of(n * half, 16), half)
    there = pl.ds(pl.multiple_of((1 - n) * half, 16), half)
    mine = attended_rows(att_ref, offset, rows)
    other = attended_rows(other_ref, offset, rows)
    width = 512
    for c in range(0, wd_ref.shape[1], width):
        at = slice(c, c + width)
        out = jnp.dot(units[...], wd_ref[:, at], preferred_element_type=jnp.float32)
        out += jnp.dot(mine, wo_ref[here, at], preferred_element_type=jnp.float32)
        out += jnp.dot(other, wo_ref[there, at], preferred_element_type=jnp.float32)
        out = out.astype(jnp.bfloat16)
        own_ref[:, at] = out[:own_rows]
        sib_ref[:, at] = out[own_rows:]


def output(n, offset, column, bias, mine, got, att, other, wo, wd):
    rows, hidden = mine.shape[0], wd.shape[0]
    shape = jax.ShapeDtypeStruct((rows // 2, wd.shape[1]), jnp.bfloat16)
    return pl.pallas_call(
        functools.partial(output_kernel, offset, column),
        out_shape=(shape, shape),
        in_specs=[SMEM] + [VMEM] * 7,
        out_specs=(VMEM, VMEM),
        scratch_shapes=[pltpu.VMEM((rows, hidden), jnp.bfloat16)],
        compiler_params=pltpu.CompilerParams(vmem_limit_bytes=5 * MIB),
        name="output",
    )(n, bias, mine, got, att, other, wo, wd)


def after(*values):
    return lax.optimization_barrier(values)


def local_ring(
    hidden_in,
    w_query,
    w_key,
    w_value,
    qkv_bias,
    w_up,
    up_bias,
    w_attn_out,
    w_down,
    out_bias,
    norm_gain,
    norm_bias,
    seq_lens,
    sink_count,
    page_table,
):
    device = lax.axis_index("wide").astype(jnp.int32).reshape(1)
    n = lax.axis_index("narrow").astype(jnp.int32)
    n_arg = n.reshape(1)
    rows, feat = hidden_in.shape
    total_tokens = rows * lax.axis_size("wide")
    half = w_query.shape[1] // 2

    fwd_pairs, bwd_pairs, swap_pairs = [], [], []
    for p in range(CHIPS):
        here, next_chip = CHIP_RING[p], CHIP_RING[(p + 1) % CHIPS]
        fwd_pairs += [(2 * here, 2 * next_chip), (2 * next_chip + 1, 2 * here + 1)]
        bwd_pairs += [(2 * next_chip, 2 * here), (2 * here + 1, 2 * next_chip + 1)]
        swap_pairs += [(2 * here, 2 * here + 1), (2 * here + 1, 2 * here)]
    fwd = lambda v: lax.ppermute(v, "wide", fwd_pairs)
    bwd = lambda v: lax.ppermute(v, "wide", bwd_pairs)
    swap = lambda v: lax.ppermute(v, "wide", swap_pairs)
    cross = lambda v: lax.ppermute(v, "narrow", [(0, 1), (1, 0)])

    first_side, n_arg = after(n == 0, n_arg)
    sums, index = pl.pallas_call(
        sums_kernel,
        out_shape=(
            jax.ShapeDtypeStruct((rows, STAT), jnp.float32),
            jax.ShapeDtypeStruct((2,), jnp.int32),
        ),
        in_specs=[SMEM, SMEM, VMEM],
        out_specs=(VMEM, SMEM),
        compiler_params=pltpu.CompilerParams(vmem_limit_bytes=8 * MIB),
        name="row_sums",
    )(device, n_arg, hidden_in)
    first_block, affine = pl.pallas_call(
        block_kernel,
        out_shape=(
            jax.ShapeDtypeStruct((rows, feat + STAT), jnp.bfloat16),
            jax.ShapeDtypeStruct((4, feat), jnp.float32),
        ),
        in_specs=[VMEM] * 5,
        out_specs=(VMEM, VMEM),
        compiler_params=pltpu.CompilerParams(vmem_limit_bytes=8 * MIB),
        name="first_block",
    )(hidden_in, norm_gain, norm_bias, sums, cross(sums))

    up_row = up_bias[None, :]

    def add(*terms):
        return sum(t.astype(jnp.float32) for t in terms).astype(jnp.bfloat16)

    def finish(name, u, v, column=0):
        return output(
            index, PAIRS.index(name) * 2 * rows, column, up_row, u, v, att, other, w_attn_out, w_down
        )

    def pair(halves, *running):
        return add(halves[0], swap(halves[1]), *running)

    per_device = page_table.shape[0] // 2
    hidden = w_up.shape[1]
    o0 = first_block
    f1, b1, s0 = fwd(o0), bwd(o0), swap(o0)
    kept0, send0, *weights = project(
        index, affine, (w_query, w_key, w_value, w_up), [o0, s0], ((0, "q"),), True
    )
    f1, b1, send0, kept0 = after(f1, b1, send0, kept0)
    got0 = cross(send0)
    f2, b2 = fwd(f1), bwd(b1)
    kept1, send1, u_f1 = project(
        index, affine, weights, [f1, swap(f1), b1, swap(b1)], ((1, "q"), (0,))
    )
    f2, b2, got0, send1, u_f1 = after(f2, b2, got0, send1, u_f1)
    got1 = cross(send1)
    f3 = fwd(f2)
    kept2, send2, u_b2 = project(
        index, affine, weights, [f2, swap(f2), b2, swap(b2)], ((0, "q"), (1,))
    )
    f3, b2, got1, send2, u_b2, late_index = after(f3, b2, got1, send2, u_b2, index)
    got2 = cross(send2)
    f4, b3 = fwd(f3), bwd(b2)
    kept3, send3 = project(index, affine, weights, [f3, swap(f3)], ((0, "q"),))
    query_info, key_token, cosine, sine = tables(total_tokens, late_index, seq_lens, sink_count)
    b3, f4, got2, send3, query_info, key_token, cosine, sine = after(
        b3, f4, got2, send3, query_info, key_token, cosine, sine
    )
    got3 = cross(send3)
    kept4, send4, u_far = project(
        index, affine, weights, [b3, swap(b3), f4, swap(f4)], (("q",), (1, 0))
    )
    got3, send4, u_far = after(got3, send4, u_far)
    got4 = cross(send4)
    early_pairs = ("o0", "b1", "f2")
    early = down(up_row, [send0, send1, send2], [got0, got1, got2], w_down)
    d_f3 = down(up_row, [send3], [got3], w_down)
    got4, early, d_f3, u_far = after(got4, early, d_f3, u_far)
    v_far = cross(u_far)
    att, kv = attend(
        total_tokens // 16, (hidden, hidden, hidden, hidden, 0), index, qkv_bias, cosine, sine,
        query_info, key_token, [kept0, kept1, kept2, kept3, kept4], [got0, got1, got2, got3, got4],
    )
    v_far, att = after(v_far, att)
    other = cross(att)
    other, u_b2, u_f1, kv = after(other, u_b2, u_f1, kv)
    v_b2 = cross(u_b2)
    s_f4, d_f3, early = after(pair(finish("f4", u_far, v_far)), d_f3, early)
    r_b = bwd(s_f4)

    def blend(names, part):
        places = tuple(PAIRS.index(p) * 2 * rows for p in names)
        return mix(index, places, part, att, other, w_attn_out)

    s_f3 = pair(blend(("f3",), d_f3))
    y_b3 = finish("b3", u_far, v_far, hidden)
    m_own, m_sib = blend(early_pairs, early)
    m_got = swap(m_sib)
    v_b2, r_b, s_f3, y_b3, m_own, m_got, u_f1, kv = after(
        v_b2, r_b, s_f3, y_b3, m_own, m_got, u_f1, kv
    )

    def mixed(name):
        at = slice(early_pairs.index(name) * rows, (early_pairs.index(name) + 1) * rows)
        return m_own[at], m_got[at]

    v_f1 = cross(u_f1)
    r_b, r_f = bwd(add(r_b, s_f3)), fwd(pair(y_b3))
    y_b2 = finish("b2", u_b2, v_b2)
    paged = ordered_pages(index, page_table, kv)
    v_f1, r_b, r_f, y_b2, m_own, m_got, paged = after(v_f1, r_b, r_f, y_b2, m_own, m_got, paged)
    cache_mine, cache_got = paged[:per_device], cross(paged[per_device:])
    r_b, r_f = bwd(add(r_b, *mixed("f2"))), fwd(pair(y_b2, r_f))
    y_f1 = finish("f1", u_f1, v_f1)
    r_b, r_f, y_f1, cache_mine, cache_got = after(r_b, r_f, y_f1, cache_mine, cache_got)
    r_f, r_b = fwd(add(r_f, *mixed("b1"))), bwd(pair(y_f1, r_b))
    summed = sum(t.astype(jnp.float32) for t in (r_b, r_f, *mixed("o0")))
    hidden_out = (hidden_in.astype(jnp.float32) + summed + out_bias).astype(jnp.bfloat16)
    left = jnp.where(first_side, cache_mine, cache_got)
    right = jnp.where(first_side, cache_got, cache_mine)
    paged_cache = jnp.stack(
        [
            jnp.concatenate([left[..., :half], right[..., :half]], axis=-1),
            jnp.concatenate([left[..., half:], right[..., half:]], axis=-1),
        ]
    )
    return (hidden_out, paged_cache)


def solution(mesh):
    in_specs = (
        P("wide", "narrow"),
        P("narrow", "wide"),
        P("narrow", "wide"),
        P("narrow", "wide"),
        P(None, "wide"),
        P("narrow", "wide"),
        P("wide"),
        P("wide", "narrow"),
        P("wide", "narrow"),
        P("narrow"),
        P(None, "narrow"),
        P(None, "narrow"),
        P(),
        P(),
        P(),
    )
    out_specs = (P("wide", "narrow"), P(None, "narrow", None, "wide"))
    ringed = mesh.shape["wide"] == 2 * CHIPS and mesh.shape["narrow"] == 2
    local = local_ring if ringed else local_generic
    return jax.shard_map(local, mesh=mesh, in_specs=in_specs, out_specs=out_specs, check_vma=False)
```

```python
import functools

import jax
import jax.numpy as jnp
import numpy as np
from jax import lax
from jax.experimental import pallas as pl
from jax.experimental.pallas import tpu as pltpu
from jax.sharding import PartitionSpec as P

D = 6144
HEAD_DIM = 96
ROTARY = 24
PAGE = 16


def segment_info(token_index, seq_lens, sink_count):
    seq_ends = jnp.cumsum(seq_lens)
    seq_starts = seq_ends - seq_lens
    inside = (token_index[:, None] >= seq_starts[None, :]) & (
        token_index[:, None] < seq_ends[None, :]
    )
    member = inside.astype(jnp.int32)
    seq_number = jnp.arange(seq_lens.shape[0], dtype=jnp.int32)
    segment = jnp.sum(member * seq_number[None, :], axis=1)
    position = token_index - jnp.sum(member * seq_starts[None, :], axis=1)
    sink_limit = jnp.sum(member * sink_count[None, :], axis=1)
    return (segment, position, sink_limit)


def rotate(values, position):
    half_rot = ROTARY // 2
    freq_index = jnp.arange(half_rot, dtype=jnp.float32)
    inverse = jnp.power(jnp.float32(10000.0), -2.0 * freq_index / ROTARY)
    angles = position.astype(jnp.float32)[:, None] * inverse[None, :]
    cosine = jnp.cos(angles)[:, None, :]
    sine_part = jnp.sin(angles)[:, None, :]
    first_half = values[..., :half_rot]
    second_half = values[..., half_rot:ROTARY]
    return jnp.concatenate(
        [
            first_half * cosine - second_half * sine_part,
            second_half * cosine + first_half * sine_part,
            values[..., ROTARY:],
        ],
        axis=-1,
    )


def local_generic(
    hidden_in,
    w_query,
    w_key,
    w_value,
    qkv_bias,
    w_up,
    up_bias,
    w_attn_out,
    w_down,
    out_bias,
    norm_gain,
    norm_bias,
    seq_lens,
    sink_count,
    page_table,
):
    wide_count = lax.axis_size("wide")
    narrow_count = lax.axis_size("narrow")
    narrow_index = lax.axis_index("narrow")
    tok_local, feat_local = hidden_in.shape
    sub_rows = tok_local // narrow_count
    total_tokens = tok_local * wide_count
    query_rows = wide_count * sub_rows
    head_cols = w_query.shape[1]
    heads_local = head_cols // HEAD_DIM
    as_float = hidden_in.astype(jnp.float32)
    partial_sum = jnp.sum(as_float, axis=1)
    partial_square = jnp.sum(as_float * as_float, axis=1)
    total_sum, total_square = lax.psum((partial_sum, partial_square), "narrow")
    average = total_sum / D
    variance = total_square / D - average * average
    scaled = (as_float - average[:, None]) * lax.rsqrt(variance + 1e-05)[:, None]
    attn_normed = (scaled * norm_gain[0] + norm_bias[0]).astype(jnp.bfloat16)
    mlp_normed = (scaled * norm_gain[1] + norm_bias[1]).astype(jnp.bfloat16)
    stacked = jnp.stack([attn_normed, mlp_normed]).reshape(2, narrow_count, sub_rows, feat_local)
    gathered = lax.all_gather(stacked, "wide", axis=2, tiled=True).reshape(
        2, total_tokens, feat_local
    )
    local_order = jnp.arange(query_rows, dtype=jnp.int32)
    local_tokens = (
        local_order // sub_rows * tok_local + narrow_index * sub_rows + local_order % sub_rows
    )
    local_seg, local_pos, local_sink = segment_info(local_tokens, seq_lens, sink_count)
    all_order = jnp.arange(total_tokens, dtype=jnp.int32)
    all_tokens = (
        all_order % query_rows // sub_rows * tok_local
        + all_order // query_rows * sub_rows
        + all_order % sub_rows
    )
    all_seg, all_pos, all_sink = segment_info(all_tokens, seq_lens, sink_count)
    qkv_weight = jnp.concatenate([w_query, w_key, w_value], axis=1)
    attn_part = gathered[0]
    mlp_part = gathered[1]
    summed = lax.psum_scatter(
        jnp.concatenate(
            [
                jnp.dot(attn_part, qkv_weight, preferred_element_type=jnp.float32),
                jnp.dot(mlp_part, w_up, preferred_element_type=jnp.float32),
            ],
            axis=1,
        ).astype(jnp.bfloat16),
        "narrow",
        scatter_dimension=0,
        tiled=True,
    ).astype(jnp.float32)
    query_sum = summed[:, :head_cols]
    key_sum = summed[:, head_cols : 2 * head_cols]
    value_sum = summed[:, 2 * head_cols : 3 * head_cols]
    unit_sum = summed[:, 3 * head_cols :]
    keys_local = (
        rotate((key_sum + qkv_bias[1]).reshape(query_rows, heads_local, HEAD_DIM), local_pos)
        .astype(jnp.bfloat16)
        .reshape(query_rows, head_cols)
    )
    values_local = (value_sum + qkv_bias[2]).astype(jnp.bfloat16)
    all_keys, all_values = (
        lax.all_gather(keys_local, "narrow", axis=0, tiled=True),
        lax.all_gather(values_local, "narrow", axis=0, tiled=True),
    )
    queries = rotate(
        (query_sum + qkv_bias[0]).reshape(query_rows, heads_local, HEAD_DIM), local_pos
    ).astype(jnp.bfloat16)
    hidden_units = jax.nn.gelu(unit_sum + up_bias, approximate=False).astype(jnp.bfloat16)
    window_span = total_tokens // 16
    allowed = (local_seg[:, None] == all_seg[None, :]) & (all_pos[None, :] <= local_pos[:, None])
    allowed = allowed & (
        (local_pos[:, None] - all_pos[None, :] < window_span)
        | (all_pos[None, :] < local_sink[:, None])
    )
    key_heads = all_keys.reshape(total_tokens, heads_local, HEAD_DIM)
    value_heads = all_values.reshape(total_tokens, heads_local, HEAD_DIM)
    scores = jnp.einsum("qhd,khd->hqk", queries, key_heads, preferred_element_type=jnp.float32) * (
        1.0 / HEAD_DIM**0.5
    )
    masked = jnp.where(allowed[None], scores, jnp.float32(-1e30))
    top_score = jnp.max(masked, axis=2, keepdims=True)
    weights = jnp.exp(masked - top_score)
    probs = (weights / jnp.sum(weights, axis=2, keepdims=True)).astype(jnp.bfloat16)
    attended = (
        jnp.einsum("hqk,khd->qhd", probs, value_heads, preferred_element_type=jnp.float32)
        .astype(jnp.bfloat16)
        .reshape(query_rows, head_cols)
    )
    full_out, full_down = (
        lax.all_gather(w_attn_out, "narrow", axis=1, tiled=True),
        lax.all_gather(w_down, "narrow", axis=1, tiled=True),
    )
    attn_part = attended
    own_rows = lax.psum_scatter(
        (
            jnp.dot(attn_part, full_out, preferred_element_type=jnp.float32)
            + jnp.dot(hidden_units, full_down, preferred_element_type=jnp.float32)
        ).astype(jnp.bfloat16),
        "wide",
        scatter_dimension=0,
        tiled=True,
    ).astype(jnp.float32)
    combined = lax.all_to_all(
        own_rows.astype(jnp.bfloat16), "narrow", split_axis=1, concat_axis=0, tiled=True
    ).astype(own_rows.dtype)
    hidden_out = (as_float + combined + out_bias).astype(jnp.bfloat16)
    pages_local = page_table.shape[0] // narrow_count
    slot_ids = narrow_index * pages_local + jnp.arange(pages_local, dtype=jnp.int32)
    matches = (page_table[None, :] == slot_ids[:, None]).astype(jnp.int32)
    source_page = jnp.sum(
        matches * jnp.arange(page_table.shape[0], dtype=jnp.int32)[None, :], axis=1
    )
    token_ids = (source_page[:, None] * PAGE + jnp.arange(PAGE, dtype=jnp.int32)[None, :]).reshape(
        -1
    )
    gather_rows = (
        token_ids % tok_local // sub_rows * query_rows
        + token_ids // tok_local * sub_rows
        + token_ids % sub_rows
    )
    cache_keys = jnp.take(all_keys, gather_rows, axis=0).reshape(pages_local, PAGE, head_cols)
    cache_values = jnp.take(all_values, gather_rows, axis=0).reshape(pages_local, PAGE, head_cols)
    paged_cache = jnp.stack([cache_keys, cache_values])
    return (hidden_out, paged_cache)


CHIP_RING = (0, 2, 4, 6, 7, 5, 3, 1)
CHIPS = len(CHIP_RING)
PAIRS = ("o0", "f1", "b1", "f2", "b2", "f3", "b3", "f4")
STAT = 128
HEAD_PAD = 128
LANE_GROUP = 32
MIB = 1 << 20
VMEM = pl.BlockSpec(memory_space=pltpu.VMEM)
HBM = pl.BlockSpec(memory_space=pltpu.HBM)
SMEM = pl.BlockSpec(memory_space=pltpu.SMEM)


def owner_table():
    table = np.zeros((2 * CHIPS, 2 * CHIPS), np.int32)
    for place, chip in enumerate(CHIP_RING):
        for core in range(2):
            order = []
            for pair in PAIRS:
                shift = (-1 if pair[0] == "f" else 1) * int(pair[1]) * (1 - 2 * core)
                order.append(CHIP_RING[(place + shift) % CHIPS] * 2 + core)
                order.append(CHIP_RING[(place - shift) % CHIPS] * 2 + 1 - core)
            table[2 * chip + core] = order
    return table


def place_table():
    owners = owner_table()
    table = np.zeros_like(owners)
    for device in range(owners.shape[0]):
        table[device, owners[device]] = np.arange(owners.shape[1])
    return table


def sums_kernel(device_ref, n_ref, x_ref, out_ref, index_ref):
    x = x_ref[...].astype(jnp.float32)
    first = jnp.sum(x, axis=1, keepdims=True)
    second = jnp.sum(x * x, axis=1, keepdims=True)
    lane = lax.broadcasted_iota(jnp.int32, out_ref.shape, 1)
    out_ref[...] = jnp.where(lane == 0, first, jnp.where(lane == 1, second, 0.0))
    index_ref[0] = device_ref[0]
    index_ref[1] = n_ref[0]


def block_kernel(x_ref, gain_ref, bias_ref, here_ref, there_ref, out_ref, affine_ref):
    feat = x_ref.shape[1]
    total = here_ref[...] + there_ref[...]
    average = total[:, 0:1] / D
    variance = total[:, 1:2] / D - average * average
    scale = lax.rsqrt(variance + 1e-05)
    lane = lax.broadcasted_iota(jnp.int32, (x_ref.shape[0], STAT), 1)
    tail = jnp.zeros((x_ref.shape[0], STAT), jnp.float32)
    for start, value in ((0, average), (3, scale)):
        for term in range(3):
            piece = value.astype(jnp.bfloat16).astype(jnp.float32)
            tail = jnp.where(lane == start + term, piece, tail)
            value = value - piece
    out_ref[:, :feat] = x_ref[...]
    out_ref[:, feat:] = tail.astype(jnp.bfloat16)
    affine_ref[0:2, :] = gain_ref[...]
    affine_ref[2:4, :] = bias_ref[...]


def tables_kernel(index_ref, owners_ref, lens_ref, sinks_ref, inverse_ref, phase_ref, info_ref, key_ref, cos_ref, sin_ref):
    device = index_ref[0]
    blocks = owners_ref.shape[1]
    rows = info_ref.shape[0] // blocks
    half_rot = ROTARY // 2
    lane = lax.broadcasted_iota(jnp.int32, (rows, HEAD_PAD), 1)
    sub = lax.broadcasted_iota(jnp.int32, (rows, HEAD_PAD), 0)
    key_lane = lax.broadcasted_iota(jnp.int32, key_ref.shape, 1)
    key = key_lane
    shared = HEAD_PAD // LANE_GROUP
    for base in range(0, blocks, shared):
        position = jnp.zeros((rows, HEAD_PAD), jnp.int32)
        for g in range(shared):
            j = base + g
            first = owners_ref[device, j] * rows
            key = jnp.where(key_lane // rows == j, first + key_lane - j * rows, key)
            token = first + sub
            begin, end = jnp.zeros_like(token), jnp.zeros_like(token)
            start = jnp.int32(0)
            for s in range(lens_ref.shape[0]):
                inside = (token >= start) & (token < start + lens_ref[s])
                begin = jnp.where(inside, start, begin)
                end = jnp.where(inside, start + sinks_ref[s], end)
                start = start + lens_ref[s]
            info_ref[j * rows : (j + 1) * rows, :] = jnp.where(
                lane == 0, token, jnp.where(lane == 1, begin, end)
            )
            position = jnp.where(lane // LANE_GROUP == g, token - begin, position)
        waves = jnp.cos(position.astype(jnp.float32) * inverse_ref[...] - phase_ref[...])
        for g in range(shared):
            at = slice((base + g) * rows, (base + g + 1) * rows)
            here = pltpu.roll(waves, (HEAD_PAD - g * LANE_GROUP) % HEAD_PAD, 1)
            later = pltpu.roll(waves, (HEAD_PAD - g * LANE_GROUP + half_rot) % HEAD_PAD, 1)
            before = pltpu.roll(waves, (2 * HEAD_PAD - g * LANE_GROUP - half_rot) % HEAD_PAD, 1)
            cosine = jnp.where(lane < half_rot, here, later)
            cos_ref[at, :] = jnp.where(lane < ROTARY, cosine, 1.0)
            sine = jnp.where(lane < half_rot, -before, here)
            sin_ref[at, :] = jnp.where(lane < ROTARY, sine, 0.0)
    key_ref[...] = key


def tables(total, index, lens, sinks):
    half_rot = ROTARY // 2
    lane = np.arange(HEAD_PAD) % LANE_GROUP
    inverse = (10000.0 ** (-2.0 * (lane % half_rot) / ROTARY)).astype(np.float32)[None, :]
    phase = np.where(lane < half_rot, 0.0, np.pi / 2).astype(np.float32)[None, :]
    wide = (total, HEAD_PAD)
    return pl.pallas_call(
        tables_kernel,
        out_shape=(
            jax.ShapeDtypeStruct(wide, jnp.int32),
            jax.ShapeDtypeStruct((1, total), jnp.int32),
            jax.ShapeDtypeStruct(wide, jnp.float32),
            jax.ShapeDtypeStruct(wide, jnp.float32),
        ),
        in_specs=[SMEM] * 4 + [VMEM] * 2,
        out_specs=(VMEM,) * 4,
        compiler_params=pltpu.CompilerParams(vmem_limit_bytes=8 * MIB),
        name="tables",
    )(index, jnp.asarray(owner_table()), lens, sinks, jnp.asarray(inverse), jnp.asarray(phase))


def pages_kernel(index_ref, places_ref, table_ref, kv_ref, out_ref):
    pages = table_ref.shape[0]
    per_owner = pages // places_ref.shape[1]
    device, shift = index_ref[0], index_ref[1] * (pages // 2)
    for p in range(pages):
        place = places_ref[device, p // per_owner] * per_owner + p % per_owner
        row = pl.multiple_of(place * PAGE, PAGE)
        out_ref[lax.rem(table_ref[p] + shift, pages)] = kv_ref[pl.ds(row, PAGE), :]


def ordered_pages(index, page_table, kv):
    return pl.pallas_call(
        pages_kernel,
        out_shape=jax.ShapeDtypeStruct((page_table.shape[0], PAGE, kv.shape[1]), kv.dtype),
        in_specs=[SMEM] * 3 + [VMEM],
        out_specs=VMEM,
        compiler_params=pltpu.CompilerParams(vmem_limit_bytes=8 * MIB),
        name="ordered_pages",
    )(index, jnp.asarray(place_table()), page_table, kv)


def normalise(blocks, affine_ref, attn, mlp):
    rows = blocks[0].shape[0]
    feat = attn.shape[1]
    step = 512
    for b, block in enumerate(blocks):
        tail = block[:, feat:].astype(jnp.float32)
        average = tail[:, 0:1] + tail[:, 1:2] + tail[:, 2:3]
        scale = tail[:, 3:4] + tail[:, 4:5] + tail[:, 5:6]
        here = slice(b * rows, (b + 1) * rows)
        for c in range(0, feat, step):
            at = slice(c, c + step)
            scaled = (block[:, at].astype(jnp.float32) - average) * scale
            attn[here, at] = (scaled * affine_ref[0:1, at] + affine_ref[2:3, at]).astype(jnp.bfloat16)
            mlp[here, at] = (scaled * affine_ref[1:2, at] + affine_ref[3:4, at]).astype(jnp.bfloat16)


def project_kernel(count, outs, first_call, index_ref, affine_ref, wq_ref, wk_ref, wv_ref, wu_ref, *refs):
    blocks, refs = refs[:count], refs[count:]
    mine_ref, refs = refs[0], refs[1:]
    sent_refs, refs = refs[: len(outs)], refs[len(outs) :]
    hidden = wu_ref.shape[1]
    width = 384
    tiles = hidden // width
    copies = []
    if first_call:
        held, (attn, mlp, sems) = refs[:4], refs[4:]
        copies = [
            pltpu.make_async_copy(src, dst, sems.at[i])
            for i, (src, dst) in enumerate(zip((wq_ref, wk_ref, wv_ref), held))
        ]
        for t in range(tiles):
            at = slice(t * width, (t + 1) * width)
            copies.append(pltpu.make_async_copy(wu_ref.at[:, at], held[3].at[:, at], sems.at[3 + t]))
        for copy in copies:
            copy.start()
        wq_ref, wk_ref, wv_ref, wu_ref = held
    else:
        attn, mlp = refs
    rows = 2 * blocks[0].shape[0]
    half = wq_ref.shape[1] // 2
    normalise(blocks, affine_ref, attn, mlp)
    low, high = [], []
    for i, weight in enumerate((wq_ref, wk_ref, wv_ref)):
        if first_call:
            copies[i].wait()
        part = jnp.dot(attn[...], weight[...], preferred_element_type=jnp.float32)
        low.append(part[:, :half])
        high.append(part[:, half:])
    low = jnp.concatenate(low, axis=1).astype(jnp.bfloat16)
    high = jnp.concatenate(high, axis=1).astype(jnp.bfloat16)
    first = index_ref[1] == 0
    mine_ref[...] = jnp.where(first, low, high)
    send = jnp.where(first, high, low)
    send = [send[p * rows : (p + 1) * rows] for p in range(count // 2)]
    gap = -(3 * half * len(send)) % 128
    if gap:
        send.append(jnp.zeros((rows, gap), jnp.bfloat16))
    send = jnp.concatenate(send, axis=1)
    for ref, items in zip(sent_refs, outs):
        if items[-1] == "q":
            ref[:, hidden * (len(items) - 1) :] = send
    for t in range(tiles):
        if first_call:
            copies[3 + t].wait()
        at = slice(t * width, (t + 1) * width)
        part = jnp.dot(mlp[...], wu_ref[:, at], preferred_element_type=jnp.float32)
        part = part.astype(jnp.bfloat16)
        for ref, items in zip(sent_refs, outs):
            for i, item in enumerate(items):
                if item != "q":
                    begin = i * hidden + t * width
                    ref[:, begin : begin + width] = part[item * rows : (item + 1) * rows]


def project(n, affine, weights, blocks, outs, first_call=False):
    count = len(blocks)
    rows = 2 * blocks[0].shape[0]
    feat, cols = weights[0].shape
    hidden = weights[3].shape[1]
    sent = 3 * cols // 2 * (count // 2)
    sent += -sent % 128
    shapes = [jax.ShapeDtypeStruct((rows * count // 2, 3 * cols // 2), jnp.bfloat16)]
    for items in outs:
        width = sum(sent if item == "q" else hidden for item in items)
        shapes.append(jax.ShapeDtypeStruct((rows, width), jnp.bfloat16))
    scratch = [pltpu.VMEM((rows * count // 2, feat), jnp.bfloat16)] * 2
    if first_call:
        shapes += [jax.ShapeDtypeStruct(w.shape, w.dtype) for w in weights]
        scratch.append(pltpu.SemaphoreType.DMA((3 + hidden // 384,)))
    return pl.pallas_call(
        functools.partial(project_kernel, count, outs, first_call),
        out_shape=tuple(shapes),
        in_specs=[SMEM, VMEM] + [HBM if first_call else VMEM] * 4 + [VMEM] * count,
        out_specs=(VMEM,) * len(shapes),
        scratch_shapes=scratch,
        compiler_params=pltpu.CompilerParams(vmem_limit_bytes=(46 if first_call else 9) * MIB),
        name="project",
    )(n, affine, *weights, *blocks)


def attend_kernel(count, span, offsets, index_ref, bias_ref, cos_ref, sin_ref, query_ref, key_ref, *refs):
    mine, got = refs[:count], refs[count : 2 * count]
    att_ref, kv_ref, queries, keys, values = refs[2 * count :]
    heads = queries.shape[0]
    half = kv_ref.shape[1] // 2
    total = kv_ref.shape[0]
    half_rot = ROTARY // 2
    bias = jnp.where(index_ref[1] == 0, bias_ref[:, :half], bias_ref[:, half:])
    offset = 0
    for g in range(count):
        rows = mine[g].shape[0]
        at = slice(offset, offset + rows)
        offset += rows
        pieces = []
        for p in range(rows // got[g].shape[0]):
            begin = offsets[g] + 3 * half * p
            pieces.append(got[g][:, begin : begin + 3 * half])
        sent = jnp.concatenate(pieces, axis=0)
        summed = mine[g][...].astype(jnp.float32) + sent.astype(jnp.float32)
        cosine, sine = cos_ref[at, :], sin_ref[at, :]
        lane = lax.broadcasted_iota(jnp.int32, (rows, HEAD_PAD), 1)
        pad = jnp.zeros((rows, HEAD_PAD - HEAD_DIM), jnp.float32)
        for kind in range(3):
            kept = []
            for h in range(heads):
                begin = kind * half + h * HEAD_DIM
                u = summed[:, begin : begin + HEAD_DIM]
                u = u + bias[kind : kind + 1, h * HEAD_DIM : (h + 1) * HEAD_DIM]
                u = jnp.concatenate([u, pad], axis=1)
                if kind < 2:
                    other = jnp.where(
                        lane < half_rot,
                        pltpu.roll(u, HEAD_PAD - half_rot, 1),
                        pltpu.roll(u, half_rot, 1),
                    )
                    u = u * cosine + other * sine
                (queries, keys, values)[kind][h, at, :] = u.astype(jnp.bfloat16)
                kept.append(u[:, :HEAD_DIM])
            if kind > 0:
                kv_ref[at, (kind - 1) * half : kind * half] = jnp.concatenate(kept, axis=1).astype(
                    jnp.bfloat16
                )
    tile = 256
    for start in range(0, total, tile):
        at = slice(start, start + tile)
        info = query_ref[at, :]
        token, begin, end = info[:, 0:1], info[:, 1:2], info[:, 2:3]
        key_token = key_ref[...]
        near = key_token > token - span
        allowed = (key_token >= begin) & (key_token <= token) & (near | (key_token < end))
        outs = []
        for h in range(heads):
            scores = lax.dot_general(
                queries[h, at, :],
                keys[h],
                (((1,), (1,)), ((), ())),
                preferred_element_type=jnp.float32,
            ) * (1.0 / HEAD_DIM**0.5)
            masked = jnp.where(allowed, scores, -1e30)
            weights = jnp.exp(masked - jnp.max(masked, axis=1, keepdims=True))
            probs = weights / jnp.sum(weights, axis=1, keepdims=True)
            out = jnp.dot(probs.astype(jnp.bfloat16), values[h], preferred_element_type=jnp.float32)
            outs.append(out[:, :HEAD_DIM])
        side = start // (total // 2)
        att_ref[start % (total // 2) : start % (total // 2) + tile, side * half : (side + 1) * half] = (
            jnp.concatenate(outs, axis=1).astype(jnp.bfloat16)
        )


def attend(span, offsets, n, bias, cosine, sine, query_info, key_token, mine, got):
    count = len(mine)
    total = cosine.shape[0]
    half = mine[0].shape[1] // 3
    heads = half // HEAD_DIM
    scratch = pltpu.VMEM((heads, total, HEAD_PAD), jnp.bfloat16)
    return pl.pallas_call(
        functools.partial(attend_kernel, count, span, offsets),
        out_shape=(
            jax.ShapeDtypeStruct((total // 2, 2 * half), jnp.bfloat16),
            jax.ShapeDtypeStruct((total, 2 * half), jnp.bfloat16),
        ),
        in_specs=[SMEM] + [VMEM] * (5 + 2 * count),
        out_specs=(VMEM, VMEM),
        scratch_shapes=[scratch, scratch, scratch],
        compiler_params=pltpu.CompilerParams(vmem_limit_bytes=10 * MIB),
        name="attend",
    )(n, bias, cosine, sine, query_info, key_token, *mine, *got)


def gelu(u):
    return u * (1.0 + lax.erf(u * (0.5**0.5))) * 0.5


def down_kernel(count, bias_ref, wd_ref, *refs):
    mine, got = refs[:count], refs[count : 2 * count]
    out_ref, units = refs[2 * count :]
    rows = mine[0].shape[0]
    step = 384
    for i in range(count):
        for c in range(0, units.shape[1], step):
            at = slice(c, c + step)
            u = mine[i][:, at].astype(jnp.float32) + got[i][:, at].astype(jnp.float32)
            u = gelu(u + bias_ref[:, at])
            units[i * rows : (i + 1) * rows, at] = u.astype(jnp.bfloat16)
    width, tall = 512, 2 * rows
    for c in range(0, wd_ref.shape[1], width):
        at = slice(c, c + width)
        for r in range(0, units.shape[0], tall):
            here = slice(r, r + tall)
            out = jnp.dot(units[here, :], wd_ref[:, at], preferred_element_type=jnp.float32)
            out_ref[here, at] = out.astype(jnp.bfloat16)


def down(bias, mine, got, wd):
    count = len(mine)
    rows, hidden = mine[0].shape[0], wd.shape[0]
    return pl.pallas_call(
        functools.partial(down_kernel, count),
        out_shape=jax.ShapeDtypeStruct((count * rows, wd.shape[1]), jnp.bfloat16),
        in_specs=[VMEM] * (2 + 2 * count),
        out_specs=VMEM,
        scratch_shapes=[pltpu.VMEM((count * rows, hidden), jnp.bfloat16)],
        compiler_params=pltpu.CompilerParams(vmem_limit_bytes=6 * MIB),
        name="down",
    )(bias, wd, *mine, *got)


def attended_rows(ref, offset, rows):
    height, half = ref.shape[0], ref.shape[1] // 2
    side = offset // height
    return ref[offset % height : offset % height + rows, side * half : (side + 1) * half]


def mix_kernel(offsets, index_ref, down_ref, att_ref, other_ref, wo_ref, own_ref, sib_ref):
    half = att_ref.shape[1] // 2
    rows = own_ref.shape[0] // len(offsets)
    n = index_ref[1]
    here = pl.ds(pl.multiple_of(n * half, 16), half)
    there = pl.ds(pl.multiple_of((1 - n) * half, 16), half)
    mine = jnp.concatenate([attended_rows(att_ref, o, 2 * rows) for o in offsets], axis=0)
    other = jnp.concatenate([attended_rows(other_ref, o, 2 * rows) for o in offsets], axis=0)
    width = 512
    for c in range(0, own_ref.shape[1], width):
        at = slice(c, c + width)
        out = down_ref[:, at].astype(jnp.float32)
        out += jnp.dot(mine, wo_ref[here, at], preferred_element_type=jnp.float32)
        out += jnp.dot(other, wo_ref[there, at], preferred_element_type=jnp.float32)
        out = out.astype(jnp.bfloat16)
        for i in range(len(offsets)):
            own_ref[i * rows : (i + 1) * rows, at] = out[2 * i * rows : (2 * i + 1) * rows]
            sib_ref[i * rows : (i + 1) * rows, at] = out[(2 * i + 1) * rows : (2 * i + 2) * rows]


def mix(n, offsets, partial_down, att, other, wo):
    rows, feat = partial_down.shape
    shape = jax.ShapeDtypeStruct((rows // 2, feat), jnp.bfloat16)
    return pl.pallas_call(
        functools.partial(mix_kernel, offsets),
        out_shape=(shape, shape),
        in_specs=[SMEM] + [VMEM] * 4,
        out_specs=(VMEM, VMEM),
        compiler_params=pltpu.CompilerParams(vmem_limit_bytes=5 * MIB),
        name="mix",
    )(n, partial_down, att, other, wo)


def output_kernel(
    offset, column, index_ref, bias_ref, mine_ref, got_ref, att_ref, other_ref, wo_ref, wd_ref, own_ref, sib_ref, units
):
    rows = mine_ref.shape[0]
    half = att_ref.shape[1] // 2
    own_rows = own_ref.shape[0]
    step = 384
    for c in range(0, units.shape[1], step):
        at = slice(c, c + step)
        there = slice(column + c, column + c + step)
        u = mine_ref[:, there].astype(jnp.float32) + got_ref[:, there].astype(jnp.float32)
        units[:, at] = gelu(u + bias_ref[:, at]).astype(jnp.bfloat16)
    n = index_ref[1]
    here = pl.ds(pl.multiple_of(n * half, 16), half)
    there = pl.ds(pl.multiple_of((1 - n) * half, 16), half)
    mine = attended_rows(att_ref, offset, rows)
    other = attended_rows(other_ref, offset, rows)
    width = 512
    for c in range(0, wd_ref.shape[1], width):
        at = slice(c, c + width)
        out = jnp.dot(units[...], wd_ref[:, at], preferred_element_type=jnp.float32)
        out += jnp.dot(mine, wo_ref[here, at], preferred_element_type=jnp.float32)
        out += jnp.dot(other, wo_ref[there, at], preferred_element_type=jnp.float32)
        out = out.astype(jnp.bfloat16)
        own_ref[:, at] = out[:own_rows]
        sib_ref[:, at] = out[own_rows:]


def output(n, offset, column, bias, mine, got, att, other, wo, wd):
    rows, hidden = mine.shape[0], wd.shape[0]
    shape = jax.ShapeDtypeStruct((rows // 2, wd.shape[1]), jnp.bfloat16)
    return pl.pallas_call(
        functools.partial(output_kernel, offset, column),
        out_shape=(shape, shape),
        in_specs=[SMEM] + [VMEM] * 7,
        out_specs=(VMEM, VMEM),
        scratch_shapes=[pltpu.VMEM((rows, hidden), jnp.bfloat16)],
        compiler_params=pltpu.CompilerParams(vmem_limit_bytes=5 * MIB),
        name="output",
    )(n, bias, mine, got, att, other, wo, wd)


def after(*values):
    return lax.optimization_barrier(values)


def local_ring(
    hidden_in,
    w_query,
    w_key,
    w_value,
    qkv_bias,
    w_up,
    up_bias,
    w_attn_out,
    w_down,
    out_bias,
    norm_gain,
    norm_bias,
    seq_lens,
    sink_count,
    page_table,
):
    device = lax.axis_index("wide").astype(jnp.int32).reshape(1)
    n = lax.axis_index("narrow").astype(jnp.int32)
    n_arg = n.reshape(1)
    rows, feat = hidden_in.shape
    total_tokens = rows * lax.axis_size("wide")
    half = w_query.shape[1] // 2

    fwd_pairs, bwd_pairs, swap_pairs = [], [], []
    for p in range(CHIPS):
        here, next_chip = CHIP_RING[p], CHIP_RING[(p + 1) % CHIPS]
        fwd_pairs += [(2 * here, 2 * next_chip), (2 * next_chip + 1, 2 * here + 1)]
        bwd_pairs += [(2 * next_chip, 2 * here), (2 * here + 1, 2 * next_chip + 1)]
        swap_pairs += [(2 * here, 2 * here + 1), (2 * here + 1, 2 * here)]
    fwd = lambda v: lax.ppermute(v, "wide", fwd_pairs)
    bwd = lambda v: lax.ppermute(v, "wide", bwd_pairs)
    swap = lambda v: lax.ppermute(v, "wide", swap_pairs)
    cross = lambda v: lax.ppermute(v, "narrow", [(0, 1), (1, 0)])

    first_side, n_arg = after(n == 0, n_arg)
    sums, index = pl.pallas_call(
        sums_kernel,
        out_shape=(
            jax.ShapeDtypeStruct((rows, STAT), jnp.float32),
            jax.ShapeDtypeStruct((2,), jnp.int32),
        ),
        in_specs=[SMEM, SMEM, VMEM],
        out_specs=(VMEM, SMEM),
        compiler_params=pltpu.CompilerParams(vmem_limit_bytes=8 * MIB),
        name="row_sums",
    )(device, n_arg, hidden_in)
    first_block, affine = pl.pallas_call(
        block_kernel,
        out_shape=(
            jax.ShapeDtypeStruct((rows, feat + STAT), jnp.bfloat16),
            jax.ShapeDtypeStruct((4, feat), jnp.float32),
        ),
        in_specs=[VMEM] * 5,
        out_specs=(VMEM, VMEM),
        compiler_params=pltpu.CompilerParams(vmem_limit_bytes=8 * MIB),
        name="first_block",
    )(hidden_in, norm_gain, norm_bias, sums, cross(sums))

    up_row = up_bias[None, :]

    def add(*terms):
        return sum(t.astype(jnp.float32) for t in terms).astype(jnp.bfloat16)

    def finish(name, u, v, column=0):
        return output(
            index, PAIRS.index(name) * 2 * rows, column, up_row, u, v, att, other, w_attn_out, w_down
        )

    def pair(halves, *running):
        return add(halves[0], swap(halves[1]), *running)

    per_device = page_table.shape[0] // 2
    hidden = w_up.shape[1]
    o0 = first_block
    f1, b1, s0 = fwd(o0), bwd(o0), swap(o0)
    kept0, send0, *weights = project(
        index, affine, (w_query, w_key, w_value, w_up), [o0, s0], ((0, "q"),), True
    )
    f1, b1, send0, kept0 = after(f1, b1, send0, kept0)
    got0 = cross(send0)
    f2, b2 = fwd(f1), bwd(b1)
    kept1, send1, u_f1 = project(
        index, affine, weights, [f1, swap(f1), b1, swap(b1)], ((1, "q"), (0,))
    )
    f2, b2, got0, send1, u_f1 = after(f2, b2, got0, send1, u_f1)
    got1 = cross(send1)
    f3 = fwd(f2)
    kept2, send2, u_b2 = project(
        index, affine, weights, [f2, swap(f2), b2, swap(b2)], ((0, "q"), (1,))
    )
    f3, b2, got1, send2, u_b2, late_index = after(f3, b2, got1, send2, u_b2, index)
    got2 = cross(send2)
    f4, b3 = fwd(f3), bwd(b2)
    kept3, send3 = project(index, affine, weights, [f3, swap(f3)], ((0, "q"),))
    query_info, key_token, cosine, sine = tables(total_tokens, late_index, seq_lens, sink_count)
    b3, f4, got2, send3, query_info, key_token, cosine, sine = after(
        b3, f4, got2, send3, query_info, key_token, cosine, sine
    )
    got3 = cross(send3)
    kept4, send4, u_far = project(
        index, affine, weights, [b3, swap(b3), f4, swap(f4)], (("q",), (1, 0))
    )
    got3, send4, u_far = after(got3, send4, u_far)
    got4 = cross(send4)
    early_pairs = ("o0", "b1", "f2", "f3")
    got4, u_far = after(got4, u_far)
    v_far = cross(u_far)
    att, kv = attend(
        total_tokens // 16, (hidden, hidden, hidden, hidden, 0), index, qkv_bias, cosine, sine,
        query_info, key_token, [kept0, kept1, kept2, kept3, kept4], [got0, got1, got2, got3, got4],
    )
    v_far, att = after(v_far, att)
    other = cross(att)
    early = down(up_row, [send0, send1, send2, send3], [got0, got1, got2, got3], w_down)
    other, early, u_b2, u_f1, kv = after(other, early, u_b2, u_f1, kv)
    v_b2 = cross(u_b2)
    r_b = bwd(pair(finish("f4", u_far, v_far)))
    y_b3 = finish("b3", u_far, v_far, hidden)
    m_own, m_sib = mix(
        index, tuple(PAIRS.index(p) * 2 * rows for p in early_pairs), early, att, other, w_attn_out
    )
    m_got = swap(m_sib)
    v_b2, r_b, y_b3, m_own, m_got, u_f1, kv = after(v_b2, r_b, y_b3, m_own, m_got, u_f1, kv)

    def mixed(name):
        at = slice(early_pairs.index(name) * rows, (early_pairs.index(name) + 1) * rows)
        return m_own[at], m_got[at]

    v_f1 = cross(u_f1)
    r_b, r_f = bwd(add(r_b, *mixed("f3"))), fwd(pair(y_b3))
    y_b2 = finish("b2", u_b2, v_b2)
    paged = ordered_pages(index, page_table, kv)
    v_f1, r_b, r_f, y_b2, m_own, m_got, paged = after(v_f1, r_b, r_f, y_b2, m_own, m_got, paged)
    cache_mine, cache_got = paged[:per_device], cross(paged[per_device:])
    r_b, r_f = bwd(add(r_b, *mixed("f2"))), fwd(pair(y_b2, r_f))
    y_f1 = finish("f1", u_f1, v_f1)
    r_b, r_f, y_f1, cache_mine, cache_got = after(r_b, r_f, y_f1, cache_mine, cache_got)
    r_f, r_b = fwd(add(r_f, *mixed("b1"))), bwd(pair(y_f1, r_b))
    summed = sum(t.astype(jnp.float32) for t in (r_b, r_f, *mixed("o0")))
    hidden_out = (hidden_in.astype(jnp.float32) + summed + out_bias).astype(jnp.bfloat16)
    left = jnp.where(first_side, cache_mine, cache_got)
    right = jnp.where(first_side, cache_got, cache_mine)
    paged_cache = jnp.stack(
        [
            jnp.concatenate([left[..., :half], right[..., :half]], axis=-1),
            jnp.concatenate([left[..., half:], right[..., half:]], axis=-1),
        ]
    )
    return (hidden_out, paged_cache)


def solution(mesh):
    in_specs = (
        P("wide", "narrow"),
        P("narrow", "wide"),
        P("narrow", "wide"),
        P("narrow", "wide"),
        P(None, "wide"),
        P("narrow", "wide"),
        P("wide"),
        P("wide", "narrow"),
        P("wide", "narrow"),
        P("narrow"),
        P(None, "narrow"),
        P(None, "narrow"),
        P(),
        P(),
        P(),
    )
    out_specs = (P("wide", "narrow"), P(None, "narrow", None, "wide"))
    ringed = mesh.shape["wide"] == 2 * CHIPS and mesh.shape["narrow"] == 2
    local = local_ring if ringed else local_generic
    return jax.shard_map(local, mesh=mesh, in_specs=in_specs, out_specs=out_specs, check_vma=False)
```

```python
import functools

import jax
import jax.numpy as jnp
import numpy as np
from jax import lax
from jax.experimental import pallas as pl
from jax.experimental.pallas import tpu as pltpu
from jax.sharding import PartitionSpec as P

D = 6144
HEAD_DIM = 96
ROTARY = 24
PAGE = 16


def segment_info(token_index, seq_lens, sink_count):
    seq_ends = jnp.cumsum(seq_lens)
    seq_starts = seq_ends - seq_lens
    inside = (token_index[:, None] >= seq_starts[None, :]) & (
        token_index[:, None] < seq_ends[None, :]
    )
    member = inside.astype(jnp.int32)
    seq_number = jnp.arange(seq_lens.shape[0], dtype=jnp.int32)
    segment = jnp.sum(member * seq_number[None, :], axis=1)
    position = token_index - jnp.sum(member * seq_starts[None, :], axis=1)
    sink_limit = jnp.sum(member * sink_count[None, :], axis=1)
    return (segment, position, sink_limit)


def rotate(values, position):
    half_rot = ROTARY // 2
    freq_index = jnp.arange(half_rot, dtype=jnp.float32)
    inverse = jnp.power(jnp.float32(10000.0), -2.0 * freq_index / ROTARY)
    angles = position.astype(jnp.float32)[:, None] * inverse[None, :]
    cosine = jnp.cos(angles)[:, None, :]
    sine_part = jnp.sin(angles)[:, None, :]
    first_half = values[..., :half_rot]
    second_half = values[..., half_rot:ROTARY]
    return jnp.concatenate(
        [
            first_half * cosine - second_half * sine_part,
            second_half * cosine + first_half * sine_part,
            values[..., ROTARY:],
        ],
        axis=-1,
    )


def local_generic(
    hidden_in,
    w_query,
    w_key,
    w_value,
    qkv_bias,
    w_up,
    up_bias,
    w_attn_out,
    w_down,
    out_bias,
    norm_gain,
    norm_bias,
    seq_lens,
    sink_count,
    page_table,
):
    wide_count = lax.axis_size("wide")
    narrow_count = lax.axis_size("narrow")
    narrow_index = lax.axis_index("narrow")
    tok_local, feat_local = hidden_in.shape
    sub_rows = tok_local // narrow_count
    total_tokens = tok_local * wide_count
    query_rows = wide_count * sub_rows
    head_cols = w_query.shape[1]
    heads_local = head_cols // HEAD_DIM
    as_float = hidden_in.astype(jnp.float32)
    partial_sum = jnp.sum(as_float, axis=1)
    partial_square = jnp.sum(as_float * as_float, axis=1)
    total_sum, total_square = lax.psum((partial_sum, partial_square), "narrow")
    average = total_sum / D
    variance = total_square / D - average * average
    scaled = (as_float - average[:, None]) * lax.rsqrt(variance + 1e-05)[:, None]
    attn_normed = (scaled * norm_gain[0] + norm_bias[0]).astype(jnp.bfloat16)
    mlp_normed = (scaled * norm_gain[1] + norm_bias[1]).astype(jnp.bfloat16)
    stacked = jnp.stack([attn_normed, mlp_normed]).reshape(2, narrow_count, sub_rows, feat_local)
    gathered = lax.all_gather(stacked, "wide", axis=2, tiled=True).reshape(
        2, total_tokens, feat_local
    )
    local_order = jnp.arange(query_rows, dtype=jnp.int32)
    local_tokens = (
        local_order // sub_rows * tok_local + narrow_index * sub_rows + local_order % sub_rows
    )
    local_seg, local_pos, local_sink = segment_info(local_tokens, seq_lens, sink_count)
    all_order = jnp.arange(total_tokens, dtype=jnp.int32)
    all_tokens = (
        all_order % query_rows // sub_rows * tok_local
        + all_order // query_rows * sub_rows
        + all_order % sub_rows
    )
    all_seg, all_pos, all_sink = segment_info(all_tokens, seq_lens, sink_count)
    qkv_weight = jnp.concatenate([w_query, w_key, w_value], axis=1)
    attn_part = gathered[0]
    mlp_part = gathered[1]
    summed = lax.psum_scatter(
        jnp.concatenate(
            [
                jnp.dot(attn_part, qkv_weight, preferred_element_type=jnp.float32),
                jnp.dot(mlp_part, w_up, preferred_element_type=jnp.float32),
            ],
            axis=1,
        ).astype(jnp.bfloat16),
        "narrow",
        scatter_dimension=0,
        tiled=True,
    ).astype(jnp.float32)
    query_sum = summed[:, :head_cols]
    key_sum = summed[:, head_cols : 2 * head_cols]
    value_sum = summed[:, 2 * head_cols : 3 * head_cols]
    unit_sum = summed[:, 3 * head_cols :]
    keys_local = (
        rotate((key_sum + qkv_bias[1]).reshape(query_rows, heads_local, HEAD_DIM), local_pos)
        .astype(jnp.bfloat16)
        .reshape(query_rows, head_cols)
    )
    values_local = (value_sum + qkv_bias[2]).astype(jnp.bfloat16)
    all_keys, all_values = (
        lax.all_gather(keys_local, "narrow", axis=0, tiled=True),
        lax.all_gather(values_local, "narrow", axis=0, tiled=True),
    )
    queries = rotate(
        (query_sum + qkv_bias[0]).reshape(query_rows, heads_local, HEAD_DIM), local_pos
    ).astype(jnp.bfloat16)
    hidden_units = jax.nn.gelu(unit_sum + up_bias, approximate=False).astype(jnp.bfloat16)
    window_span = total_tokens // 16
    allowed = (local_seg[:, None] == all_seg[None, :]) & (all_pos[None, :] <= local_pos[:, None])
    allowed = allowed & (
        (local_pos[:, None] - all_pos[None, :] < window_span)
        | (all_pos[None, :] < local_sink[:, None])
    )
    key_heads = all_keys.reshape(total_tokens, heads_local, HEAD_DIM)
    value_heads = all_values.reshape(total_tokens, heads_local, HEAD_DIM)
    scores = jnp.einsum("qhd,khd->hqk", queries, key_heads, preferred_element_type=jnp.float32) * (
        1.0 / HEAD_DIM**0.5
    )
    masked = jnp.where(allowed[None], scores, jnp.float32(-1e30))
    top_score = jnp.max(masked, axis=2, keepdims=True)
    weights = jnp.exp(masked - top_score)
    probs = (weights / jnp.sum(weights, axis=2, keepdims=True)).astype(jnp.bfloat16)
    attended = (
        jnp.einsum("hqk,khd->qhd", probs, value_heads, preferred_element_type=jnp.float32)
        .astype(jnp.bfloat16)
        .reshape(query_rows, head_cols)
    )
    full_out, full_down = (
        lax.all_gather(w_attn_out, "narrow", axis=1, tiled=True),
        lax.all_gather(w_down, "narrow", axis=1, tiled=True),
    )
    attn_part = attended
    own_rows = lax.psum_scatter(
        (
            jnp.dot(attn_part, full_out, preferred_element_type=jnp.float32)
            + jnp.dot(hidden_units, full_down, preferred_element_type=jnp.float32)
        ).astype(jnp.bfloat16),
        "wide",
        scatter_dimension=0,
        tiled=True,
    ).astype(jnp.float32)
    combined = lax.all_to_all(
        own_rows.astype(jnp.bfloat16), "narrow", split_axis=1, concat_axis=0, tiled=True
    ).astype(own_rows.dtype)
    hidden_out = (as_float + combined + out_bias).astype(jnp.bfloat16)
    pages_local = page_table.shape[0] // narrow_count
    slot_ids = narrow_index * pages_local + jnp.arange(pages_local, dtype=jnp.int32)
    matches = (page_table[None, :] == slot_ids[:, None]).astype(jnp.int32)
    source_page = jnp.sum(
        matches * jnp.arange(page_table.shape[0], dtype=jnp.int32)[None, :], axis=1
    )
    token_ids = (source_page[:, None] * PAGE + jnp.arange(PAGE, dtype=jnp.int32)[None, :]).reshape(
        -1
    )
    gather_rows = (
        token_ids % tok_local // sub_rows * query_rows
        + token_ids // tok_local * sub_rows
        + token_ids % sub_rows
    )
    cache_keys = jnp.take(all_keys, gather_rows, axis=0).reshape(pages_local, PAGE, head_cols)
    cache_values = jnp.take(all_values, gather_rows, axis=0).reshape(pages_local, PAGE, head_cols)
    paged_cache = jnp.stack([cache_keys, cache_values])
    return (hidden_out, paged_cache)


CHIP_RING = (0, 2, 4, 6, 7, 5, 3, 1)
CHIPS = len(CHIP_RING)
PAIRS = ("o0", "f1", "b1", "f2", "b2", "f3", "b3", "f4")
STAT = 128
HEAD_PAD = 128
LANE_GROUP = 32
MIB = 1 << 20
VMEM = pl.BlockSpec(memory_space=pltpu.VMEM)
HBM = pl.BlockSpec(memory_space=pltpu.HBM)
SMEM = pl.BlockSpec(memory_space=pltpu.SMEM)


def owner_table():
    table = np.zeros((2 * CHIPS, 2 * CHIPS), np.int32)
    for place, chip in enumerate(CHIP_RING):
        for core in range(2):
            order = []
            for pair in PAIRS:
                shift = (-1 if pair[0] == "f" else 1) * int(pair[1]) * (1 - 2 * core)
                order.append(CHIP_RING[(place + shift) % CHIPS] * 2 + core)
                order.append(CHIP_RING[(place - shift) % CHIPS] * 2 + 1 - core)
            table[2 * chip + core] = order
    return table


def place_table():
    owners = owner_table()
    table = np.zeros_like(owners)
    for device in range(owners.shape[0]):
        table[device, owners[device]] = np.arange(owners.shape[1])
    return table


def sums_kernel(device_ref, n_ref, x_ref, out_ref, index_ref, copy_ref):
    x = x_ref[...].astype(jnp.float32)
    first = jnp.sum(x, axis=1, keepdims=True)
    second = jnp.sum(x * x, axis=1, keepdims=True)
    lane = lax.broadcasted_iota(jnp.int32, out_ref.shape, 1)
    out_ref[...] = jnp.where(lane == 0, first, jnp.where(lane == 1, second, 0.0))
    copy_ref[...] = x_ref[...]
    index_ref[0] = device_ref[0]
    index_ref[1] = n_ref[0]


def block_kernel(x_ref, here_ref, there_ref, out_ref):
    feat = x_ref.shape[1]
    total = here_ref[...] + there_ref[...]
    average = total[:, 0:1] / D
    variance = total[:, 1:2] / D - average * average
    scale = lax.rsqrt(variance + 1e-05)
    lane = lax.broadcasted_iota(jnp.int32, (x_ref.shape[0], STAT), 1)
    tail = jnp.zeros((x_ref.shape[0], STAT), jnp.float32)
    for start, value in ((0, average), (3, scale)):
        for term in range(3):
            piece = value.astype(jnp.bfloat16).astype(jnp.float32)
            tail = jnp.where(lane == start + term, piece, tail)
            value = value - piece
    out_ref[:, :feat] = x_ref[...]
    out_ref[:, feat:] = tail.astype(jnp.bfloat16)


def tables_kernel(index_ref, owners_ref, lens_ref, sinks_ref, inverse_ref, phase_ref, info_ref, key_ref, cos_ref, sin_ref):
    device = index_ref[0]
    blocks = owners_ref.shape[1]
    rows = info_ref.shape[0] // blocks
    half_rot = ROTARY // 2
    lane = lax.broadcasted_iota(jnp.int32, (rows, HEAD_PAD), 1)
    sub = lax.broadcasted_iota(jnp.int32, (rows, HEAD_PAD), 0)
    key_lane = lax.broadcasted_iota(jnp.int32, key_ref.shape, 1)
    key = key_lane
    shared = HEAD_PAD // LANE_GROUP
    for base in range(0, blocks, shared):
        position = jnp.zeros((rows, HEAD_PAD), jnp.int32)
        for g in range(shared):
            j = base + g
            first = owners_ref[device, j] * rows
            key = jnp.where(key_lane // rows == j, first + key_lane - j * rows, key)
            token = first + sub
            begin, end = jnp.zeros_like(token), jnp.zeros_like(token)
            start = jnp.int32(0)
            for s in range(lens_ref.shape[0]):
                inside = (token >= start) & (token < start + lens_ref[s])
                begin = jnp.where(inside, start, begin)
                end = jnp.where(inside, start + sinks_ref[s], end)
                start = start + lens_ref[s]
            info_ref[j * rows : (j + 1) * rows, :] = jnp.where(
                lane == 0, token, jnp.where(lane == 1, begin, end)
            )
            position = jnp.where(lane // LANE_GROUP == g, token - begin, position)
        waves = jnp.cos(position.astype(jnp.float32) * inverse_ref[...] - phase_ref[...])
        for g in range(shared):
            at = slice((base + g) * rows, (base + g + 1) * rows)
            here = pltpu.roll(waves, (HEAD_PAD - g * LANE_GROUP) % HEAD_PAD, 1)
            later = pltpu.roll(waves, (HEAD_PAD - g * LANE_GROUP + half_rot) % HEAD_PAD, 1)
            before = pltpu.roll(waves, (2 * HEAD_PAD - g * LANE_GROUP - half_rot) % HEAD_PAD, 1)
            cosine = jnp.where(lane < half_rot, here, later)
            cos_ref[at, :] = jnp.where(lane < ROTARY, cosine, 1.0)
            sine = jnp.where(lane < half_rot, -before, here)
            sin_ref[at, :] = jnp.where(lane < ROTARY, sine, 0.0)
    key_ref[...] = key


def tables(total, index, lens, sinks):
    half_rot = ROTARY // 2
    lane = np.arange(HEAD_PAD) % LANE_GROUP
    inverse = (10000.0 ** (-2.0 * (lane % half_rot) / ROTARY)).astype(np.float32)[None, :]
    phase = np.where(lane < half_rot, 0.0, np.pi / 2).astype(np.float32)[None, :]
    wide = (total, HEAD_PAD)
    return pl.pallas_call(
        tables_kernel,
        out_shape=(
            jax.ShapeDtypeStruct(wide, jnp.int32),
            jax.ShapeDtypeStruct((1, total), jnp.int32),
            jax.ShapeDtypeStruct(wide, jnp.float32),
            jax.ShapeDtypeStruct(wide, jnp.float32),
        ),
        in_specs=[SMEM] * 4 + [VMEM] * 2,
        out_specs=(VMEM,) * 4,
        compiler_params=pltpu.CompilerParams(vmem_limit_bytes=8 * MIB),
        name="tables",
    )(index, jnp.asarray(owner_table()), lens, sinks, jnp.asarray(inverse), jnp.asarray(phase))


def pages_kernel(index_ref, places_ref, table_ref, kv_ref, out_ref):
    pages = table_ref.shape[0]
    per_owner = pages // places_ref.shape[1]
    device, shift = index_ref[0], index_ref[1] * (pages // 2)
    for p in range(pages):
        place = places_ref[device, p // per_owner] * per_owner + p % per_owner
        row = pl.multiple_of(place * PAGE, PAGE)
        out_ref[lax.rem(table_ref[p] + shift, pages)] = kv_ref[pl.ds(row, PAGE), :]


def ordered_pages(index, page_table, kv):
    return pl.pallas_call(
        pages_kernel,
        out_shape=jax.ShapeDtypeStruct((page_table.shape[0], PAGE, kv.shape[1]), kv.dtype),
        in_specs=[SMEM] * 3 + [VMEM],
        out_specs=VMEM,
        compiler_params=pltpu.CompilerParams(vmem_limit_bytes=8 * MIB),
        name="ordered_pages",
    )(index, jnp.asarray(place_table()), page_table, kv)


def normalise(blocks, gain_ref, bias_ref, attn, mlp):
    rows = blocks[0].shape[0]
    feat = attn.shape[1]
    step = 512
    for b, block in enumerate(blocks):
        tail = block[:, feat:].astype(jnp.float32)
        average = tail[:, 0:1] + tail[:, 1:2] + tail[:, 2:3]
        scale = tail[:, 3:4] + tail[:, 4:5] + tail[:, 5:6]
        here = slice(b * rows, (b + 1) * rows)
        for c in range(0, feat, step):
            at = slice(c, c + step)
            scaled = (block[:, at].astype(jnp.float32) - average) * scale
            attn[here, at] = (scaled * gain_ref[0:1, at] + bias_ref[0:1, at]).astype(jnp.bfloat16)
            mlp[here, at] = (scaled * gain_ref[1:2, at] + bias_ref[1:2, at]).astype(jnp.bfloat16)


def project_kernel(count, outs, first_call, index_ref, gain_ref, bias_ref, wq_ref, wk_ref, wv_ref, wu_ref, *refs):
    blocks, refs = refs[:count], refs[count:]
    mine_ref, refs = refs[0], refs[1:]
    sent_refs, refs = refs[: len(outs)], refs[len(outs) :]
    hidden = wu_ref.shape[1]
    width = 384
    tiles = hidden // width
    copies = []
    if first_call:
        held, (attn, mlp, gain, bias, sems) = refs[:4], refs[4:]
        small = [
            pltpu.make_async_copy(gain_ref, gain, sems.at[3 + tiles]),
            pltpu.make_async_copy(bias_ref, bias, sems.at[4 + tiles]),
        ]
        for copy in small:
            copy.start()
        gain_ref, bias_ref = gain, bias
        copies = [
            pltpu.make_async_copy(src, dst, sems.at[i])
            for i, (src, dst) in enumerate(zip((wq_ref, wk_ref, wv_ref), held))
        ]
        for t in range(tiles):
            at = slice(t * width, (t + 1) * width)
            copies.append(pltpu.make_async_copy(wu_ref.at[:, at], held[3].at[:, at], sems.at[3 + t]))
        for copy in copies:
            copy.start()
        for copy in small:
            copy.wait()
        wq_ref, wk_ref, wv_ref, wu_ref = held
    else:
        attn, mlp = refs
    rows = 2 * blocks[0].shape[0]
    half = wq_ref.shape[1] // 2
    normalise(blocks, gain_ref, bias_ref, attn, mlp)
    low, high = [], []
    for i, weight in enumerate((wq_ref, wk_ref, wv_ref)):
        if first_call:
            copies[i].wait()
        part = jnp.dot(attn[...], weight[...], preferred_element_type=jnp.float32)
        low.append(part[:, :half])
        high.append(part[:, half:])
    low = jnp.concatenate(low, axis=1).astype(jnp.bfloat16)
    high = jnp.concatenate(high, axis=1).astype(jnp.bfloat16)
    first = index_ref[1] == 0
    mine_ref[...] = jnp.where(first, low, high)
    send = jnp.where(first, high, low)
    send = [send[p * rows : (p + 1) * rows] for p in range(count // 2)]
    gap = -(3 * half * len(send)) % 128
    if gap:
        send.append(jnp.zeros((rows, gap), jnp.bfloat16))
    send = jnp.concatenate(send, axis=1)
    for ref, items in zip(sent_refs, outs):
        if items[-1] == "q":
            ref[:, hidden * (len(items) - 1) :] = send
    for t in range(tiles):
        if first_call:
            copies[3 + t].wait()
        at = slice(t * width, (t + 1) * width)
        part = jnp.dot(mlp[...], wu_ref[:, at], preferred_element_type=jnp.float32)
        part = part.astype(jnp.bfloat16)
        for ref, items in zip(sent_refs, outs):
            for i, item in enumerate(items):
                if item != "q":
                    begin = i * hidden + t * width
                    ref[:, begin : begin + width] = part[item * rows : (item + 1) * rows]


def project(n, affine, weights, blocks, outs, first_call=False):
    count = len(blocks)
    rows = 2 * blocks[0].shape[0]
    feat, cols = weights[0].shape
    hidden = weights[3].shape[1]
    sent = 3 * cols // 2 * (count // 2)
    sent += -sent % 128
    shapes = [jax.ShapeDtypeStruct((rows * count // 2, 3 * cols // 2), jnp.bfloat16)]
    for items in outs:
        width = sum(sent if item == "q" else hidden for item in items)
        shapes.append(jax.ShapeDtypeStruct((rows, width), jnp.bfloat16))
    scratch = [pltpu.VMEM((rows * count // 2, feat), jnp.bfloat16)] * 2
    if first_call:
        shapes += [jax.ShapeDtypeStruct(w.shape, w.dtype) for w in weights]
        scratch += [pltpu.VMEM(v.shape, v.dtype) for v in affine]
        scratch.append(pltpu.SemaphoreType.DMA((5 + hidden // 384,)))
    return pl.pallas_call(
        functools.partial(project_kernel, count, outs, first_call),
        out_shape=tuple(shapes),
        in_specs=[SMEM] + [HBM if first_call else VMEM] * 6 + [VMEM] * count,
        out_specs=(VMEM,) * len(shapes),
        scratch_shapes=scratch,
        compiler_params=pltpu.CompilerParams(vmem_limit_bytes=(46 if first_call else 9) * MIB),
        name="project",
    )(n, *affine, *weights, *blocks)


def attend_kernel(count, span, offsets, index_ref, bias_ref, cos_ref, sin_ref, query_ref, key_ref, *refs):
    mine, got = refs[:count], refs[count : 2 * count]
    att_ref, kv_ref, queries, keys, values = refs[2 * count :]
    heads = queries.shape[0]
    half = kv_ref.shape[1] // 2
    total = kv_ref.shape[0]
    half_rot = ROTARY // 2
    bias = jnp.where(index_ref[1] == 0, bias_ref[:, :half], bias_ref[:, half:])
    offset = 0
    for g in range(count):
        rows = mine[g].shape[0]
        at = slice(offset, offset + rows)
        offset += rows
        pieces = []
        for p in range(rows // got[g].shape[0]):
            begin = offsets[g] + 3 * half * p
            pieces.append(got[g][:, begin : begin + 3 * half])
        sent = jnp.concatenate(pieces, axis=0)
        summed = mine[g][...].astype(jnp.float32) + sent.astype(jnp.float32)
        cosine, sine = cos_ref[at, :], sin_ref[at, :]
        lane = lax.broadcasted_iota(jnp.int32, (rows, HEAD_PAD), 1)
        pad = jnp.zeros((rows, HEAD_PAD - HEAD_DIM), jnp.float32)
        for kind in range(3):
            kept = []
            for h in range(heads):
                begin = kind * half + h * HEAD_DIM
                u = summed[:, begin : begin + HEAD_DIM]
                u = u + bias[kind : kind + 1, h * HEAD_DIM : (h + 1) * HEAD_DIM]
                u = jnp.concatenate([u, pad], axis=1)
                if kind < 2:
                    other = jnp.where(
                        lane < half_rot,
                        pltpu.roll(u, HEAD_PAD - half_rot, 1),
                        pltpu.roll(u, half_rot, 1),
                    )
                    u = u * cosine + other * sine
                (queries, keys, values)[kind][h, at, :] = u.astype(jnp.bfloat16)
                kept.append(u[:, :HEAD_DIM])
            if kind > 0:
                kv_ref[at, (kind - 1) * half : kind * half] = jnp.concatenate(kept, axis=1).astype(
                    jnp.bfloat16
                )
    tile = 256
    for start in range(0, total, tile):
        at = slice(start, start + tile)
        info = query_ref[at, :]
        token, begin, end = info[:, 0:1], info[:, 1:2], info[:, 2:3]
        key_token = key_ref[...]
        near = key_token > token - span
        allowed = (key_token >= begin) & (key_token <= token) & (near | (key_token < end))
        outs = []
        for h in range(heads):
            scores = lax.dot_general(
                queries[h, at, :],
                keys[h],
                (((1,), (1,)), ((), ())),
                preferred_element_type=jnp.float32,
            ) * (1.0 / HEAD_DIM**0.5)
            masked = jnp.where(allowed, scores, -1e30)
            weights = jnp.exp(masked - jnp.max(masked, axis=1, keepdims=True))
            probs = weights / jnp.sum(weights, axis=1, keepdims=True)
            out = jnp.dot(probs.astype(jnp.bfloat16), values[h], preferred_element_type=jnp.float32)
            outs.append(out[:, :HEAD_DIM])
        side = start // (total // 2)
        att_ref[start % (total // 2) : start % (total // 2) + tile, side * half : (side + 1) * half] = (
            jnp.concatenate(outs, axis=1).astype(jnp.bfloat16)
        )


def attend(span, offsets, n, bias, cosine, sine, query_info, key_token, mine, got):
    count = len(mine)
    total = cosine.shape[0]
    half = mine[0].shape[1] // 3
    heads = half // HEAD_DIM
    scratch = pltpu.VMEM((heads, total, HEAD_PAD), jnp.bfloat16)
    return pl.pallas_call(
        functools.partial(attend_kernel, count, span, offsets),
        out_shape=(
            jax.ShapeDtypeStruct((total // 2, 2 * half), jnp.bfloat16),
            jax.ShapeDtypeStruct((total, 2 * half), jnp.bfloat16),
        ),
        in_specs=[SMEM] + [VMEM] * (5 + 2 * count),
        out_specs=(VMEM, VMEM),
        scratch_shapes=[scratch, scratch, scratch],
        compiler_params=pltpu.CompilerParams(vmem_limit_bytes=10 * MIB),
        name="attend",
    )(n, bias, cosine, sine, query_info, key_token, *mine, *got)


def gelu(u):
    return u * (1.0 + lax.erf(u * (0.5**0.5))) * 0.5


def down_kernel(count, bias_ref, wd_ref, *refs):
    mine, got = refs[:count], refs[count : 2 * count]
    out_ref, units = refs[2 * count :]
    rows = mine[0].shape[0]
    step = 384
    for i in range(count):
        for c in range(0, units.shape[1], step):
            at = slice(c, c + step)
            u = mine[i][:, at].astype(jnp.float32) + got[i][:, at].astype(jnp.float32)
            u = gelu(u + bias_ref[:, at])
            units[i * rows : (i + 1) * rows, at] = u.astype(jnp.bfloat16)
    width, tall = 512, 2 * rows
    for c in range(0, wd_ref.shape[1], width):
        at = slice(c, c + width)
        for r in range(0, units.shape[0], tall):
            here = slice(r, r + tall)
            out = jnp.dot(units[here, :], wd_ref[:, at], preferred_element_type=jnp.float32)
            out_ref[here, at] = out.astype(jnp.bfloat16)


def down(bias, mine, got, wd):
    count = len(mine)
    rows, hidden = mine[0].shape[0], wd.shape[0]
    return pl.pallas_call(
        functools.partial(down_kernel, count),
        out_shape=jax.ShapeDtypeStruct((count * rows, wd.shape[1]), jnp.bfloat16),
        in_specs=[VMEM] * (2 + 2 * count),
        out_specs=VMEM,
        scratch_shapes=[pltpu.VMEM((count * rows, hidden), jnp.bfloat16)],
        compiler_params=pltpu.CompilerParams(vmem_limit_bytes=6 * MIB),
        name="down",
    )(bias, wd, *mine, *got)


def attended_rows(ref, offset, rows):
    height, half = ref.shape[0], ref.shape[1] // 2
    side = offset // height
    return ref[offset % height : offset % height + rows, side * half : (side + 1) * half]


def mix_kernel(offsets, index_ref, down_ref, att_ref, other_ref, wo_ref, own_ref, sib_ref):
    half = att_ref.shape[1] // 2
    rows = own_ref.shape[0] // len(offsets)
    n = index_ref[1]
    here = pl.ds(pl.multiple_of(n * half, 16), half)
    there = pl.ds(pl.multiple_of((1 - n) * half, 16), half)
    mine = jnp.concatenate([attended_rows(att_ref, o, 2 * rows) for o in offsets], axis=0)
    other = jnp.concatenate([attended_rows(other_ref, o, 2 * rows) for o in offsets], axis=0)
    width = 512
    for c in range(0, own_ref.shape[1], width):
        at = slice(c, c + width)
        out = down_ref[:, at].astype(jnp.float32)
        out += jnp.dot(mine, wo_ref[here, at], preferred_element_type=jnp.float32)
        out += jnp.dot(other, wo_ref[there, at], preferred_element_type=jnp.float32)
        out = out.astype(jnp.bfloat16)
        for i in range(len(offsets)):
            own_ref[i * rows : (i + 1) * rows, at] = out[2 * i * rows : (2 * i + 1) * rows]
            sib_ref[i * rows : (i + 1) * rows, at] = out[(2 * i + 1) * rows : (2 * i + 2) * rows]


def mix(n, offsets, partial_down, att, other, wo):
    rows, feat = partial_down.shape
    shape = jax.ShapeDtypeStruct((rows // 2, feat), jnp.bfloat16)
    return pl.pallas_call(
        functools.partial(mix_kernel, offsets),
        out_shape=(shape, shape),
        in_specs=[SMEM] + [VMEM] * 4,
        out_specs=(VMEM, VMEM),
        compiler_params=pltpu.CompilerParams(vmem_limit_bytes=5 * MIB),
        name="mix",
    )(n, partial_down, att, other, wo)


def output_kernel(
    offset, column, index_ref, bias_ref, mine_ref, got_ref, att_ref, other_ref, wo_ref, wd_ref, own_ref, sib_ref, units
):
    rows = mine_ref.shape[0]
    half = att_ref.shape[1] // 2
    own_rows = own_ref.shape[0]
    step = 384
    for c in range(0, units.shape[1], step):
        at = slice(c, c + step)
        there = slice(column + c, column + c + step)
        u = mine_ref[:, there].astype(jnp.float32) + got_ref[:, there].astype(jnp.float32)
        units[:, at] = gelu(u + bias_ref[:, at]).astype(jnp.bfloat16)
    n = index_ref[1]
    here = pl.ds(pl.multiple_of(n * half, 16), half)
    there = pl.ds(pl.multiple_of((1 - n) * half, 16), half)
    mine = attended_rows(att_ref, offset, rows)
    other = attended_rows(other_ref, offset, rows)
    width = 512
    for c in range(0, wd_ref.shape[1], width):
        at = slice(c, c + width)
        out = jnp.dot(units[...], wd_ref[:, at], preferred_element_type=jnp.float32)
        out += jnp.dot(mine, wo_ref[here, at], preferred_element_type=jnp.float32)
        out += jnp.dot(other, wo_ref[there, at], preferred_element_type=jnp.float32)
        out = out.astype(jnp.bfloat16)
        own_ref[:, at] = out[:own_rows]
        sib_ref[:, at] = out[own_rows:]


def output(n, offset, column, bias, mine, got, att, other, wo, wd):
    rows, hidden = mine.shape[0], wd.shape[0]
    shape = jax.ShapeDtypeStruct((rows // 2, wd.shape[1]), jnp.bfloat16)
    return pl.pallas_call(
        functools.partial(output_kernel, offset, column),
        out_shape=(shape, shape),
        in_specs=[SMEM] + [VMEM] * 7,
        out_specs=(VMEM, VMEM),
        scratch_shapes=[pltpu.VMEM((rows, hidden), jnp.bfloat16)],
        compiler_params=pltpu.CompilerParams(vmem_limit_bytes=5 * MIB),
        name="output",
    )(n, bias, mine, got, att, other, wo, wd)


def after(*values):
    return lax.optimization_barrier(values)


def local_ring(
    hidden_in,
    w_query,
    w_key,
    w_value,
    qkv_bias,
    w_up,
    up_bias,
    w_attn_out,
    w_down,
    out_bias,
    norm_gain,
    norm_bias,
    seq_lens,
    sink_count,
    page_table,
):
    device = lax.axis_index("wide").astype(jnp.int32).reshape(1)
    n = lax.axis_index("narrow").astype(jnp.int32)
    n_arg = n.reshape(1)
    rows, feat = hidden_in.shape
    total_tokens = rows * lax.axis_size("wide")
    half = w_query.shape[1] // 2

    fwd_pairs, bwd_pairs, swap_pairs = [], [], []
    for p in range(CHIPS):
        here, next_chip = CHIP_RING[p], CHIP_RING[(p + 1) % CHIPS]
        fwd_pairs += [(2 * here, 2 * next_chip), (2 * next_chip + 1, 2 * here + 1)]
        bwd_pairs += [(2 * next_chip, 2 * here), (2 * here + 1, 2 * next_chip + 1)]
        swap_pairs += [(2 * here, 2 * here + 1), (2 * here + 1, 2 * here)]
    fwd = lambda v: lax.ppermute(v, "wide", fwd_pairs)
    bwd = lambda v: lax.ppermute(v, "wide", bwd_pairs)
    swap = lambda v: lax.ppermute(v, "wide", swap_pairs)
    cross = lambda v: lax.ppermute(v, "narrow", [(0, 1), (1, 0)])

    first_side, n_arg = after(n == 0, n_arg)
    sums, index, copied = pl.pallas_call(
        sums_kernel,
        out_shape=(
            jax.ShapeDtypeStruct((rows, STAT), jnp.float32),
            jax.ShapeDtypeStruct((2,), jnp.int32),
            jax.ShapeDtypeStruct((rows, feat), jnp.bfloat16),
        ),
        in_specs=[SMEM, SMEM, VMEM],
        out_specs=(VMEM, SMEM, VMEM),
        compiler_params=pltpu.CompilerParams(vmem_limit_bytes=8 * MIB),
        name="row_sums",
    )(device, n_arg, hidden_in)
    first_block = pl.pallas_call(
        block_kernel,
        out_shape=jax.ShapeDtypeStruct((rows, feat + STAT), jnp.bfloat16),
        in_specs=[VMEM] * 3,
        out_specs=VMEM,
        compiler_params=pltpu.CompilerParams(vmem_limit_bytes=8 * MIB),
        name="first_block",
    )(copied, sums, cross(sums))
    affine = (norm_gain, norm_bias)

    up_row = up_bias[None, :]

    def add(*terms):
        return sum(t.astype(jnp.float32) for t in terms).astype(jnp.bfloat16)

    def finish(name, u, v, column=0):
        return output(
            index, PAIRS.index(name) * 2 * rows, column, up_row, u, v, att, other, w_attn_out, w_down
        )

    def pair(halves, *running):
        return add(halves[0], swap(halves[1]), *running)

    per_device = page_table.shape[0] // 2
    hidden = w_up.shape[1]
    o0 = first_block
    f1, b1, s0 = fwd(o0), bwd(o0), swap(o0)
    kept0, send0, *weights = project(
        index, affine, (w_query, w_key, w_value, w_up), [o0, s0], ((0, "q"),), True
    )
    f1, b1, send0, kept0 = after(f1, b1, send0, kept0)
    got0 = cross(send0)
    f2, b2 = fwd(f1), bwd(b1)
    kept1, send1, u_f1 = project(
        index, affine, weights, [f1, swap(f1), b1, swap(b1)], ((1, "q"), (0,))
    )
    f2, b2, got0, send1, u_f1 = after(f2, b2, got0, send1, u_f1)
    got1 = cross(send1)
    f3 = fwd(f2)
    kept2, send2, u_b2 = project(
        index, affine, weights, [f2, swap(f2), b2, swap(b2)], ((0, "q"), (1,))
    )
    f3, b2, got1, send2, u_b2, late_index = after(f3, b2, got1, send2, u_b2, index)
    got2 = cross(send2)
    f4, b3 = fwd(f3), bwd(b2)
    kept3, send3 = project(index, affine, weights, [f3, swap(f3)], ((0, "q"),))
    query_info, key_token, cosine, sine = tables(total_tokens, late_index, seq_lens, sink_count)
    b3, f4, got2, send3, query_info, key_token, cosine, sine = after(
        b3, f4, got2, send3, query_info, key_token, cosine, sine
    )
    got3 = cross(send3)
    kept4, send4, u_far = project(
        index, affine, weights, [b3, swap(b3), f4, swap(f4)], (("q",), (1, 0))
    )
    got3, send4, u_far = after(got3, send4, u_far)
    got4 = cross(send4)
    early_pairs = ("o0", "b1", "f2", "f3")
    got4, u_far = after(got4, u_far)
    v_far = cross(u_far)
    att, kv = attend(
        total_tokens // 16, (hidden, hidden, hidden, hidden, 0), index, qkv_bias, cosine, sine,
        query_info, key_token, [kept0, kept1, kept2, kept3, kept4], [got0, got1, got2, got3, got4],
    )
    v_far, att = after(v_far, att)
    other = cross(att)
    early = down(up_row, [send0, send1, send2, send3], [got0, got1, got2, got3], w_down)
    other, early, u_b2, u_f1, kv = after(other, early, u_b2, u_f1, kv)
    v_b2 = cross(u_b2)
    r_b = bwd(pair(finish("f4", u_far, v_far)))
    y_b3 = finish("b3", u_far, v_far, hidden)
    m_own, m_sib = mix(
        index, tuple(PAIRS.index(p) * 2 * rows for p in early_pairs), early, att, other, w_attn_out
    )
    m_got = swap(m_sib)
    v_b2, r_b, y_b3, m_own, m_got, u_f1, kv = after(v_b2, r_b, y_b3, m_own, m_got, u_f1, kv)

    def mixed(name):
        at = slice(early_pairs.index(name) * rows, (early_pairs.index(name) + 1) * rows)
        return m_own[at], m_got[at]

    v_f1 = cross(u_f1)
    r_b, r_f = bwd(add(r_b, *mixed("f3"))), fwd(pair(y_b3))
    y_b2 = finish("b2", u_b2, v_b2)
    paged = ordered_pages(index, page_table, kv)
    v_f1, r_b, r_f, y_b2, m_own, m_got, paged = after(v_f1, r_b, r_f, y_b2, m_own, m_got, paged)
    cache_mine, cache_got = paged[:per_device], cross(paged[per_device:])
    r_b, r_f = bwd(add(r_b, *mixed("f2"))), fwd(pair(y_b2, r_f))
    y_f1 = finish("f1", u_f1, v_f1)
    r_b, r_f, y_f1, cache_mine, cache_got = after(r_b, r_f, y_f1, cache_mine, cache_got)
    r_f, r_b = fwd(add(r_f, *mixed("b1"))), bwd(pair(y_f1, r_b))
    summed = sum(t.astype(jnp.float32) for t in (r_b, r_f, *mixed("o0")))
    hidden_out = (hidden_in.astype(jnp.float32) + summed + out_bias).astype(jnp.bfloat16)
    left = jnp.where(first_side, cache_mine, cache_got)
    right = jnp.where(first_side, cache_got, cache_mine)
    paged_cache = jnp.stack(
        [
            jnp.concatenate([left[..., :half], right[..., :half]], axis=-1),
            jnp.concatenate([left[..., half:], right[..., half:]], axis=-1),
        ]
    )
    return (hidden_out, paged_cache)


def solution(mesh):
    in_specs = (
        P("wide", "narrow"),
        P("narrow", "wide"),
        P("narrow", "wide"),
        P("narrow", "wide"),
        P(None, "wide"),
        P("narrow", "wide"),
        P("wide"),
        P("wide", "narrow"),
        P("wide", "narrow"),
        P("narrow"),
        P(None, "narrow"),
        P(None, "narrow"),
        P(),
        P(),
        P(),
    )
    out_specs = (P("wide", "narrow"), P(None, "narrow", None, "wide"))
    ringed = mesh.shape["wide"] == 2 * CHIPS and mesh.shape["narrow"] == 2
    local = local_ring if ringed else local_generic
    return jax.shard_map(local, mesh=mesh, in_specs=in_specs, out_specs=out_specs, check_vma=False)
```
